32 devices in a mesh: group: 8 (over z, y), expert: 4 (over x, core).
Axes of the slice: x: 2, y: 2, z: 4, core: 2. Of those that a mesh axis runs over, the one named last changes fastest.
Arguments:
- tokens: bfloat16 [2, 2560, 2048], P(None, ('group', 'expert')), may hold values from -6 to 6
- cotangent: bfloat16 [2, 2560, 2048], P(None, ('group', 'expert')), may hold values from -6 to 6
- gain_attn: float32 [2048], replicated, may hold values from 0.5 to 1.5
- gain_mlp: float32 [2048], replicated, may hold values from 0.5 to 1.5
- w_kv: bfloat16 [2048, 4096], P(('group', 'expert')), may hold values from -0.125 to 0.125
- w_query: bfloat16 [4, 2048, 2048], P('expert', 'group'), may hold values from -0.125 to 0.125
- w_out: bfloat16 [4, 2048, 2048], P('expert', 'group'), may hold values from -1 to 1
- w_gate_up: bfloat16 [4, 2048, 11264], P('expert', 'group'), may hold values from -0.125 to 0.125
- w_down: bfloat16 [4, 5632, 2048], P('expert', 'group'), may hold values from -0.078125 to 0.078125
- att_routes: int32 [2, 2560, 2], P(None, 'group'), may hold values from 0 to 3, all different within a row; in each aligned block of 80 rows (0 to 79, 80 to 159, ..., all dimensions but the last counted through in order) at most 50 rows name the same one
- att_gates: float32 [2, 2560, 2], P(None, ('group', 'expert')), may hold values from 0.25 to 0.75
- mlp_routes: int32 [2, 2560, 2], P(None, 'group'), may hold values from 0 to 3, all different within a row; in each aligned block of 80 rows (0 to 79, 80 to 159, ..., all dimensions but the last counted through in order) at most 50 rows name the same one
- mlp_gates: float32 [2, 2560, 2], P(None, ('group', 'expert')), may hold values from 0.25 to 0.75
- blocks: int32 [2, 8, 320], P(None, 'group'), may hold values from 0 to 2, never falling along the last dimension, each value on 1 to 256 neighbouring positions
Outputs:
- output: bfloat16 [2, 2560, 2048], P(None, ('group', 'expert'))
- grad_input: bfloat16 [2, 2560, 2048], P(None, ('group', 'expert'))
- grad_gain_attn: float32 [2048], P(('group', 'expert'))
- grad_gain_mlp: float32 [2048], P(('group', 'expert'))
- grad_kv: float32 [2048, 4096], P(('group', 'expert'))
- grad_query: float32 [4, 2048, 2048], P('expert', 'group')
- grad_out: float32 [4, 2048, 2048], P('expert', 'group')
- grad_gate_up: float32 [4, 2048, 11264], P('expert', 'group')
- grad_down: float32 [4, 5632, 2048], P('expert', 'group')
The draws below stay inside these ranges and needn't reach their ends.
Inputs may be any that keep to these rules, and one draw needn't show every extreme that they name: `att_routes`: each row names 2 different experts; among the 80 rows of one device in one micro-batch no expert is named more than 50 times. `mlp_routes`: each row names 2 different experts; among the 80 rows of one device in one micro-batch no expert is named more than 50 times. `blocks`: block numbers never fall along a sequence; a block has at most 256 positions.
All inputs are finite; a program needn't handle non-finite values.
Results may differ from the reference program's by a relative error of at most 0.019.
Values may be sent and summed in bfloat16 or wider, within the bound.
A program may use at most 448 MiB of HBM per device.

```python
import math
import jax
import jax.numpy as jnp
import numpy as np
from jax import lax

D = 2048
HEADS = 16
HDIM = 128
FF = 5632
TOP_K = 2
BLOCK = 256
MICRO = 2
TOK_DEV = 80
HQ = 2048
EXPERTS = 4
CAP = 50
LENGTH = 320
TOKENS = 2560
N_GROUP = 8
N_EXPERT = 4


def steps_of(rng, extent, pieces, least, high):
    level = 1.0
    for position, shards_of in pieces:
        draws = jax.random.uniform(jax.random.fold_in(jax.random.fold_in(rng, 6), position), (shards_of,), jnp.float32, least / len(pieces), high / len(pieces))
        level = level * jnp.repeat(jnp.exp(draws), extent[position] // shards_of).reshape((-1,) + (1,) * (len(extent) - 1 - position))
    return level


def length_profile(number_of, total, bound, skew):
    portions = [(1 << 20) // math.isqrt(rank ** skew) + 1 for rank in range(2, number_of + 1)]
    spare, holding = total - bound - (number_of - 1), [1] * (number_of - 1)
    while spare > 0:
        candidates = [i for i in range(number_of - 1) if holding[i] < bound]
        mass, remaining = sum([portions[i] for i in candidates]), spare
        for i in candidates:
            addition = min(bound - holding[i], max(1, remaining * portions[i] // mass), spare)
            holding[i] = holding[i] + addition
            spare = spare - addition
    return np.array([bound] + holding)


def ragged_sizes(rng, count, total, reach, slope):
    if count == 2:
        one = jax.random.randint(rng, (), max(1, total - reach), min(reach, total - 1) + 1)
        return jnp.stack([one, total - one])
    sizes = jnp.asarray(length_profile(count, total, reach, slope), jnp.int32)
    pairs = (count - 1) // 2
    source_of, sink = sizes[1:1 + 2 * pairs:2], sizes[2:2 + 2 * pairs:2]
    margin = jnp.minimum(source_of - 1, reach - sink)
    shifted = jax.random.randint(jax.random.fold_in(rng, 1), (pairs,), 0, 1 << 20) % (margin + 1)
    sizes = sizes.at[1:1 + 2 * pairs:2].set(source_of - shifted).at[2:2 + 2 * pairs:2].set(sink + shifted)
    return sizes[jax.random.permutation(jax.random.fold_in(rng, 2), count)]


def assign_block(own_key, own, number, rows, count, top, limit, slope):
    ranking = jax.random.permutation(own_key, count)
    heavy_load, usual = shares(count, rows * top, limit, slope, True), shares(count, rows * top, limit, slope, False)
    places = jnp.arange(count)

    def named(sizes, turn):
        used = int((sizes > 0).sum())
        fixed = max(1, used // 4)
        shifted = fixed + (places - fixed + turn * (used - fixed)) % max(1, count - fixed)
        return jnp.zeros((count,), jnp.int32).at[ranking[jnp.where(places < fixed, places, shifted)]].set(jnp.asarray(sizes, jnp.int32))

    sizes = jnp.where(number % 4 == 0, named(heavy_load, number // 4), named(usual, number - number // 4 - 1))
    mixed = jax.random.permutation(jax.random.fold_in(own, 3), count)
    giver, taker = mixed[0:count // 2 * 2:2], mixed[1:count // 2 * 2:2]
    room = jnp.minimum(sizes[giver] - 1, limit - sizes[taker]) // 2
    room = jnp.where((giver == ranking[0]) | (taker == ranking[0]) | (sizes[taker] == 0), 0, jnp.maximum(room, 0))
    shifted = jax.random.randint(jax.random.fold_in(own, 4), (count // 2,), 0, 1 << 20) % (room + 1)
    sizes = sizes.at[giver].add(-shifted).at[taker].add(shifted)
    members = jnp.searchsorted(jnp.cumsum(sizes), jnp.arange(rows * top), side="right").astype(jnp.int32)
    listing = members.reshape(top, rows).T
    listing = listing[jax.random.permutation(jax.random.fold_in(own, 1), rows)]
    turn = jax.random.randint(jax.random.fold_in(own, 2), (rows, 1), 0, top)
    return jnp.take_along_axis(listing, (jnp.arange(top)[None, :] + turn) % top, axis=1)


def shares(count, total, most, skew, full):
    portions = [(1 << 20) // math.isqrt(standing ** skew) + 1 for standing in range(1, count + 1)]
    largest = most if full else min(most, max(-(-total // count), total * portions[0] // sum(portions)))
    least = 1 if total - largest >= count - 1 else 0
    given, surplus = [largest] + [least] * (count - 1), total - largest - least * (count - 1)
    while surplus > 0:
        free = [i for i in range(1, count) if given[i] < largest] or [i for i in range(1, count) if given[i] < most]
        pool, left = sum([portions[i] for i in free]), surplus
        for i in free:
            addition = min(most - given[i], max(1, left * portions[i] // pool), surplus)
            given[i] = given[i] + addition
            surplus = surplus - addition
    return np.array(given)


def centred(key, dims, deviation, limit, shards=(), kind=jnp.bfloat16):
    entries = deviation * jax.random.normal(key, dims, jnp.float32)
    if shards:
        entries = entries * steps_of(key, dims, shards, -0.22, 0.18)
    return jnp.clip(entries, -limit, limit).astype(kind)


def setup_inputs(seed: int = 0) -> dict:
    key_list = jax.random.split(jax.random.key(seed), 15)
    tokens = centred(key_list[0], (MICRO, TOKENS, D), 1.0, 6.0, ((1, 32),))
    cotangent = centred(key_list[1], (MICRO, TOKENS, D), 1.0, 6.0, ((1, 32),))
    gain_attn = jnp.clip(1.0 + 0.1 * jax.random.normal(key_list[2], (D,), jnp.float32), 0.5, 1.5)
    gain_mlp = jnp.clip(1.0 + 0.1 * jax.random.normal(key_list[3], (D,), jnp.float32), 0.5, 1.5)
    w_kv = centred(key_list[4], (D, 2 * HQ), D ** -0.5, 0.125, ((0, 32),))
    w_query = centred(key_list[5], (EXPERTS, D, HQ), D ** -0.5, 0.125, ((0, 4), (1, 8)))
    w_out = centred(key_list[6], (EXPERTS, HQ, D), (HQ // 64) ** -0.5, 1.0, ((0, 4), (1, 8)))
    w_gate_up = centred(key_list[7], (EXPERTS, D, 2 * FF), D ** -0.5, 0.125, ((0, 4), (1, 8)))
    w_down = centred(key_list[8], (EXPERTS, FF, D), FF ** -0.5, 0.078125, ((0, 4), (1, 8)))
    att_routes_keys = jax.random.split(jax.random.fold_in(key_list[9], 1), MICRO * TOKENS // TOK_DEV)
    att_routes_turns = jax.random.permutation(jax.random.fold_in(key_list[9], 3), MICRO * TOKENS // TOK_DEV)
    att_routes = jax.vmap(lambda own, number: assign_block(jax.random.fold_in(key_list[9], 2), own, number, TOK_DEV, EXPERTS, TOP_K, CAP, 2))(att_routes_keys, att_routes_turns).reshape((MICRO, TOKENS, TOP_K))
    att_gates = jnp.clip(0.25 + 0.5 * jax.random.uniform(key_list[10], (MICRO, TOKENS, TOP_K), jnp.float32) ** steps_of(key_list[10], (MICRO, TOKENS, TOP_K), ((1, 32),), -0.2, 0.2), 0.25, 0.75)
    mlp_routes_keys = jax.random.split(jax.random.fold_in(key_list[11], 1), MICRO * TOKENS // TOK_DEV)
    mlp_routes_turns = jax.random.permutation(jax.random.fold_in(key_list[11], 3), MICRO * TOKENS // TOK_DEV)
    mlp_routes = jax.vmap(lambda own, number: assign_block(jax.random.fold_in(key_list[11], 2), own, number, TOK_DEV, EXPERTS, TOP_K, CAP, 2))(mlp_routes_keys, mlp_routes_turns).reshape((MICRO, TOKENS, TOP_K))
    mlp_gates = jnp.clip(0.25 + 0.5 * jax.random.uniform(key_list[12], (MICRO, TOKENS, TOP_K), jnp.float32) ** steps_of(key_list[12], (MICRO, TOKENS, TOP_K), ((1, 32),), -0.2, 0.2), 0.25, 0.75)
    blocks = jax.vmap(lambda own: jnp.searchsorted(jnp.cumsum(ragged_sizes(own, LENGTH // BLOCK + 2, LENGTH, BLOCK, 2)), jnp.arange(LENGTH), side="right"))(jax.random.split(key_list[13], MICRO * N_GROUP)).reshape((MICRO, N_GROUP, LENGTH)).astype(jnp.int32)
    return dict(tokens=tokens, cotangent=cotangent, gain_attn=gain_attn, gain_mlp=gain_mlp, w_kv=w_kv, w_query=w_query, w_out=w_out, w_gate_up=w_gate_up, w_down=w_down, att_routes=att_routes, att_gates=att_gates, mlp_routes=mlp_routes, mlp_gates=mlp_gates, blocks=blocks)


@jax.custom_vjp
def low(v):
    return lax.optimization_barrier(v.astype(jnp.bfloat16)).astype(jnp.float32)

@jax.custom_vjp
def low_back(v):
    return v

def low_keep(v):
    return (low(v), None)

def low_pass(kept, grad):
    return (grad,)

def back_keep(v):
    return (v, None)

def back_low(kept, grad):
    return (low(grad),)
low.defvjp(low_keep, low_pass)
low_back.defvjp(back_keep, back_low)
EPS = 1e-06
HIGH = lax.Precision.HIGHEST

def angles(positions):
    half = HDIM // 2
    freq = 10000.0 ** (-jnp.arange(half).astype(jnp.float32) / half)
    turn = positions.astype(jnp.float32)[:, None] * freq[None, :]
    return (jnp.cos(turn), jnp.sin(turn))

def rotate(values, cosine, sine):
    count = values.shape[0]
    split = values.reshape(count, HEADS, 2, HDIM // 2)
    first = split[:, :, 0]
    second = split[:, :, 1]
    cosine = cosine[:, None, :]
    sine = sine[:, None, :]
    turned = jnp.stack([first * cosine - second * sine, second * cosine + first * sine], axis=2)
    return turned.reshape(count, HEADS * HDIM)

def routing(routes, block_ids):
    per = routes.reshape(N_EXPERT, TOK_DEV, TOP_K)
    flat = per.reshape(N_EXPERT, TOK_DEV * TOP_K)
    ids = jnp.arange(N_EXPERT).astype(jnp.int32)
    onehot = (flat[:, :, None] == ids[None, None, :]).astype(jnp.int32)
    before = jnp.cumsum(onehot, axis=1) - onehot
    slots = lax.optimization_barrier(jnp.sum(before * onehot, axis=2)).reshape(N_EXPERT, TOK_DEV, TOP_K)
    places = jnp.arange(CAP).astype(jnp.int32)
    hits = ((per[None, :, None] == ids[:, None, None, None, None]) & (slots[None, :, None] == places[None, None, :, None, None])).astype(jnp.int32)
    count = N_EXPERT * CAP
    spots = jnp.arange(LENGTH).astype(jnp.int32).reshape(1, N_EXPERT, 1, TOK_DEV, 1)
    marks = block_ids.reshape(1, N_EXPERT, 1, TOK_DEV, 1)
    valid = lax.optimization_barrier(jnp.sum(hits, axis=(3, 4))).reshape(N_EXPERT, count)
    row_pos = lax.optimization_barrier(jnp.sum(hits * spots, axis=(3, 4))).reshape(N_EXPERT, count)
    row_block = lax.optimization_barrier(jnp.sum(hits * marks, axis=(3, 4))).reshape(N_EXPERT, count) + (1 - valid) * LENGTH
    diagonal = jnp.eye(N_EXPERT, dtype=jnp.int32)
    select = hits[:, :, :, None] * diagonal[None, :, None, :, None, None]
    select = select.reshape(N_EXPERT, count, LENGTH * TOP_K).astype(jnp.float32)
    return (select, row_pos, row_block)

def layer(x, params, att_table, att_gates, mlp_table, mlp_gates, block_ids):
    gain_attn, gain_mlp, w_kv, w_query, w_out, w_gate_up, w_down = params
    att_select, att_pos, att_block = att_table
    mlp_select = mlp_table[0]
    scale = lax.rsqrt(lax.optimization_barrier(jnp.mean(x * x, axis=1, keepdims=True)) + EPS)
    normed = low(x * scale * gain_attn)
    cos_keys, sin_keys = angles(jnp.arange(LENGTH))
    mixed = low_back(jnp.dot(normed, w_kv, precision=HIGH))
    keys = low(rotate(mixed[:, :HQ], cos_keys, sin_keys)).reshape(LENGTH, HEADS, HDIM)
    values = low(mixed[:, HQ:]).reshape(LENGTH, HEADS, HDIM)
    pairs = jnp.stack([low_back(normed) for slot in range(TOP_K)], axis=1).reshape(LENGTH * TOP_K, D)
    returned = jnp.zeros((LENGTH * TOP_K, D), jnp.float32)
    for expert in range(N_EXPERT):
        rows = jnp.dot(att_select[expert], pairs, precision=HIGH)
        query = low_back(jnp.dot(rows, w_query[expert], precision=HIGH))
        cos_rows, sin_rows = angles(att_pos[expert])
        query = low(rotate(query, cos_rows, sin_rows)).reshape(N_EXPERT * CAP, HEADS, HDIM)
        raw = low_back(jnp.einsum('rhd,khd->hrk', query, keys, precision=HIGH))
        visible = block_ids[None, None, :] <= att_block[expert][None, :, None]
        scores = jnp.where(visible, raw * HDIM ** (-0.5), -1e+30)
        top = lax.optimization_barrier(jnp.max(scores, axis=2, keepdims=True))
        powers = jnp.exp(scores - top)
        probs = low(powers / lax.optimization_barrier(jnp.sum(powers, axis=2, keepdims=True)))
        attended = jnp.einsum('hrk,khd->rhd', probs, values, precision=HIGH).reshape(N_EXPERT * CAP, HQ)
        attended = low(low_back(attended))
        result = low(low_back(jnp.dot(attended, w_out[expert], precision=HIGH)))
        returned = returned + jnp.dot(att_select[expert].T, result, precision=HIGH)
    returned = returned.reshape(LENGTH, TOP_K, D)
    middle = x + lax.optimization_barrier(jnp.sum(att_gates[:, :, None] * returned, axis=1))
    scale_two = lax.rsqrt(lax.optimization_barrier(jnp.mean(middle * middle, axis=1, keepdims=True)) + EPS)
    normed_two = low(middle * scale_two * gain_mlp)
    pairs_two = jnp.stack([low_back(normed_two) for slot in range(TOP_K)], axis=1).reshape(LENGTH * TOP_K, D)
    returned_two = jnp.zeros((LENGTH * TOP_K, D), jnp.float32)
    for expert in range(N_EXPERT):
        rows = jnp.dot(mlp_select[expert], pairs_two, precision=HIGH)
        both = low_back(jnp.dot(rows, w_gate_up[expert], precision=HIGH))
        gate = both[:, :FF]
        up = both[:, FF:]
        hidden = low(gate / (1.0 + jnp.exp(-gate)) * up)
        result = low(low_back(jnp.dot(hidden, w_down[expert], precision=HIGH)))
        returned_two = returned_two + jnp.dot(mlp_select[expert].T, result, precision=HIGH)
    returned_two = returned_two.reshape(LENGTH, TOP_K, D)
    return middle + lax.optimization_barrier(jnp.sum(mlp_gates[:, :, None] * returned_two, axis=1))

def reference(tokens, cotangent, gain_attn, gain_mlp, w_kv, w_query, w_out, w_gate_up, w_down, att_routes, att_gates, mlp_routes, mlp_gates, blocks):
    count = MICRO * N_GROUP
    items = (tokens.astype(jnp.float32).reshape(count, LENGTH, D), cotangent.astype(jnp.float32).reshape(count, LENGTH, D), att_routes.reshape(count, LENGTH, TOP_K), att_gates.reshape(count, LENGTH, TOP_K), mlp_routes.reshape(count, LENGTH, TOP_K), mlp_gates.reshape(count, LENGTH, TOP_K), blocks.reshape(count, LENGTH))
    params = (gain_attn.astype(jnp.float32), gain_mlp.astype(jnp.float32), w_kv.astype(jnp.float32), w_query.astype(jnp.float32), w_out.astype(jnp.float32), w_gate_up.astype(jnp.float32), w_down.astype(jnp.float32))

    def step(totals, item):
        inputs, upstream, a_routes, a_gates, m_routes, m_gates, block_ids = item
        att_table = routing(a_routes, block_ids)
        mlp_table = routing(m_routes, block_ids)

        def forward(values, weights):
            return layer(values, weights, att_table, a_gates, mlp_table, m_gates, block_ids)
        result, pullback = jax.vjp(forward, inputs, params)
        input_grad, param_grads = pullback(upstream)
        totals = jax.tree.map(lambda first, second: first + second, totals, param_grads)
        return (totals, (result, input_grad))
    zeros = jax.tree.map(jnp.zeros_like, params)
    totals, (results, input_grads) = lax.scan(step, zeros, items)
    output = results.reshape(MICRO, TOKENS, D).astype(jnp.bfloat16)
    grad_input = input_grads.reshape(MICRO, TOKENS, D).astype(jnp.bfloat16)
    return (output, grad_input, totals[0], totals[1], totals[2], totals[3], totals[4], totals[5], totals[6])
```

```python
import functools

import jax
import jax.numpy as jnp
from jax import lax
from jax.experimental import pallas as pl
from jax.experimental.pallas import tpu as pltpu
from jax.sharding import PartitionSpec as P

HEADS = 16
HDIM = 128
CAP = 50


EPS = 1e-06
HIGH = lax.Precision.HIGHEST


def angles(positions):
    half = HDIM // 2
    freq = 10000.0 ** (-jnp.arange(half, dtype=jnp.float32) / half)
    turn = positions.astype(jnp.float32)[:, None] * freq[None, :]
    return (jnp.cos(turn), jnp.sin(turn))


def rotate(values, cosine, sine):
    count = values.shape[0]
    split = values.reshape(count, HEADS, 2, HDIM // 2)
    first = split[:, :, 0]
    second = split[:, :, 1]
    cosine = cosine[:, None, :]
    sine = sine[:, None, :]
    turned = jnp.stack([first * cosine - second * sine, second * cosine + first * sine], axis=2)
    return turned.reshape(count, HEADS * HDIM)


def routing(routes, gates, block_ids, owner, experts):
    local = routes.shape[0] // experts
    per = routes.reshape(experts, local, routes.shape[1])
    flat = per.reshape(experts, -1)
    ids = jnp.arange(experts, dtype=jnp.int32)
    onehot = (flat[:, :, None] == ids[None, None, :]).astype(jnp.int32)
    before = jnp.cumsum(onehot, axis=1) - onehot
    slots = jnp.sum(before * onehot, axis=2).reshape(per.shape)
    places = jnp.arange(CAP, dtype=jnp.int32)
    own_ids = lax.dynamic_index_in_dim(per, owner, 0, keepdims=False)
    own_slots = lax.dynamic_index_in_dim(slots, owner, 0, keepdims=False)
    sent = (
        (own_ids[None, None] == ids[:, None, None, None])
        & (own_slots[None, None] == places[None, :, None, None])
    ).astype(jnp.float32)
    pick = jnp.sum(sent, axis=3)
    weighted = jnp.sum(sent * gates[None, None], axis=3)
    arrived = ((per == owner)[:, None] & (slots[:, None] == places[None, :, None, None])).astype(
        jnp.int32
    )
    length = experts * local
    spots = jnp.arange(length, dtype=jnp.int32).reshape(experts, 1, local, 1)
    marks = block_ids.reshape(experts, 1, local, 1)
    valid = jnp.sum(arrived, axis=(2, 3)).reshape(-1)
    row_pos = jnp.sum(arrived * spots, axis=(2, 3)).reshape(-1)
    row_block = jnp.sum(arrived * marks, axis=(2, 3)).reshape(-1) + (1 - valid) * length
    return (pick, weighted, row_pos, row_block)


def score_block(queries, keys, row_block, key_block):
    count = queries.shape[0]
    raw = jnp.einsum(
        "rhd,khd->hrk",
        queries.reshape(count, HEADS, HDIM),
        keys.reshape(keys.shape[0], HEADS, HDIM),
        preferred_element_type=jnp.float32,
    )
    visible = key_block[None, None, :] <= row_block[None, :, None]
    return jnp.where(visible, raw * HDIM ** (-0.5), -1e30)


def spread(pick, normed):
    return jnp.einsum(
        "ect,td->ecd", pick.astype(jnp.bfloat16), normed, preferred_element_type=jnp.float32
    ).astype(jnp.bfloat16)


def collect(weights, arrived):
    return jnp.einsum("ect,ecd->td", weights, arrived.astype(jnp.float32), precision=HIGH)


def joined_rows(store, chosen, name):
    return jnp.concatenate([store[name][index] for index in chosen], axis=0)


def expert_reduce(store, chosen):
    pairs = (
        ("rows", "query_grad"),
        ("attended", "result_grad"),
        ("rows_two", "both_grad"),
        ("hidden", "down_grad"),
    )
    groups = lax.axis_size("group")
    results = []
    for left_name, right_name in pairs:
        left = joined_rows(store, chosen, left_name)
        right = joined_rows(store, chosen, right_name)

        def term(start, count, left=left, right=right):
            return jnp.einsum("rd,rf->df", left, right, preferred_element_type=jnp.float32)

        shard = lax.psum_scatter(
            term(jnp.int32(0), lax.axis_size("group") * (left.shape[1] // groups)).astype(
                jnp.bfloat16
            ),
            "group",
            scatter_dimension=0,
            tiled=True,
        ).astype(jnp.float32)
        results.append(shard[None])
    return tuple(results)


def reduce_all(store, chosen):
    expert_parts = expert_reduce(store, chosen)
    shared_term = jnp.einsum(
        "td,tf->df",
        joined_rows(store, chosen, "normed"),
        joined_rows(store, chosen, "mixed_grad"),
        preferred_element_type=jnp.float32,
    )
    gain_first = jnp.sum(joined_rows(store, chosen, "gain_first"), axis=0)
    gain_second = jnp.sum(joined_rows(store, chosen, "gain_second"), axis=0)
    shared_parts = (
        lax.psum_scatter(shared_term, ("group", "expert"), scatter_dimension=0, tiled=True),
        lax.psum_scatter(gain_first, ("group", "expert"), scatter_dimension=0, tiled=True),
        lax.psum_scatter(gain_second, ("group", "expert"), scatter_dimension=0, tiled=True),
    )
    return tuple(expert_parts) + tuple(shared_parts)


def on_device(
    tokens,
    cotangent,
    gain_attn,
    gain_mlp,
    w_kv,
    w_query,
    w_out,
    w_gate_up,
    w_down,
    att_routes,
    att_gates,
    mlp_routes,
    mlp_gates,
    blocks,
):
    experts = lax.axis_size("expert")
    owner = lax.axis_index("expert")
    shared_full = lax.all_gather(w_kv, ("group", "expert"), axis=0, tiled=True)
    gathered = (
        lax.all_gather(w_query, "group", axis=1, tiled=True),
        lax.all_gather(w_out, "group", axis=1, tiled=True),
        lax.all_gather(w_gate_up, "group", axis=1, tiled=True),
        lax.all_gather(w_down, "group", axis=1, tiled=True),
    )
    query_full = gathered[0][0]
    output_full = gathered[1][0]
    gate_up_full = gathered[2][0]
    down_full = gathered[3][0]
    micro = tokens.shape[0]
    local = tokens.shape[1]
    model = tokens.shape[2]
    length = local * experts
    width = HEADS * HDIM
    hidden_width = gate_up_full.shape[1] // 2
    own_cos, own_sin = angles(owner * local + jnp.arange(local, dtype=jnp.int32))
    names = (
        "rows",
        "query_grad",
        "attended",
        "result_grad",
        "rows_two",
        "both_grad",
        "hidden",
        "down_grad",
        "normed",
        "mixed_grad",
        "gain_first",
        "gain_second",
    )
    store = {name: [] for name in names}
    outputs = []
    input_grads = []
    for index in range(micro):
        inputs = tokens[index].astype(jnp.float32)
        block_ids = blocks[index, 0]
        att_pick, att_weight, row_pos, row_block = routing(
            att_routes[index], att_gates[index], block_ids, owner, experts
        )
        mlp_pick, mlp_weight, unused_pos, unused_block = routing(
            mlp_routes[index], mlp_gates[index], block_ids, owner, experts
        )
        scale = lax.rsqrt(jnp.mean(inputs * inputs, axis=1, keepdims=True) + EPS)
        normed = (inputs * scale * gain_attn).astype(jnp.bfloat16)
        mixed = jnp.dot(normed, shared_full, preferred_element_type=jnp.float32)
        keys_here = rotate(mixed[:, :width], own_cos, own_sin).astype(jnp.bfloat16)
        local_kv = jnp.concatenate([keys_here, mixed[:, width:].astype(jnp.bfloat16)], axis=1)
        sequence_kv = lax.all_gather(local_kv, "expert", axis=0, tiled=True)
        keys = sequence_kv[:, :width]
        values = sequence_kv[:, width:].reshape(length, HEADS, HDIM)
        rows = lax.all_to_all(
            spread(att_pick, normed), "expert", split_axis=0, concat_axis=0, tiled=True
        ).reshape(-1, model)
        row_cos, row_sin = angles(row_pos)
        queries = rotate(
            jnp.dot(rows, query_full, preferred_element_type=jnp.float32), row_cos, row_sin
        ).astype(jnp.bfloat16)
        scores = score_block(queries, keys, row_block, block_ids)
        top = jnp.max(scores, axis=2, keepdims=True)
        powers = jnp.exp(scores - top)
        total = jnp.sum(powers, axis=2, keepdims=True)
        log_total = top + jnp.log(total)
        probs = (powers / total).astype(jnp.bfloat16)
        attended = jnp.einsum("hrk,khd->rhd", probs, values, preferred_element_type=jnp.float32)
        attended = attended.reshape(-1, width).astype(jnp.bfloat16)
        result = jnp.dot(attended, output_full, preferred_element_type=jnp.float32).astype(
            jnp.bfloat16
        )
        back = lax.all_to_all(
            result.reshape(experts, CAP, model), "expert", split_axis=0, concat_axis=0, tiled=True
        )
        middle = inputs + collect(att_weight, back)
        scale_two = lax.rsqrt(jnp.mean(middle * middle, axis=1, keepdims=True) + EPS)
        normed_two = (middle * scale_two * gain_mlp).astype(jnp.bfloat16)
        rows_two = lax.all_to_all(
            spread(mlp_pick, normed_two), "expert", split_axis=0, concat_axis=0, tiled=True
        ).reshape(-1, model)
        both = jnp.dot(rows_two, gate_up_full, preferred_element_type=jnp.float32)
        gate = both[:, :hidden_width]
        up = both[:, hidden_width:]
        sigma = 1.0 / (1.0 + jnp.exp(-gate))
        hidden = (gate * sigma * up).astype(jnp.bfloat16)
        result_two = jnp.dot(hidden, down_full, preferred_element_type=jnp.float32).astype(
            jnp.bfloat16
        )
        back_two = lax.all_to_all(
            result_two.reshape(experts, CAP, model),
            "expert",
            split_axis=0,
            concat_axis=0,
            tiled=True,
        )
        final = middle + collect(mlp_weight, back_two)
        outputs.append(final.astype(jnp.bfloat16))
        upstream = cotangent[index].astype(jnp.float32)
        outgoing = jnp.einsum("ect,td->ecd", mlp_weight, upstream, precision=HIGH).astype(
            jnp.bfloat16
        )
        down_grad = lax.all_to_all(
            outgoing, "expert", split_axis=0, concat_axis=0, tiled=True
        ).reshape(-1, model)
        hidden_grad = jnp.einsum(
            "rd,fd->rf", down_grad, down_full, preferred_element_type=jnp.float32
        )
        slope = sigma * (1.0 + gate * (1.0 - sigma))
        both_grad = jnp.concatenate(
            [hidden_grad * up * slope, hidden_grad * gate * sigma], axis=1
        ).astype(jnp.bfloat16)
        row_grad_two = jnp.einsum(
            "rf,df->rd", both_grad, gate_up_full, preferred_element_type=jnp.float32
        ).astype(jnp.bfloat16)
        returned_two = lax.all_to_all(
            row_grad_two.reshape(experts, CAP, model),
            "expert",
            split_axis=0,
            concat_axis=0,
            tiled=True,
        )
        normed_two_grad = collect(mlp_pick, returned_two)
        scaled_two = normed_two_grad * gain_mlp
        gain_second = jnp.sum(normed_two_grad * middle * scale_two, axis=0, keepdims=True)
        middle_grad = (
            upstream
            + scale_two * scaled_two
            - middle * scale_two**3 * jnp.mean(scaled_two * middle, axis=1, keepdims=True)
        )
        outgoing_att = jnp.einsum("ect,td->ecd", att_weight, middle_grad, precision=HIGH).astype(
            jnp.bfloat16
        )
        result_grad = lax.all_to_all(
            outgoing_att, "expert", split_axis=0, concat_axis=0, tiled=True
        ).reshape(-1, model)
        attended_grad = jnp.einsum(
            "rd,fd->rf", result_grad, output_full, preferred_element_type=jnp.float32
        ).astype(jnp.bfloat16)
        again = jnp.exp(score_block(queries, keys, row_block, block_ids) - log_total)
        heads_grad = attended_grad.reshape(-1, HEADS, HDIM)
        value_grad = jnp.einsum(
            "hrk,rhd->khd",
            again.astype(jnp.bfloat16),
            heads_grad,
            preferred_element_type=jnp.float32,
        )
        prob_grad = jnp.einsum(
            "rhd,khd->hrk", heads_grad, values, preferred_element_type=jnp.float32
        )
        inner = jnp.sum(again * prob_grad, axis=2, keepdims=True)
        raw_grad = (again * (prob_grad - inner) * HDIM ** (-0.5)).astype(jnp.bfloat16)
        query_grad = jnp.einsum(
            "hrk,khd->rhd",
            raw_grad,
            keys.reshape(length, HEADS, HDIM),
            preferred_element_type=jnp.float32,
        ).reshape(-1, width)
        query_grad = rotate(query_grad, row_cos, -row_sin).astype(jnp.bfloat16)
        key_grad = jnp.einsum(
            "hrk,rhd->khd",
            raw_grad,
            queries.reshape(-1, HEADS, HDIM),
            preferred_element_type=jnp.float32,
        ).reshape(length, width)
        row_grad = jnp.einsum(
            "rf,df->rd", query_grad, query_full, preferred_element_type=jnp.float32
        ).astype(jnp.bfloat16)
        returned = lax.all_to_all(
            row_grad.reshape(experts, CAP, model), "expert", split_axis=0, concat_axis=0, tiled=True
        )
        kv_grad = lax.psum_scatter(
            jnp.concatenate([key_grad, value_grad.reshape(length, width)], axis=1).astype(
                jnp.bfloat16
            ),
            "expert",
            scatter_dimension=0,
            tiled=True,
        ).astype(jnp.float32)
        mixed_grad = jnp.concatenate(
            [rotate(kv_grad[:, :width], own_cos, -own_sin), kv_grad[:, width:]], axis=1
        ).astype(jnp.bfloat16)
        normed_grad = collect(att_pick, returned) + jnp.einsum(
            "tf,df->td", mixed_grad, shared_full, preferred_element_type=jnp.float32
        )
        scaled = normed_grad * gain_attn
        gain_first = jnp.sum(normed_grad * inputs * scale, axis=0, keepdims=True)
        input_grad = (
            middle_grad
            + scale * scaled
            - inputs * scale**3 * jnp.mean(scaled * inputs, axis=1, keepdims=True)
        )
        input_grads.append(input_grad.astype(jnp.bfloat16))
        kept = (
            rows,
            query_grad,
            attended,
            result_grad,
            rows_two,
            both_grad,
            hidden,
            down_grad,
            normed,
            mixed_grad,
            gain_first,
            gain_second,
        )
        for name, value in zip(names, kept):
            store[name].append(value)
    reduced = reduce_all(store, list(range(micro)))
    grad_query, grad_out, grad_gate_up, grad_down, grad_kv, grad_gain_attn, grad_gain_mlp = reduced
    return (
        jnp.stack(outputs, axis=0),
        jnp.stack(input_grads, axis=0),
        grad_gain_attn,
        grad_gain_mlp,
        grad_kv,
        grad_query,
        grad_out,
        grad_gate_up,
        grad_down,
    )


ZS, YS, XS, CS = 4, 2, 2, 2
SEQ = 320
F32 = jnp.float32
BF16 = jnp.bfloat16


def fits(mesh):
    return mesh.shape["group"] == ZS * YS and mesh.shape["expert"] == XS * CS


def group_move(value, move):
    pairs = []
    for z in range(ZS):
        for y in range(YS):
            to_z, to_y = move(z, y)
            pairs.append((z * YS + y, to_z * YS + to_y))
    return lax.ppermute(value, "group", pairs)


def z_move(value, step):
    return group_move(value, lambda z, y: ((z + step) % ZS, y))


def y_move(value):
    return group_move(value, lambda z, y: (z, 1 - y))


def x_move(value):
    return lax.ppermute(value, "expert", [(x * CS + c, (1 - x) * CS + c) for x in range(XS) for c in range(CS)])


def c_move(value):
    return lax.ppermute(value, "expert", [(x * CS + c, x * CS + 1 - c) for x in range(XS) for c in range(CS)])


def z_exchange(value):
    columns = [[z * YS + y for z in range(ZS)] for y in range(YS)]
    return lax.all_to_all(
        value, "group", split_axis=0, concat_axis=0, tiled=True, axis_index_groups=columns
    )


def gather_tokens(own):
    column = jnp.stack([own] + [z_move(own, -step) for step in range(1, ZS)], axis=0)
    plane = jnp.stack([column, x_move(column)], axis=1)
    plane = plane.reshape((ZS, XS * own.shape[0]) + own.shape[1:])
    return jnp.stack([plane, c_move(plane)], axis=0)


def reduce_tokens(other, mine):
    local = mine.shape[1] // XS
    total = mine.astype(F32) + c_move(other).astype(F32)
    arrived = x_move(total[:, local:].astype(BF16))
    total = total[:, :local] + arrived.astype(F32)
    result = total[0]
    for step in range(1, ZS):
        result = result + z_move(total[step].astype(BF16), step).astype(F32)
    return result


def merge(index, own, other, axis):
    return jnp.where(index == 0, jnp.stack([own, other], axis), jnp.stack([other, own], axis))


def take(value, index, axis):
    return lax.dynamic_index_in_dim(value, index, axis, keepdims=False)


def dot(left, right):
    return jnp.dot(left, right, preferred_element_type=F32)


def dot_t(left, right):
    return lax.dot_general(left, right, (((1,), (1,)), ((), ())), preferred_element_type=F32)


def dot_l(left, right):
    return lax.dot_general(left, right, (((0,), (0,)), ((), ())), preferred_element_type=F32)


def turned(value, cosine, sine):
    return value * cosine + pltpu.roll(value, HDIM // 2, 1) * sine


def masked_probs(query, key, row_block, key_block):
    scores = jnp.where(key_block <= row_block, dot_t(query, key) * HDIM ** (-0.5), -1e30)
    powers = jnp.exp(scores - jnp.max(scores, axis=1, keepdims=True))
    return powers / jnp.sum(powers, axis=1, keepdims=True)


def attend_kernel(qkv_ref, cos_ref, sin_ref, row_ref, key_ref, turned_ref, out_ref):
    cosine, sine = cos_ref[...], sin_ref[...]
    rows, width = cosine.shape[0], out_ref.shape[3]
    half = rows // 2
    for head in range(width // HDIM):
        parts = []
        for kind in range(3):
            span = slice(kind * width + head * HDIM, kind * width + (head + 1) * HDIM)
            value = qkv_ref[:, 0, :, span].reshape(rows, HDIM)
            if kind < 2:
                value = turned(value, cosine, sine)
            value = value.astype(BF16)
            turned_ref[:, 0, :, span] = value.reshape(2, half, HDIM)
            parts.append(value)
        query, key, value = parts
        probs = masked_probs(query, key, row_ref[0], key_ref[0]).astype(BF16)
        span = slice(head * HDIM, (head + 1) * HDIM)
        out_ref[:, 0, :, span] = dot(probs, value).astype(BF16).reshape(2, half, HDIM)


def attend(qkv, cosine, sine, row_blocks, key_blocks):
    cores, seqs, half, triple = qkv.shape
    width = triple // 3
    rows = cores * half
    return pl.pallas_call(
        attend_kernel,
        grid=(seqs,),
        in_specs=[
            pl.BlockSpec((cores, 1, half, triple), lambda k: (0, k, 0, 0)),
            pl.BlockSpec((rows, HDIM), lambda k: (0, 0)),
            pl.BlockSpec((rows, HDIM), lambda k: (0, 0)),
            pl.BlockSpec((1, rows, 1), lambda k: (k, 0, 0)),
            pl.BlockSpec((1, 1, rows), lambda k: (k, 0, 0)),
        ],
        out_specs=[
            pl.BlockSpec((cores, 1, half, triple), lambda k: (0, k, 0, 0)),
            pl.BlockSpec((cores, 1, half, width), lambda k: (0, k, 0, 0)),
        ],
        out_shape=[
            jax.ShapeDtypeStruct(qkv.shape, BF16),
            jax.ShapeDtypeStruct((cores, seqs, half, width), BF16),
        ],
        compiler_params=pltpu.CompilerParams(vmem_limit_bytes=40 << 20),
        cost_estimate=pl.CostEstimate(
            flops=4 * seqs * rows * rows * width,
            bytes_accessed=qkv.size * 6 + qkv.size,
            transcendentals=seqs * rows * rows * width // HDIM,
        ),
    )(qkv, cosine, sine, row_blocks, key_blocks)


def attend_back_kernel(turned_ref, grad_ref, cos_ref, sin_ref, row_ref, key_ref, out_ref):
    cosine, sine = cos_ref[...], -sin_ref[...]
    rows, width = cosine.shape[0], grad_ref.shape[3]
    half = rows // 2
    for head in range(width // HDIM):
        spans = [slice(kind * width + head * HDIM, kind * width + (head + 1) * HDIM) for kind in range(3)]
        query, key, value = [turned_ref[:, 0, :, span].reshape(rows, HDIM) for span in spans]
        grad = grad_ref[:, 0, :, spans[0]].reshape(rows, HDIM)
        probs = masked_probs(query, key, row_ref[0], key_ref[0])
        prob_grad = dot_t(grad, value)
        inner = jnp.sum(probs * prob_grad, axis=1, keepdims=True)
        raw_grad = (probs * (prob_grad - inner) * HDIM ** (-0.5)).astype(BF16)
        results = [
            turned(dot(raw_grad, key), cosine, sine),
            turned(dot_l(raw_grad, query), cosine, sine),
            dot_l(probs.astype(BF16), grad),
        ]
        for span, result in zip(spans, results):
            out_ref[:, 0, :, span] = result.astype(BF16).reshape(2, half, HDIM)


def attend_back(kept, grad, cosine, sine, row_blocks, key_blocks):
    cores, seqs, half, triple = kept.shape
    width = triple // 3
    rows = cores * half
    return pl.pallas_call(
        attend_back_kernel,
        grid=(seqs,),
        in_specs=[
            pl.BlockSpec((cores, 1, half, triple), lambda k: (0, k, 0, 0)),
            pl.BlockSpec((cores, 1, half, width), lambda k: (0, k, 0, 0)),
            pl.BlockSpec((rows, HDIM), lambda k: (0, 0)),
            pl.BlockSpec((rows, HDIM), lambda k: (0, 0)),
            pl.BlockSpec((1, rows, 1), lambda k: (k, 0, 0)),
            pl.BlockSpec((1, 1, rows), lambda k: (k, 0, 0)),
        ],
        out_specs=pl.BlockSpec((cores, 1, half, triple), lambda k: (0, k, 0, 0)),
        out_shape=jax.ShapeDtypeStruct(kept.shape, BF16),
        compiler_params=pltpu.CompilerParams(vmem_limit_bytes=40 << 20),
        cost_estimate=pl.CostEstimate(
            flops=10 * seqs * rows * rows * width,
            bytes_accessed=kept.size * 4 + grad.size * 2,
            transcendentals=seqs * rows * rows * width // HDIM,
        ),
    )(kept, grad, cosine, sine, row_blocks, key_blocks)


def columns_of(parts, kinds):
    width = parts.shape[2] // kinds
    return jnp.concatenate(
        [parts[z, :, kind * width : (kind + 1) * width] for kind in range(kinds) for z in range(ZS)], axis=1
    )


def fast_device(
    tokens,
    cotangent,
    gain_attn,
    gain_mlp,
    w_kv,
    w_query,
    w_out,
    w_gate_up,
    w_down,
    att_routes,
    att_gates,
    mlp_routes,
    mlp_gates,
    blocks,
):
    group, owner = lax.axis_index("group"), lax.axis_index("expert")
    y = group % YS
    x, core = owner // CS, owner % CS
    micro, local, model = tokens.shape
    wide = w_query.shape[2] // ZS
    hidden_width = w_gate_up.shape[2] // (2 * ZS)
    kv_rows = w_kv.shape[0]
    model_rows = w_query.shape[1]

    def own_rows(table):
        return lax.dynamic_slice_in_dim(table, owner * local, local, 0).astype(F32)

    columns = []
    for index in range(micro):
        columns += [own_rows(att_routes[index]), att_gates[index], own_rows(mlp_routes[index]), mlp_gates[index]]
        columns += [own_rows(blocks[index, 0][:, None])]
    table = gather_tokens(jnp.concatenate(columns, axis=1))
    table = table.reshape(CS, ZS, XS * local, micro, 9)

    positions = (
        (x ^ jnp.arange(XS)[None, :, None]) * CS + (core ^ jnp.arange(CS)[:, None, None])
    ) * local + jnp.arange(local)[None, None, :]
    cosine, sine = angles(positions.reshape(-1))
    cosine = jnp.concatenate([cosine, cosine], axis=1)
    sine = jnp.concatenate([-sine, sine], axis=1)

    kv_part = w_kv.reshape(kv_rows, 2, ZS, wide).transpose(2, 0, 1, 3).reshape(ZS, kv_rows, 2 * wide)
    kv_part = z_exchange(kv_part)
    kv_part = merge(y, kv_part, y_move(kv_part), 1)
    kv_part = merge(x, kv_part, x_move(kv_part), 2)
    kv_part = merge(core, kv_part, c_move(kv_part), 3)
    kv_part = kv_part.reshape(model, 2 * wide)
    query_part = z_exchange(w_query[0].reshape(model_rows, ZS, wide).transpose(1, 0, 2))
    query_part = merge(y, query_part, y_move(query_part), 1).reshape(model, wide)
    qkv_weight = jnp.concatenate([query_part, kv_part], axis=1)
    out_weight = merge(y, w_out[0], y_move(w_out[0]), 0).reshape(wide, model)
    down_weight = merge(y, w_down[0], y_move(w_down[0]), 0).reshape(hidden_width, model)
    gate_up = w_gate_up[0].reshape(model_rows, 2, ZS, hidden_width).transpose(2, 0, 1, 3)
    gate_up = z_exchange(gate_up.reshape(ZS, model_rows, 2 * hidden_width))
    gate_up = merge(y, gate_up, y_move(gate_up), 1).reshape(model, 2 * hidden_width)

    outputs, input_grads, kept = [], [], []
    before_mask = jnp.arange(SEQ)[:, None] < jnp.arange(SEQ)[None, :]
    for index in range(micro):
        part = table[:, :, :, index]
        att_weight = jnp.sum(jnp.where(part[..., 0:2] == owner, part[..., 2:4], 0.0), axis=-1)
        mlp_hit = jnp.any(part[..., 4:6] == owner, axis=-1)
        mlp_weight = jnp.sum(jnp.where(part[..., 4:6] == owner, part[..., 6:8], 0.0), axis=-1)
        seq_blocks = part[..., 8].transpose(1, 0, 2).reshape(ZS, -1).astype(jnp.int32)
        row_blocks, key_blocks = seq_blocks[:, :, None], seq_blocks[:, None, :]
        hit = mlp_hit.transpose(1, 0, 2).reshape(ZS, -1)
        before = jnp.einsum(
            "kt,tu->ku", hit.astype(BF16), before_mask.astype(BF16), preferred_element_type=F32
        ).astype(jnp.int32)
        places = jnp.arange(owner_cap(local))
        chosen = hit[:, None, :] & (before[:, None, :] == places[None, :, None])
        row_gate = jnp.sum(
            jnp.where(chosen, mlp_weight.transpose(1, 0, 2).reshape(ZS, 1, -1), 0.0), axis=2
        )
        select = chosen.astype(BF16).reshape(ZS, -1, CS, XS * local)
        halves = [select[:, :, half] for half in range(CS)]

        def to_rows(gathered, halves=halves):
            return sum(
                jnp.einsum("kru,kud->krd", halves[half], gathered[half], preferred_element_type=F32)
                for half in range(CS)
            )

        def to_tokens(rows, halves=halves):
            return [
                jnp.einsum("kru,krd->kud", halves[half], rows, preferred_element_type=F32).astype(BF16)
                for half in range(CS)
            ]

        inputs = tokens[index].astype(F32)
        upstream = cotangent[index].astype(F32)
        scale = lax.rsqrt(jnp.mean(inputs * inputs, axis=1, keepdims=True) + EPS)
        normed = gather_tokens((inputs * scale * gain_attn).astype(BF16))
        qkv = dot(normed.reshape(-1, model), qkv_weight).reshape(CS, ZS, XS * local, 3 * wide)
        turned_qkv, attended = attend(qkv, cosine, sine, row_blocks, key_blocks)
        result = [
            (dot(attended[half].reshape(-1, wide), out_weight) * att_weight[half].reshape(-1, 1))
            .astype(BF16)
            .reshape(ZS, XS * local, model)
            for half in range(CS)
        ]
        middle = inputs + reduce_tokens(result[1], result[0])
        scale_two = lax.rsqrt(jnp.mean(middle * middle, axis=1, keepdims=True) + EPS)
        normed_two = gather_tokens((middle * scale_two * gain_mlp).astype(BF16))
        cotangents = gather_tokens(cotangent[index])
        rows_two = to_rows(normed_two).astype(BF16).reshape(-1, model)
        down_grad = (to_rows(cotangents) * row_gate[:, :, None]).astype(BF16).reshape(-1, model)
        both = dot(rows_two, gate_up)
        gate, up = both[:, :hidden_width], both[:, hidden_width:]
        sigma = 1.0 / (1.0 + jnp.exp(-gate))
        hidden = (gate * sigma * up).astype(BF16)
        hidden_grad = dot_t(down_grad, down_weight)
        slope = sigma * (1.0 + gate * (1.0 - sigma))
        both_grad = jnp.concatenate(
            [hidden_grad * up * slope, hidden_grad * gate * sigma], axis=1
        ).astype(BF16)
        row_grad = dot_t(both_grad, gate_up).astype(BF16).reshape(ZS, -1, model)
        row_grad = to_tokens(row_grad)
        normed_two_grad = reduce_tokens(row_grad[1], row_grad[0])
        scaled_two = normed_two_grad * gain_mlp
        gain_second = jnp.sum(normed_two_grad * middle * scale_two, axis=0, keepdims=True)
        middle_grad = (
            upstream
            + scale_two * scaled_two
            - middle * scale_two**3 * jnp.mean(scaled_two * middle, axis=1, keepdims=True)
        )
        middle_grads = gather_tokens(middle_grad.astype(BF16))

        result_two = (dot(hidden, down_weight) * row_gate.reshape(-1, 1)).astype(BF16)
        result_two = to_tokens(result_two.reshape(ZS, -1, model))
        outputs.append((middle + reduce_tokens(result_two[1], result_two[0])).astype(BF16))

        result_grad = (middle_grads.astype(F32) * att_weight[..., None]).astype(BF16).reshape(-1, model)
        attended_grad = dot_t(result_grad, out_weight).astype(BF16).reshape(attended.shape)
        qkv_grad = attend_back(turned_qkv, attended_grad, cosine, sine, row_blocks, key_blocks)
        normed_part = [
            dot_t(qkv_grad[half].reshape(-1, 3 * wide), qkv_weight)
            .astype(BF16)
            .reshape(ZS, XS * local, model)
            for half in range(CS)
        ]
        normed_grad = reduce_tokens(normed_part[1], normed_part[0])
        scaled = normed_grad * gain_attn
        gain_first = jnp.sum(normed_grad * inputs * scale, axis=0, keepdims=True)
        input_grad = (
            middle_grad
            + scale * scaled
            - inputs * scale**3 * jnp.mean(scaled * inputs, axis=1, keepdims=True)
        )
        input_grads.append(input_grad.astype(BF16))
        kept.append(
            (
                rows_two,
                both_grad,
                hidden,
                down_grad,
                attended.reshape(-1, wide),
                result_grad,
                normed.reshape(-1, model),
                qkv_grad.reshape(-1, 3 * wide),
                gain_first,
                gain_second,
            )
        )

    def joined(place):
        return jnp.concatenate([entry[place] for entry in kept], axis=0)

    def halve(value, index, axis, move):
        return take(value, index, axis) + move(take(value, 1 - index, axis).astype(BF16)).astype(F32)

    grad_gate_up = dot_l(joined(0), joined(1)).reshape(ZS, YS, model_rows, 2 * hidden_width)
    grad_gate_up = z_exchange(halve(grad_gate_up, y, 1, y_move).astype(BF16)).astype(F32)
    grad_gate_up = columns_of(grad_gate_up, 2)[None]
    grad_down = dot_l(joined(2), joined(3)).reshape(YS, -1, model)
    grad_down = halve(grad_down, y, 0, y_move)[None]
    grad_out = dot_l(joined(4), joined(5)).reshape(YS, -1, model)
    grad_out = halve(grad_out, y, 0, y_move)[None]
    grad_qkv = dot_l(joined(6), joined(7))
    grad_query = grad_qkv[:, :wide].reshape(ZS, YS, model_rows, wide)
    grad_query = z_exchange(halve(grad_query, y, 1, y_move).astype(BF16)).astype(F32)
    grad_query = columns_of(grad_query, 1)[None]
    grad_kv = grad_qkv[:, wide:].reshape(ZS, YS, XS, CS, kv_rows, 2 * wide)
    grad_kv = halve(grad_kv, core, 3, c_move)
    grad_kv = halve(grad_kv, x, 2, x_move)
    grad_kv = z_exchange(halve(grad_kv, y, 1, y_move).astype(BF16)).astype(F32)
    grad_kv = columns_of(grad_kv, 2)
    gains = jnp.stack([jnp.sum(joined(8), axis=0), jnp.sum(joined(9), axis=0)], axis=0)
    for move in (c_move, x_move, y_move):
        gains = gains + move(gains)
    gains = gains + sum(z_move(gains, step) for step in range(1, ZS))
    devices = ZS * YS * XS * CS
    gains = take(gains.reshape(2, devices, model // devices), group * XS * CS + owner, 1)
    return (
        jnp.stack(outputs, axis=0),
        jnp.stack(input_grads, axis=0),
        gains[0],
        gains[1],
        grad_kv,
        grad_query,
        grad_out,
        grad_gate_up,
        grad_down,
    )


def owner_cap(local):
    return XS * CS * CAP


def solution(mesh):
    in_specs = (
        P(None, ("group", "expert"), None),
        P(None, ("group", "expert"), None),
        P(),
        P(),
        P(("group", "expert"), None),
        P("expert", "group", None),
        P("expert", "group", None),
        P("expert", "group", None),
        P("expert", "group", None),
        P(None, "group", None),
        P(None, ("group", "expert"), None),
        P(None, "group", None),
        P(None, ("group", "expert"), None),
        P(None, "group", None),
    )
    out_specs = (
        P(None, ("group", "expert"), None),
        P(None, ("group", "expert"), None),
        P(("group", "expert")),
        P(("group", "expert")),
        P(("group", "expert"), None),
        P("expert", "group", None),
        P("expert", "group", None),
        P("expert", "group", None),
        P("expert", "group", None),
    )
    body = fast_device if fits(mesh) else on_device
    return jax.shard_map(
        body, mesh=mesh, in_specs=in_specs, out_specs=out_specs, check_vma=False
    )
```

```python
import functools

import jax
import jax.numpy as jnp
from jax import lax
from jax.experimental import pallas as pl
from jax.experimental.pallas import tpu as pltpu
from jax.sharding import PartitionSpec as P

HEADS = 16
HDIM = 128
CAP = 50


EPS = 1e-06
HIGH = lax.Precision.HIGHEST


def angles(positions):
    half = HDIM // 2
    freq = 10000.0 ** (-jnp.arange(half, dtype=jnp.float32) / half)
    turn = positions.astype(jnp.float32)[:, None] * freq[None, :]
    return (jnp.cos(turn), jnp.sin(turn))


def rotate(values, cosine, sine):
    count = values.shape[0]
    split = values.reshape(count, HEADS, 2, HDIM // 2)
    first = split[:, :, 0]
    second = split[:, :, 1]
    cosine = cosine[:, None, :]
    sine = sine[:, None, :]
    turned = jnp.stack([first * cosine - second * sine, second * cosine + first * sine], axis=2)
    return turned.reshape(count, HEADS * HDIM)


def routing(routes, gates, block_ids, owner, experts):
    local = routes.shape[0] // experts
    per = routes.reshape(experts, local, routes.shape[1])
    flat = per.reshape(experts, -1)
    ids = jnp.arange(experts, dtype=jnp.int32)
    onehot = (flat[:, :, None] == ids[None, None, :]).astype(jnp.int32)
    before = jnp.cumsum(onehot, axis=1) - onehot
    slots = jnp.sum(before * onehot, axis=2).reshape(per.shape)
    places = jnp.arange(CAP, dtype=jnp.int32)
    own_ids = lax.dynamic_index_in_dim(per, owner, 0, keepdims=False)
    own_slots = lax.dynamic_index_in_dim(slots, owner, 0, keepdims=False)
    sent = (
        (own_ids[None, None] == ids[:, None, None, None])
        & (own_slots[None, None] == places[None, :, None, None])
    ).astype(jnp.float32)
    pick = jnp.sum(sent, axis=3)
    weighted = jnp.sum(sent * gates[None, None], axis=3)
    arrived = ((per == owner)[:, None] & (slots[:, None] == places[None, :, None, None])).astype(
        jnp.int32
    )
    length = experts * local
    spots = jnp.arange(length, dtype=jnp.int32).reshape(experts, 1, local, 1)
    marks = block_ids.reshape(experts, 1, local, 1)
    valid = jnp.sum(arrived, axis=(2, 3)).reshape(-1)
    row_pos = jnp.sum(arrived * spots, axis=(2, 3)).reshape(-1)
    row_block = jnp.sum(arrived * marks, axis=(2, 3)).reshape(-1) + (1 - valid) * length
    return (pick, weighted, row_pos, row_block)


def score_block(queries, keys, row_block, key_block):
    count = queries.shape[0]
    raw = jnp.einsum(
        "rhd,khd->hrk",
        queries.reshape(count, HEADS, HDIM),
        keys.reshape(keys.shape[0], HEADS, HDIM),
        preferred_element_type=jnp.float32,
    )
    visible = key_block[None, None, :] <= row_block[None, :, None]
    return jnp.where(visible, raw * HDIM ** (-0.5), -1e30)


def spread(pick, normed):
    return jnp.einsum(
        "ect,td->ecd", pick.astype(jnp.bfloat16), normed, preferred_element_type=jnp.float32
    ).astype(jnp.bfloat16)


def collect(weights, arrived):
    return jnp.einsum("ect,ecd->td", weights, arrived.astype(jnp.float32), precision=HIGH)


def joined_rows(store, chosen, name):
    return jnp.concatenate([store[name][index] for index in chosen], axis=0)


def expert_reduce(store, chosen):
    pairs = (
        ("rows", "query_grad"),
        ("attended", "result_grad"),
        ("rows_two", "both_grad"),
        ("hidden", "down_grad"),
    )
    groups = lax.axis_size("group")
    results = []
    for left_name, right_name in pairs:
        left = joined_rows(store, chosen, left_name)
        right = joined_rows(store, chosen, right_name)

        def term(start, count, left=left, right=right):
            return jnp.einsum("rd,rf->df", left, right, preferred_element_type=jnp.float32)

        shard = lax.psum_scatter(
            term(jnp.int32(0), lax.axis_size("group") * (left.shape[1] // groups)).astype(
                jnp.bfloat16
            ),
            "group",
            scatter_dimension=0,
            tiled=True,
        ).astype(jnp.float32)
        results.append(shard[None])
    return tuple(results)


def reduce_all(store, chosen):
    expert_parts = expert_reduce(store, chosen)
    shared_term = jnp.einsum(
        "td,tf->df",
        joined_rows(store, chosen, "normed"),
        joined_rows(store, chosen, "mixed_grad"),
        preferred_element_type=jnp.float32,
    )
    gain_first = jnp.sum(joined_rows(store, chosen, "gain_first"), axis=0)
    gain_second = jnp.sum(joined_rows(store, chosen, "gain_second"), axis=0)
    shared_parts = (
        lax.psum_scatter(shared_term, ("group", "expert"), scatter_dimension=0, tiled=True),
        lax.psum_scatter(gain_first, ("group", "expert"), scatter_dimension=0, tiled=True),
        lax.psum_scatter(gain_second, ("group", "expert"), scatter_dimension=0, tiled=True),
    )
    return tuple(expert_parts) + tuple(shared_parts)


def on_device(
    tokens,
    cotangent,
    gain_attn,
    gain_mlp,
    w_kv,
    w_query,
    w_out,
    w_gate_up,
    w_down,
    att_routes,
    att_gates,
    mlp_routes,
    mlp_gates,
    blocks,
):
    experts = lax.axis_size("expert")
    owner = lax.axis_index("expert")
    shared_full = lax.all_gather(w_kv, ("group", "expert"), axis=0, tiled=True)
    gathered = (
        lax.all_gather(w_query, "group", axis=1, tiled=True),
        lax.all_gather(w_out, "group", axis=1, tiled=True),
        lax.all_gather(w_gate_up, "group", axis=1, tiled=True),
        lax.all_gather(w_down, "group", axis=1, tiled=True),
    )
    query_full = gathered[0][0]
    output_full = gathered[1][0]
    gate_up_full = gathered[2][0]
    down_full = gathered[3][0]
    micro = tokens.shape[0]
    local = tokens.shape[1]
    model = tokens.shape[2]
    length = local * experts
    width = HEADS * HDIM
    hidden_width = gate_up_full.shape[1] // 2
    own_cos, own_sin = angles(owner * local + jnp.arange(local, dtype=jnp.int32))
    names = (
        "rows",
        "query_grad",
        "attended",
        "result_grad",
        "rows_two",
        "both_grad",
        "hidden",
        "down_grad",
        "normed",
        "mixed_grad",
        "gain_first",
        "gain_second",
    )
    store = {name: [] for name in names}
    outputs = []
    input_grads = []
    for index in range(micro):
        inputs = tokens[index].astype(jnp.float32)
        block_ids = blocks[index, 0]
        att_pick, att_weight, row_pos, row_block = routing(
            att_routes[index], att_gates[index], block_ids, owner, experts
        )
        mlp_pick, mlp_weight, unused_pos, unused_block = routing(
            mlp_routes[index], mlp_gates[index], block_ids, owner, experts
        )
        scale = lax.rsqrt(jnp.mean(inputs * inputs, axis=1, keepdims=True) + EPS)
        normed = (inputs * scale * gain_attn).astype(jnp.bfloat16)
        mixed = jnp.dot(normed, shared_full, preferred_element_type=jnp.float32)
        keys_here = rotate(mixed[:, :width], own_cos, own_sin).astype(jnp.bfloat16)
        local_kv = jnp.concatenate([keys_here, mixed[:, width:].astype(jnp.bfloat16)], axis=1)
        sequence_kv = lax.all_gather(local_kv, "expert", axis=0, tiled=True)
        keys = sequence_kv[:, :width]
        values = sequence_kv[:, width:].reshape(length, HEADS, HDIM)
        rows = lax.all_to_all(
            spread(att_pick, normed), "expert", split_axis=0, concat_axis=0, tiled=True
        ).reshape(-1, model)
        row_cos, row_sin = angles(row_pos)
        queries = rotate(
            jnp.dot(rows, query_full, preferred_element_type=jnp.float32), row_cos, row_sin
        ).astype(jnp.bfloat16)
        scores = score_block(queries, keys, row_block, block_ids)
        top = jnp.max(scores, axis=2, keepdims=True)
        powers = jnp.exp(scores - top)
        total = jnp.sum(powers, axis=2, keepdims=True)
        log_total = top + jnp.log(total)
        probs = (powers / total).astype(jnp.bfloat16)
        attended = jnp.einsum("hrk,khd->rhd", probs, values, preferred_element_type=jnp.float32)
        attended = attended.reshape(-1, width).astype(jnp.bfloat16)
        result = jnp.dot(attended, output_full, preferred_element_type=jnp.float32).astype(
            jnp.bfloat16
        )
        back = lax.all_to_all(
            result.reshape(experts, CAP, model), "expert", split_axis=0, concat_axis=0, tiled=True
        )
        middle = inputs + collect(att_weight, back)
        scale_two = lax.rsqrt(jnp.mean(middle * middle, axis=1, keepdims=True) + EPS)
        normed_two = (middle * scale_two * gain_mlp).astype(jnp.bfloat16)
        rows_two = lax.all_to_all(
            spread(mlp_pick, normed_two), "expert", split_axis=0, concat_axis=0, tiled=True
        ).reshape(-1, model)
        both = jnp.dot(rows_two, gate_up_full, preferred_element_type=jnp.float32)
        gate = both[:, :hidden_width]
        up = both[:, hidden_width:]
        sigma = 1.0 / (1.0 + jnp.exp(-gate))
        hidden = (gate * sigma * up).astype(jnp.bfloat16)
        result_two = jnp.dot(hidden, down_full, preferred_element_type=jnp.float32).astype(
            jnp.bfloat16
        )
        back_two = lax.all_to_all(
            result_two.reshape(experts, CAP, model),
            "expert",
            split_axis=0,
            concat_axis=0,
            tiled=True,
        )
        final = middle + collect(mlp_weight, back_two)
        outputs.append(final.astype(jnp.bfloat16))
        upstream = cotangent[index].astype(jnp.float32)
        outgoing = jnp.einsum("ect,td->ecd", mlp_weight, upstream, precision=HIGH).astype(
            jnp.bfloat16
        )
        down_grad = lax.all_to_all(
            outgoing, "expert", split_axis=0, concat_axis=0, tiled=True
        ).reshape(-1, model)
        hidden_grad = jnp.einsum(
            "rd,fd->rf", down_grad, down_full, preferred_element_type=jnp.float32
        )
        slope = sigma * (1.0 + gate * (1.0 - sigma))
        both_grad = jnp.concatenate(
            [hidden_grad * up * slope, hidden_grad * gate * sigma], axis=1
        ).astype(jnp.bfloat16)
        row_grad_two = jnp.einsum(
            "rf,df->rd", both_grad, gate_up_full, preferred_element_type=jnp.float32
        ).astype(jnp.bfloat16)
        returned_two = lax.all_to_all(
            row_grad_two.reshape(experts, CAP, model),
            "expert",
            split_axis=0,
            concat_axis=0,
            tiled=True,
        )
        normed_two_grad = collect(mlp_pick, returned_two)
        scaled_two = normed_two_grad * gain_mlp
        gain_second = jnp.sum(normed_two_grad * middle * scale_two, axis=0, keepdims=True)
        middle_grad = (
            upstream
            + scale_two * scaled_two
            - middle * scale_two**3 * jnp.mean(scaled_two * middle, axis=1, keepdims=True)
        )
        outgoing_att = jnp.einsum("ect,td->ecd", att_weight, middle_grad, precision=HIGH).astype(
            jnp.bfloat16
        )
        result_grad = lax.all_to_all(
            outgoing_att, "expert", split_axis=0, concat_axis=0, tiled=True
        ).reshape(-1, model)
        attended_grad = jnp.einsum(
            "rd,fd->rf", result_grad, output_full, preferred_element_type=jnp.float32
        ).astype(jnp.bfloat16)
        again = jnp.exp(score_block(queries, keys, row_block, block_ids) - log_total)
        heads_grad = attended_grad.reshape(-1, HEADS, HDIM)
        value_grad = jnp.einsum(
            "hrk,rhd->khd",
            again.astype(jnp.bfloat16),
            heads_grad,
            preferred_element_type=jnp.float32,
        )
        prob_grad = jnp.einsum(
            "rhd,khd->hrk", heads_grad, values, preferred_element_type=jnp.float32
        )
        inner = jnp.sum(again * prob_grad, axis=2, keepdims=True)
        raw_grad = (again * (prob_grad - inner) * HDIM ** (-0.5)).astype(jnp.bfloat16)
        query_grad = jnp.einsum(
            "hrk,khd->rhd",
            raw_grad,
            keys.reshape(length, HEADS, HDIM),
            preferred_element_type=jnp.float32,
        ).reshape(-1, width)
        query_grad = rotate(query_grad, row_cos, -row_sin).astype(jnp.bfloat16)
        key_grad = jnp.einsum(
            "hrk,rhd->khd",
            raw_grad,
            queries.reshape(-1, HEADS, HDIM),
            preferred_element_type=jnp.float32,
        ).reshape(length, width)
        row_grad = jnp.einsum(
            "rf,df->rd", query_grad, query_full, preferred_element_type=jnp.float32
        ).astype(jnp.bfloat16)
        returned = lax.all_to_all(
            row_grad.reshape(experts, CAP, model), "expert", split_axis=0, concat_axis=0, tiled=True
        )
        kv_grad = lax.psum_scatter(
            jnp.concatenate([key_grad, value_grad.reshape(length, width)], axis=1).astype(
                jnp.bfloat16
            ),
            "expert",
            scatter_dimension=0,
            tiled=True,
        ).astype(jnp.float32)
        mixed_grad = jnp.concatenate(
            [rotate(kv_grad[:, :width], own_cos, -own_sin), kv_grad[:, width:]], axis=1
        ).astype(jnp.bfloat16)
        normed_grad = collect(att_pick, returned) + jnp.einsum(
            "tf,df->td", mixed_grad, shared_full, preferred_element_type=jnp.float32
        )
        scaled = normed_grad * gain_attn
        gain_first = jnp.sum(normed_grad * inputs * scale, axis=0, keepdims=True)
        input_grad = (
            middle_grad
            + scale * scaled
            - inputs * scale**3 * jnp.mean(scaled * inputs, axis=1, keepdims=True)
        )
        input_grads.append(input_grad.astype(jnp.bfloat16))
        kept = (
            rows,
            query_grad,
            attended,
            result_grad,
            rows_two,
            both_grad,
            hidden,
            down_grad,
            normed,
            mixed_grad,
            gain_first,
            gain_second,
        )
        for name, value in zip(names, kept):
            store[name].append(value)
    reduced = reduce_all(store, list(range(micro)))
    grad_query, grad_out, grad_gate_up, grad_down, grad_kv, grad_gain_attn, grad_gain_mlp = reduced
    return (
        jnp.stack(outputs, axis=0),
        jnp.stack(input_grads, axis=0),
        grad_gain_attn,
        grad_gain_mlp,
        grad_kv,
        grad_query,
        grad_out,
        grad_gate_up,
        grad_down,
    )


ZS, YS, XS, CS = 4, 2, 2, 2
SEQ = 320
F32 = jnp.float32
BF16 = jnp.bfloat16


def fits(mesh):
    return mesh.shape["group"] == ZS * YS and mesh.shape["expert"] == XS * CS


def group_move(value, move):
    pairs = []
    for z in range(ZS):
        for y in range(YS):
            to_z, to_y = move(z, y)
            pairs.append((z * YS + y, to_z * YS + to_y))
    return lax.ppermute(value, "group", pairs)


def z_move(value, step):
    return group_move(value, lambda z, y: ((z + step) % ZS, y))


def y_move(value):
    return group_move(value, lambda z, y: (z, 1 - y))


def x_move(value):
    return lax.ppermute(value, "expert", [(x * CS + c, (1 - x) * CS + c) for x in range(XS) for c in range(CS)])


def c_move(value):
    return lax.ppermute(value, "expert", [(x * CS + c, x * CS + 1 - c) for x in range(XS) for c in range(CS)])


def z_exchange(value):
    columns = [[z * YS + y for z in range(ZS)] for y in range(YS)]
    return lax.all_to_all(
        value, "group", split_axis=0, concat_axis=0, tiled=True, axis_index_groups=columns
    )


def gather_tokens(own):
    column = jnp.stack([own] + [z_move(own, -step) for step in range(1, ZS)], axis=0)
    plane = jnp.stack([column, x_move(column)], axis=1)
    plane = plane.reshape((ZS, XS * own.shape[0]) + own.shape[1:])
    return jnp.stack([plane, c_move(plane)], axis=0)


def reduce_tokens(other, mine):
    local = mine.shape[1] // XS
    total = mine.astype(F32) + c_move(other).astype(F32)
    arrived = x_move(total[:, local:].astype(BF16))
    total = total[:, :local] + arrived.astype(F32)
    result = total[0]
    for step in range(1, ZS):
        result = result + z_move(total[step].astype(BF16), step).astype(F32)
    return result


def merge(index, own, other, axis):
    return jnp.where(index == 0, jnp.stack([own, other], axis), jnp.stack([other, own], axis))


def take(value, index, axis):
    return lax.dynamic_index_in_dim(value, index, axis, keepdims=False)


def dot(left, right):
    return jnp.dot(left, right, preferred_element_type=F32)


def dot_t(left, right):
    return lax.dot_general(left, right, (((1,), (1,)), ((), ())), preferred_element_type=F32)


def dot_l(left, right):
    return lax.dot_general(left, right, (((0,), (0,)), ((), ())), preferred_element_type=F32)


def turned(value, cosine, sine):
    return value * cosine + pltpu.roll(value, HDIM // 2, 1) * sine


def masked_probs(query, key, row_block, key_block):
    scores = jnp.where(key_block <= row_block, dot_t(query, key) * HDIM ** (-0.5), -1e30)
    powers = jnp.exp(scores - jnp.max(scores, axis=1, keepdims=True))
    return powers / jnp.sum(powers, axis=1, keepdims=True)


MESH = pl.DeviceIdType.MESH
ORDER = (3, 1, 2, 0)
STEP = 16
DMA = pltpu.SemaphoreType.DMA
ANY = pl.BlockSpec(memory_space=pl.ANY)
VMEM = pl.BlockSpec(memory_space=pltpu.VMEM)


def by_rows(rows, body):
    def step(index, carry):
        body(pl.ds(pl.multiple_of(index * STEP, STEP), STEP))
        return carry

    lax.fori_loop(0, rows // STEP, step, 0)


class Place:
    def __init__(self):
        group, owner = lax.axis_index("group"), lax.axis_index("expert")
        self.z, self.y = lax.div(group, YS), lax.rem(group, YS)
        self.x, self.core = lax.div(owner, CS), lax.rem(owner, CS)
        self.group, self.owner = group, owner

        def device(z, y, x, core):
            return (z * YS + y, x * CS + core)

        self.x_peer = device(self.z, self.y, 1 - self.x, self.core)
        self.y_peer = device(self.z, 1 - self.y, self.x, self.core)
        self.core_peer = device(self.z, self.y, self.x, 1 - self.core)
        self.z_peers = [device(lax.rem(self.z + step, ZS), self.y, self.x, self.core) for step in range(ZS)]

    def enter(self, with_y):
        peers = [self.x_peer, self.core_peer] + self.z_peers[1:] + ([self.y_peer] if with_y else [])
        barrier = pltpu.get_barrier_semaphore()
        for peer in peers:
            pl.semaphore_signal(barrier, inc=1, device_id=peer, device_id_type=MESH)
        pl.semaphore_wait(barrier, len(peers))


def remote(src, dst, send, arrive, peer):
    return pltpu.make_async_remote_copy(
        src_ref=src, dst_ref=dst, send_sem=send, recv_sem=arrive, device_id=peer, device_id_type=MESH
    )


class Reduce:
    @staticmethod
    def scratch(micro, rows, model):
        return [
            pltpu.VMEM((micro, ZS, XS, rows, model), BF16),
            pltpu.VMEM((micro, ZS, XS, rows, model), BF16),
            pltpu.VMEM((micro, ZS, rows, model), BF16),
            pltpu.VMEM((micro, 2, ZS - 1, rows, model), BF16),
            pltpu.VMEM((micro, rows, model), F32),
            DMA((micro, ZS, XS)),
            DMA((micro, ZS, XS)),
            DMA((micro, ZS, XS)),
            DMA((micro, ZS)),
            DMA((micro, ZS)),
            DMA((micro, 2, ZS)),
            DMA((micro, 2, ZS)),
        ]

    def __init__(self, place, part, refs):
        self.place, self.part = place, part
        self.core_in, self.kept, self.x_in, self.z_in, self.total = [refs.pop(0) for _ in range(5)]
        self.sems = [refs.pop(0) for _ in range(7)]
        self.micro, self.rows = part.shape[0], part.shape[4]

    def core_copy(self, m, k, dx):
        send, arrive = self.sems[:2]
        return remote(
            self.part.at[m, k, 1, dx],
            self.core_in.at[m, k, dx],
            send.at[m, k, dx],
            arrive.at[m, k, dx],
            self.place.core_peer,
        )

    def kept_copy(self, m, k, dx):
        return pltpu.make_async_copy(
            self.part.at[m, k, 0, dx], self.kept.at[m, k, dx], self.sems[2].at[m, k, dx]
        )

    def x_copy(self, m, k):
        send, arrive = self.sems[3:5]
        return remote(
            self.core_in.at[m, k, 1], self.x_in.at[m, k], send.at[m, k], arrive.at[m, k], self.place.x_peer
        )

    def z_copy(self, m, down, far):
        send, arrive = self.sems[5:7]
        return remote(
            self.x_in.at[m, ZS - far if down else far],
            self.z_in.at[m, down, far - 1],
            send.at[m, down, far - 1],
            arrive.at[m, down, far - 1],
            self.place.z_peers[ZS - 1 if down else 1],
        )

    def begin(self):
        for m in range(self.micro):
            for dx in (1, 0):
                for k in ORDER:
                    self.core_copy(m, k, dx).start()
                    self.kept_copy(m, k, dx).start()

    def pass_x(self, m):
        for k in ORDER:
            self.core_copy(m, k, 1).wait_recv()
            self.kept_copy(m, k, 1).wait()

            def add(span, k=k):
                value = self.core_in[m, k, 1, span, :].astype(F32) + self.kept[m, k, 1, span, :].astype(F32)
                self.core_in[m, k, 1, span, :] = value.astype(BF16)

            by_rows(self.rows, add)
            self.x_copy(m, k).start()

    def z_unit(self, m, k):
        self.x_copy(m, k).wait_recv()
        self.core_copy(m, k, 0).wait_recv()
        self.kept_copy(m, k, 0).wait()

        def add(span):
            value = (
                self.x_in[m, k, span, :].astype(F32)
                + self.core_in[m, k, 0, span, :].astype(F32)
                + self.kept[m, k, 0, span, :].astype(F32)
            )
            if k:
                self.x_in[m, k, span, :] = value.astype(BF16)
            else:
                self.total[m, span, :] = value

        by_rows(self.rows, add)

    def beyond(self, down, far):
        return self.place.z >= far if down else self.place.z + far < ZS

    def chain(self, m, far):
        for down in (0, 1):

            def send(down=down):
                if far < ZS - 1:
                    pl.when(self.beyond(1 - down, 1))(functools.partial(self.join, m, down, far))
                self.z_copy(m, down, far).start()

            pl.when(self.beyond(down, far))(send)

    def join(self, m, down, far):
        self.z_copy(m, down, far + 1).wait_recv()
        place = ZS - far if down else far

        def add(span):
            value = self.x_in[m, place, span, :].astype(F32) + self.z_in[m, down, far, span, :].astype(F32)
            self.x_in[m, place, span, :] = value.astype(BF16)

        by_rows(self.rows, add)

    def finish(self, m):
        for down in (0, 1):

            def last(down=down):
                self.z_copy(m, down, 1).wait_recv()

                def add(span):
                    self.total[m, span, :] += self.z_in[m, down, 0, span, :].astype(F32)

                by_rows(self.rows, add)

            pl.when(self.beyond(1 - down, 1))(last)

    def sums(self, m):
        for turn, k in enumerate(ORDER):
            self.z_unit(m, k)
            if m and turn < 2:
                self.chain(m - 1, 2 - turn)
        self.chain(m, ZS - 1)

    def end_chain(self):
        for far in range(ZS - 2, 0, -1):
            self.chain(self.micro - 1, far)

    def run(self):
        self.begin()
        for m in range(self.micro):
            self.pass_x(m)
        for m in range(self.micro):
            self.sums(m)
        self.end_chain()

    def drain(self):
        for m in range(self.micro):
            for k in ORDER:
                for dx in range(XS):
                    self.core_copy(m, k, dx).wait_send()
                self.x_copy(m, k).wait_send()
            for down in (0, 1):
                for far in range(1, ZS):
                    pl.when(self.beyond(down, far))(self.z_copy(m, down, far).wait_send)


class Gather:
    @staticmethod
    def scratch(micro):
        return [
            DMA((micro,)),
            DMA((micro, ZS)),
            DMA((micro, ZS)),
            DMA((micro, ZS)),
            DMA((micro, ZS, XS)),
            DMA((micro, ZS, CS, XS)),
        ]

    def __init__(self, place, own, out, refs):
        self.place, self.own, self.out = place, own, out
        self.sems = [refs.pop(0) for _ in range(6)]
        self.micro = out.shape[0]

    def slot(self, m, k, dc, dx):
        return self.out.at[m, k, dc, dx]

    def local(self, m):
        return pltpu.make_async_copy(self.own.at[m], self.slot(m, 0, 0, 0), self.sems[0].at[m])

    def up(self, m, source, k):
        return remote(
            source, self.slot(m, k, 0, 0), self.sems[1].at[m, k], self.sems[5].at[m, k, 0, 0], self.place.z_peers[1]
        )

    def down(self, m, source, k):
        return remote(
            source,
            self.slot(m, k, 0, 0),
            self.sems[2].at[m, k],
            self.sems[5].at[m, k, 0, 0],
            self.place.z_peers[ZS - 1],
        )

    def over_x(self, m, source, k):
        return remote(
            source, self.slot(m, k, 0, 1), self.sems[3].at[m, k], self.sems[5].at[m, k, 0, 1], self.place.x_peer
        )

    def over_core(self, m, source, k, dx):
        return remote(
            source,
            self.slot(m, k, 1, dx),
            self.sems[4].at[m, k, dx],
            self.sems[5].at[m, k, 1, dx],
            self.place.core_peer,
        )

    def send_own(self, m):
        source, z = self.own.at[m], self.place.z
        pl.when(z < ZS - 1)(lambda: self.up(m, source, ZS - 1).start())
        pl.when(z > 0)(lambda: self.down(m, source, 1).start())
        self.over_x(m, source, 0).start()
        self.over_core(m, source, 0, 0).start()
        self.local(m).start()

    def pass_on(self, m, k):
        self.over_x(m, self.slot(m, k, 0, 0), k).start()
        self.over_core(m, self.slot(m, k, 0, 0), k, 0).start()

    def from_above(self, m, far):
        self.up(m, self.own.at[m], far).wait_recv()
        pl.when(self.place.z > 0)(lambda: self.down(m, self.slot(m, far, 0, 0), far + 1).start())
        self.pass_on(m, far)

    def from_below(self, m, far):
        self.up(m, self.own.at[m], ZS - far).wait_recv()
        source = self.slot(m, ZS - far, 0, 0)
        pl.when(self.place.z < ZS - 1)(lambda: self.up(m, source, ZS - far - 1).start())
        self.pass_on(m, ZS - far)

    def z_arrival(self, m, far):
        pl.when(self.place.z + far < ZS)(lambda: self.from_above(m, far))
        pl.when(self.place.z - far >= 0)(lambda: self.from_below(m, far))

    def x_arrival(self, m, k):
        self.over_x(m, self.own.at[m], k).wait_recv()
        self.over_core(m, self.slot(m, k, 0, 1), k, 1).start()

    def z_round(self, far):
        for m in range(self.micro):
            self.z_arrival(m, far)

    def x_round(self, far):
        for m in range(self.micro):
            if far == 0:
                self.x_arrival(m, 0)
            else:
                pl.when(self.place.z + far < ZS)(lambda: self.x_arrival(m, far))
                pl.when(self.place.z - far >= 0)(lambda: self.x_arrival(m, ZS - far))

    def run(self):
        self.z_round(1)
        self.x_round(0)
        self.z_round(2)
        self.x_round(1)
        self.z_round(3)
        self.x_round(2)
        self.x_round(3)

    def drain(self):
        z = self.place.z
        for m in range(self.micro):
            own = self.own.at[m]
            for k in range(ZS):
                for dx in range(XS):
                    self.over_core(m, own, k, dx).wait_recv()
            self.local(m).wait()
            pl.when(z < ZS - 1)(lambda: self.up(m, own, ZS - 1).wait_send())
            pl.when(z > 0)(lambda: self.down(m, own, 1).wait_send())
            for far in range(1, ZS - 1):
                pl.when((z + far < ZS) & (z > 0))(lambda: self.down(m, own, far + 1).wait_send())
                pl.when((z - far >= 0) & (z < ZS - 1))(lambda: self.up(m, own, ZS - far - 1).wait_send())
            for k in range(ZS):
                self.over_x(m, own, k).wait_send()
                for dx in range(XS):
                    self.over_core(m, own, k, dx).wait_send()


class Spread:
    @staticmethod
    def scratch(pieces, depth):
        return [DMA((pieces,)), DMA((ZS, pieces)), DMA((ZS, pieces))] + [
            DMA((ZS << step,)) for step in range(depth) for _ in range(2)
        ]

    def __init__(self, place, sources, targets, view, depth, refs):
        self.place, self.sources, self.targets, self.view, self.depth = place, sources, targets, view, depth
        self.local_sem, self.z_send, self.z_recv = [refs.pop(0) for _ in range(3)]
        self.sems = [(refs.pop(0), refs.pop(0)) for _ in range(depth)]
        self.pieces = self.local_sem.shape[0]

    def z_copy(self, step, piece):
        place = self.place
        mine = self.targets(self.view(place.z, place.y, place.x, place.core))
        return remote(
            self.sources(lax.rem(place.z + step, ZS))[piece],
            mine[piece],
            self.z_send.at[step, piece],
            self.z_recv.at[step, piece],
            place.z_peers[step],
        )

    def local(self, piece):
        place = self.place
        mine = self.targets(self.view(place.z, place.y, place.x, place.core))
        return pltpu.make_async_copy(self.sources(place.z)[piece], mine[piece], self.local_sem.at[piece])

    def hop(self, axis, index):
        place = self.place
        z = lax.rem(place.z - (index >> axis) + ZS, ZS)
        y = place.y if axis < 1 else (place.y + ((index >> (axis - 1)) & 1)) % 2
        x = place.x if axis < 2 else (place.x + (index & 1)) % 2
        block = self.view(z, y, x, place.core)
        peer = (place.y_peer, place.x_peer, place.core_peer)[axis]
        send, arrive = self.sems[axis]
        return remote(block, block, send.at[index], arrive.at[index], peer)

    def begin(self):
        for piece in range(self.pieces):
            self.local(piece).start()
        for step in (1, 3, 2):
            for piece in range(self.pieces):
                self.z_copy(step, piece).start()

    def forward(self, axis, index):
        for later in range(axis, self.depth):
            self.hop(later, index << (later - axis)).start()

    def z_round(self, step):
        for piece in range(self.pieces):
            if step:
                self.z_copy(step, piece).wait_recv()
            else:
                self.local(piece).wait()
        self.forward(0, step)

    def hop_round(self, axis, index):
        self.hop(axis, index).wait_recv()
        self.forward(axis + 1, index * 2 + 1)

    def drain(self):
        for step in range(1, ZS):
            for piece in range(self.pieces):
                self.z_copy(step, piece).wait_send()
        for axis in range(self.depth):
            for index in range(ZS << axis):
                self.hop(axis, index).wait_send()


class Share:
    @staticmethod
    def scratch(pieces):
        return [DMA((pieces,)), DMA((pieces,)), DMA((pieces,))]

    def __init__(self, place, blocks, refs):
        local, send, arrive = [refs.pop(0) for _ in range(3)]
        self.copies = []
        for index, (source, target) in enumerate(blocks):
            self.copies.append(pltpu.make_async_copy(source, target, local.at[index]))
            self.copies.append(remote(source, target, send.at[index], arrive.at[index], place.y_peer))

    def begin(self):
        for copy in self.copies:
            copy.start()

    def drain(self):
        for copy in self.copies:
            copy.wait()


def normed_rows(rows, gain):
    return rows * lax.rsqrt(jnp.mean(rows * rows, axis=1, keepdims=True) + EPS) * gain


def norm_back(grad, rows, upstream, gain):
    scale = lax.rsqrt(jnp.mean(rows * rows, axis=1, keepdims=True) + EPS)
    scaled = grad * gain
    inner = jnp.mean(scaled * rows, axis=1, keepdims=True)
    return upstream + scale * scaled - rows * (scale * scale * scale) * inner, grad * rows * scale


def start_kernel(sizes, tokens, cotangent, gain, table, w_kv, w_query, w_out, w_down, *refs):
    refs = list(refs)
    normed_out, cotangent_out, table_out, qkv_weight, out_weight, down_weight = [refs.pop(0) for _ in range(6)]
    wide, kv_rows, model_rows, out_rows, down_rows = sizes
    place = Place()
    normed_own = refs.pop(0)
    normed = Gather(place, normed_own, normed_out, refs)
    upstream = Gather(place, cotangent, cotangent_out, refs)
    tables = Gather(place, table, table_out, refs)

    def lanes(start):
        return pl.ds(pl.multiple_of(start, HDIM), wide)

    def kv_view(z, y, x, core):
        row = ((z * YS + y) * (XS * CS) + x * CS + core) * kv_rows
        return qkv_weight.at[pl.ds(pl.multiple_of(row, kv_rows), kv_rows), pl.ds(wide, 2 * wide)]

    def query_view(z, y, x, core):
        row = (z * YS + y) * model_rows
        return qkv_weight.at[pl.ds(pl.multiple_of(row, model_rows), model_rows), pl.ds(0, wide)]

    kv = Spread(
        place,
        lambda z: [w_kv.at[:, lanes(z * wide)], w_kv.at[:, lanes((ZS + z) * wide)]],
        lambda block: [block.at[:, pl.ds(0, wide)], block.at[:, pl.ds(wide, wide)]],
        kv_view,
        3,
        refs,
    )
    query = Spread(
        place, lambda z: [w_query.at[0, :, lanes(z * wide)]], lambda block: [block], query_view, 1, refs
    )

    def half(target, rows):
        return target.at[pl.ds(pl.multiple_of(place.y * rows, rows), rows)]

    shared = Share(
        place,
        [(w_out.at[0], half(out_weight, out_rows)), (w_down.at[0], half(down_weight, down_rows))],
        refs,
    )
    place.enter(True)
    kv.begin()
    tables.send_own(0)
    for m in range(normed.micro):

        def body(span, m=m):
            normed_own[m, span, :] = normed_rows(tokens[m, span, :].astype(F32), gain[...]).astype(BF16)

        by_rows(tokens.shape[1], body)
        normed.send_own(m)
    query.begin()
    shared.begin()
    kv.z_round(0)
    tables.z_round(1)
    kv.z_round(1)
    kv.z_round(3)
    normed.z_round(1)
    for m in range(upstream.micro):
        upstream.send_own(m)
    kv.z_round(2)
    for index in (0, 1, 3, 2):
        kv.hop_round(0, index)
    normed.x_round(0)
    tables.z_round(2)
    normed.z_round(2)
    for step in (0, 1, 3, 2):
        query.z_round(step)
    for index in (0, 2, 6, 4, 1, 3, 7, 5):
        kv.hop_round(1, index)
    normed.z_round(3)
    normed.x_round(1)
    tables.z_round(3)
    for far in range(ZS):
        tables.x_round(far)
    upstream.z_round(1)
    normed.x_round(2)
    upstream.x_round(0)
    upstream.z_round(2)
    normed.x_round(3)
    upstream.x_round(1)
    upstream.z_round(3)
    upstream.x_round(2)
    upstream.x_round(3)
    for index in range(ZS << 2):
        kv.hop_round(2, index)
    for index in range(ZS):
        query.hop_round(0, index)
    for part in (tables, normed, kv, query, shared, upstream):
        part.drain()


def first_kernel(sizes, part, tokens, gain, w_gate_up, gate_part, *refs):
    refs = list(refs)
    rows_out, weight, middle_out, own = [refs.pop(0) for _ in range(4)]
    model_rows, hidden_width = sizes
    place = Place()
    reduce = Reduce(place, part, refs)
    gather = Gather(place, own, rows_out, refs)

    def view(z, y, column):
        row = pl.multiple_of((z * YS + y) * model_rows, model_rows)
        return weight.at[pl.ds(row, model_rows), pl.ds(column, hidden_width)]

    shared = Share(place, [(gate_part.at[z], view(z, place.y, 0)) for z in range(ZS)], refs)
    up = Spread(
        place,
        lambda z: [w_gate_up.at[0, :, pl.ds(pl.multiple_of((ZS + z) * hidden_width, HDIM), hidden_width)]],
        lambda block: [block],
        lambda z, y, x, core: view(z, y, hidden_width),
        1,
        refs,
    )
    place.enter(True)
    reduce.begin()
    up.begin()
    shared.begin()
    reduce.pass_x(0)
    up.z_round(0)
    reduce.pass_x(1)
    reduce.sums(0)
    up.z_round(1)
    up.z_round(3)
    reduce.sums(1)
    up.z_round(2)
    reduce.end_chain()
    for m in range(gather.micro):
        reduce.finish(m)

        def body(span, m=m):
            middle = tokens[m, span, :].astype(F32) + reduce.total[m, span, :]
            middle_out[m, span, :] = middle
            own[m, span, :] = normed_rows(middle, gain[...]).astype(BF16)

        by_rows(reduce.rows, body)
        gather.send_own(m)
    gather.run()
    for index in range(ZS):
        up.hop_round(0, index)
    for part in (gather, shared, up, reduce):
        part.drain()


def second_kernel(part, middle, cotangent, gain, gate_grad, up_grad, down_grad, *refs):
    refs = list(refs)
    rows_out, grad_out, terms_out, gate_out, up_out, down_out, own = [refs.pop(0) for _ in range(7)]
    place = Place()
    reduce = Reduce(place, part, refs)
    gather = Gather(place, own, rows_out, refs)
    local, send, arrive, y_send, y_recv = [refs.pop(0) for _ in range(5)]
    width = gate_grad.shape[2]
    columns = gate_out.at[:, pl.ds(pl.multiple_of(place.z * width, HDIM), width)]
    kept = pltpu.make_async_copy(gate_grad.at[place.z], columns, local)

    def give(step):
        return remote(
            gate_grad.at[lax.rem(place.z + step, ZS)],
            columns,
            send.at[step],
            arrive.at[step],
            place.z_peers[step],
        )

    halves = [
        remote(up_grad.at[:, 1 - place.y], up_out, y_send.at[0], y_recv.at[0], place.y_peer),
        remote(down_grad.at[1 - place.y], down_out, y_send.at[1], y_recv.at[1], place.y_peer),
    ]
    place.enter(True)
    kept.start()
    reduce.begin()
    for copy in halves:
        copy.start()
    for step in (1, 3, 2):
        give(step).start()
    for m in range(reduce.micro):
        reduce.pass_x(m)
    for m in range(reduce.micro):
        reduce.sums(m)
    reduce.end_chain()
    terms_out[...] = jnp.zeros_like(terms_out)
    for m in range(gather.micro):
        reduce.finish(m)

        def body(span, m=m):
            result, terms = norm_back(
                reduce.total[m, span, :], middle[m, span, :], cotangent[m, span, :].astype(F32), gain[...]
            )
            grad_out[m, span, :] = result
            own[m, span, :] = result.astype(BF16)
            terms_out[...] += terms

        by_rows(reduce.rows, body)
        gather.send_own(m)
    gather.run()
    gather.drain()
    reduce.drain()
    kept.wait()
    for copy in halves:
        copy.wait()
    for step in (1, 3, 2):
        give(step).wait()


class Halves:
    def __init__(self, own, other, copies):
        self.own, self.other, self.copies = own, other, copies

    def begin(self):
        for copy in self.copies:
            copy.start()

    def add(self):
        for copy in self.copies:
            copy.wait()

        def body(index, carry):
            value = self.own[index].astype(F32) + self.other[index].astype(F32)
            self.other[index] = value.astype(BF16)
            return carry

        lax.fori_loop(0, self.other.shape[0], body, 0)


def last_kernel(part, other, tokens, middle, middle_grad, gain, terms_in, query_grad, kv_grad, out_grad, *refs):
    refs = list(refs)
    input_out, output, gains_out, query_out, kv_out, out_out = [refs.pop(0) for _ in range(6)]
    place = Place()
    first = Reduce(place, part, refs)
    second = Reduce(place, other, refs)
    query_own, query_in, kv_own, core_in, x_in, y_in = [refs.pop(0) for _ in range(6)]
    hop_send, hop_recv, hop_local, z_send, z_recv, z_local = [refs.pop(0) for _ in range(6)]
    terms, gain_in, gain_send, gain_recv = [refs.pop(0) for _ in range(4)]
    wide, kv_rows = query_out.shape[1] // ZS, kv_out.shape[0]

    def swap(number, source, target, peer):
        return remote(source, target, hop_send.at[number], hop_recv.at[number], peer)

    query = Halves(
        query_own,
        query_in,
        [
            pltpu.make_async_copy(query_grad.at[:, place.y], query_own, hop_local.at[0]),
            swap(0, query_grad.at[:, 1 - place.y], query_in, place.y_peer),
        ],
    )
    over_core = Halves(
        kv_own,
        core_in,
        [
            pltpu.make_async_copy(kv_grad.at[:, place.core], kv_own, hop_local.at[1]),
            swap(1, kv_grad.at[:, 1 - place.core], core_in, place.core_peer),
        ],
    )
    by_x = core_in.reshape(ZS * YS, XS, kv_rows, 2 * wide)
    over_x = Halves(by_x.at[:, place.x], x_in, [swap(2, by_x.at[:, 1 - place.x], x_in, place.x_peer)])
    by_y = x_in.reshape(ZS, YS, kv_rows, 2 * wide)
    over_y = Halves(by_y.at[:, place.y], y_in, [swap(3, by_y.at[:, 1 - place.y], y_in, place.y_peer)])
    over_out = swap(4, out_grad.at[1 - place.y], out_out, place.y_peer)

    def lanes(start):
        return pl.ds(pl.multiple_of(start, HDIM), wide)

    def z_parts(step):
        to = lax.rem(place.z + step, ZS)
        pairs = [(query_in.at[to], query_out.at[:, lanes(place.z * wide)])]
        for kind in range(2):
            pairs.append(
                (y_in.at[to, :, pl.ds(kind * wide, wide)], kv_out.at[:, lanes((kind * ZS + place.z) * wide)])
            )
        return pairs

    def z_copy(step, piece):
        source, target = z_parts(step)[piece]
        if step == 0:
            return pltpu.make_async_copy(source, target, z_local.at[piece])
        return remote(source, target, z_send.at[step, piece], z_recv.at[step, piece], place.z_peers[step])

    def add_gains(number, peers):
        copies = [
            remote(terms, gain_in.at[number + i], gain_send.at[number + i], gain_recv.at[number + i], peer)
            for i, peer in enumerate(peers)
        ]
        for copy in copies:
            copy.start()
        for copy in copies:
            copy.wait()
        for i in range(len(peers)):
            terms[...] += gain_in[number + i]

    place.enter(True)
    first.begin()
    over_core.begin()
    query.begin()
    over_out.start()
    second.begin()
    for m in range(first.micro):
        first.pass_x(m)
    over_core.add()
    over_x.begin()
    first.sums(0)
    query.add()
    for step in (1, 3, 2, 0):
        z_copy(step, 0).start()
    for m in range(second.micro):
        second.pass_x(m)
    first.sums(1)
    over_x.add()
    over_y.begin()
    first.end_chain()
    second.sums(0)
    over_y.add()
    for step in (1, 3, 2, 0):
        for piece in (1, 2):
            z_copy(step, piece).start()
    terms[...] = jnp.zeros_like(terms)
    for m in range(first.micro):
        first.finish(m)

        def body(span, m=m):
            result, found = norm_back(
                first.total[m, span, :], tokens[m, span, :].astype(F32), middle_grad[m, span, :], gain[...]
            )
            input_out[m, span, :] = result.astype(BF16)
            terms[0:1, :] += jnp.sum(found, axis=0, keepdims=True)

        by_rows(first.rows, body)
    terms[1:2, :] = jnp.sum(terms_in[...], axis=0, keepdims=True)
    add_gains(0, [place.core_peer])
    second.sums(1)
    add_gains(1, [place.x_peer])
    second.end_chain()
    add_gains(2, [place.y_peer])
    for m in range(second.micro):
        second.finish(m)

        def finish(span, m=m):
            output[m, span, :] = (middle[m, span, :] + second.total[m, span, :]).astype(BF16)

        by_rows(second.rows, finish)
    add_gains(3, place.z_peers[1:])
    gains_out[...] = terms[...]
    first.drain()
    second.drain()
    over_out.wait()
    for step in range(ZS):
        for piece in range(3):
            z_copy(step, piece).wait()


def connect(kernel, operands, spaces, out_shapes, out_spaces, scratch, number, seconds):
    return pl.pallas_call(
        kernel,
        in_specs=spaces,
        out_specs=out_spaces,
        out_shape=out_shapes,
        scratch_shapes=scratch,
        compiler_params=pltpu.CompilerParams(
            collective_id=number, has_side_effects=True, vmem_limit_bytes=60 << 20
        ),
        cost_estimate=pl.CostEstimate(flops=0, bytes_accessed=int(seconds * 3e12), transcendentals=0),
    )(*operands)


def attend_kernel(qkv_ref, cos_ref, sin_ref, row_ref, key_ref, turned_ref, out_ref):
    cosine, sine = cos_ref[...], sin_ref[...]
    width = out_ref.shape[2]
    for head in range(width // HDIM):
        parts = []
        for kind in range(3):
            span = slice(kind * width + head * HDIM, kind * width + (head + 1) * HDIM)
            value = qkv_ref[0, :, span]
            if kind < 2:
                value = turned(value, cosine, sine)
            value = value.astype(BF16)
            turned_ref[0, :, span] = value
            parts.append(value)
        query, key, value = parts
        probs = masked_probs(query, key, row_ref[0], key_ref[0]).astype(BF16)
        out_ref[0, :, head * HDIM : (head + 1) * HDIM] = dot(probs, value).astype(BF16)


def attend_back_kernel(turned_ref, grad_ref, cos_ref, sin_ref, row_ref, key_ref, out_ref):
    cosine, sine = cos_ref[...], -sin_ref[...]
    width = grad_ref.shape[2]
    for head in range(width // HDIM):
        spans = [slice(kind * width + head * HDIM, kind * width + (head + 1) * HDIM) for kind in range(3)]
        query, key, value = [turned_ref[0, :, span] for span in spans]
        grad = grad_ref[0, :, spans[0]]
        probs = masked_probs(query, key, row_ref[0], key_ref[0])
        prob_grad = dot_t(grad, value)
        inner = jnp.sum(probs * prob_grad, axis=1, keepdims=True)
        raw_grad = (probs * (prob_grad - inner) * HDIM ** (-0.5)).astype(BF16)
        results = [
            turned(dot(raw_grad, key), cosine, sine),
            turned(dot_l(raw_grad, query), cosine, sine),
            dot_l(probs.astype(BF16), grad),
        ]
        for span, result in zip(spans, results):
            out_ref[0, :, span] = result.astype(BF16)


def per_sequence(kernel, operands, tables, out_widths, matmuls):
    seqs, rows = operands[0].shape[:2]
    own = [pl.BlockSpec((1,) + value.shape[1:], lambda k: (k, 0, 0)) for value in operands]
    shared = [pl.BlockSpec(value.shape, lambda k: (0, 0)) for value in tables[:2]]
    blocks = [pl.BlockSpec((1,) + value.shape[1:], lambda k: (k, 0, 0)) for value in tables[2:]]
    width = out_widths[-1] if len(out_widths) > 1 else out_widths[0] // 3
    moved = sum(value.size * value.dtype.itemsize for value in operands) + 2 * seqs * rows * sum(out_widths)
    return pl.pallas_call(
        kernel,
        grid=(seqs,),
        in_specs=own + shared + blocks,
        out_specs=[pl.BlockSpec((1, rows, out), lambda k: (k, 0, 0)) for out in out_widths],
        out_shape=[jax.ShapeDtypeStruct((seqs, rows, out), BF16) for out in out_widths],
        compiler_params=pltpu.CompilerParams(vmem_limit_bytes=40 << 20),
        cost_estimate=pl.CostEstimate(
            flops=2 * matmuls * seqs * rows * rows * width,
            bytes_accessed=moved,
            transcendentals=seqs * rows * rows * width // HDIM,
        ),
    )(*operands, *tables)


def fast_device(
    tokens,
    cotangent,
    gain_attn,
    gain_mlp,
    w_kv,
    w_query,
    w_out,
    w_gate_up,
    w_down,
    att_routes,
    att_gates,
    mlp_routes,
    mlp_gates,
    blocks,
):
    group, owner = lax.axis_index("group"), lax.axis_index("expert")
    y = group % YS
    x, core = owner // CS, owner % CS
    micro, local, model = tokens.shape
    wide = w_query.shape[2] // ZS
    hidden_width = w_gate_up.shape[2] // (2 * ZS)
    kv_rows = w_kv.shape[0]
    model_rows = w_query.shape[1]

    def own_rows(table):
        return lax.dynamic_slice_in_dim(table, owner * local, local, 0).astype(F32)

    lines = []
    for m in range(micro):
        lines += [own_rows(att_routes[m]).T, att_gates[m].T, own_rows(mlp_routes[m]).T, mlp_gates[m].T]
        lines += [own_rows(blocks[m, 0][:, None]).T]
    table = jnp.concatenate(lines, axis=0)
    table = jnp.pad(table, ((0, -table.shape[0] % 8), (0, -local % HDIM)))[None]

    positions = (
        (x ^ jnp.arange(XS)[None, :, None]) * CS + (core ^ jnp.arange(CS)[:, None, None])
    ) * local + jnp.arange(local)[None, None, :]
    cosine, sine = angles(positions.reshape(-1))
    cosine = jnp.concatenate([cosine, cosine], axis=1)
    sine = jnp.concatenate([-sine, sine], axis=1)

    shape = (micro, local, model)
    everyone = (micro, ZS, CS, XS, local, model)
    seqs = micro * ZS
    first_gain, second_gain = gain_attn[None], gain_mlp[None]
    tall = jax.ShapeDtypeStruct(shape, F32)
    short = jax.ShapeDtypeStruct(shape, BF16)
    gathered = jax.ShapeDtypeStruct(everyone, BF16)
    terms = jax.ShapeDtypeStruct((STEP, model), F32)
    own_buffer = pltpu.VMEM(shape, BF16)
    normed, cotangents, table, qkv_weight, out_weight, down_weight = connect(
        functools.partial(
            start_kernel, (wide, kv_rows, model_rows, w_out.shape[1], w_down.shape[1])
        ),
        [tokens, cotangent, first_gain, table, w_kv, w_query, w_out, w_down],
        [VMEM, VMEM, VMEM, VMEM, ANY, ANY, ANY, ANY],
        [
            gathered,
            gathered,
            jax.ShapeDtypeStruct((1, ZS, CS, XS) + table.shape[1:], F32),
            jax.ShapeDtypeStruct((model, 3 * wide), BF16),
            jax.ShapeDtypeStruct((wide, model), BF16),
            jax.ShapeDtypeStruct((hidden_width, model), BF16),
        ],
        [ANY] * 6,
        [own_buffer]
        + Gather.scratch(micro)
        + Gather.scratch(micro)
        + Gather.scratch(1)
        + Spread.scratch(2, 3)
        + Spread.scratch(1, 1)
        + Share.scratch(2),
        1,
        140e-6,
    )
    cotangents = cotangents.reshape(seqs, SEQ, model)
    normed = normed.reshape(-1, model)
    gate_part = w_gate_up[0, :, : ZS * hidden_width]
    gate_part, normed = lax.optimization_barrier((gate_part, normed))
    gate_part = z_exchange(gate_part.reshape(model_rows, ZS, hidden_width).transpose(1, 0, 2))

    part = table[0, ..., : 9 * micro, :local].reshape(ZS, CS, XS, micro, 9, local)
    part = part.transpose(3, 0, 1, 2, 5, 4).reshape(seqs, SEQ, 9)
    att_weight = jnp.sum(jnp.where(part[..., 0:2] == owner, part[..., 2:4], 0.0), axis=-1).reshape(-1, 1)
    hit = jnp.any(part[..., 4:6] == owner, axis=-1)
    mlp_weight = jnp.sum(jnp.where(part[..., 4:6] == owner, part[..., 6:8], 0.0), axis=-1)
    seq_blocks = part[..., 8].astype(jnp.int32)
    tables = [cosine, sine, seq_blocks[:, :, None], seq_blocks[:, None, :]]
    before_mask = jnp.arange(SEQ)[:, None] < jnp.arange(SEQ)[None, :]
    before = dot(hit.astype(BF16), before_mask.astype(BF16)).astype(jnp.int32)
    slots = jnp.arange(XS * CS * CAP)
    chosen = hit[:, None, :] & (before[:, None, :] == slots[None, :, None])
    row_gate = jnp.sum(jnp.where(chosen, mlp_weight[:, None, :], 0.0), axis=2)
    select = chosen.astype(BF16)

    def to_rows(gathered):
        return jnp.einsum("gru,gud->grd", select, gathered, preferred_element_type=F32)

    def to_tokens(rows):
        rows = rows.reshape(seqs, -1, model)
        rows = jnp.einsum("gru,grd->gud", select, rows, preferred_element_type=F32).astype(BF16)
        return rows.reshape(everyone)

    qkv = dot(normed, qkv_weight).reshape(seqs, SEQ, 3 * wide)
    turned_qkv, attended = per_sequence(attend_kernel, [qkv], tables, [3 * wide, wide], 2)
    attended = attended.reshape(-1, wide)
    result = (dot(attended, out_weight) * att_weight).astype(BF16).reshape(everyone)
    normed_two, gate_up, middle = connect(
        functools.partial(first_kernel, (model_rows, hidden_width)),
        [result, tokens, second_gain, w_gate_up, gate_part],
        [ANY, VMEM, VMEM, ANY, ANY],
        [gathered, jax.ShapeDtypeStruct((model, 2 * hidden_width), BF16), tall],
        [ANY, ANY, VMEM],
        [own_buffer]
        + Reduce.scratch(*shape)
        + Gather.scratch(micro)
        + Share.scratch(ZS)
        + Spread.scratch(1, 1),
        2,
        150e-6,
    )
    rows_two = to_rows(normed_two.reshape(seqs, SEQ, model)).astype(BF16).reshape(-1, model)
    down_grad = (to_rows(cotangents) * row_gate[:, :, None]).astype(BF16).reshape(-1, model)
    both = dot(rows_two, gate_up)
    gate, up = both[:, :hidden_width], both[:, hidden_width:]
    sigma = 1.0 / (1.0 + jnp.exp(-gate))
    hidden = (gate * sigma * up).astype(BF16)
    hidden_grad = dot_t(down_grad, down_weight)
    slope = sigma * (1.0 + gate * (1.0 - sigma))
    both_grad = jnp.concatenate(
        [hidden_grad * up * slope, hidden_grad * gate * sigma], axis=1
    ).astype(BF16)
    row_grad = to_tokens(dot_t(both_grad, gate_up).astype(BF16))
    result_two = to_tokens((dot(hidden, down_weight) * row_gate.reshape(-1, 1)).astype(BF16))

    def halved(value, other):
        return (take(value, y, 1).astype(F32) + other.astype(F32)).astype(BF16)

    def by_y(value):
        return value.astype(BF16).reshape(ZS, YS, model_rows, hidden_width)

    gate_grad = by_y(dot_l(rows_two, both_grad[:, :hidden_width]))
    gate_grad = halved(gate_grad, y_move(take(gate_grad, 1 - y, 1)))
    up_grad = by_y(dot_l(rows_two, both_grad[:, hidden_width:]))
    grad_down = dot_l(hidden, down_grad).reshape(YS, -1, model)
    middle_grads, middle_grad, gain_second, gate_grad, up_other, down_other = connect(
        second_kernel,
        [row_grad, middle, cotangent, second_gain, gate_grad, up_grad, grad_down.astype(BF16)],
        [ANY, VMEM, VMEM, VMEM, ANY, ANY, ANY],
        [
            gathered,
            tall,
            terms,
            jax.ShapeDtypeStruct((model_rows, ZS * hidden_width), BF16),
            jax.ShapeDtypeStruct((ZS, model_rows, hidden_width), BF16),
            jax.ShapeDtypeStruct(w_down.shape[1:], BF16),
        ],
        [ANY, VMEM, VMEM, ANY, ANY, ANY],
        [own_buffer]
        + Reduce.scratch(*shape)
        + Gather.scratch(micro)
        + [DMA, DMA((ZS,)), DMA((ZS,)), DMA((2,)), DMA((2,))],
        3,
        130e-6,
    )
    up_grad = z_exchange(halved(up_grad, up_other))
    grad_down = (take(grad_down, y, 0) + down_other.astype(F32))[None]
    result_grad = (middle_grads.reshape(-1, model).astype(F32) * att_weight).astype(BF16)
    attended_grad = dot_t(result_grad, out_weight).astype(BF16).reshape(seqs, SEQ, wide)
    qkv_grad = per_sequence(attend_back_kernel, [turned_qkv, attended_grad], tables, [3 * wide], 5)[0]
    qkv_grad = qkv_grad.reshape(-1, 3 * wide)
    normed_part = dot_t(qkv_grad, qkv_weight).astype(BF16).reshape(everyone)
    grad_out = dot_l(attended, result_grad).reshape(YS, -1, model)
    query_grad = dot_l(normed, qkv_grad[:, :wide]).astype(BF16).reshape(ZS, YS, model_rows, wide)
    kv_grad = dot_l(normed, qkv_grad[:, wide:]).astype(BF16).reshape(-1, CS, kv_rows, 2 * wide)
    normed_part, up_grad = lax.optimization_barrier((normed_part, up_grad))
    input_grad, output, gains, query_grad, kv_grad, out_other = connect(
        last_kernel,
        [
            normed_part,
            result_two,
            tokens,
            middle,
            middle_grad,
            first_gain,
            gain_second,
            query_grad,
            kv_grad,
            grad_out.astype(BF16),
        ],
        [ANY, ANY, VMEM, VMEM, VMEM, VMEM, VMEM, ANY, ANY, ANY],
        [
            short,
            short,
            jax.ShapeDtypeStruct((8, model), F32),
            jax.ShapeDtypeStruct((model_rows, ZS * wide), BF16),
            jax.ShapeDtypeStruct((kv_rows, 2 * ZS * wide), BF16),
            jax.ShapeDtypeStruct(w_out.shape[1:], BF16),
        ],
        [VMEM, VMEM, VMEM, ANY, ANY, ANY],
        Reduce.scratch(*shape)
        + Reduce.scratch(*shape)
        + [pltpu.VMEM((ZS, model_rows, wide), BF16) for _ in range(2)]
        + [pltpu.VMEM((ZS * YS * XS, kv_rows, 2 * wide), BF16) for _ in range(2)]
        + [pltpu.VMEM((ZS * YS, kv_rows, 2 * wide), BF16), pltpu.VMEM((ZS, kv_rows, 2 * wide), BF16)]
        + [DMA((5,)), DMA((5,)), DMA((2,)), DMA((ZS, 3)), DMA((ZS, 3)), DMA((3,))]
        + [pltpu.VMEM((8, model), F32), pltpu.VMEM((6, 8, model), F32), DMA((6,)), DMA((6,))],
        4,
        130e-6,
    )
    devices = ZS * YS * XS * CS
    gains = take(gains[:2].reshape(2, devices, model // devices), group * XS * CS + owner, 1)
    gate_up_grad = [gate_grad.astype(F32)] + [up_grad[z].astype(F32) for z in range(ZS)]
    return (
        output,
        input_grad,
        gains[0],
        gains[1],
        kv_grad.astype(F32),
        query_grad.astype(F32)[None],
        (take(grad_out, y, 0) + out_other.astype(F32))[None],
        jnp.concatenate(gate_up_grad, axis=1)[None],
        grad_down,
    )


def solution(mesh):
    in_specs = (
        P(None, ("group", "expert"), None),
        P(None, ("group", "expert"), None),
        P(),
        P(),
        P(("group", "expert"), None),
        P("expert", "group", None),
        P("expert", "group", None),
        P("expert", "group", None),
        P("expert", "group", None),
        P(None, "group", None),
        P(None, ("group", "expert"), None),
        P(None, "group", None),
        P(None, ("group", "expert"), None),
        P(None, "group", None),
    )
    out_specs = (
        P(None, ("group", "expert"), None),
        P(None, ("group", "expert"), None),
        P(("group", "expert")),
        P(("group", "expert")),
        P(("group", "expert"), None),
        P("expert", "group", None),
        P("expert", "group", None),
        P("expert", "group", None),
        P("expert", "group", None),
    )
    body = fast_device if fits(mesh) else on_device
    return jax.shard_map(
        body, mesh=mesh, in_specs=in_specs, out_specs=out_specs, check_vma=False
    )
```

```python
import functools

import jax
import jax.numpy as jnp
from jax import lax
from jax.experimental import pallas as pl
from jax.experimental.pallas import tpu as pltpu
from jax.sharding import PartitionSpec as P

HEADS = 16
HDIM = 128
CAP = 50


EPS = 1e-06
HIGH = lax.Precision.HIGHEST


def angles(positions):
    half = HDIM // 2
    freq = 10000.0 ** (-jnp.arange(half, dtype=jnp.float32) / half)
    turn = positions.astype(jnp.float32)[:, None] * freq[None, :]
    return (jnp.cos(turn), jnp.sin(turn))


def rotate(values, cosine, sine):
    count = values.shape[0]
    split = values.reshape(count, HEADS, 2, HDIM // 2)
    first = split[:, :, 0]
    second = split[:, :, 1]
    cosine = cosine[:, None, :]
    sine = sine[:, None, :]
    turned = jnp.stack([first * cosine - second * sine, second * cosine + first * sine], axis=2)
    return turned.reshape(count, HEADS * HDIM)


def routing(routes, gates, block_ids, owner, experts):
    local = routes.shape[0] // experts
    per = routes.reshape(experts, local, routes.shape[1])
    flat = per.reshape(experts, -1)
    ids = jnp.arange(experts, dtype=jnp.int32)
    onehot = (flat[:, :, None] == ids[None, None, :]).astype(jnp.int32)
    before = jnp.cumsum(onehot, axis=1) - onehot
    slots = jnp.sum(before * onehot, axis=2).reshape(per.shape)
    places = jnp.arange(CAP, dtype=jnp.int32)
    own_ids = lax.dynamic_index_in_dim(per, owner, 0, keepdims=False)
    own_slots = lax.dynamic_index_in_dim(slots, owner, 0, keepdims=False)
    sent = (
        (own_ids[None, None] == ids[:, None, None, None])
        & (own_slots[None, None] == places[None, :, None, None])
    ).astype(jnp.float32)
    pick = jnp.sum(sent, axis=3)
    weighted = jnp.sum(sent * gates[None, None], axis=3)
    arrived = ((per == owner)[:, None] & (slots[:, None] == places[None, :, None, None])).astype(
        jnp.int32
    )
    length = experts * local
    spots = jnp.arange(length, dtype=jnp.int32).reshape(experts, 1, local, 1)
    marks = block_ids.reshape(experts, 1, local, 1)
    valid = jnp.sum(arrived, axis=(2, 3)).reshape(-1)
    row_pos = jnp.sum(arrived * spots, axis=(2, 3)).reshape(-1)
    row_block = jnp.sum(arrived * marks, axis=(2, 3)).reshape(-1) + (1 - valid) * length
    return (pick, weighted, row_pos, row_block)


def score_block(queries, keys, row_block, key_block):
    count = queries.shape[0]
    raw = jnp.einsum(
        "rhd,khd->hrk",
        queries.reshape(count, HEADS, HDIM),
        keys.reshape(keys.shape[0], HEADS, HDIM),
        preferred_element_type=jnp.float32,
    )
    visible = key_block[None, None, :] <= row_block[None, :, None]
    return jnp.where(visible, raw * HDIM ** (-0.5), -1e30)


def spread(pick, normed):
    return jnp.einsum(
        "ect,td->ecd", pick.astype(jnp.bfloat16), normed, preferred_element_type=jnp.float32
    ).astype(jnp.bfloat16)


def collect(weights, arrived):
    return jnp.einsum("ect,ecd->td", weights, arrived.astype(jnp.float32), precision=HIGH)


def joined_rows(store, chosen, name):
    return jnp.concatenate([store[name][index] for index in chosen], axis=0)


def expert_reduce(store, chosen):
    pairs = (
        ("rows", "query_grad"),
        ("attended", "result_grad"),
        ("rows_two", "both_grad"),
        ("hidden", "down_grad"),
    )
    groups = lax.axis_size("group")
    results = []
    for left_name, right_name in pairs:
        left = joined_rows(store, chosen, left_name)
        right = joined_rows(store, chosen, right_name)

        def term(start, count, left=left, right=right):
            return jnp.einsum("rd,rf->df", left, right, preferred_element_type=jnp.float32)

        shard = lax.psum_scatter(
            term(jnp.int32(0), lax.axis_size("group") * (left.shape[1] // groups)).astype(
                jnp.bfloat16
            ),
            "group",
            scatter_dimension=0,
            tiled=True,
        ).astype(jnp.float32)
        results.append(shard[None])
    return tuple(results)


def reduce_all(store, chosen):
    expert_parts = expert_reduce(store, chosen)
    shared_term = jnp.einsum(
        "td,tf->df",
        joined_rows(store, chosen, "normed"),
        joined_rows(store, chosen, "mixed_grad"),
        preferred_element_type=jnp.float32,
    )
    gain_first = jnp.sum(joined_rows(store, chosen, "gain_first"), axis=0)
    gain_second = jnp.sum(joined_rows(store, chosen, "gain_second"), axis=0)
    shared_parts = (
        lax.psum_scatter(shared_term, ("group", "expert"), scatter_dimension=0, tiled=True),
        lax.psum_scatter(gain_first, ("group", "expert"), scatter_dimension=0, tiled=True),
        lax.psum_scatter(gain_second, ("group", "expert"), scatter_dimension=0, tiled=True),
    )
    return tuple(expert_parts) + tuple(shared_parts)


def on_device(
    tokens,
    cotangent,
    gain_attn,
    gain_mlp,
    w_kv,
    w_query,
    w_out,
    w_gate_up,
    w_down,
    att_routes,
    att_gates,
    mlp_routes,
    mlp_gates,
    blocks,
):
    experts = lax.axis_size("expert")
    owner = lax.axis_index("expert")
    shared_full = lax.all_gather(w_kv, ("group", "expert"), axis=0, tiled=True)
    gathered = (
        lax.all_gather(w_query, "group", axis=1, tiled=True),
        lax.all_gather(w_out, "group", axis=1, tiled=True),
        lax.all_gather(w_gate_up, "group", axis=1, tiled=True),
        lax.all_gather(w_down, "group", axis=1, tiled=True),
    )
    query_full = gathered[0][0]
    output_full = gathered[1][0]
    gate_up_full = gathered[2][0]
    down_full = gathered[3][0]
    micro = tokens.shape[0]
    local = tokens.shape[1]
    model = tokens.shape[2]
    length = local * experts
    width = HEADS * HDIM
    hidden_width = gate_up_full.shape[1] // 2
    own_cos, own_sin = angles(owner * local + jnp.arange(local, dtype=jnp.int32))
    names = (
        "rows",
        "query_grad",
        "attended",
        "result_grad",
        "rows_two",
        "both_grad",
        "hidden",
        "down_grad",
        "normed",
        "mixed_grad",
        "gain_first",
        "gain_second",
    )
    store = {name: [] for name in names}
    outputs = []
    input_grads = []
    for index in range(micro):
        inputs = tokens[index].astype(jnp.float32)
        block_ids = blocks[index, 0]
        att_pick, att_weight, row_pos, row_block = routing(
            att_routes[index], att_gates[index], block_ids, owner, experts
        )
        mlp_pick, mlp_weight, unused_pos, unused_block = routing(
            mlp_routes[index], mlp_gates[index], block_ids, owner, experts
        )
        scale = lax.rsqrt(jnp.mean(inputs * inputs, axis=1, keepdims=True) + EPS)
        normed = (inputs * scale * gain_attn).astype(jnp.bfloat16)
        mixed = jnp.dot(normed, shared_full, preferred_element_type=jnp.float32)
        keys_here = rotate(mixed[:, :width], own_cos, own_sin).astype(jnp.bfloat16)
        local_kv = jnp.concatenate([keys_here, mixed[:, width:].astype(jnp.bfloat16)], axis=1)
        sequence_kv = lax.all_gather(local_kv, "expert", axis=0, tiled=True)
        keys = sequence_kv[:, :width]
        values = sequence_kv[:, width:].reshape(length, HEADS, HDIM)
        rows = lax.all_to_all(
            spread(att_pick, normed), "expert", split_axis=0, concat_axis=0, tiled=True
        ).reshape(-1, model)
        row_cos, row_sin = angles(row_pos)
        queries = rotate(
            jnp.dot(rows, query_full, preferred_element_type=jnp.float32), row_cos, row_sin
        ).astype(jnp.bfloat16)
        scores = score_block(queries, keys, row_block, block_ids)
        top = jnp.max(scores, axis=2, keepdims=True)
        powers = jnp.exp(scores - top)
        total = jnp.sum(powers, axis=2, keepdims=True)
        log_total = top + jnp.log(total)
        probs = (powers / total).astype(jnp.bfloat16)
        attended = jnp.einsum("hrk,khd->rhd", probs, values, preferred_element_type=jnp.float32)
        attended = attended.reshape(-1, width).astype(jnp.bfloat16)
        result = jnp.dot(attended, output_full, preferred_element_type=jnp.float32).astype(
            jnp.bfloat16
        )
        back = lax.all_to_all(
            result.reshape(experts, CAP, model), "expert", split_axis=0, concat_axis=0, tiled=True
        )
        middle = inputs + collect(att_weight, back)
        scale_two = lax.rsqrt(jnp.mean(middle * middle, axis=1, keepdims=True) + EPS)
        normed_two = (middle * scale_two * gain_mlp).astype(jnp.bfloat16)
        rows_two = lax.all_to_all(
            spread(mlp_pick, normed_two), "expert", split_axis=0, concat_axis=0, tiled=True
        ).reshape(-1, model)
        both = jnp.dot(rows_two, gate_up_full, preferred_element_type=jnp.float32)
        gate = both[:, :hidden_width]
        up = both[:, hidden_width:]
        sigma = 1.0 / (1.0 + jnp.exp(-gate))
        hidden = (gate * sigma * up).astype(jnp.bfloat16)
        result_two = jnp.dot(hidden, down_full, preferred_element_type=jnp.float32).astype(
            jnp.bfloat16
        )
        back_two = lax.all_to_all(
            result_two.reshape(experts, CAP, model),
            "expert",
            split_axis=0,
            concat_axis=0,
            tiled=True,
        )
        final = middle + collect(mlp_weight, back_two)
        outputs.append(final.astype(jnp.bfloat16))
        upstream = cotangent[index].astype(jnp.float32)
        outgoing = jnp.einsum("ect,td->ecd", mlp_weight, upstream, precision=HIGH).astype(
            jnp.bfloat16
        )
        down_grad = lax.all_to_all(
            outgoing, "expert", split_axis=0, concat_axis=0, tiled=True
        ).reshape(-1, model)
        hidden_grad = jnp.einsum(
            "rd,fd->rf", down_grad, down_full, preferred_element_type=jnp.float32
        )
        slope = sigma * (1.0 + gate * (1.0 - sigma))
        both_grad = jnp.concatenate(
            [hidden_grad * up * slope, hidden_grad * gate * sigma], axis=1
        ).astype(jnp.bfloat16)
        row_grad_two = jnp.einsum(
            "rf,df->rd", both_grad, gate_up_full, preferred_element_type=jnp.float32
        ).astype(jnp.bfloat16)
        returned_two = lax.all_to_all(
            row_grad_two.reshape(experts, CAP, model),
            "expert",
            split_axis=0,
            concat_axis=0,
            tiled=True,
        )
        normed_two_grad = collect(mlp_pick, returned_two)
        scaled_two = normed_two_grad * gain_mlp
        gain_second = jnp.sum(normed_two_grad * middle * scale_two, axis=0, keepdims=True)
        middle_grad = (
            upstream
            + scale_two * scaled_two
            - middle * scale_two**3 * jnp.mean(scaled_two * middle, axis=1, keepdims=True)
        )
        outgoing_att = jnp.einsum("ect,td->ecd", att_weight, middle_grad, precision=HIGH).astype(
            jnp.bfloat16
        )
        result_grad = lax.all_to_all(
            outgoing_att, "expert", split_axis=0, concat_axis=0, tiled=True
        ).reshape(-1, model)
        attended_grad = jnp.einsum(
            "rd,fd->rf", result_grad, output_full, preferred_element_type=jnp.float32
        ).astype(jnp.bfloat16)
        again = jnp.exp(score_block(queries, keys, row_block, block_ids) - log_total)
        heads_grad = attended_grad.reshape(-1, HEADS, HDIM)
        value_grad = jnp.einsum(
            "hrk,rhd->khd",
            again.astype(jnp.bfloat16),
            heads_grad,
            preferred_element_type=jnp.float32,
        )
        prob_grad = jnp.einsum(
            "rhd,khd->hrk", heads_grad, values, preferred_element_type=jnp.float32
        )
        inner = jnp.sum(again * prob_grad, axis=2, keepdims=True)
        raw_grad = (again * (prob_grad - inner) * HDIM ** (-0.5)).astype(jnp.bfloat16)
        query_grad = jnp.einsum(
            "hrk,khd->rhd",
            raw_grad,
            keys.reshape(length, HEADS, HDIM),
            preferred_element_type=jnp.float32,
        ).reshape(-1, width)
        query_grad = rotate(query_grad, row_cos, -row_sin).astype(jnp.bfloat16)
        key_grad = jnp.einsum(
            "hrk,rhd->khd",
            raw_grad,
            queries.reshape(-1, HEADS, HDIM),
            preferred_element_type=jnp.float32,
        ).reshape(length, width)
        row_grad = jnp.einsum(
            "rf,df->rd", query_grad, query_full, preferred_element_type=jnp.float32
        ).astype(jnp.bfloat16)
        returned = lax.all_to_all(
            row_grad.reshape(experts, CAP, model), "expert", split_axis=0, concat_axis=0, tiled=True
        )
        kv_grad = lax.psum_scatter(
            jnp.concatenate([key_grad, value_grad.reshape(length, width)], axis=1).astype(
                jnp.bfloat16
            ),
            "expert",
            scatter_dimension=0,
            tiled=True,
        ).astype(jnp.float32)
        mixed_grad = jnp.concatenate(
            [rotate(kv_grad[:, :width], own_cos, -own_sin), kv_grad[:, width:]], axis=1
        ).astype(jnp.bfloat16)
        normed_grad = collect(att_pick, returned) + jnp.einsum(
            "tf,df->td", mixed_grad, shared_full, preferred_element_type=jnp.float32
        )
        scaled = normed_grad * gain_attn
        gain_first = jnp.sum(normed_grad * inputs * scale, axis=0, keepdims=True)
        input_grad = (
            middle_grad
            + scale * scaled
            - inputs * scale**3 * jnp.mean(scaled * inputs, axis=1, keepdims=True)
        )
        input_grads.append(input_grad.astype(jnp.bfloat16))
        kept = (
            rows,
            query_grad,
            attended,
            result_grad,
            rows_two,
            both_grad,
            hidden,
            down_grad,
            normed,
            mixed_grad,
            gain_first,
            gain_second,
        )
        for name, value in zip(names, kept):
            store[name].append(value)
    reduced = reduce_all(store, list(range(micro)))
    grad_query, grad_out, grad_gate_up, grad_down, grad_kv, grad_gain_attn, grad_gain_mlp = reduced
    return (
        jnp.stack(outputs, axis=0),
        jnp.stack(input_grads, axis=0),
        grad_gain_attn,
        grad_gain_mlp,
        grad_kv,
        grad_query,
        grad_out,
        grad_gate_up,
        grad_down,
    )


ZS, YS, XS, CS = 4, 2, 2, 2
SEQ = 320
F32 = jnp.float32
BF16 = jnp.bfloat16


def fits(mesh):
    return mesh.shape["group"] == ZS * YS and mesh.shape["expert"] == XS * CS


def group_move(value, move):
    pairs = []
    for z in range(ZS):
        for y in range(YS):
            to_z, to_y = move(z, y)
            pairs.append((z * YS + y, to_z * YS + to_y))
    return lax.ppermute(value, "group", pairs)


def z_move(value, step):
    return group_move(value, lambda z, y: ((z + step) % ZS, y))


def y_move(value):
    return group_move(value, lambda z, y: (z, 1 - y))


def x_move(value):
    return lax.ppermute(value, "expert", [(x * CS + c, (1 - x) * CS + c) for x in range(XS) for c in range(CS)])


def c_move(value):
    return lax.ppermute(value, "expert", [(x * CS + c, x * CS + 1 - c) for x in range(XS) for c in range(CS)])


def z_exchange(value):
    columns = [[z * YS + y for z in range(ZS)] for y in range(YS)]
    return lax.all_to_all(
        value, "group", split_axis=0, concat_axis=0, tiled=True, axis_index_groups=columns
    )


def gather_tokens(own):
    column = jnp.stack([own] + [z_move(own, -step) for step in range(1, ZS)], axis=0)
    plane = jnp.stack([column, x_move(column)], axis=1)
    plane = plane.reshape((ZS, XS * own.shape[0]) + own.shape[1:])
    return jnp.stack([plane, c_move(plane)], axis=0)


def reduce_tokens(other, mine):
    local = mine.shape[1] // XS
    total = mine.astype(F32) + c_move(other).astype(F32)
    arrived = x_move(total[:, local:].astype(BF16))
    total = total[:, :local] + arrived.astype(F32)
    result = total[0]
    for step in range(1, ZS):
        result = result + z_move(total[step].astype(BF16), step).astype(F32)
    return result


def merge(index, own, other, axis):
    return jnp.where(index == 0, jnp.stack([own, other], axis), jnp.stack([other, own], axis))


def take(value, index, axis):
    return lax.dynamic_index_in_dim(value, index, axis, keepdims=False)


def dot(left, right):
    return jnp.dot(left, right, preferred_element_type=F32)


def dot_t(left, right):
    return lax.dot_general(left, right, (((1,), (1,)), ((), ())), preferred_element_type=F32)


def dot_l(left, right):
    return lax.dot_general(left, right, (((0,), (0,)), ((), ())), preferred_element_type=F32)


def turned(value, cosine, sine):
    return value * cosine + pltpu.roll(value, HDIM // 2, 1) * sine


def masked_probs(query, key, row_block, key_block):
    scores = jnp.where(key_block <= row_block, dot_t(query, key) * HDIM ** (-0.5), -1e30)
    powers = jnp.exp(scores - jnp.max(scores, axis=1, keepdims=True))
    return powers / jnp.sum(powers, axis=1, keepdims=True)


MESH = pl.DeviceIdType.MESH
ORDER = (3, 1, 2, 0)
STEP = 16
DMA = pltpu.SemaphoreType.DMA
ANY = pl.BlockSpec(memory_space=pl.ANY)
VMEM = pl.BlockSpec(memory_space=pltpu.VMEM)


def by_rows(rows, body):
    def step(index, carry):
        body(pl.ds(pl.multiple_of(index * STEP, STEP), STEP))
        return carry

    lax.fori_loop(0, rows // STEP, step, 0)


class Place:
    def __init__(self):
        group, owner = lax.axis_index("group"), lax.axis_index("expert")
        self.z, self.y = lax.div(group, YS), lax.rem(group, YS)
        self.x, self.core = lax.div(owner, CS), lax.rem(owner, CS)
        self.group, self.owner = group, owner

        def device(z, y, x, core):
            return (z * YS + y, x * CS + core)

        self.x_peer = device(self.z, self.y, 1 - self.x, self.core)
        self.y_peer = device(self.z, 1 - self.y, self.x, self.core)
        self.core_peer = device(self.z, self.y, self.x, 1 - self.core)
        self.z_peers = [device(lax.rem(self.z + step, ZS), self.y, self.x, self.core) for step in range(ZS)]

    def enter(self, with_y):
        peers = [self.x_peer, self.core_peer] + self.z_peers[1:] + ([self.y_peer] if with_y else [])
        barrier = pltpu.get_barrier_semaphore()
        for peer in peers:
            pl.semaphore_signal(barrier, inc=1, device_id=peer, device_id_type=MESH)
        pl.semaphore_wait(barrier, len(peers))


def remote(src, dst, send, arrive, peer):
    return pltpu.make_async_remote_copy(
        src_ref=src, dst_ref=dst, send_sem=send, recv_sem=arrive, device_id=peer, device_id_type=MESH
    )


class Reduce:
    @staticmethod
    def scratch(micro, rows, model):
        return [
            pltpu.VMEM((micro, ZS, XS, rows, model), BF16),
            pltpu.VMEM((micro, ZS, XS, rows, model), BF16),
            pltpu.VMEM((micro, ZS, rows, model), BF16),
            pltpu.VMEM((micro, 2, ZS - 1, rows, model), BF16),
            pltpu.VMEM((micro, rows, model), F32),
            DMA((micro, ZS, XS)),
            DMA((micro, ZS, XS)),
            DMA((micro, ZS, XS)),
            DMA((micro, ZS)),
            DMA((micro, ZS)),
            DMA((micro, 2, ZS)),
            DMA((micro, 2, ZS)),
        ]

    def __init__(self, place, part, refs):
        self.place, self.part = place, part
        self.core_in, self.kept, self.x_in, self.z_in, self.total = [refs.pop(0) for _ in range(5)]
        self.sems = [refs.pop(0) for _ in range(7)]
        self.micro, self.rows = part.shape[0], part.shape[4]

    def core_copy(self, m, k, dx):
        send, arrive = self.sems[:2]
        return remote(
            self.part.at[m, k, 1, dx],
            self.core_in.at[m, k, dx],
            send.at[m, k, dx],
            arrive.at[m, k, dx],
            self.place.core_peer,
        )

    def kept_copy(self, m, k, dx):
        return pltpu.make_async_copy(
            self.part.at[m, k, 0, dx], self.kept.at[m, k, dx], self.sems[2].at[m, k, dx]
        )

    def x_copy(self, m, k):
        send, arrive = self.sems[3:5]
        return remote(
            self.core_in.at[m, k, 1], self.x_in.at[m, k], send.at[m, k], arrive.at[m, k], self.place.x_peer
        )

    def z_copy(self, m, down, far):
        send, arrive = self.sems[5:7]
        return remote(
            self.x_in.at[m, ZS - far if down else far],
            self.z_in.at[m, down, far - 1],
            send.at[m, down, far - 1],
            arrive.at[m, down, far - 1],
            self.place.z_peers[ZS - 1 if down else 1],
        )

    def begin(self):
        for m in range(self.micro):
            for dx in (1, 0):
                for k in ORDER:
                    self.core_copy(m, k, dx).start()
                    self.kept_copy(m, k, dx).start()

    def pass_x(self, m):
        for k in ORDER:
            self.core_copy(m, k, 1).wait_recv()
            self.kept_copy(m, k, 1).wait()

            def add(span, k=k):
                value = self.core_in[m, k, 1, span, :].astype(F32) + self.kept[m, k, 1, span, :].astype(F32)
                self.core_in[m, k, 1, span, :] = value.astype(BF16)

            by_rows(self.rows, add)
            self.x_copy(m, k).start()

    def z_unit(self, m, k):
        self.x_copy(m, k).wait_recv()
        self.core_copy(m, k, 0).wait_recv()
        self.kept_copy(m, k, 0).wait()

        def add(span):
            value = (
                self.x_in[m, k, span, :].astype(F32)
                + self.core_in[m, k, 0, span, :].astype(F32)
                + self.kept[m, k, 0, span, :].astype(F32)
            )
            if k:
                self.x_in[m, k, span, :] = value.astype(BF16)
            else:
                self.total[m, span, :] = value

        by_rows(self.rows, add)

    def beyond(self, down, far):
        return self.place.z >= far if down else self.place.z + far < ZS

    def chain(self, m, far):
        for down in (0, 1):

            def send(down=down):
                if far < ZS - 1:
                    pl.when(self.beyond(1 - down, 1))(functools.partial(self.join, m, down, far))
                self.z_copy(m, down, far).start()

            pl.when(self.beyond(down, far))(send)

    def join(self, m, down, far):
        self.z_copy(m, down, far + 1).wait_recv()
        place = ZS - far if down else far

        def add(span):
            value = self.x_in[m, place, span, :].astype(F32) + self.z_in[m, down, far, span, :].astype(F32)
            self.x_in[m, place, span, :] = value.astype(BF16)

        by_rows(self.rows, add)

    def finish(self, m):
        for down in (0, 1):

            def last(down=down):
                self.z_copy(m, down, 1).wait_recv()

                def add(span):
                    self.total[m, span, :] += self.z_in[m, down, 0, span, :].astype(F32)

                by_rows(self.rows, add)

            pl.when(self.beyond(1 - down, 1))(last)

    def sums(self, m):
        for turn, k in enumerate(ORDER):
            self.z_unit(m, k)
            if m and turn < 2:
                self.chain(m - 1, 2 - turn)
        self.chain(m, ZS - 1)

    def end_chain(self):
        for far in range(ZS - 2, 0, -1):
            self.chain(self.micro - 1, far)

    def run(self):
        self.begin()
        for m in range(self.micro):
            self.pass_x(m)
        for m in range(self.micro):
            self.sums(m)
        self.end_chain()

    def drain(self):
        for m in range(self.micro):
            for k in ORDER:
                for dx in range(XS):
                    self.core_copy(m, k, dx).wait_send()
                self.x_copy(m, k).wait_send()
            for down in (0, 1):
                for far in range(1, ZS):
                    pl.when(self.beyond(down, far))(self.z_copy(m, down, far).wait_send)


class Gather:
    @staticmethod
    def scratch(micro):
        return [
            DMA((micro,)),
            DMA((micro, ZS)),
            DMA((micro, ZS)),
            DMA((micro, ZS)),
            DMA((micro, ZS, XS)),
            DMA((micro, ZS, CS, XS)),
        ]

    def __init__(self, place, own, out, refs):
        self.place, self.own, self.out = place, own, out
        self.sems = [refs.pop(0) for _ in range(6)]
        self.micro = out.shape[0]

    def slot(self, m, k, dc, dx):
        return self.out.at[m, k, dc, dx]

    def local(self, m):
        return pltpu.make_async_copy(self.own.at[m], self.slot(m, 0, 0, 0), self.sems[0].at[m])

    def up(self, m, source, k):
        return remote(
            source, self.slot(m, k, 0, 0), self.sems[1].at[m, k], self.sems[5].at[m, k, 0, 0], self.place.z_peers[1]
        )

    def down(self, m, source, k):
        return remote(
            source,
            self.slot(m, k, 0, 0),
            self.sems[2].at[m, k],
            self.sems[5].at[m, k, 0, 0],
            self.place.z_peers[ZS - 1],
        )

    def over_x(self, m, source, k):
        return remote(
            source, self.slot(m, k, 0, 1), self.sems[3].at[m, k], self.sems[5].at[m, k, 0, 1], self.place.x_peer
        )

    def over_core(self, m, source, k, dx):
        return remote(
            source,
            self.slot(m, k, 1, dx),
            self.sems[4].at[m, k, dx],
            self.sems[5].at[m, k, 1, dx],
            self.place.core_peer,
        )

    def send_own(self, m):
        source, z = self.own.at[m], self.place.z
        pl.when(z < ZS - 1)(lambda: self.up(m, source, ZS - 1).start())
        pl.when(z > 0)(lambda: self.down(m, source, 1).start())
        self.over_x(m, source, 0).start()
        self.over_core(m, source, 0, 0).start()
        self.local(m).start()

    def pass_on(self, m, k):
        self.over_x(m, self.slot(m, k, 0, 0), k).start()
        self.over_core(m, self.slot(m, k, 0, 0), k, 0).start()

    def from_above(self, m, far):
        self.up(m, self.own.at[m], far).wait_recv()
        pl.when(self.place.z > 0)(lambda: self.down(m, self.slot(m, far, 0, 0), far + 1).start())
        self.pass_on(m, far)

    def from_below(self, m, far):
        self.up(m, self.own.at[m], ZS - far).wait_recv()
        source = self.slot(m, ZS - far, 0, 0)
        pl.when(self.place.z < ZS - 1)(lambda: self.up(m, source, ZS - far - 1).start())
        self.pass_on(m, ZS - far)

    def z_arrival(self, m, far):
        pl.when(self.place.z + far < ZS)(lambda: self.from_above(m, far))
        pl.when(self.place.z - far >= 0)(lambda: self.from_below(m, far))

    def x_arrival(self, m, k):
        self.over_x(m, self.own.at[m], k).wait_recv()
        self.over_core(m, self.slot(m, k, 0, 1), k, 1).start()

    def piece_arrival(self, m, k):
        for dx in range(XS):
            self.over_core(m, self.own.at[m], k, dx).wait_recv()

    def z_round(self, far, chosen=None):
        for m in range(self.micro) if chosen is None else [chosen]:
            self.z_arrival(m, far)

    def x_round(self, far, chosen=None):
        for m in range(self.micro) if chosen is None else [chosen]:
            if far == 0:
                self.x_arrival(m, 0)
            else:
                pl.when(self.place.z + far < ZS)(lambda: self.x_arrival(m, far))
                pl.when(self.place.z - far >= 0)(lambda: self.x_arrival(m, ZS - far))

    def run(self):
        self.z_round(1)
        self.x_round(0)
        self.z_round(2)
        self.x_round(1)
        self.z_round(3)
        self.x_round(2)
        self.x_round(3)

    def drain(self, waited=False):
        z = self.place.z
        for m in range(self.micro):
            own = self.own.at[m]
            if not waited:
                for k in range(ZS):
                    self.piece_arrival(m, k)
                self.local(m).wait()
            pl.when(z < ZS - 1)(lambda: self.up(m, own, ZS - 1).wait_send())
            pl.when(z > 0)(lambda: self.down(m, own, 1).wait_send())
            for far in range(1, ZS - 1):
                pl.when((z + far < ZS) & (z > 0))(lambda: self.down(m, own, far + 1).wait_send())
                pl.when((z - far >= 0) & (z < ZS - 1))(lambda: self.up(m, own, ZS - far - 1).wait_send())
            for k in range(ZS):
                self.over_x(m, own, k).wait_send()
                for dx in range(XS):
                    self.over_core(m, own, k, dx).wait_send()


class PieceReduce(Reduce):
    @staticmethod
    def scratch(micro, rows, model):
        return [
            pltpu.VMEM((micro, ZS, CS * XS * rows, model), BF16),
            pltpu.VMEM((micro, ZS, XS, rows, model), BF16),
            pltpu.VMEM((micro, ZS, rows, model), BF16),
            pltpu.VMEM((micro, 2, ZS - 1, rows, model), BF16),
            pltpu.VMEM((micro, rows, model), F32),
            DMA((micro, ZS, XS)),
            DMA((micro, ZS, XS)),
            DMA((micro, ZS)),
            DMA((micro, ZS)),
            DMA((micro, 2, ZS)),
            DMA((micro, 2, ZS)),
        ]

    def __init__(self, place, refs):
        self.place = place
        self.part, self.core_in, self.x_in, self.z_in, self.total = [refs.pop(0) for _ in range(5)]
        core_send, core_recv, x_send, x_recv, z_send, z_recv = [refs.pop(0) for _ in range(6)]
        self.sems = [core_send, core_recv, None, x_send, x_recv, z_send, z_recv]
        self.micro, self.rows = self.total.shape[0], self.total.shape[1]

    def unit(self, m, k, dc, dx):
        return self.part.at[m, k, pl.ds((dc * XS + dx) * self.rows, self.rows)]

    def core_copy(self, m, k, dx):
        send, arrive = self.sems[:2]
        return remote(
            self.unit(m, k, 1, dx),
            self.core_in.at[m, k, dx],
            send.at[m, k, dx],
            arrive.at[m, k, dx],
            self.place.core_peer,
        )

    def begin_piece(self, m, k):
        for dx in (1, 0):
            self.core_copy(m, k, dx).start()

    def x_piece(self, m, k):
        self.core_copy(m, k, 1).wait_recv()
        kept = self.unit(m, k, 0, 1)

        def add(span):
            value = self.core_in[m, k, 1, span, :].astype(F32) + kept[span, :].astype(F32)
            self.core_in[m, k, 1, span, :] = value.astype(BF16)

        by_rows(self.rows, add)
        self.x_copy(m, k).start()

    def z_piece(self, m, k):
        self.x_copy(m, k).wait_recv()
        self.core_copy(m, k, 0).wait_recv()
        kept = self.unit(m, k, 0, 0)

        def sum_of(span):
            return (
                self.x_in[m, k, span, :].astype(F32)
                + self.core_in[m, k, 0, span, :].astype(F32)
                + kept[span, :].astype(F32)
            )

        def away(span):
            self.x_in[m, k, span, :] = sum_of(span).astype(BF16)

        def here(span):
            self.total[m, span, :] = sum_of(span)

        pl.when(k != 0)(lambda: by_rows(self.rows, away))
        pl.when(k == 0)(lambda: by_rows(self.rows, here))

    def drain(self):
        for m in range(self.micro):
            for k in range(ZS):
                for dx in range(XS):
                    self.core_copy(m, k, dx).wait_send()
                self.x_copy(m, k).wait_send()
            for down in (0, 1):
                for far in range(1, ZS):
                    pl.when(self.beyond(down, far))(self.z_copy(m, down, far).wait_send)


def piece_of(place, index):
    turn = lax.rem(index, ZS)
    inner = turn + lax.div(turn, 2) * (5 - 2 * turn)
    last = lax.rem(ZS - turn, ZS)
    z = place.z
    return lax.div(index, ZS), jnp.where(z == 0, turn, jnp.where(z == ZS - 1, last, inner))


def run_pieces(place, reduce, piece, between):
    pieces = reduce.micro * ZS

    def step(index, carry):
        @pl.when(index < pieces)
        def _():
            m, k = piece_of(place, index)
            piece(index, m, k)
            reduce.begin_piece(m, k)

        between(index)

        @pl.when((index >= 1) & (index < pieces + 1))
        def _():
            reduce.x_piece(*piece_of(place, index - 1))

        @pl.when(index >= 3)
        def _():
            reduce.z_piece(*piece_of(place, index - 3))

        for m in range(reduce.micro - 1):
            for far in range(1, ZS):
                pl.when(index == (m + 1) * ZS + 2 + ZS - far)(functools.partial(reduce.chain, m, far))
        return carry

    lax.fori_loop(0, pieces + 3, step, 0)
    for far in range(ZS - 1, 0, -1):
        reduce.chain(reduce.micro - 1, far)


def begin_gathers(gathers):
    for m in range(gathers[0].micro):
        for gather in gathers:
            gather.send_own(m)
        if m == 0:
            for gather in gathers:
                gather.z_round(1, 0)
            for gather in gathers:
                gather.x_round(0, 0)


def gather_steps(gathers, index):
    for m in range(gathers[0].micro):
        for far in range(0 if m else 1, ZS):

            @pl.when(index == (max(0, m * (ZS - 2) - 1) + far if m else far - 1))
            def _(m=m, far=far):
                for gather in gathers:
                    if far + 1 < ZS:
                        gather.z_round(far + 1, m)
                for gather in gathers:
                    gather.x_round(far, m)


def wait_local(gather, m):
    gather.local(m).wait()


def by_lanes(count, width, body):
    def step(index, carry):
        body(pl.ds(pl.multiple_of(index * width, width), width))
        return carry

    lax.fori_loop(0, count, step, 0)


class Spread:
    @staticmethod
    def scratch(pieces, depth):
        return [DMA((pieces,)), DMA((ZS, pieces)), DMA((ZS, pieces))] + [
            DMA((ZS << step,)) for step in range(depth) for _ in range(2)
        ]

    def __init__(self, place, sources, targets, view, depth, refs):
        self.place, self.sources, self.targets, self.view, self.depth = place, sources, targets, view, depth
        self.local_sem, self.z_send, self.z_recv = [refs.pop(0) for _ in range(3)]
        self.sems = [(refs.pop(0), refs.pop(0)) for _ in range(depth)]
        self.pieces = self.local_sem.shape[0]

    def z_copy(self, step, piece):
        place = self.place
        mine = self.targets(self.view(place.z, place.y, place.x, place.core))
        return remote(
            self.sources(lax.rem(place.z + step, ZS))[piece],
            mine[piece],
            self.z_send.at[step, piece],
            self.z_recv.at[step, piece],
            place.z_peers[step],
        )

    def local(self, piece):
        place = self.place
        mine = self.targets(self.view(place.z, place.y, place.x, place.core))
        return pltpu.make_async_copy(self.sources(place.z)[piece], mine[piece], self.local_sem.at[piece])

    def hop(self, axis, index):
        place = self.place
        z = lax.rem(place.z - (index >> axis) + ZS, ZS)
        y = place.y if axis < 1 else (place.y + ((index >> (axis - 1)) & 1)) % 2
        x = place.x if axis < 2 else (place.x + (index & 1)) % 2
        block = self.view(z, y, x, place.core)
        peer = (place.y_peer, place.x_peer, place.core_peer)[axis]
        send, arrive = self.sems[axis]
        return remote(block, block, send.at[index], arrive.at[index], peer)

    def begin(self):
        for piece in range(self.pieces):
            self.local(piece).start()
        for step in (1, 3, 2):
            for piece in range(self.pieces):
                self.z_copy(step, piece).start()

    def forward(self, axis, index):
        for later in range(axis, self.depth):
            self.hop(later, index << (later - axis)).start()

    def begin_slowly(self):
        for piece in range(self.pieces):
            self.local(piece).start()
            self.z_copy(1, piece).start()

    def slow_round(self, turn):
        steps = (0, 1, 3, 2)
        self.z_round(steps[turn])
        if 0 < turn < ZS - 1:
            for piece in range(self.pieces):
                self.z_copy(steps[turn + 1], piece).start()

    def z_round(self, step):
        for piece in range(self.pieces):
            if step:
                self.z_copy(step, piece).wait_recv()
            else:
                self.local(piece).wait()
        self.forward(0, step)

    def hop_round(self, axis, index):
        self.hop(axis, index).wait_recv()
        self.forward(axis + 1, index * 2 + 1)

    def drain(self):
        for step in range(1, ZS):
            for piece in range(self.pieces):
                self.z_copy(step, piece).wait_send()
        for axis in range(self.depth):
            for index in range(ZS << axis):
                self.hop(axis, index).wait_send()


class Share:
    @staticmethod
    def scratch(pieces):
        return [DMA((pieces,)), DMA((pieces,)), DMA((pieces,))]

    def __init__(self, place, blocks, refs):
        local, send, arrive = [refs.pop(0) for _ in range(3)]
        self.copies = []
        for index, (source, target) in enumerate(blocks):
            self.copies.append(pltpu.make_async_copy(source, target, local.at[index]))
            self.copies.append(remote(source, target, send.at[index], arrive.at[index], place.y_peer))

    def begin(self):
        for copy in self.copies:
            copy.start()

    def drain(self):
        for copy in self.copies:
            copy.wait()


def normed_rows(rows, gain):
    return rows * lax.rsqrt(jnp.mean(rows * rows, axis=1, keepdims=True) + EPS) * gain


def norm_back(grad, rows, upstream, gain):
    scale = lax.rsqrt(jnp.mean(rows * rows, axis=1, keepdims=True) + EPS)
    scaled = grad * gain
    inner = jnp.mean(scaled * rows, axis=1, keepdims=True)
    return upstream + scale * scaled - rows * (scale * scale * scale) * inner, grad * rows * scale


def y_half(place, target, rows):
    return target.at[pl.ds(pl.multiple_of(place.y * rows, rows), rows)]


def gate_up_spread(place, source, kind, target, rows, refs):
    width = target.shape[1]

    def columns(z):
        return source.at[0, :, pl.ds(pl.multiple_of((kind * ZS + z) * width, HDIM), width)]

    def view(z, y, x, core):
        return target.at[pl.ds(pl.multiple_of((z * YS + y) * rows, rows), rows)]

    return Spread(place, lambda z: [columns(z)], lambda block: [block], view, 1, refs)


def by_heads(width, body):
    def step(head, carry):
        body(lambda kind: pl.ds(pl.multiple_of(kind * width + head * HDIM, HDIM), HDIM))
        return carry

    lax.fori_loop(0, width // HDIM, step, 0)


def start_kernel(sizes, tokens, gain, table, w_kv, w_query, w_out, w_gate, *refs):
    refs = list(refs)
    normed_out, table_out, qkv_weight, out_weight, gate_weight = [refs.pop(0) for _ in range(5)]
    wide, kv_rows, model_rows, out_rows = sizes
    place = Place()
    normed_own = refs.pop(0)
    normed = Gather(place, normed_own, normed_out, refs)
    tables = Gather(place, table, table_out, refs)

    def lanes(start):
        return pl.ds(pl.multiple_of(start, HDIM), wide)

    def kv_view(z, y, x, core):
        row = ((z * YS + y) * (XS * CS) + x * CS + core) * kv_rows
        return qkv_weight.at[pl.ds(pl.multiple_of(row, kv_rows), kv_rows), pl.ds(wide, 2 * wide)]

    def query_view(z, y, x, core):
        row = (z * YS + y) * model_rows
        return qkv_weight.at[pl.ds(pl.multiple_of(row, model_rows), model_rows), pl.ds(0, wide)]

    kv = Spread(
        place,
        lambda z: [w_kv.at[:, lanes(z * wide)], w_kv.at[:, lanes((ZS + z) * wide)]],
        lambda block: [block.at[:, pl.ds(0, wide)], block.at[:, pl.ds(wide, wide)]],
        kv_view,
        3,
        refs,
    )
    query = Spread(
        place, lambda z: [w_query.at[0, :, lanes(z * wide)]], lambda block: [block], query_view, 1, refs
    )

    shared = Share(place, [(w_out.at[0], y_half(place, out_weight, out_rows))], refs)
    gate = gate_up_spread(place, w_gate, 0, gate_weight, model_rows, refs)
    place.enter(True)
    kv.begin()
    tables.send_own(0)
    for m in range(normed.micro):

        def body(span, m=m):
            normed_own[m, span, :] = normed_rows(tokens[m, span, :].astype(F32), gain[...]).astype(BF16)

        by_rows(tokens.shape[1], body)
        normed.send_own(m)
    query.begin()
    kv.z_round(0)
    tables.z_round(1)
    kv.z_round(1)
    kv.z_round(3)
    normed.z_round(1)
    kv.z_round(2)
    normed.x_round(0)
    for index in (0, 1, 3, 2):
        kv.hop_round(0, index)
    tables.z_round(2)
    for step in (0, 1, 3, 2):
        query.z_round(step)
    normed.z_round(2)
    gate.begin_slowly()
    normed.x_round(1)
    gate.slow_round(0)
    normed.z_round(3)
    for index in (0, 2, 6, 4, 1, 3, 7, 5):
        kv.hop_round(1, index)
    tables.z_round(3)
    gate.slow_round(1)
    for far in range(ZS):
        tables.x_round(far)
    normed.x_round(2)
    normed.x_round(3)
    gate.slow_round(2)
    for index in range(ZS << 2):
        kv.hop_round(2, index)
    for index in range(ZS):
        query.hop_round(0, index)
    shared.begin()
    gate.slow_round(3)
    for index in range(ZS):
        gate.hop_round(0, index)
    for part in (tables, normed, kv, query, shared, gate):
        part.drain()


def attend_kernel(
    sizes, normed, weight, out_weight, row_gate, cosine, sine, row_blocks, key_blocks, tokens, gain, w_up, w_down, *refs
):
    refs = list(refs)
    normed_out, middle_out, turned_out, attended_out, up_weight, down_weight = [refs.pop(0) for _ in range(6)]
    model_rows, down_rows = sizes
    place = Place()
    reduce = PieceReduce(place, refs)
    up = gate_up_spread(place, w_up, 1, up_weight, model_rows, refs)
    shared = Share(place, [(w_down.at[0], y_half(place, down_weight, down_rows))], refs)
    arrived, qkv, attended, load, store = [refs.pop(0) for _ in range(5)]
    wide = out_weight.shape[0]
    model = out_weight.shape[1]
    tile = model // 2
    pieces = reduce.micro * ZS

    def load_of(index):
        m, k = piece_of(place, index)
        return pltpu.make_async_copy(normed.at[m * ZS + k], arrived, load)

    def stores(sequence):
        return [
            pltpu.make_async_copy(qkv, turned_out.at[sequence], store.at[0]),
            pltpu.make_async_copy(attended, attended_out.at[sequence], store.at[1]),
        ]

    def piece(index, m, k):
        sequence = m * ZS + k

        @pl.when(index > 0)
        def _():
            for copy in stores(0):
                copy.wait()

        load_of(index).wait()
        for kind in range(3):
            value = dot(arrived[...], weight[:, kind * wide : (kind + 1) * wide])
            for head in range(wide // HDIM):
                part = value[:, head * HDIM : (head + 1) * HDIM]
                if kind < 2:
                    part = turned(part, cosine[...], sine[...])
                start = kind * wide + head * HDIM
                qkv[:, start : start + HDIM] = part.astype(BF16)

        @pl.when(index + 1 < pieces)
        def _():
            load_of(index + 1).start()

        def head(span_of):
            query, key, value = [qkv[:, span_of(kind)] for kind in range(3)]
            probs = masked_probs(query, key, row_blocks[sequence], key_blocks[sequence]).astype(BF16)
            attended[:, span_of(0)] = dot(probs, value).astype(BF16)

        by_heads(wide, head)
        for start in range(0, model, tile):
            value = dot(attended[...], out_weight[:, start : start + tile]) * row_gate[sequence]
            reduce.part[m, k, :, start : start + tile] = value.astype(BF16)
        for copy in stores(sequence):
            copy.start()

    def between(index):
        for turn, at in enumerate((1, 4, 7)):
            pl.when(index == at)(functools.partial(up.slow_round, turn))

    place.enter(True)
    load_of(0).start()
    up.begin_slowly()
    shared.begin()
    run_pieces(place, reduce, piece, between)
    up.slow_round(3)
    for m in range(reduce.micro):
        reduce.finish(m)

        def body(span, m=m):
            middle = tokens[m, span, :].astype(F32) + reduce.total[m, span, :]
            middle_out[m, span, :] = middle
            normed_out[m, span, :] = normed_rows(middle, gain[...]).astype(BF16)

        by_rows(reduce.rows, body)
    for copy in stores(0):
        copy.wait()
    for index in range(ZS):
        up.hop_round(0, index)
    for part in (shared, up, reduce):
        part.drain()


def attend_back_kernel(
    rows, weight, out_weight, row_gate, cosine, sine, row_blocks, key_blocks, turned_qkv, tokens, middle_grad, gain, gate_grads, up_grads, *refs
):
    refs = list(refs)
    input_out, terms_out, row_grad_out, qkv_grad_out, weight_grad_out, other_out, everyone = [
        refs.pop(0) for _ in range(7)
    ]
    place = Place()
    gather = Gather(place, rows, everyone, refs)
    reduce = PieceReduce(place, refs)
    arrived, kept, row_grad, qkv_grad, load, store = [refs.pop(0) for _ in range(6)]
    mine, theirs, mine_sem, y_send, y_recv, z_send, z_recv, z_local = [refs.pop(0) for _ in range(8)]
    wide, model = out_weight.shape
    tile = model // 2
    width = mine.shape[2]

    def stores(sequence):
        return [
            pltpu.make_async_copy(row_grad, row_grad_out.at[sequence], store.at[0]),
            pltpu.make_async_copy(qkv_grad, qkv_grad_out.at[sequence], store.at[1]),
        ]

    def piece(index, m, k):
        sequence = m * ZS + k
        gather.piece_arrival(m, k)
        pl.when(k == 0)(lambda: gather.local(m).wait())
        loads = [
            pltpu.make_async_copy(everyone.at[m, k, dc, dx], arrived.at[dc, dx], load.at[dc, dx])
            for dc in range(CS)
            for dx in range(XS)
        ]
        loads.append(pltpu.make_async_copy(turned_qkv.at[sequence], kept, load.at[CS, 0]))
        for copy in loads:
            copy.start()

        @pl.when(index > 0)
        def _():
            for copy in stores(0):
                copy.wait()

        for copy in loads:
            copy.wait()
        length = kept.shape[0]
        for start in range(0, model, tile):
            value = arrived[:, :, :, start : start + tile].astype(F32).reshape(length, tile) * row_gate[sequence]
            row_grad[:, start : start + tile] = value.astype(BF16)
        qkv_grad[:, :wide] = dot_t(row_grad[...], out_weight[...]).astype(BF16)

        def head(span_of):
            query, key, value = [kept[:, span_of(kind)] for kind in range(3)]
            grad = qkv_grad[:, span_of(0)]
            probs = masked_probs(query, key, row_blocks[sequence], key_blocks[sequence])
            prob_grad = dot_t(grad, value)
            inner = jnp.sum(probs * prob_grad, axis=1, keepdims=True)
            raw_grad = (probs * (prob_grad - inner) * HDIM ** (-0.5)).astype(BF16)
            qkv_grad[:, span_of(0)] = turned(dot(raw_grad, key), cosine[...], -sine[...]).astype(BF16)
            qkv_grad[:, span_of(1)] = turned(dot_l(raw_grad, query), cosine[...], -sine[...]).astype(BF16)
            qkv_grad[:, span_of(2)] = dot_l(probs.astype(BF16), grad).astype(BF16)

        by_heads(wide, head)
        for start in range(0, model, tile):
            value = dot_t(qkv_grad[...], weight[start : start + tile, :])
            reduce.part[m, k, :, start : start + tile] = value.astype(BF16)
        for copy in stores(sequence):
            copy.start()

    steps = (1, 3, 2, 0)

    def z_of(turn):
        return lax.rem(place.z + steps[turn], ZS)

    def own_copy(turn):
        return pltpu.make_async_copy(gate_grads.at[z_of(turn), place.y], mine.at[turn], mine_sem.at[turn])

    def y_copy(part):
        turn = part % ZS
        grads, target = (up_grads, other_out.at[z_of(turn)]) if part >= ZS else (gate_grads, theirs.at[turn])
        return remote(
            grads.at[z_of(turn), 1 - place.y], target, y_send.at[part], y_recv.at[part], place.y_peer
        )

    columns = weight_grad_out.at[:, pl.ds(pl.multiple_of(place.z * width, HDIM), width)]

    def z_copy(turn):
        if steps[turn] == 0:
            return pltpu.make_async_copy(theirs.at[turn], columns, z_local)
        return remote(
            theirs.at[turn], columns, z_send.at[steps[turn]], z_recv.at[steps[turn]], place.z_peers[steps[turn]]
        )

    def pass_grads(part):
        y_copy(part).wait()
        if part + 2 < 2 * ZS:
            y_copy(part + 2).start()
        if part >= ZS:
            return
        own_copy(part).wait()

        def add(span):
            value = mine[part, span, :].astype(F32) + theirs[part, span, :].astype(F32)
            theirs[part, span, :] = value.astype(BF16)

        by_rows(mine.shape[1], add)
        z_copy(part).start()

    def between(index):
        gather_steps([gather], index)
        for part, at in enumerate((2, 3, 5, 6, 8, 9)):
            pl.when(index == at)(functools.partial(pass_grads, part))

    place.enter(True)
    for turn in range(ZS):
        own_copy(turn).start()
    for part in range(2):
        y_copy(part).start()
    begin_gathers([gather])
    run_pieces(place, reduce, piece, between)
    for part in range(6, 2 * ZS):
        pass_grads(part)
    terms_out[...] = jnp.zeros_like(terms_out)
    for m in range(gather.micro):
        reduce.finish(m)

        def body(span, m=m):
            result, found = norm_back(
                reduce.total[m, span, :], tokens[m, span, :].astype(F32), middle_grad[m, span, :], gain[...]
            )
            input_out[m, span, :] = result.astype(BF16)
            terms_out[...] += found

        by_rows(reduce.rows, body)
    for copy in stores(0):
        copy.wait()
    gather.drain(True)
    reduce.drain()
    for turn in range(ZS):
        z_copy(turn).wait()


def mlp_kernel(normed, gate_weight, up_weight, down, select, select_back, gates, middle, cotangent, gain, *refs):
    refs = list(refs)
    own_out, grad_out, terms_out, rows_out, up_grad_out, hidden_out, down_grad_out, result_out = [
        refs.pop(0) for _ in range(8)
    ]
    everyone, upstreams = [refs.pop(0) for _ in range(2)]
    place = Place()
    gathers = [Gather(place, normed, everyone, refs), Gather(place, cotangent, upstreams, refs)]
    reduce = PieceReduce(place, refs)
    arrived, upstream, rows, down_grad, hidden, both_grad, result = [refs.pop(0) for _ in range(7)]
    load, store = [refs.pop(0) for _ in range(2)]
    width = down.shape[0]
    model = middle.shape[2]
    tile = model // 2

    def stores(index):
        pairs = (
            (rows, rows_out),
            (down_grad, down_grad_out),
            (hidden, hidden_out),
            (both_grad, up_grad_out),
            (result, result_out),
        )
        return [
            pltpu.make_async_copy(here, there.at[index], store.at[i]) for i, (here, there) in enumerate(pairs)
        ]

    def piece(index, m, k):
        for gather in gathers:
            gather.piece_arrival(m, k)
            pl.when(k == 0)(functools.partial(wait_local, gather, m))
        sequence = m * ZS + k
        loads = [
            pltpu.make_async_copy(source.at[m, k, dc, dx], target.at[dc, dx], load.at[i, dc, dx])
            for i, (source, target) in enumerate(((everyone, arrived), (upstreams, upstream)))
            for dc in range(CS)
            for dx in range(XS)
        ]
        for copy in loads:
            copy.start()

        @pl.when(index > 0)
        def _():
            for copy in stores(0):
                copy.wait()

        for copy in loads:
            copy.wait()
        chosen, back, gate_of_row = select[sequence], select_back[sequence], gates[sequence]
        length = select.shape[2]

        def to_rows(span):
            rows[:, span] = dot(chosen, arrived[:, :, :, span].reshape(length, tile)).astype(BF16)
            down_grad[:, span] = (dot(chosen, upstream[:, :, :, span].reshape(length, tile)) * gate_of_row).astype(BF16)

        by_lanes(model // tile, tile, to_rows)

        half = width // (2 * HDIM) * HDIM
        for start, stop in ((0, half), (half, width)):
            gate = dot(rows[...], gate_weight[:, start:stop])
            up = dot(rows[...], up_weight[:, start:stop])
            hidden_grad = dot_t(down_grad[...], down[start:stop, :])
            sigma = 0.5 * jnp.tanh(0.5 * gate) + 0.5
            silu = gate * sigma
            hidden[:, start:stop] = (silu * up).astype(BF16)
            slope = sigma + silu * (1.0 - sigma)
            both_grad[:, start:stop] = (hidden_grad * up * slope).astype(BF16)
            both_grad[:, width + start : width + stop] = (hidden_grad * silu).astype(BF16)

        def to_tokens(span):
            row_grad = dot_t(both_grad[:, :width], gate_weight[span, :])
            row_grad = (row_grad + dot_t(both_grad[:, width:], up_weight[span, :])).astype(BF16)
            reduce.part[m, k, :, span] = dot(back, row_grad).astype(BF16)
            value = (dot(hidden[...], down[:, span]) * gate_of_row).astype(BF16)
            result[:, span] = dot(back, value).astype(BF16)

        by_lanes(model // tile, tile, to_tokens)
        for copy in stores(sequence):
            copy.start()

    place.enter(False)
    begin_gathers(gathers)
    run_pieces(place, reduce, piece, functools.partial(gather_steps, gathers))
    terms_out[...] = jnp.zeros_like(terms_out)
    for m in range(reduce.micro):
        reduce.finish(m)

        def body(span, m=m):
            found, terms = norm_back(
                reduce.total[m, span, :], middle[m, span, :], cotangent[m, span, :].astype(F32), gain[...]
            )
            grad_out[m, span, :] = found
            own_out[m, span, :] = found.astype(BF16)
            terms_out[...] += terms

        by_rows(reduce.rows, body)
    for copy in stores(0):
        copy.wait()
    for gather in gathers:
        gather.drain(True)
    reduce.drain()


class Halves:
    def __init__(self, own, other, copies):
        self.own, self.other, self.copies = own, other, copies

    def begin(self):
        for copy in self.copies:
            copy.start()

    def add(self):
        for copy in self.copies:
            copy.wait()

        def body(index, carry):
            value = self.own[index].astype(F32) + self.other[index].astype(F32)
            self.other[index] = value.astype(BF16)
            return carry

        lax.fori_loop(0, self.other.shape[0], body, 0)


def last_kernel(part, middle, first_terms, second_terms, query_grad, kv_grad, out_grad, *refs):
    refs = list(refs)
    output, gains_out, query_out, kv_out, out_out = [refs.pop(0) for _ in range(5)]
    place = Place()
    reduce = Reduce(place, part, refs)
    query_own, query_in, kv_own, core_in, x_in, y_in = [refs.pop(0) for _ in range(6)]
    hop_send, hop_recv, hop_local, z_send, z_recv, z_local = [refs.pop(0) for _ in range(6)]
    terms, gain_in, gain_send, gain_recv = [refs.pop(0) for _ in range(4)]
    wide, kv_rows = query_out.shape[1] // ZS, kv_out.shape[0]

    def swap(number, source, target, peer):
        return remote(source, target, hop_send.at[number], hop_recv.at[number], peer)

    query = Halves(
        query_own,
        query_in,
        [
            pltpu.make_async_copy(query_grad.at[:, place.y], query_own, hop_local.at[0]),
            swap(0, query_grad.at[:, 1 - place.y], query_in, place.y_peer),
        ],
    )
    over_core = Halves(
        kv_own,
        core_in,
        [
            pltpu.make_async_copy(kv_grad.at[:, place.core], kv_own, hop_local.at[1]),
            swap(1, kv_grad.at[:, 1 - place.core], core_in, place.core_peer),
        ],
    )
    by_x = core_in.reshape(ZS * YS, XS, kv_rows, 2 * wide)
    over_x = Halves(by_x.at[:, place.x], x_in, [swap(2, by_x.at[:, 1 - place.x], x_in, place.x_peer)])
    by_y = x_in.reshape(ZS, YS, kv_rows, 2 * wide)
    over_y = Halves(by_y.at[:, place.y], y_in, [swap(3, by_y.at[:, 1 - place.y], y_in, place.y_peer)])
    over_out = swap(4, out_grad.at[1 - place.y], out_out, place.y_peer)

    def lanes(start):
        return pl.ds(pl.multiple_of(start, HDIM), wide)

    def z_parts(step):
        to = lax.rem(place.z + step, ZS)
        pairs = [(query_in.at[to], query_out.at[:, lanes(place.z * wide)])]
        for kind in range(2):
            pairs.append(
                (y_in.at[to, :, pl.ds(kind * wide, wide)], kv_out.at[:, lanes((kind * ZS + place.z) * wide)])
            )
        return pairs

    def z_copy(step, piece):
        source, target = z_parts(step)[piece]
        if step == 0:
            return pltpu.make_async_copy(source, target, z_local.at[piece])
        return remote(source, target, z_send.at[step, piece], z_recv.at[step, piece], place.z_peers[step])

    def add_gains(number, peers):
        copies = [
            remote(terms, gain_in.at[number + i], gain_send.at[number + i], gain_recv.at[number + i], peer)
            for i, peer in enumerate(peers)
        ]
        for copy in copies:
            copy.start()
        for copy in copies:
            copy.wait()
        for i in range(len(peers)):
            terms[...] += gain_in[number + i]

    place.enter(True)
    over_core.begin()
    query.begin()
    reduce.begin()
    terms[...] = jnp.zeros_like(terms)
    terms[0:1, :] = jnp.sum(first_terms[...], axis=0, keepdims=True)
    terms[1:2, :] = jnp.sum(second_terms[...], axis=0, keepdims=True)
    over_core.add()
    over_x.begin()
    add_gains(0, [place.core_peer])
    reduce.pass_x(0)
    query.add()
    for step in (1, 3, 2, 0):
        z_copy(step, 0).start()
    over_out.start()
    add_gains(1, [place.x_peer])
    over_x.add()
    over_y.begin()
    for m in range(1, reduce.micro):
        reduce.pass_x(m)
    add_gains(2, [place.y_peer])
    reduce.sums(0)
    over_y.add()
    for step in (1, 3, 2, 0):
        for piece in (1, 2):
            z_copy(step, piece).start()
    add_gains(3, place.z_peers[1:])
    gains_out[...] = terms[...]
    for m in range(1, reduce.micro):
        reduce.sums(m)
    reduce.end_chain()
    for m in range(reduce.micro):
        reduce.finish(m)

        def finish(span, m=m):
            output[m, span, :] = (middle[m, span, :] + reduce.total[m, span, :]).astype(BF16)

        by_rows(reduce.rows, finish)
    reduce.drain()
    over_out.wait()
    for step in range(ZS):
        for piece in range(3):
            z_copy(step, piece).wait()


def connect(kernel, operands, spaces, out_shapes, out_spaces, scratch, number, seconds):
    return pl.pallas_call(
        kernel,
        in_specs=spaces,
        out_specs=out_spaces,
        out_shape=out_shapes,
        scratch_shapes=scratch,
        compiler_params=pltpu.CompilerParams(
            collective_id=number, has_side_effects=True, vmem_limit_bytes=60 << 20
        ),
        cost_estimate=pl.CostEstimate(flops=0, bytes_accessed=int(seconds * 3e12), transcendentals=0),
    )(*operands)


def fast_device(
    tokens,
    cotangent,
    gain_attn,
    gain_mlp,
    w_kv,
    w_query,
    w_out,
    w_gate_up,
    w_down,
    att_routes,
    att_gates,
    mlp_routes,
    mlp_gates,
    blocks,
):
    group, owner = lax.axis_index("group"), lax.axis_index("expert")
    y = group % YS
    x, core = owner // CS, owner % CS
    micro, local, model = tokens.shape
    wide = w_query.shape[2] // ZS
    hidden_width = w_gate_up.shape[2] // (2 * ZS)
    kv_rows = w_kv.shape[0]
    model_rows = w_query.shape[1]

    def own_rows(table):
        return lax.dynamic_slice_in_dim(table, owner * local, local, 0).astype(F32)

    lines = []
    for m in range(micro):
        lines += [own_rows(att_routes[m]).T, att_gates[m].T, own_rows(mlp_routes[m]).T, mlp_gates[m].T]
        lines += [own_rows(blocks[m, 0][:, None]).T]
    table = jnp.concatenate(lines, axis=0)
    table = jnp.pad(table, ((0, -table.shape[0] % 8), (0, -local % HDIM)))[None]

    positions = (
        (x ^ jnp.arange(XS)[None, :, None]) * CS + (core ^ jnp.arange(CS)[:, None, None])
    ) * local + jnp.arange(local)[None, None, :]
    cosine, sine = angles(positions.reshape(-1))
    cosine = jnp.concatenate([cosine, cosine], axis=1)
    sine = jnp.concatenate([-sine, sine], axis=1)

    shape = (micro, local, model)
    everyone = (micro, ZS, CS, XS, local, model)
    seqs = micro * ZS
    first_gain, second_gain = gain_attn[None], gain_mlp[None]
    tall = jax.ShapeDtypeStruct(shape, F32)
    short = jax.ShapeDtypeStruct(shape, BF16)
    gathered = jax.ShapeDtypeStruct(everyone, BF16)
    terms = jax.ShapeDtypeStruct((STEP, model), F32)
    own_buffer = pltpu.VMEM(shape, BF16)
    gate_weight = jax.ShapeDtypeStruct((model, hidden_width), BF16)
    normed, table, qkv_weight, out_weight, gate_weight = connect(
        functools.partial(start_kernel, (wide, kv_rows, model_rows, w_out.shape[1])),
        [tokens, first_gain, table, w_kv, w_query, w_out, w_gate_up],
        [VMEM, VMEM, VMEM, ANY, ANY, ANY, ANY],
        [
            gathered,
            jax.ShapeDtypeStruct((1, ZS, CS, XS) + table.shape[1:], F32),
            jax.ShapeDtypeStruct((model, 3 * wide), BF16),
            jax.ShapeDtypeStruct((wide, model), BF16),
            gate_weight,
        ],
        [ANY] * 5,
        [own_buffer]
        + Gather.scratch(micro)
        + Gather.scratch(1)
        + Spread.scratch(2, 3)
        + Spread.scratch(1, 1)
        + Share.scratch(1)
        + Spread.scratch(1, 1),
        1,
        130e-6,
    )

    part = table[0, ..., : 9 * micro, :local].reshape(ZS, CS, XS, micro, 9, local)
    part = part.transpose(3, 0, 1, 2, 5, 4).reshape(seqs, SEQ, 9)
    att_weight = jnp.sum(jnp.where(part[..., 0:2] == owner, part[..., 2:4], 0.0), axis=-1)[..., None]
    hit = jnp.any(part[..., 4:6] == owner, axis=-1)
    mlp_weight = jnp.sum(jnp.where(part[..., 4:6] == owner, part[..., 6:8], 0.0), axis=-1)
    seq_blocks = part[..., 8].astype(jnp.int32)
    tables = [cosine, sine, seq_blocks[:, :, None], seq_blocks[:, None, :]]
    before_mask = jnp.arange(SEQ)[:, None] < jnp.arange(SEQ)[None, :]
    before = dot(hit.astype(BF16), before_mask.astype(BF16)).astype(jnp.int32)
    slots = jnp.arange(XS * CS * CAP + -XS * CS * CAP % STEP)
    chosen = hit[:, None, :] & (before[:, None, :] == slots[None, :, None])
    row_gate = jnp.sum(jnp.where(chosen, mlp_weight[:, None, :], 0.0), axis=2)
    select = chosen.astype(BF16)
    slot_count = select.shape[1]

    def kept(width, rows=SEQ):
        return jax.ShapeDtypeStruct((seqs, rows, width), BF16)

    normed_two, middle, turned_qkv, attended, up_weight, down_weight = connect(
        functools.partial(attend_kernel, (model_rows, w_down.shape[1])),
        [
            normed.reshape(seqs, SEQ, model),
            qkv_weight,
            out_weight,
            att_weight,
            *tables,
            tokens,
            second_gain,
            w_gate_up,
            w_down,
        ],
        [ANY] + [VMEM] * 9 + [ANY] * 2,
        [
            short,
            tall,
            kept(3 * wide),
            kept(wide),
            jax.ShapeDtypeStruct(gate_weight.shape, BF16),
            jax.ShapeDtypeStruct((hidden_width, model), BF16),
        ],
        [VMEM, VMEM] + [ANY] * 4,
        PieceReduce.scratch(*shape)
        + Spread.scratch(1, 1)
        + Share.scratch(1)
        + [
            pltpu.VMEM((SEQ, model), BF16),
            pltpu.VMEM((SEQ, 3 * wide), BF16),
            pltpu.VMEM((SEQ, wide), BF16),
            DMA,
            DMA((2,)),
        ],
        2,
        130e-6,
    )

    middle_rows, middle_grad, gain_second, rows_two, both_grad, hidden, down_grad, result_two, *_ = connect(
        mlp_kernel,
        [
            normed_two,
            gate_weight,
            up_weight,
            down_weight,
            select,
            select.transpose(0, 2, 1),
            row_gate[:, :, None],
            middle,
            cotangent,
            second_gain,
        ],
        [VMEM] * 10,
        [
            short,
            tall,
            terms,
            kept(model, slot_count),
            kept(2 * hidden_width, slot_count),
            kept(hidden_width, slot_count),
            kept(model, slot_count),
            kept(model),
            gathered,
            gathered,
        ],
        [VMEM, VMEM, VMEM] + [ANY] * 7,
        Gather.scratch(micro)
        + Gather.scratch(micro)
        + PieceReduce.scratch(*shape)
        + [
            pltpu.VMEM((CS, XS, local, model), BF16),
            pltpu.VMEM((CS, XS, local, model), BF16),
            pltpu.VMEM((slot_count, model), BF16),
            pltpu.VMEM((slot_count, model), BF16),
            pltpu.VMEM((slot_count, hidden_width), BF16),
            pltpu.VMEM((slot_count, 2 * hidden_width), BF16),
            pltpu.VMEM((SEQ, model), BF16),
            DMA((2, CS, XS)),
            DMA((5,)),
        ],
        5,
        150e-6,
    )
    rows_two, both_grad, hidden, down_grad = [
        value.reshape(-1, value.shape[2]) for value in (rows_two, both_grad, hidden, down_grad)
    ]
    result_two = result_two.reshape(everyone)

    def by_y(value):
        return value.astype(BF16).reshape(ZS, YS, model_rows, hidden_width)

    gate_grad = by_y(dot_l(rows_two, both_grad[:, :hidden_width]))
    up_grad = by_y(dot_l(rows_two, both_grad[:, hidden_width:]))
    grad_down = dot_l(hidden, down_grad).reshape(YS, -1, model)
    down_other = y_move(take(grad_down, 1 - y, 0).astype(BF16))
    input_grad, gain_first, result_grad, qkv_grad, gate_grad, up_other, _ = connect(
        attend_back_kernel,
        [
            middle_rows,
            qkv_weight,
            out_weight,
            att_weight,
            *tables,
            turned_qkv,
            tokens,
            middle_grad,
            first_gain,
            gate_grad,
            up_grad,
        ],
        [VMEM] * 8 + [ANY] + [VMEM] * 3 + [ANY] * 2,
        [
            short,
            terms,
            kept(model),
            kept(3 * wide),
            jax.ShapeDtypeStruct((model_rows, ZS * hidden_width), BF16),
            jax.ShapeDtypeStruct((ZS, model_rows, hidden_width), BF16),
            gathered,
        ],
        [VMEM, VMEM] + [ANY] * 5,
        Gather.scratch(micro)
        + PieceReduce.scratch(*shape)
        + [
            pltpu.VMEM((CS, XS, local, model), BF16),
            pltpu.VMEM((SEQ, 3 * wide), BF16),
            pltpu.VMEM((SEQ, model), BF16),
            pltpu.VMEM((SEQ, 3 * wide), BF16),
            DMA((CS + 1, XS)),
            DMA((2,)),
            pltpu.VMEM((ZS, model_rows, hidden_width), BF16),
            pltpu.VMEM((ZS, model_rows, hidden_width), BF16),
            DMA((ZS,)),
            DMA((2 * ZS,)),
            DMA((2 * ZS,)),
            DMA((ZS,)),
            DMA((ZS,)),
            DMA,
        ],
        3,
        150e-6,
    )
    up_grad = (take(up_grad, y, 1).astype(F32) + up_other.astype(F32)).astype(BF16)
    up_grad = z_exchange(up_grad)
    result_grad, qkv_grad, attended, normed = [
        value.reshape(-1, value.shape[-1]) for value in (result_grad, qkv_grad, attended, normed)
    ]
    grad_out = dot_l(attended, result_grad).reshape(YS, -1, model)
    query_grad = dot_l(normed, qkv_grad[:, :wide]).astype(BF16).reshape(ZS, YS, model_rows, wide)
    kv_grad = dot_l(normed, qkv_grad[:, wide:]).astype(BF16).reshape(-1, CS, kv_rows, 2 * wide)
    output, gains, query_grad, kv_grad, out_other = connect(
        last_kernel,
        [
            result_two,
            middle,
            gain_first,
            gain_second,
            query_grad,
            kv_grad,
            grad_out.astype(BF16),
        ],
        [ANY, VMEM, VMEM, VMEM] + [ANY] * 3,
        [
            short,
            jax.ShapeDtypeStruct((8, model), F32),
            jax.ShapeDtypeStruct((model_rows, ZS * wide), BF16),
            jax.ShapeDtypeStruct((kv_rows, 2 * ZS * wide), BF16),
            jax.ShapeDtypeStruct(w_out.shape[1:], BF16),
        ],
        [VMEM, VMEM] + [ANY] * 3,
        Reduce.scratch(*shape)
        + [pltpu.VMEM((ZS, model_rows, wide), BF16) for _ in range(2)]
        + [pltpu.VMEM((ZS * YS * XS, kv_rows, 2 * wide), BF16) for _ in range(2)]
        + [pltpu.VMEM((ZS * YS, kv_rows, 2 * wide), BF16), pltpu.VMEM((ZS, kv_rows, 2 * wide), BF16)]
        + [DMA((6,)), DMA((6,)), DMA((2,)), DMA((ZS, 3)), DMA((ZS, 3)), DMA((3,))]
        + [pltpu.VMEM((8, model), F32), pltpu.VMEM((6, 8, model), F32), DMA((6,)), DMA((6,))],
        4,
        90e-6,
    )
    devices = ZS * YS * XS * CS
    gains = take(gains[:2].reshape(2, devices, model // devices), group * XS * CS + owner, 1)
    return (
        output,
        input_grad,
        gains[0],
        gains[1],
        kv_grad.astype(F32),
        query_grad.astype(F32)[None],
        (take(grad_out, y, 0) + out_other.astype(F32))[None],
        jnp.concatenate([gate_grad.astype(F32)] + [up_grad[z].astype(F32) for z in range(ZS)], axis=1)[None],
        (take(grad_down, y, 0) + down_other.astype(F32))[None],
    )


def solution(mesh):
    in_specs = (
        P(None, ("group", "expert"), None),
        P(None, ("group", "expert"), None),
        P(),
        P(),
        P(("group", "expert"), None),
        P("expert", "group", None),
        P("expert", "group", None),
        P("expert", "group", None),
        P("expert", "group", None),
        P(None, "group", None),
        P(None, ("group", "expert"), None),
        P(None, "group", None),
        P(None, ("group", "expert"), None),
        P(None, "group", None),
    )
    out_specs = (
        P(None, ("group", "expert"), None),
        P(None, ("group", "expert"), None),
        P(("group", "expert")),
        P(("group", "expert")),
        P(("group", "expert"), None),
        P("expert", "group", None),
        P("expert", "group", None),
        P("expert", "group", None),
        P("expert", "group", None),
    )
    body = fast_device if fits(mesh) else on_device
    return jax.shard_map(
        body, mesh=mesh, in_specs=in_specs, out_specs=out_specs, check_vma=False
    )
```

```python
import functools

import jax
import jax.numpy as jnp
from jax import lax
from jax.experimental import pallas as pl
from jax.experimental.pallas import tpu as pltpu
from jax.sharding import PartitionSpec as P

HEADS = 16
HDIM = 128
CAP = 50


EPS = 1e-06
HIGH = lax.Precision.HIGHEST


def angles(positions):
    half = HDIM // 2
    freq = 10000.0 ** (-jnp.arange(half, dtype=jnp.float32) / half)
    turn = positions.astype(jnp.float32)[:, None] * freq[None, :]
    return (jnp.cos(turn), jnp.sin(turn))


def rotate(values, cosine, sine):
    count = values.shape[0]
    split = values.reshape(count, HEADS, 2, HDIM // 2)
    first = split[:, :, 0]
    second = split[:, :, 1]
    cosine = cosine[:, None, :]
    sine = sine[:, None, :]
    turned = jnp.stack([first * cosine - second * sine, second * cosine + first * sine], axis=2)
    return turned.reshape(count, HEADS * HDIM)


def routing(routes, gates, block_ids, owner, experts):
    local = routes.shape[0] // experts
    per = routes.reshape(experts, local, routes.shape[1])
    flat = per.reshape(experts, -1)
    ids = jnp.arange(experts, dtype=jnp.int32)
    onehot = (flat[:, :, None] == ids[None, None, :]).astype(jnp.int32)
    before = jnp.cumsum(onehot, axis=1) - onehot
    slots = jnp.sum(before * onehot, axis=2).reshape(per.shape)
    places = jnp.arange(CAP, dtype=jnp.int32)
    own_ids = lax.dynamic_index_in_dim(per, owner, 0, keepdims=False)
    own_slots = lax.dynamic_index_in_dim(slots, owner, 0, keepdims=False)
    sent = (
        (own_ids[None, None] == ids[:, None, None, None])
        & (own_slots[None, None] == places[None, :, None, None])
    ).astype(jnp.float32)
    pick = jnp.sum(sent, axis=3)
    weighted = jnp.sum(sent * gates[None, None], axis=3)
    arrived = ((per == owner)[:, None] & (slots[:, None] == places[None, :, None, None])).astype(
        jnp.int32
    )
    length = experts * local
    spots = jnp.arange(length, dtype=jnp.int32).reshape(experts, 1, local, 1)
    marks = block_ids.reshape(experts, 1, local, 1)
    valid = jnp.sum(arrived, axis=(2, 3)).reshape(-1)
    row_pos = jnp.sum(arrived * spots, axis=(2, 3)).reshape(-1)
    row_block = jnp.sum(arrived * marks, axis=(2, 3)).reshape(-1) + (1 - valid) * length
    return (pick, weighted, row_pos, row_block)


def score_block(queries, keys, row_block, key_block):
    count = queries.shape[0]
    raw = jnp.einsum(
        "rhd,khd->hrk",
        queries.reshape(count, HEADS, HDIM),
        keys.reshape(keys.shape[0], HEADS, HDIM),
        preferred_element_type=jnp.float32,
    )
    visible = key_block[None, None, :] <= row_block[None, :, None]
    return jnp.where(visible, raw * HDIM ** (-0.5), -1e30)


def spread(pick, normed):
    return jnp.einsum(
        "ect,td->ecd", pick.astype(jnp.bfloat16), normed, preferred_element_type=jnp.float32
    ).astype(jnp.bfloat16)


def collect(weights, arrived):
    return jnp.einsum("ect,ecd->td", weights, arrived.astype(jnp.float32), precision=HIGH)


def joined_rows(store, chosen, name):
    return jnp.concatenate([store[name][index] for index in chosen], axis=0)


def expert_reduce(store, chosen):
    pairs = (
        ("rows", "query_grad"),
        ("attended", "result_grad"),
        ("rows_two", "both_grad"),
        ("hidden", "down_grad"),
    )
    groups = lax.axis_size("group")
    results = []
    for left_name, right_name in pairs:
        left = joined_rows(store, chosen, left_name)
        right = joined_rows(store, chosen, right_name)

        def term(start, count, left=left, right=right):
            return jnp.einsum("rd,rf->df", left, right, preferred_element_type=jnp.float32)

        shard = lax.psum_scatter(
            term(jnp.int32(0), lax.axis_size("group") * (left.shape[1] // groups)).astype(
                jnp.bfloat16
            ),
            "group",
            scatter_dimension=0,
            tiled=True,
        ).astype(jnp.float32)
        results.append(shard[None])
    return tuple(results)


def reduce_all(store, chosen):
    expert_parts = expert_reduce(store, chosen)
    shared_term = jnp.einsum(
        "td,tf->df",
        joined_rows(store, chosen, "normed"),
        joined_rows(store, chosen, "mixed_grad"),
        preferred_element_type=jnp.float32,
    )
    gain_first = jnp.sum(joined_rows(store, chosen, "gain_first"), axis=0)
    gain_second = jnp.sum(joined_rows(store, chosen, "gain_second"), axis=0)
    shared_parts = (
        lax.psum_scatter(shared_term, ("group", "expert"), scatter_dimension=0, tiled=True),
        lax.psum_scatter(gain_first, ("group", "expert"), scatter_dimension=0, tiled=True),
        lax.psum_scatter(gain_second, ("group", "expert"), scatter_dimension=0, tiled=True),
    )
    return tuple(expert_parts) + tuple(shared_parts)


def on_device(
    tokens,
    cotangent,
    gain_attn,
    gain_mlp,
    w_kv,
    w_query,
    w_out,
    w_gate_up,
    w_down,
    att_routes,
    att_gates,
    mlp_routes,
    mlp_gates,
    blocks,
):
    experts = lax.axis_size("expert")
    owner = lax.axis_index("expert")
    shared_full = lax.all_gather(w_kv, ("group", "expert"), axis=0, tiled=True)
    gathered = (
        lax.all_gather(w_query, "group", axis=1, tiled=True),
        lax.all_gather(w_out, "group", axis=1, tiled=True),
        lax.all_gather(w_gate_up, "group", axis=1, tiled=True),
        lax.all_gather(w_down, "group", axis=1, tiled=True),
    )
    query_full = gathered[0][0]
    output_full = gathered[1][0]
    gate_up_full = gathered[2][0]
    down_full = gathered[3][0]
    micro = tokens.shape[0]
    local = tokens.shape[1]
    model = tokens.shape[2]
    length = local * experts
    width = HEADS * HDIM
    hidden_width = gate_up_full.shape[1] // 2
    own_cos, own_sin = angles(owner * local + jnp.arange(local, dtype=jnp.int32))
    names = (
        "rows",
        "query_grad",
        "attended",
        "result_grad",
        "rows_two",
        "both_grad",
        "hidden",
        "down_grad",
        "normed",
        "mixed_grad",
        "gain_first",
        "gain_second",
    )
    store = {name: [] for name in names}
    outputs = []
    input_grads = []
    for index in range(micro):
        inputs = tokens[index].astype(jnp.float32)
        block_ids = blocks[index, 0]
        att_pick, att_weight, row_pos, row_block = routing(
            att_routes[index], att_gates[index], block_ids, owner, experts
        )
        mlp_pick, mlp_weight, unused_pos, unused_block = routing(
            mlp_routes[index], mlp_gates[index], block_ids, owner, experts
        )
        scale = lax.rsqrt(jnp.mean(inputs * inputs, axis=1, keepdims=True) + EPS)
        normed = (inputs * scale * gain_attn).astype(jnp.bfloat16)
        mixed = jnp.dot(normed, shared_full, preferred_element_type=jnp.float32)
        keys_here = rotate(mixed[:, :width], own_cos, own_sin).astype(jnp.bfloat16)
        local_kv = jnp.concatenate([keys_here, mixed[:, width:].astype(jnp.bfloat16)], axis=1)
        sequence_kv = lax.all_gather(local_kv, "expert", axis=0, tiled=True)
        keys = sequence_kv[:, :width]
        values = sequence_kv[:, width:].reshape(length, HEADS, HDIM)
        rows = lax.all_to_all(
            spread(att_pick, normed), "expert", split_axis=0, concat_axis=0, tiled=True
        ).reshape(-1, model)
        row_cos, row_sin = angles(row_pos)
        queries = rotate(
            jnp.dot(rows, query_full, preferred_element_type=jnp.float32), row_cos, row_sin
        ).astype(jnp.bfloat16)
        scores = score_block(queries, keys, row_block, block_ids)
        top = jnp.max(scores, axis=2, keepdims=True)
        powers = jnp.exp(scores - top)
        total = jnp.sum(powers, axis=2, keepdims=True)
        log_total = top + jnp.log(total)
        probs = (powers / total).astype(jnp.bfloat16)
        attended = jnp.einsum("hrk,khd->rhd", probs, values, preferred_element_type=jnp.float32)
        attended = attended.reshape(-1, width).astype(jnp.bfloat16)
        result = jnp.dot(attended, output_full, preferred_element_type=jnp.float32).astype(
            jnp.bfloat16
        )
        back = lax.all_to_all(
            result.reshape(experts, CAP, model), "expert", split_axis=0, concat_axis=0, tiled=True
        )
        middle = inputs + collect(att_weight, back)
        scale_two = lax.rsqrt(jnp.mean(middle * middle, axis=1, keepdims=True) + EPS)
        normed_two = (middle * scale_two * gain_mlp).astype(jnp.bfloat16)
        rows_two = lax.all_to_all(
            spread(mlp_pick, normed_two), "expert", split_axis=0, concat_axis=0, tiled=True
        ).reshape(-1, model)
        both = jnp.dot(rows_two, gate_up_full, preferred_element_type=jnp.float32)
        gate = both[:, :hidden_width]
        up = both[:, hidden_width:]
        sigma = 1.0 / (1.0 + jnp.exp(-gate))
        hidden = (gate * sigma * up).astype(jnp.bfloat16)
        result_two = jnp.dot(hidden, down_full, preferred_element_type=jnp.float32).astype(
            jnp.bfloat16
        )
        back_two = lax.all_to_all(
            result_two.reshape(experts, CAP, model),
            "expert",
            split_axis=0,
            concat_axis=0,
            tiled=True,
        )
        final = middle + collect(mlp_weight, back_two)
        outputs.append(final.astype(jnp.bfloat16))
        upstream = cotangent[index].astype(jnp.float32)
        outgoing = jnp.einsum("ect,td->ecd", mlp_weight, upstream, precision=HIGH).astype(
            jnp.bfloat16
        )
        down_grad = lax.all_to_all(
            outgoing, "expert", split_axis=0, concat_axis=0, tiled=True
        ).reshape(-1, model)
        hidden_grad = jnp.einsum(
            "rd,fd->rf", down_grad, down_full, preferred_element_type=jnp.float32
        )
        slope = sigma * (1.0 + gate * (1.0 - sigma))
        both_grad = jnp.concatenate(
            [hidden_grad * up * slope, hidden_grad * gate * sigma], axis=1
        ).astype(jnp.bfloat16)
        row_grad_two = jnp.einsum(
            "rf,df->rd", both_grad, gate_up_full, preferred_element_type=jnp.float32
        ).astype(jnp.bfloat16)
        returned_two = lax.all_to_all(
            row_grad_two.reshape(experts, CAP, model),
            "expert",
            split_axis=0,
            concat_axis=0,
            tiled=True,
        )
        normed_two_grad = collect(mlp_pick, returned_two)
        scaled_two = normed_two_grad * gain_mlp
        gain_second = jnp.sum(normed_two_grad * middle * scale_two, axis=0, keepdims=True)
        middle_grad = (
            upstream
            + scale_two * scaled_two
            - middle * scale_two**3 * jnp.mean(scaled_two * middle, axis=1, keepdims=True)
        )
        outgoing_att = jnp.einsum("ect,td->ecd", att_weight, middle_grad, precision=HIGH).astype(
            jnp.bfloat16
        )
        result_grad = lax.all_to_all(
            outgoing_att, "expert", split_axis=0, concat_axis=0, tiled=True
        ).reshape(-1, model)
        attended_grad = jnp.einsum(
            "rd,fd->rf", result_grad, output_full, preferred_element_type=jnp.float32
        ).astype(jnp.bfloat16)
        again = jnp.exp(score_block(queries, keys, row_block, block_ids) - log_total)
        heads_grad = attended_grad.reshape(-1, HEADS, HDIM)
        value_grad = jnp.einsum(
            "hrk,rhd->khd",
            again.astype(jnp.bfloat16),
            heads_grad,
            preferred_element_type=jnp.float32,
        )
        prob_grad = jnp.einsum(
            "rhd,khd->hrk", heads_grad, values, preferred_element_type=jnp.float32
        )
        inner = jnp.sum(again * prob_grad, axis=2, keepdims=True)
        raw_grad = (again * (prob_grad - inner) * HDIM ** (-0.5)).astype(jnp.bfloat16)
        query_grad = jnp.einsum(
            "hrk,khd->rhd",
            raw_grad,
            keys.reshape(length, HEADS, HDIM),
            preferred_element_type=jnp.float32,
        ).reshape(-1, width)
        query_grad = rotate(query_grad, row_cos, -row_sin).astype(jnp.bfloat16)
        key_grad = jnp.einsum(
            "hrk,rhd->khd",
            raw_grad,
            queries.reshape(-1, HEADS, HDIM),
            preferred_element_type=jnp.float32,
        ).reshape(length, width)
        row_grad = jnp.einsum(
            "rf,df->rd", query_grad, query_full, preferred_element_type=jnp.float32
        ).astype(jnp.bfloat16)
        returned = lax.all_to_all(
            row_grad.reshape(experts, CAP, model), "expert", split_axis=0, concat_axis=0, tiled=True
        )
        kv_grad = lax.psum_scatter(
            jnp.concatenate([key_grad, value_grad.reshape(length, width)], axis=1).astype(
                jnp.bfloat16
            ),
            "expert",
            scatter_dimension=0,
            tiled=True,
        ).astype(jnp.float32)
        mixed_grad = jnp.concatenate(
            [rotate(kv_grad[:, :width], own_cos, -own_sin), kv_grad[:, width:]], axis=1
        ).astype(jnp.bfloat16)
        normed_grad = collect(att_pick, returned) + jnp.einsum(
            "tf,df->td", mixed_grad, shared_full, preferred_element_type=jnp.float32
        )
        scaled = normed_grad * gain_attn
        gain_first = jnp.sum(normed_grad * inputs * scale, axis=0, keepdims=True)
        input_grad = (
            middle_grad
            + scale * scaled
            - inputs * scale**3 * jnp.mean(scaled * inputs, axis=1, keepdims=True)
        )
        input_grads.append(input_grad.astype(jnp.bfloat16))
        kept = (
            rows,
            query_grad,
            attended,
            result_grad,
            rows_two,
            both_grad,
            hidden,
            down_grad,
            normed,
            mixed_grad,
            gain_first,
            gain_second,
        )
        for name, value in zip(names, kept):
            store[name].append(value)
    reduced = reduce_all(store, list(range(micro)))
    grad_query, grad_out, grad_gate_up, grad_down, grad_kv, grad_gain_attn, grad_gain_mlp = reduced
    return (
        jnp.stack(outputs, axis=0),
        jnp.stack(input_grads, axis=0),
        grad_gain_attn,
        grad_gain_mlp,
        grad_kv,
        grad_query,
        grad_out,
        grad_gate_up,
        grad_down,
    )


ZS, YS, XS, CS = 4, 2, 2, 2
SEQ = 320
MICRO = 2
KINDS = 9
F32 = jnp.float32
BF16 = jnp.bfloat16


def fits(mesh):
    return mesh.shape["group"] == ZS * YS and mesh.shape["expert"] == XS * CS


def group_move(value, move):
    pairs = []
    for z in range(ZS):
        for y in range(YS):
            to_z, to_y = move(z, y)
            pairs.append((z * YS + y, to_z * YS + to_y))
    return lax.ppermute(value, "group", pairs)


def z_move(value, step):
    return group_move(value, lambda z, y: ((z + step) % ZS, y))


def y_move(value):
    return group_move(value, lambda z, y: (z, 1 - y))


def x_move(value):
    return lax.ppermute(value, "expert", [(x * CS + c, (1 - x) * CS + c) for x in range(XS) for c in range(CS)])


def c_move(value):
    return lax.ppermute(value, "expert", [(x * CS + c, x * CS + 1 - c) for x in range(XS) for c in range(CS)])


def z_exchange(value):
    columns = [[z * YS + y for z in range(ZS)] for y in range(YS)]
    return lax.all_to_all(
        value, "group", split_axis=0, concat_axis=0, tiled=True, axis_index_groups=columns
    )


def gather_tokens(own):
    column = jnp.stack([own] + [z_move(own, -step) for step in range(1, ZS)], axis=0)
    plane = jnp.stack([column, x_move(column)], axis=1)
    plane = plane.reshape((ZS, XS * own.shape[0]) + own.shape[1:])
    return jnp.stack([plane, c_move(plane)], axis=0)


def reduce_tokens(other, mine):
    local = mine.shape[1] // XS
    total = mine.astype(F32) + c_move(other).astype(F32)
    arrived = x_move(total[:, local:].astype(BF16))
    total = total[:, :local] + arrived.astype(F32)
    result = total[0]
    for step in range(1, ZS):
        result = result + z_move(total[step].astype(BF16), step).astype(F32)
    return result


def merge(index, own, other, axis):
    return jnp.where(index == 0, jnp.stack([own, other], axis), jnp.stack([other, own], axis))


def take(value, index, axis):
    return lax.dynamic_index_in_dim(value, index, axis, keepdims=False)


def dot(left, right):
    return jnp.dot(left, right, preferred_element_type=F32)


def dot_t(left, right):
    return lax.dot_general(left, right, (((1,), (1,)), ((), ())), preferred_element_type=F32)


def dot_l(left, right):
    return lax.dot_general(left, right, (((0,), (0,)), ((), ())), preferred_element_type=F32)


def turned(value, cosine, sine):
    return value * cosine + pltpu.roll(value, HDIM // 2, 1) * sine


def masked_probs(query, key, row_block, key_block):
    scores = jnp.where(key_block <= row_block, dot_t(query, key) * HDIM ** (-0.5), -1e30)
    powers = jnp.exp(scores - jnp.max(scores, axis=1, keepdims=True))
    return powers / jnp.sum(powers, axis=1, keepdims=True)


MESH = pl.DeviceIdType.MESH
ORDER = (3, 1, 2, 0)
STEP = 16
DMA = pltpu.SemaphoreType.DMA
ANY = pl.BlockSpec(memory_space=pl.ANY)
VMEM = pl.BlockSpec(memory_space=pltpu.VMEM)


def by_rows(rows, body):
    def step(index, carry):
        body(pl.ds(pl.multiple_of(index * STEP, STEP), STEP))
        return carry

    lax.fori_loop(0, rows // STEP, step, 0)


class Place:
    def __init__(self):
        group, owner = lax.axis_index("group"), lax.axis_index("expert")
        self.z, self.y = lax.div(group, YS), lax.rem(group, YS)
        self.x, self.core = lax.div(owner, CS), lax.rem(owner, CS)
        self.group, self.owner = group, owner

        def device(z, y, x, core):
            return (z * YS + y, x * CS + core)

        self.x_peer = device(self.z, self.y, 1 - self.x, self.core)
        self.y_peer = device(self.z, 1 - self.y, self.x, self.core)
        self.core_peer = device(self.z, self.y, self.x, 1 - self.core)
        self.z_peers = [device(lax.rem(self.z + step, ZS), self.y, self.x, self.core) for step in range(ZS)]

    def enter(self, with_y):
        peers = [self.x_peer, self.core_peer] + self.z_peers[1:] + ([self.y_peer] if with_y else [])
        barrier = pltpu.get_barrier_semaphore()
        for peer in peers:
            pl.semaphore_signal(barrier, inc=1, device_id=peer, device_id_type=MESH)
        pl.semaphore_wait(barrier, len(peers))


def remote(src, dst, send, arrive, peer):
    return pltpu.make_async_remote_copy(
        src_ref=src, dst_ref=dst, send_sem=send, recv_sem=arrive, device_id=peer, device_id_type=MESH
    )


class Reduce:
    @staticmethod
    def scratch(micro, rows, model):
        return [
            pltpu.VMEM((micro, ZS, XS, rows, model), BF16),
            pltpu.VMEM((micro, ZS, XS, rows, model), BF16),
            pltpu.VMEM((micro, ZS, rows, model), BF16),
            pltpu.VMEM((micro, 2, ZS - 1, rows, model), BF16),
            pltpu.VMEM((micro, rows, model), F32),
            DMA((micro, ZS, XS)),
            DMA((micro, ZS, XS)),
            DMA((micro, ZS, XS)),
            DMA((micro, ZS)),
            DMA((micro, ZS)),
            DMA((micro, 2, ZS)),
            DMA((micro, 2, ZS)),
        ]

    def __init__(self, place, part, refs):
        self.place, self.part = place, part
        self.core_in, self.kept, self.x_in, self.z_in, self.total = [refs.pop(0) for _ in range(5)]
        self.sems = [refs.pop(0) for _ in range(7)]
        self.micro, self.rows = part.shape[0], part.shape[4]

    def core_copy(self, m, k, dx):
        send, arrive = self.sems[:2]
        return remote(
            self.part.at[m, k, 1, dx],
            self.core_in.at[m, k, dx],
            send.at[m, k, dx],
            arrive.at[m, k, dx],
            self.place.core_peer,
        )

    def kept_copy(self, m, k, dx):
        return pltpu.make_async_copy(
            self.part.at[m, k, 0, dx], self.kept.at[m, k, dx], self.sems[2].at[m, k, dx]
        )

    def x_copy(self, m, k):
        send, arrive = self.sems[3:5]
        return remote(
            self.core_in.at[m, k, 1], self.x_in.at[m, k], send.at[m, k], arrive.at[m, k], self.place.x_peer
        )

    def z_copy(self, m, down, far):
        send, arrive = self.sems[5:7]
        return remote(
            self.x_in.at[m, ZS - far if down else far],
            self.z_in.at[m, down, far - 1],
            send.at[m, down, far - 1],
            arrive.at[m, down, far - 1],
            self.place.z_peers[ZS - 1 if down else 1],
        )

    def begin(self):
        for m in range(self.micro):
            for dx in (1, 0):
                for k in ORDER:
                    self.core_copy(m, k, dx).start()
                    self.kept_copy(m, k, dx).start()

    def pass_x(self, m):
        for k in ORDER:
            self.core_copy(m, k, 1).wait_recv()
            self.kept_copy(m, k, 1).wait()

            def add(span, k=k):
                value = self.core_in[m, k, 1, span, :].astype(F32) + self.kept[m, k, 1, span, :].astype(F32)
                self.core_in[m, k, 1, span, :] = value.astype(BF16)

            by_rows(self.rows, add)
            self.x_copy(m, k).start()

    def z_unit(self, m, k):
        self.x_copy(m, k).wait_recv()
        self.core_copy(m, k, 0).wait_recv()
        self.kept_copy(m, k, 0).wait()

        def add(span):
            value = (
                self.x_in[m, k, span, :].astype(F32)
                + self.core_in[m, k, 0, span, :].astype(F32)
                + self.kept[m, k, 0, span, :].astype(F32)
            )
            if k:
                self.x_in[m, k, span, :] = value.astype(BF16)
            else:
                self.total[m, span, :] = value

        by_rows(self.rows, add)

    def beyond(self, down, far):
        return self.place.z >= far if down else self.place.z + far < ZS

    def chain(self, m, far):
        for down in (0, 1):

            def send(down=down):
                if far < ZS - 1:
                    pl.when(self.beyond(1 - down, 1))(functools.partial(self.join, m, down, far))
                self.z_copy(m, down, far).start()

            pl.when(self.beyond(down, far))(send)

    def join(self, m, down, far):
        self.z_copy(m, down, far + 1).wait_recv()
        place = ZS - far if down else far

        def add(span):
            value = self.x_in[m, place, span, :].astype(F32) + self.z_in[m, down, far, span, :].astype(F32)
            self.x_in[m, place, span, :] = value.astype(BF16)

        by_rows(self.rows, add)

    def finish(self, m):
        for down in (0, 1):

            def last(down=down):
                self.z_copy(m, down, 1).wait_recv()

                def add(span):
                    self.total[m, span, :] += self.z_in[m, down, 0, span, :].astype(F32)

                by_rows(self.rows, add)

            pl.when(self.beyond(1 - down, 1))(last)

    def sums(self, m):
        for turn, k in enumerate(ORDER):
            self.z_unit(m, k)
            if turn:
                self.chain(m, ZS - turn)

    def run(self):
        self.begin()
        for m in range(self.micro):
            self.pass_x(m)
        for m in range(self.micro):
            self.sums(m)

    def drain(self):
        for m in range(self.micro):
            for k in ORDER:
                for dx in range(XS):
                    self.core_copy(m, k, dx).wait_send()
                self.x_copy(m, k).wait_send()
            for down in (0, 1):
                for far in range(1, ZS):
                    pl.when(self.beyond(down, far))(self.z_copy(m, down, far).wait_send)


class Gather:
    @staticmethod
    def scratch(micro):
        return [
            DMA((micro,)),
            DMA((micro, ZS)),
            DMA((micro, ZS)),
            DMA((micro, ZS)),
            DMA((micro, ZS, XS)),
            DMA((micro, ZS, CS, XS)),
        ]

    def __init__(self, place, own, out, refs):
        self.place, self.own, self.out = place, own, out
        self.sems = [refs.pop(0) for _ in range(6)]
        self.micro = out.shape[0]

    def slot(self, m, k, dc, dx):
        return self.out.at[m, k, dc, dx]

    def local(self, m):
        return pltpu.make_async_copy(self.own.at[m], self.slot(m, 0, 0, 0), self.sems[0].at[m])

    def up(self, m, source, k):
        return remote(
            source, self.slot(m, k, 0, 0), self.sems[1].at[m, k], self.sems[5].at[m, k, 0, 0], self.place.z_peers[1]
        )

    def down(self, m, source, k):
        return remote(
            source,
            self.slot(m, k, 0, 0),
            self.sems[2].at[m, k],
            self.sems[5].at[m, k, 0, 0],
            self.place.z_peers[ZS - 1],
        )

    def over_x(self, m, source, k):
        return remote(
            source, self.slot(m, k, 0, 1), self.sems[3].at[m, k], self.sems[5].at[m, k, 0, 1], self.place.x_peer
        )

    def over_core(self, m, source, k, dx):
        return remote(
            source,
            self.slot(m, k, 1, dx),
            self.sems[4].at[m, k, dx],
            self.sems[5].at[m, k, 1, dx],
            self.place.core_peer,
        )

    def send_own(self, m):
        source, z = self.own.at[m], self.place.z
        pl.when(z < ZS - 1)(lambda: self.up(m, source, ZS - 1).start())
        pl.when(z > 0)(lambda: self.down(m, source, 1).start())
        self.over_x(m, source, 0).start()
        self.over_core(m, source, 0, 0).start()
        self.local(m).start()

    def pass_on(self, m, k):
        self.over_x(m, self.slot(m, k, 0, 0), k).start()
        self.over_core(m, self.slot(m, k, 0, 0), k, 0).start()

    def from_above(self, m, far):
        self.up(m, self.own.at[m], far).wait_recv()
        pl.when(self.place.z > 0)(lambda: self.down(m, self.slot(m, far, 0, 0), far + 1).start())
        self.pass_on(m, far)

    def from_below(self, m, far):
        self.up(m, self.own.at[m], ZS - far).wait_recv()
        source = self.slot(m, ZS - far, 0, 0)
        pl.when(self.place.z < ZS - 1)(lambda: self.up(m, source, ZS - far - 1).start())
        self.pass_on(m, ZS - far)

    def z_arrival(self, m, far):
        pl.when(self.place.z + far < ZS)(lambda: self.from_above(m, far))
        pl.when(self.place.z - far >= 0)(lambda: self.from_below(m, far))

    def x_arrival(self, m, k):
        self.over_x(m, self.own.at[m], k).wait_recv()
        self.over_core(m, self.slot(m, k, 0, 1), k, 1).start()

    def piece_arrival(self, m, k):
        for dx in range(XS):
            self.over_core(m, self.own.at[m], k, dx).wait_recv()

    def arrivals(self, m=0):
        for k in range(ZS):
            self.piece_arrival(m, k)
        self.local(m).wait()

    def z_round(self, far, chosen=None):
        for m in range(self.micro) if chosen is None else [chosen]:
            self.z_arrival(m, far)

    def x_round(self, far, chosen=None):
        for m in range(self.micro) if chosen is None else [chosen]:
            if far == 0:
                self.x_arrival(m, 0)
            else:
                pl.when(self.place.z + far < ZS)(lambda: self.x_arrival(m, far))
                pl.when(self.place.z - far >= 0)(lambda: self.x_arrival(m, ZS - far))

    def run(self):
        self.z_round(1)
        self.x_round(0)
        self.z_round(2)
        self.x_round(1)
        self.z_round(3)
        self.x_round(2)
        self.x_round(3)

    def drain(self, waited=False):
        z = self.place.z
        for m in range(self.micro):
            own = self.own.at[m]
            if not waited:
                self.arrivals(m)
            pl.when(z < ZS - 1)(lambda: self.up(m, own, ZS - 1).wait_send())
            pl.when(z > 0)(lambda: self.down(m, own, 1).wait_send())
            for far in range(1, ZS - 1):
                pl.when((z + far < ZS) & (z > 0))(lambda: self.down(m, own, far + 1).wait_send())
                pl.when((z - far >= 0) & (z < ZS - 1))(lambda: self.up(m, own, ZS - far - 1).wait_send())
            for k in range(ZS):
                self.over_x(m, own, k).wait_send()
                for dx in range(XS):
                    self.over_core(m, own, k, dx).wait_send()


class PieceReduce(Reduce):
    @staticmethod
    def scratch(micro, rows, model):
        return [
            pltpu.VMEM((micro, ZS, CS * XS * rows, model), BF16),
            pltpu.VMEM((micro, ZS, XS, rows, model), BF16),
            pltpu.VMEM((micro, ZS, rows, model), BF16),
            pltpu.VMEM((micro, 2, ZS - 1, rows, model), BF16),
            pltpu.VMEM((micro, rows, model), F32),
            DMA((micro, ZS, XS)),
            DMA((micro, ZS, XS)),
            DMA((micro, ZS)),
            DMA((micro, ZS)),
            DMA((micro, 2, ZS)),
            DMA((micro, 2, ZS)),
        ]

    def __init__(self, place, refs):
        self.place = place
        self.part, self.core_in, self.x_in, self.z_in, self.total = [refs.pop(0) for _ in range(5)]
        core_send, core_recv, x_send, x_recv, z_send, z_recv = [refs.pop(0) for _ in range(6)]
        self.sems = [core_send, core_recv, None, x_send, x_recv, z_send, z_recv]
        self.micro, self.rows = self.total.shape[0], self.total.shape[1]

    def unit(self, m, k, dc, dx):
        return self.part.at[m, k, pl.ds((dc * XS + dx) * self.rows, self.rows)]

    def core_copy(self, m, k, dx):
        send, arrive = self.sems[:2]
        return remote(
            self.unit(m, k, 1, dx),
            self.core_in.at[m, k, dx],
            send.at[m, k, dx],
            arrive.at[m, k, dx],
            self.place.core_peer,
        )

    def begin_piece(self, m, k):
        for dx in (1, 0):
            self.core_copy(m, k, dx).start()

    def x_piece(self, m, k):
        self.core_copy(m, k, 1).wait_recv()
        kept = self.unit(m, k, 0, 1)

        def add(span):
            value = self.core_in[m, k, 1, span, :].astype(F32) + kept[span, :].astype(F32)
            self.core_in[m, k, 1, span, :] = value.astype(BF16)

        by_rows(self.rows, add)
        self.x_copy(m, k).start()

    def z_piece(self, m, k):
        self.x_copy(m, k).wait_recv()
        self.core_copy(m, k, 0).wait_recv()
        kept = self.unit(m, k, 0, 0)

        def sum_of(span):
            return (
                self.x_in[m, k, span, :].astype(F32)
                + self.core_in[m, k, 0, span, :].astype(F32)
                + kept[span, :].astype(F32)
            )

        def away(span):
            self.x_in[m, k, span, :] = sum_of(span).astype(BF16)

        def here(span):
            self.total[m, span, :] = sum_of(span)

        pl.when(k != 0)(lambda: by_rows(self.rows, away))
        pl.when(k == 0)(lambda: by_rows(self.rows, here))

    def drain(self):
        for m in range(self.micro):
            for k in range(ZS):
                for dx in range(XS):
                    self.core_copy(m, k, dx).wait_send()
                self.x_copy(m, k).wait_send()
            for down in (0, 1):
                for far in range(1, ZS):
                    pl.when(self.beyond(down, far))(self.z_copy(m, down, far).wait_send)


def piece_of(place, index, micro):
    turn = lax.rem(index, ZS)
    inner = turn + lax.div(turn, 2) * (5 - 2 * turn)
    last = lax.rem(ZS - turn, ZS)
    z = place.z
    return lax.div(index, ZS), jnp.where(z == 0, turn, jnp.where(z == ZS - 1, last, inner))


def run_pieces(place, reduce, piece, between):
    pieces = reduce.micro * ZS

    def step(index, carry):
        @pl.when(index < pieces)
        def _():
            m, k = piece_of(place, index, reduce.micro)
            piece(index, m, k)
            reduce.begin_piece(m, k)

        between(index)

        @pl.when((index >= 1) & (index < pieces + 1))
        def _():
            reduce.x_piece(*piece_of(place, index - 1, reduce.micro))

        @pl.when((index >= 3) & (index < pieces + 3))
        def _():
            reduce.z_piece(*piece_of(place, index - 3, reduce.micro))

        for m in range(reduce.micro):
            first = (m + 1) * ZS + 2
            for far in range(1, ZS):
                pl.when(index == first + ZS - 1 - far)(functools.partial(reduce.chain, m, far))
        return carry

    lax.fori_loop(0, pieces + 5, step, 0)


def begin_gathers(gathers):
    for m in range(gathers[0].micro):
        for gather in gathers:
            gather.send_own(m)
        if m == 0:
            for gather in gathers:
                gather.z_round(1, 0)
            for gather in gathers:
                gather.x_round(0, 0)


def gather_steps(gathers, index):
    for m in range(gathers[0].micro):
        for far in range(0 if m else 1, ZS):

            @pl.when(index == (max(0, m * (ZS - 2) - 1) + far if m else far - 1))
            def _(m=m, far=far):
                for gather in gathers:
                    if far + 1 < ZS:
                        gather.z_round(far + 1, m)
                for gather in gathers:
                    gather.x_round(far, m)


def wait_local(gather, m):
    gather.local(m).wait()


def by_lanes(count, width, body):
    def step(index, carry):
        body(pl.ds(pl.multiple_of(index * width, width), width))
        return carry

    lax.fori_loop(0, count, step, 0)


class Spread:
    @staticmethod
    def scratch(pieces, depth):
        return [DMA((pieces,)), DMA((ZS, pieces)), DMA((ZS, pieces))] + [
            DMA((ZS << step,)) for step in range(depth) for _ in range(2)
        ]

    def __init__(self, place, sources, targets, view, depth, refs):
        self.place, self.sources, self.targets, self.view, self.depth = place, sources, targets, view, depth
        self.local_sem, self.z_send, self.z_recv = [refs.pop(0) for _ in range(3)]
        self.sems = [(refs.pop(0), refs.pop(0)) for _ in range(depth)]
        self.pieces = self.local_sem.shape[0]

    def z_copy(self, step, piece):
        place = self.place
        mine = self.targets(self.view(place.z, place.y, place.x, place.core))
        return remote(
            self.sources(lax.rem(place.z + step, ZS))[piece],
            mine[piece],
            self.z_send.at[step, piece],
            self.z_recv.at[step, piece],
            place.z_peers[step],
        )

    def local(self, piece):
        place = self.place
        mine = self.targets(self.view(place.z, place.y, place.x, place.core))
        return pltpu.make_async_copy(self.sources(place.z)[piece], mine[piece], self.local_sem.at[piece])

    def hop(self, axis, index):
        place = self.place
        z = lax.rem(place.z - (index >> axis) + ZS, ZS)
        y = place.y if axis < 1 else (place.y + ((index >> (axis - 1)) & 1)) % 2
        x = place.x if axis < 2 else (place.x + (index & 1)) % 2
        block = self.view(z, y, x, place.core)
        peer = (place.y_peer, place.x_peer, place.core_peer)[axis]
        send, arrive = self.sems[axis]
        return remote(block, block, send.at[index], arrive.at[index], peer)

    def begin(self):
        for piece in range(self.pieces):
            self.local(piece).start()
        for step in (1, 3, 2):
            for piece in range(self.pieces):
                self.z_copy(step, piece).start()

    def forward(self, axis, index):
        for later in range(axis, self.depth):
            self.hop(later, index << (later - axis)).start()

    def begin_slowly(self):
        for piece in range(self.pieces):
            self.local(piece).start()
            self.z_copy(1, piece).start()

    def slow_round(self, turn):
        steps = (0, 1, 3, 2)
        self.z_round(steps[turn])
        if 0 < turn < ZS - 1:
            for piece in range(self.pieces):
                self.z_copy(steps[turn + 1], piece).start()

    def z_round(self, step):
        for piece in range(self.pieces):
            if step:
                self.z_copy(step, piece).wait_recv()
            else:
                self.local(piece).wait()
        self.forward(0, step)

    def hop_round(self, axis, index):
        self.hop(axis, index).wait_recv()
        self.forward(axis + 1, index * 2 + 1)

    def drain(self):
        for step in range(1, ZS):
            for piece in range(self.pieces):
                self.z_copy(step, piece).wait_send()
        for axis in range(self.depth):
            for index in range(ZS << axis):
                self.hop(axis, index).wait_send()


class Share:
    @staticmethod
    def scratch(pieces):
        return [DMA((pieces,)), DMA((pieces,)), DMA((pieces,))]

    def __init__(self, place, blocks, refs):
        local, send, arrive = [refs.pop(0) for _ in range(3)]
        self.copies = []
        for index, (source, target) in enumerate(blocks):
            self.copies.append(pltpu.make_async_copy(source, target, local.at[index]))
            self.copies.append(remote(source, target, send.at[index], arrive.at[index], place.y_peer))

    def begin(self):
        for copy in self.copies:
            copy.start()

    def drain(self):
        for copy in self.copies:
            copy.wait()


def normed_rows(rows, gain):
    return rows * lax.rsqrt(jnp.mean(rows * rows, axis=1, keepdims=True) + EPS) * gain


def norm_back(grad, rows, upstream, gain):
    scale = lax.rsqrt(jnp.mean(rows * rows, axis=1, keepdims=True) + EPS)
    scaled = grad * gain
    inner = jnp.mean(scaled * rows, axis=1, keepdims=True)
    return upstream + scale * scaled - rows * (scale * scale * scale) * inner, grad * rows * scale


def y_half(place, target, rows):
    return target.at[pl.ds(pl.multiple_of(place.y * rows, rows), rows)]


def by_heads(width, body):
    def step(head, carry):
        body(lambda kind: pl.ds(pl.multiple_of(kind * width + head * HDIM, HDIM), HDIM))
        return carry

    lax.fori_loop(0, width // HDIM, step, 0)


def columns_of(marks, place, m, k):
    local, lanes = marks.shape[3:]
    length = CS * XS * local
    block = marks[k].reshape(length, lanes)
    across = jnp.transpose(block)

    def pick(kind, source, axis):
        value = None
        for index in range(MICRO):
            at = index * KINDS + kind
            part = source[:, at : at + 1] if axis else source[at : at + 1, :]
            value = part if value is None else jnp.where(m == index, part, value)
        return value

    owner = place.owner.astype(F32)
    gates = [jnp.where(pick(kind, block, 1) == owner, pick(kind + 2, block, 1), 0.0) for kind in range(2)]
    return gates[0] + gates[1], pick(KINDS - 1, block, 1), pick(KINDS - 1, across, 0)


def attention_kernel(
    sizes,
    tokens,
    cotangent,
    first_gain,
    second_gain,
    table,
    cosine,
    sine,
    w_kv,
    w_query,
    w_out,
    w_gate_up,
    w_down,
    *refs,
):
    refs = list(refs)
    normed_out, middle_out, everyone, cotangent_out, table_out, turned_out, attended_out = [
        refs.pop(0) for _ in range(7)
    ]
    qkv_weight, out_weight, gate_up_weight, down_weight = [refs.pop(0) for _ in range(4)]
    wide, kv_rows, model_rows, out_rows, down_rows = sizes
    place = Place()
    own = refs.pop(0)
    normed = Gather(place, own, everyone, refs)
    upstream = Gather(place, cotangent, cotangent_out, refs)
    tables = Gather(place, table, table_out, refs)
    reduce = PieceReduce(place, refs)

    def lanes(start, width):
        return pl.ds(pl.multiple_of(start, HDIM), width)

    def kv_view(z, y, x, core):
        row = ((z * YS + y) * (XS * CS) + x * CS + core) * kv_rows
        return qkv_weight.at[pl.ds(pl.multiple_of(row, kv_rows), kv_rows), pl.ds(wide, 2 * wide)]

    def rows_of(z, y):
        return pl.ds(pl.multiple_of((z * YS + y) * model_rows, model_rows), model_rows)

    kv = Spread(
        place,
        lambda z: [w_kv.at[:, lanes((kind * ZS + z) * wide, wide)] for kind in range(2)],
        lambda block: [block.at[:, pl.ds(kind * wide, wide)] for kind in range(2)],
        kv_view,
        3,
        refs,
    )
    query = Spread(
        place,
        lambda z: [w_query.at[0, :, lanes(z * wide, wide)]],
        lambda block: [block],
        lambda z, y, x, core: qkv_weight.at[rows_of(z, y), pl.ds(0, wide)],
        1,
        refs,
    )
    hidden_width = gate_up_weight.shape[2]
    gate_up = Spread(
        place,
        lambda z: [w_gate_up.at[0, :, lanes((kind * ZS + z) * hidden_width, hidden_width)] for kind in range(2)],
        lambda block: [block.at[kind] for kind in range(2)],
        lambda z, y, x, core: gate_up_weight.at[:, rows_of(z, y)],
        1,
        refs,
    )
    shared = Share(place, [(w_out.at[0], y_half(place, out_weight, out_rows))], refs)
    down = Share(place, [(w_down.at[0], y_half(place, down_weight, down_rows))], refs)
    arrived, qkv, attended, marks, weight, out_here, load, store, late_load = [refs.pop(0) for _ in range(9)]
    model = tokens.shape[2]
    tile = model // 2
    late_loads = [
        pltpu.make_async_copy(qkv_weight, weight, late_load.at[0]),
        pltpu.make_async_copy(out_weight, out_here, late_load.at[1]),
        pltpu.make_async_copy(table_out.at[0], marks, late_load.at[2]),
    ]

    def stores(sequence):
        return [
            pltpu.make_async_copy(qkv, turned_out.at[sequence], store.at[0]),
            pltpu.make_async_copy(attended, attended_out.at[sequence], store.at[1]),
        ]

    def piece(index, m, k):
        sequence = m * ZS + k
        normed.piece_arrival(m, k)
        pl.when(k == 0)(functools.partial(wait_local, normed, m))
        loads = [
            pltpu.make_async_copy(everyone.at[m, k, dc, dx], arrived.at[dc, dx], load.at[dc, dx])
            for dc in range(CS)
            for dx in range(XS)
        ]
        for copy in loads:
            copy.start()

        @pl.when(index == 0)
        def _():
            for copy in late_loads:
                copy.wait()

        @pl.when(index > 0)
        def _():
            for copy in stores(0):
                copy.wait()

        row_gate, row_block, key_block = columns_of(marks, place, m, k)
        for copy in loads:
            copy.wait()
        length = qkv.shape[0]
        for kind in range(3):
            value = dot(arrived[...].reshape(length, model), weight[:, kind * wide : (kind + 1) * wide])
            for head in range(wide // HDIM):
                part = value[:, head * HDIM : (head + 1) * HDIM]
                if kind < 2:
                    part = turned(part, cosine[...], sine[...])
                start = kind * wide + head * HDIM
                qkv[:, start : start + HDIM] = part.astype(BF16)

        def head(span_of):
            query, key, value = [qkv[:, span_of(kind)] for kind in range(3)]
            probs = masked_probs(query, key, row_block, key_block).astype(BF16)
            attended[:, span_of(0)] = dot(probs, value).astype(BF16)

        by_heads(wide, head)
        for start in range(0, model, tile):
            value = dot(attended[...], out_here[:, start : start + tile]) * row_gate
            reduce.part[m, k, :, start : start + tile] = value.astype(BF16)
        for copy in stores(sequence):
            copy.start()

    def between(index):
        for far in range(1, ZS):
            pl.when(index == far - 1)(functools.partial(upstream.z_round, far))
            pl.when(index == far)(functools.partial(upstream.x_round, far - 1))
        pl.when(index == ZS)(functools.partial(upstream.x_round, ZS - 1))
        pl.when(index == 4)(functools.partial(gate_up.slow_round, 2))

    place.enter(True)
    shared.begin()
    kv.begin()
    tables.send_own(0)
    for m in range(normed.micro):

        def body(span, m=m):
            own[m, span, :] = normed_rows(tokens[m, span, :].astype(F32), first_gain[...]).astype(BF16)

        by_rows(tokens.shape[1], body)
        normed.send_own(m)
    query.begin()
    kv.z_round(0)
    tables.z_round(1)
    kv.z_round(1)
    kv.z_round(3)
    normed.z_round(1)
    kv.z_round(2)
    for index in (0, 1, 3, 2):
        kv.hop_round(0, index)
    normed.x_round(0)
    gate_up.begin_slowly()
    gate_up.slow_round(0)
    tables.z_round(2)
    normed.z_round(2)
    normed.x_round(1)
    for step in (0, 1, 3, 2):
        query.z_round(step)
    for index in (0, 2, 6, 4, 1, 3, 7, 5):
        kv.hop_round(1, index)
    normed.z_round(3)
    tables.z_round(3)
    for far in range(ZS):
        tables.x_round(far)
    normed.x_round(2)
    normed.x_round(3)
    for m in range(upstream.micro):
        upstream.send_own(m)
    for index in range(ZS << 2):
        kv.hop_round(2, index)
    for index in range(ZS):
        query.hop_round(0, index)
    shared.drain()
    tables.arrivals()
    for copy in late_loads:
        copy.start()
    down.begin()
    gate_up.slow_round(1)
    run_pieces(place, reduce, piece, between)
    for m in range(reduce.micro):
        reduce.finish(m)

        def body(span, m=m):
            middle = tokens[m, span, :].astype(F32) + reduce.total[m, span, :]
            middle_out[m, span, :] = middle
            normed_out[m, span, :] = normed_rows(middle, second_gain[...]).astype(BF16)

        by_rows(reduce.rows, body)
    for copy in stores(0):
        copy.wait()
    gate_up.slow_round(3)
    for index in range(ZS):
        gate_up.hop_round(0, index)
    for gather in (tables, normed):
        gather.drain(True)
    for part in (upstream, kv, query, gate_up, down, reduce):
        part.drain()


def attend_back_kernel(
    rows, weight_in, out_in, marks, cosine, sine, turned_qkv, tokens, middle_grad, gain, gate_grads, up_grads, *refs
):
    refs = list(refs)
    input_out, terms_out, row_grad_out, qkv_grad_out, weight_grad_out, sums_out, everyone = [
        refs.pop(0) for _ in range(7)
    ]
    place = Place()
    gather = Gather(place, rows, everyone, refs)
    reduce = PieceReduce(place, refs)
    arrived, kept, row_grad, qkv_grad, load, store = [refs.pop(0) for _ in range(6)]
    mine, theirs, mine_sem, y_send, y_recv, z_send, z_recv, sum_local = [refs.pop(0) for _ in range(8)]
    weight, out_weight, weight_load = [refs.pop(0) for _ in range(3)]
    weight_loads = [
        pltpu.make_async_copy(weight_in, weight, weight_load.at[0]),
        pltpu.make_async_copy(out_in, out_weight, weight_load.at[1]),
    ]
    wide, model = out_weight.shape
    tile = model // 2
    width = mine.shape[2]

    def stores(sequence):
        return [
            pltpu.make_async_copy(row_grad, row_grad_out.at[sequence], store.at[0]),
            pltpu.make_async_copy(qkv_grad, qkv_grad_out.at[sequence], store.at[1]),
        ]

    def piece(index, m, k):
        sequence = m * ZS + k
        gather.piece_arrival(m, k)
        pl.when(k == 0)(lambda: gather.local(m).wait())
        loads = [
            pltpu.make_async_copy(everyone.at[m, k, dc, dx], arrived.at[dc, dx], load.at[dc, dx])
            for dc in range(CS)
            for dx in range(XS)
        ]
        loads.append(pltpu.make_async_copy(turned_qkv.at[sequence], kept, load.at[CS, 0]))
        for copy in loads:
            copy.start()

        @pl.when(index == 0)
        def _():
            for copy in weight_loads:
                copy.wait()

        @pl.when(index > 0)
        def _():
            for copy in stores(0):
                copy.wait()

        for copy in loads:
            copy.wait()
        length = kept.shape[0]
        row_gate, row_block, key_block = columns_of(marks, place, m, k)
        for start in range(0, model, tile):
            value = arrived[:, :, :, start : start + tile].astype(F32).reshape(length, tile) * row_gate
            row_grad[:, start : start + tile] = value.astype(BF16)
        qkv_grad[:, :wide] = dot_t(row_grad[...], out_weight[...]).astype(BF16)

        def head(span_of):
            query, key, value = [kept[:, span_of(kind)] for kind in range(3)]
            grad = qkv_grad[:, span_of(0)]
            probs = masked_probs(query, key, row_block, key_block)
            prob_grad = dot_t(grad, value)
            inner = jnp.sum(probs * prob_grad, axis=1, keepdims=True)
            raw_grad = (probs * (prob_grad - inner) * HDIM ** (-0.5)).astype(BF16)
            qkv_grad[:, span_of(0)] = turned(dot(raw_grad, key), cosine[...], -sine[...]).astype(BF16)
            qkv_grad[:, span_of(1)] = turned(dot_l(raw_grad, query), cosine[...], -sine[...]).astype(BF16)
            qkv_grad[:, span_of(2)] = dot_l(probs.astype(BF16), grad).astype(BF16)

        by_heads(wide, head)
        for start in range(0, model, tile):
            value = dot_t(qkv_grad[...], weight[start : start + tile, :])
            reduce.part[m, k, :, start : start + tile] = value.astype(BF16)
        for copy in stores(sequence):
            copy.start()

    steps = (1, 3, 2, 0)
    sources = (gate_grads, up_grads)

    def z_of(turn):
        return lax.rem(place.z + steps[turn], ZS)

    def own_copy(part):
        kind, turn = divmod(part, ZS)
        return pltpu.make_async_copy(sources[kind].at[z_of(turn), place.y], mine.at[part], mine_sem.at[part])

    def y_copy(part):
        kind, turn = divmod(part, ZS)
        return remote(
            sources[kind].at[z_of(turn), 1 - place.y],
            theirs.at[part],
            y_send.at[part],
            y_recv.at[part],
            place.y_peer,
        )

    columns = weight_grad_out.at[:, pl.ds(pl.multiple_of(place.z * width, HDIM), width)]

    def sum_copy(part):
        kind, turn = divmod(part, ZS)
        if kind:
            return pltpu.make_async_copy(theirs.at[part], sums_out.at[z_of(turn)], sum_local.at[part])
        if steps[turn] == 0:
            return pltpu.make_async_copy(theirs.at[part], columns, sum_local.at[part])
        return remote(
            theirs.at[part], columns, z_send.at[steps[turn]], z_recv.at[steps[turn]], place.z_peers[steps[turn]]
        )

    def pass_grads(part):
        y_copy(part).wait()
        if part + 2 < 2 * ZS:
            y_copy(part + 2).start()
        own_copy(part).wait()

        def add(span):
            value = mine[part, span, :].astype(F32) + theirs[part, span, :].astype(F32)
            theirs[part, span, :] = value.astype(BF16)

        by_rows(mine.shape[1], add)
        sum_copy(part).start()

    def between(index):
        gather_steps([gather], index)
        for part, at in enumerate((2, 3, 5, 6, 8, 9)):
            pl.when(index == at)(functools.partial(pass_grads, part))

    for copy in weight_loads:
        copy.start()
    for part in range(2 * ZS):
        own_copy(part).start()
    place.enter(True)
    for part in range(2):
        y_copy(part).start()
    begin_gathers([gather])
    run_pieces(place, reduce, piece, between)
    for part in range(6, 2 * ZS):
        pass_grads(part)
    terms_out[...] = jnp.zeros_like(terms_out)
    for m in range(gather.micro):
        reduce.finish(m)

        def body(span, m=m):
            result, found = norm_back(
                reduce.total[m, span, :], tokens[m, span, :].astype(F32), middle_grad[m, span, :], gain[...]
            )
            input_out[m, span, :] = result.astype(BF16)
            terms_out[...] += found

        by_rows(reduce.rows, body)
    for copy in stores(0):
        copy.wait()
    gather.drain(True)
    reduce.drain()
    for part in range(2 * ZS):
        sum_copy(part).wait()


def mlp_kernel(
    normed, gate_up_part, down_part, select, select_back, gates, cotangents, middle, cotangent, gain, *refs
):
    refs = list(refs)
    own_out, grad_out, terms_out, rows_out, up_grad_out, hidden_out, down_grad_out, result_out = [
        refs.pop(0) for _ in range(8)
    ]
    everyone = refs.pop(0)
    place = Place()
    gathers = [Gather(place, normed, everyone, refs)]
    reduce = PieceReduce(place, refs)
    arrived, upstream, rows, down_grad, hidden, both_grad, result = [refs.pop(0) for _ in range(7)]
    gate_weight, up_weight, down, load, store, weight_load = [refs.pop(0) for _ in range(6)]
    width = down.shape[0]
    model = middle.shape[2]
    tile = model // 2
    weight_loads = [
        pltpu.make_async_copy(source, target, weight_load.at[i])
        for i, (source, target) in enumerate(
            ((gate_up_part.at[0], gate_weight), (gate_up_part.at[1], up_weight), (down_part, down))
        )
    ]

    def stores(index):
        pairs = (
            (rows, rows_out),
            (down_grad, down_grad_out),
            (hidden, hidden_out),
            (both_grad, up_grad_out),
            (result, result_out),
        )
        return [
            pltpu.make_async_copy(here, there.at[index], store.at[i]) for i, (here, there) in enumerate(pairs)
        ]

    def piece(index, m, k):
        for gather in gathers:
            gather.piece_arrival(m, k)
            pl.when(k == 0)(functools.partial(wait_local, gather, m))
        sequence = m * ZS + k
        loads = [
            pltpu.make_async_copy(source.at[m, k, dc, dx], target.at[dc, dx], load.at[i, dc, dx])
            for i, (source, target) in enumerate(((everyone, arrived), (cotangents, upstream)))
            for dc in range(CS)
            for dx in range(XS)
        ]
        for copy in loads:
            copy.start()

        @pl.when(index == 0)
        def _():
            for copy in weight_loads:
                copy.wait()

        @pl.when(index > 0)
        def _():
            for copy in stores(0):
                copy.wait()

        for copy in loads:
            copy.wait()
        chosen, back, gate_of_row = select[sequence], select_back[sequence], gates[sequence]
        length = select.shape[2]

        def to_rows(span):
            rows[:, span] = dot(chosen, arrived[:, :, :, span].reshape(length, tile)).astype(BF16)
            down_grad[:, span] = (dot(chosen, upstream[:, :, :, span].reshape(length, tile)) * gate_of_row).astype(BF16)

        by_lanes(model // tile, tile, to_rows)

        half = width // (2 * HDIM) * HDIM
        for start, stop in ((0, half), (half, width)):
            gate = dot(rows[...], gate_weight[:, start:stop])
            up = dot(rows[...], up_weight[:, start:stop])
            hidden_grad = dot_t(down_grad[...], down[start:stop, :])
            sigma = 0.5 * jnp.tanh(0.5 * gate) + 0.5
            silu = gate * sigma
            hidden[:, start:stop] = (silu * up).astype(BF16)
            slope = sigma + silu * (1.0 - sigma)
            both_grad[:, start:stop] = (hidden_grad * up * slope).astype(BF16)
            both_grad[:, width + start : width + stop] = (hidden_grad * silu).astype(BF16)

        def to_tokens(span):
            row_grad = dot_t(both_grad[:, :width], gate_weight[span, :])
            row_grad = (row_grad + dot_t(both_grad[:, width:], up_weight[span, :])).astype(BF16)
            reduce.part[m, k, :, span] = dot(back, row_grad).astype(BF16)
            value = (dot(hidden[...], down[:, span]) * gate_of_row).astype(BF16)
            result[:, span] = dot(back, value).astype(BF16)

        by_lanes(model // tile, tile, to_tokens)
        for copy in stores(sequence):
            copy.start()

    for copy in weight_loads:
        copy.start()
    place.enter(False)
    begin_gathers(gathers)
    run_pieces(place, reduce, piece, functools.partial(gather_steps, gathers))
    terms_out[...] = jnp.zeros_like(terms_out)
    for m in range(reduce.micro):
        reduce.finish(m)

        def body(span, m=m):
            found, terms = norm_back(
                reduce.total[m, span, :], middle[m, span, :], cotangent[m, span, :].astype(F32), gain[...]
            )
            grad_out[m, span, :] = found
            own_out[m, span, :] = found.astype(BF16)
            terms_out[...] += terms

        by_rows(reduce.rows, body)
    for copy in stores(0):
        copy.wait()
    for gather in gathers:
        gather.drain(True)
    reduce.drain()


class Halves:
    def __init__(self, own, other, copy):
        self.own, self.other, self.copy = own, other, copy

    def begin(self):
        self.copy.start()

    def add(self):
        self.copy.wait()

        def body(index, carry):
            value = self.own[index].astype(F32) + self.other[index].astype(F32)
            self.other[index] = value.astype(BF16)
            return carry

        lax.fori_loop(0, self.other.shape[0], body, 0)


def last_kernel(part, middle, first_terms, second_terms, rows, grads, attended, row_grads, up_grad, *refs):
    refs = list(refs)
    output, gains_out, query_out, kv_out, out_out, up_out = [refs.pop(0) for _ in range(6)]
    place = Place()
    reduce = Reduce(place, part, refs)
    tall, long, load = [refs.pop(0) for _ in range(3)]
    query_all, query_in, kv_all, core_in, x_in, y_in, out_own, out_send, out_in = [refs.pop(0) for _ in range(9)]
    hop_send, hop_recv, z_send, z_recv, z_local = [refs.pop(0) for _ in range(5)]
    terms, gain_in, gain_send, gain_recv = [refs.pop(0) for _ in range(4)]
    up_send, up_recv, up_local = [refs.pop(0) for _ in range(3)]
    wide, kv_rows = query_out.shape[1] // ZS, kv_out.shape[0]
    model = tall.shape[1]
    tile = model // ZS

    def swap(number, source, target, peer):
        return remote(source, target, hop_send.at[number], hop_recv.at[number], peer)

    query = Halves(
        query_all.at[:, place.y], query_in, swap(0, query_all.at[:, 1 - place.y], query_in, place.y_peer)
    )
    over_core = Halves(
        kv_all.at[:, place.core], core_in, swap(1, kv_all.at[:, 1 - place.core], core_in, place.core_peer)
    )
    by_x = core_in.reshape(ZS * YS, XS, kv_rows, 2 * wide)
    over_x = Halves(by_x.at[:, place.x], x_in, swap(2, by_x.at[:, 1 - place.x], x_in, place.x_peer))
    by_y = x_in.reshape(ZS, YS, kv_rows, 2 * wide)
    over_y = Halves(by_y.at[:, place.y], y_in, swap(3, by_y.at[:, 1 - place.y], y_in, place.y_peer))
    over_out = swap(4, out_send, out_in, place.y_peer)

    def lanes(start):
        return pl.ds(pl.multiple_of(start, HDIM), wide)

    def z_parts(step):
        to = lax.rem(place.z + step, ZS)
        pairs = [(query_in.at[to], query_out.at[:, lanes(place.z * wide)])]
        for kind in range(2):
            pairs.append(
                (y_in.at[to, :, pl.ds(kind * wide, wide)], kv_out.at[:, lanes((kind * ZS + place.z) * wide)])
            )
        return pairs

    def z_copy(step, piece):
        source, target = z_parts(step)[piece]
        if step == 0:
            return pltpu.make_async_copy(source, target, z_local.at[piece])
        return remote(source, target, z_send.at[step, piece], z_recv.at[step, piece], place.z_peers[step])

    hops = [[place.core_peer], [place.x_peer], [place.y_peer], place.z_peers[1:]]

    def gain_copies(hop):
        return [
            remote(terms, gain_in.at[hop + i], gain_send.at[hop + i], gain_recv.at[hop + i], peer)
            for i, peer in enumerate(hops[hop])
        ]

    def send_gains(hop):
        for copy in gain_copies(hop):
            copy.start()

    def add_gains(hop):
        copies = gain_copies(hop)
        for copy in copies:
            copy.wait()
        for i in range(len(copies)):
            terms[...] += gain_in[hop + i]
        if hop + 1 < len(hops):
            send_gains(hop + 1)

    width = up_grad.shape[2]
    columns = up_out.at[:, pl.ds(pl.multiple_of(place.z * width, HDIM), width)]
    up_copies = [pltpu.make_async_copy(up_grad.at[place.z], columns, up_local)]
    for step in (1, 3, 2):
        source = up_grad.at[lax.rem(place.z + step, ZS)]
        up_copies.append(remote(source, columns, up_send.at[step], up_recv.at[step], place.z_peers[step]))
    loads = [pltpu.make_async_copy(rows, tall, load.at[0]), pltpu.make_async_copy(grads, long, load.at[1])]
    later_loads = [
        pltpu.make_async_copy(row_grads, tall, load.at[2]),
        pltpu.make_async_copy(attended, long.at[:, pl.ds(0, wide)], load.at[3]),
    ]

    def small_grads(z):
        span = slice(z * tile, (z + 1) * tile)
        value = dot_l(tall[:, span], long[:, :wide]).astype(BF16)
        query_all[z] = value.reshape(query_all.shape[1:])
        blocks = kv_all.shape[0] // ZS
        for kind in range(2):
            value = dot_l(tall[:, span], long[:, (kind + 1) * wide : (kind + 2) * wide]).astype(BF16)
            kv_all[z * blocks : (z + 1) * blocks, :, :, kind * wide : (kind + 1) * wide] = value.reshape(
                (blocks,) + kv_all.shape[1:3] + (wide,)
            )

    def out_grads():
        out_rows = out_own.shape[0]
        for start in range(0, model, model // 2):
            span = slice(start, start + model // 2)
            value = dot_l(long[:, :wide], tall[:, span])
            first, second = value[:out_rows], value[out_rows:]
            out_own[:, span] = jnp.where(place.y == 0, first, second)
            out_send[:, span] = jnp.where(place.y == 0, second, first).astype(BF16)

    for copy in loads:
        copy.start()
    place.enter(True)
    reduce.begin()
    for copy in up_copies:
        copy.start()
    terms[...] = jnp.zeros_like(terms)
    terms[0:1, :] = jnp.sum(first_terms[...], axis=0, keepdims=True)
    terms[1:2, :] = jnp.sum(second_terms[...], axis=0, keepdims=True)
    send_gains(0)
    for copy in loads:
        copy.wait()
    small_grads(0)
    reduce.pass_x(0)
    for z in range(1, ZS):
        small_grads(z)
    for copy in later_loads:
        copy.start()
    over_core.begin()
    query.begin()
    add_gains(0)
    over_core.add()
    over_x.begin()
    for m in range(1, reduce.micro):
        reduce.pass_x(m)
    add_gains(1)
    for copy in later_loads:
        copy.wait()
    out_grads()
    over_out.start()
    reduce.sums(0)
    over_x.add()
    over_y.begin()
    query.add()
    for step in (1, 3, 2, 0):
        z_copy(step, 0).start()
    add_gains(2)
    for m in range(1, reduce.micro):
        reduce.sums(m)
    over_y.add()
    for step in (1, 3, 2, 0):
        for piece in (1, 2):
            z_copy(step, piece).start()
    add_gains(3)
    gains_out[...] = terms[...]
    for m in range(reduce.micro):
        reduce.finish(m)

        def finish(span, m=m):
            output[m, span, :] = (middle[m, span, :] + reduce.total[m, span, :]).astype(BF16)

        by_rows(reduce.rows, finish)
    over_out.wait()

    def add_out(span):
        out_out[span, :] = out_own[span, :] + out_in[span, :].astype(F32)

    by_rows(out_own.shape[0], add_out)
    reduce.drain()
    for copy in up_copies:
        copy.wait()
    for step in range(ZS):
        for piece in range(3):
            z_copy(step, piece).wait()


def gate_up_grads_kernel(rows, both_grad, gate_out, up_out):
    value = dot_l(rows[...], both_grad[...]).astype(BF16)
    width = both_grad.shape[1] // 2
    gate_out[0] = value[:, :width].reshape(gate_out.shape[1:])
    up_out[0] = value[:, width:].reshape(up_out.shape[1:])


def gate_up_grads(rows, both_grad, model_rows):
    count, model = rows.shape
    width = both_grad.shape[1] // 2
    block = pl.BlockSpec((1, YS, model_rows, width), lambda z: (z, 0, 0, 0))
    return pl.pallas_call(
        gate_up_grads_kernel,
        grid=(ZS,),
        in_specs=[
            pl.BlockSpec((count, model // ZS), lambda z: (0, z)),
            pl.BlockSpec((count, 2 * width), lambda z: (0, 0)),
        ],
        out_specs=[block, block],
        out_shape=[jax.ShapeDtypeStruct((ZS, YS, model_rows, width), BF16)] * 2,
        compiler_params=pltpu.CompilerParams(vmem_limit_bytes=60 << 20),
        cost_estimate=pl.CostEstimate(
            flops=4 * count * model * width, bytes_accessed=12 * model * width, transcendentals=0
        ),
    )(rows, both_grad)


def down_grads_kernel(hidden, down_grad, down_out, small_out):
    value = dot_l(hidden[...], down_grad[...])
    down_out[...] = value
    small_out[...] = value.astype(BF16)


def down_grads(hidden, down_grad):
    count, model = down_grad.shape
    width = hidden.shape[1]
    tile = model // ZS
    return pl.pallas_call(
        down_grads_kernel,
        grid=(ZS,),
        in_specs=[
            pl.BlockSpec((count, width), lambda z: (0, 0)),
            pl.BlockSpec((count, tile), lambda z: (0, z)),
        ],
        out_specs=[pl.BlockSpec((width, tile), lambda z: (0, z))] * 2,
        out_shape=[jax.ShapeDtypeStruct((width, model), F32), jax.ShapeDtypeStruct((width, model), BF16)],
        compiler_params=pltpu.CompilerParams(vmem_limit_bytes=60 << 20),
        cost_estimate=pl.CostEstimate(
            flops=2 * count * model * width, bytes_accessed=10 * model * width, transcendentals=0
        ),
    )(hidden, down_grad)


def widen_kernel(first, second, own, other, kv, query, weight_out, down_out, kv_out, query_out):
    step = pl.program_id(0)
    pl.when(step < ZS)(lambda: weight_out.__setitem__(..., first[...].astype(F32)))
    pl.when(step >= ZS)(lambda: weight_out.__setitem__(..., second[...].astype(F32)))
    down_out[...] = own[0] + other[...].astype(F32)
    kv_out[...] = kv[...].astype(F32)
    query_out[...] = query[...].astype(F32)


def widen(first, second, own, other, kv, query, y):
    steps = 2 * ZS
    rows, width = first.shape[0], first.shape[1] // ZS
    down_rows, model = other.shape
    down_step = down_rows // ZS

    def block(*dims):
        return pl.BlockSpec(dims, lambda i, y: (i // 2,) + (0,) * (len(dims) - 1))

    small = [(value.shape[0] // ZS, value.shape[1]) for value in (kv, query)]
    return pl.pallas_call(
        lambda y, *refs: widen_kernel(*refs),
        grid_spec=pltpu.PrefetchScalarGridSpec(
            num_scalar_prefetch=1,
            grid=(steps,),
            in_specs=[
                pl.BlockSpec((rows, width), lambda i, y: (0, jnp.minimum(i, ZS - 1))),
                pl.BlockSpec((rows, width), lambda i, y: (0, jnp.maximum(i - ZS, 0))),
                pl.BlockSpec((1, down_step, model), lambda i, y: (y[0], i // 2, 0)),
                block(down_step, model),
                block(*small[0]),
                block(*small[1]),
            ],
            out_specs=[
                pl.BlockSpec((rows, width), lambda i, y: (0, i)),
                block(down_step, model),
                block(*small[0]),
                block(*small[1]),
            ],
        ),
        out_shape=[
            jax.ShapeDtypeStruct((rows, steps * width), F32),
            jax.ShapeDtypeStruct(other.shape, F32),
            jax.ShapeDtypeStruct(kv.shape, F32),
            jax.ShapeDtypeStruct(query.shape, F32),
        ],
        compiler_params=pltpu.CompilerParams(vmem_limit_bytes=60 << 20),
        cost_estimate=pl.CostEstimate(flops=0, bytes_accessed=12 * rows * steps * width, transcendentals=0),
    )(jnp.full((1,), y, jnp.int32), first, second, own, other, kv, query)


def connect(kernel, operands, spaces, out_shapes, out_spaces, scratch, number, seconds):
    return pl.pallas_call(
        kernel,
        in_specs=spaces,
        out_specs=out_spaces,
        out_shape=out_shapes,
        scratch_shapes=scratch,
        compiler_params=pltpu.CompilerParams(
            collective_id=number, has_side_effects=True, vmem_limit_bytes=60 << 20
        ),
        cost_estimate=pl.CostEstimate(flops=0, bytes_accessed=int(seconds * 3e12), transcendentals=0),
    )(*operands)


def fast_device(
    tokens,
    cotangent,
    gain_attn,
    gain_mlp,
    w_kv,
    w_query,
    w_out,
    w_gate_up,
    w_down,
    att_routes,
    att_gates,
    mlp_routes,
    mlp_gates,
    blocks,
):
    group, owner = lax.axis_index("group"), lax.axis_index("expert")
    y = group % YS
    x, core = owner // CS, owner % CS
    micro, local, model = tokens.shape
    wide = w_query.shape[2] // ZS
    hidden_width = w_gate_up.shape[2] // (2 * ZS)
    kv_rows = w_kv.shape[0]
    model_rows = w_query.shape[1]

    def own_rows(table):
        return lax.dynamic_slice_in_dim(table, owner * local, local, 0).astype(F32)

    lines = []
    for m in range(micro):
        lines += [own_rows(att_routes[m]), att_gates[m], own_rows(mlp_routes[m]), mlp_gates[m]]
        lines += [own_rows(blocks[m, 0][:, None])]
    table = jnp.concatenate(lines, axis=1)
    table = jnp.pad(table, ((0, 0), (0, -table.shape[1] % HDIM)))[None]

    positions = (
        (x ^ jnp.arange(XS)[None, :, None]) * CS + (core ^ jnp.arange(CS)[:, None, None])
    ) * local + jnp.arange(local)[None, None, :]
    cosine, sine = angles(positions.reshape(-1))
    cosine = jnp.concatenate([cosine, cosine], axis=1)
    sine = jnp.concatenate([-sine, sine], axis=1)

    shape = (micro, local, model)
    everyone = (micro, ZS, CS, XS, local, model)
    seqs = micro * ZS
    first_gain, second_gain = gain_attn[None], gain_mlp[None]
    tall = jax.ShapeDtypeStruct(shape, F32)
    short = jax.ShapeDtypeStruct(shape, BF16)
    gathered = jax.ShapeDtypeStruct(everyone, BF16)
    terms = jax.ShapeDtypeStruct((STEP, model), F32)
    own_buffer = pltpu.VMEM(shape, BF16)

    def kept(width, rows=SEQ):
        return jax.ShapeDtypeStruct((seqs, rows, width), BF16)

    def weight(*dims):
        return jax.ShapeDtypeStruct(dims, BF16)

    marks = (ZS, CS, XS) + table.shape[1:]
    (
        normed_two,
        middle,
        normed,
        cotangents,
        table,
        turned_qkv,
        attended,
        qkv_weight,
        out_weight,
        gate_up_weight,
        down_weight,
    ) = connect(
        functools.partial(attention_kernel, (wide, kv_rows, model_rows, w_out.shape[1], w_down.shape[1])),
        [
            tokens,
            cotangent,
            first_gain,
            second_gain,
            table,
            cosine,
            sine,
            w_kv,
            w_query,
            w_out,
            w_gate_up,
            w_down,
        ],
        [VMEM] * 7 + [ANY] * 5,
        [
            short,
            tall,
            gathered,
            gathered,
            jax.ShapeDtypeStruct((1,) + marks, F32),
            kept(3 * wide),
            kept(wide),
            weight(model, 3 * wide),
            weight(wide, model),
            weight(2, model, hidden_width),
            weight(hidden_width, model),
        ],
        [VMEM, VMEM] + [ANY] * 9,
        [own_buffer]
        + Gather.scratch(micro)
        + Gather.scratch(micro)
        + Gather.scratch(1)
        + PieceReduce.scratch(*shape)
        + Spread.scratch(2, 3)
        + Spread.scratch(1, 1)
        + Spread.scratch(2, 1)
        + Share.scratch(1)
        + Share.scratch(1)
        + [
            pltpu.VMEM((CS, XS, local, model), BF16),
            pltpu.VMEM((SEQ, 3 * wide), BF16),
            pltpu.VMEM((SEQ, wide), BF16),
            pltpu.VMEM(marks, F32),
            pltpu.VMEM((model, 3 * wide), BF16),
            pltpu.VMEM((wide, model), BF16),
            DMA((CS, XS)),
            DMA((2,)),
            DMA((3,)),
        ],
        1,
        250e-6,
    )
    table = table[0]
    part = table[..., : KINDS * micro].reshape(ZS, SEQ, micro, KINDS).transpose(2, 0, 1, 3)
    part = part.reshape(seqs, SEQ, KINDS)
    hit = jnp.any(part[..., 4:6] == owner, axis=-1)
    mlp_weight = jnp.sum(jnp.where(part[..., 4:6] == owner, part[..., 6:8], 0.0), axis=-1)
    before_mask = jnp.arange(SEQ)[:, None] < jnp.arange(SEQ)[None, :]
    before = dot(hit.astype(BF16), before_mask.astype(BF16)).astype(jnp.int32)
    slots = jnp.arange(XS * CS * CAP + -XS * CS * CAP % STEP)
    chosen = hit[:, None, :] & (before[:, None, :] == slots[None, :, None])
    row_gate = jnp.sum(jnp.where(chosen, mlp_weight[:, None, :], 0.0), axis=2)
    select = chosen.astype(BF16)
    slot_count = select.shape[1]
    middle_rows, middle_grad, gain_second, rows_two, both_grad, hidden, down_grad, result_two, *_ = connect(
        mlp_kernel,
        [
            normed_two,
            gate_up_weight,
            down_weight,
            select,
            select.transpose(0, 2, 1),
            row_gate[:, :, None],
            cotangents,
            middle,
            cotangent,
            second_gain,
        ],
        [VMEM] + [ANY] * 2 + [VMEM] * 3 + [ANY] + [VMEM] * 3,
        [
            short,
            tall,
            terms,
            kept(model, slot_count),
            kept(2 * hidden_width, slot_count),
            kept(hidden_width, slot_count),
            kept(model, slot_count),
            kept(model),
            gathered,
        ],
        [VMEM, VMEM, VMEM] + [ANY] * 6,
        Gather.scratch(micro)
        + PieceReduce.scratch(*shape)
        + [
            pltpu.VMEM((CS, XS, local, model), BF16),
            pltpu.VMEM((CS, XS, local, model), BF16),
            pltpu.VMEM((slot_count, model), BF16),
            pltpu.VMEM((slot_count, model), BF16),
            pltpu.VMEM((slot_count, hidden_width), BF16),
            pltpu.VMEM((slot_count, 2 * hidden_width), BF16),
            pltpu.VMEM((SEQ, model), BF16),
            pltpu.VMEM((model, hidden_width), BF16),
            pltpu.VMEM((model, hidden_width), BF16),
            pltpu.VMEM((hidden_width, model), BF16),
            DMA((2, CS, XS)),
            DMA((5,)),
            DMA((3,)),
        ],
        5,
        150e-6,
    )
    rows_two, both_grad, hidden, down_grad = [
        value.reshape(-1, value.shape[2]) for value in (rows_two, both_grad, hidden, down_grad)
    ]
    result_two = result_two.reshape(everyone)

    grad_down, down_small = [value.reshape(YS, -1, model) for value in down_grads(hidden, down_grad)]
    down_small = take(down_small, 1 - y, 0)
    rows_two, down_small = lax.optimization_barrier((rows_two, down_small))
    down_small = y_move(down_small)
    gate_grad, up_grad = gate_up_grads(rows_two, both_grad, model_rows)
    input_grad, gain_first, result_grad, qkv_grad, gate_grad, up_grad, _ = connect(
        attend_back_kernel,
        [
            middle_rows,
            qkv_weight,
            out_weight,
            table,
            cosine,
            sine,
            turned_qkv,
            tokens,
            middle_grad,
            first_gain,
            gate_grad,
            up_grad,
        ],
        [VMEM] + [ANY] * 2 + [VMEM] * 3 + [ANY] + [VMEM] * 3 + [ANY] * 2,
        [
            short,
            terms,
            kept(model),
            kept(3 * wide),
            jax.ShapeDtypeStruct((model_rows, ZS * hidden_width), BF16),
            jax.ShapeDtypeStruct((ZS, model_rows, hidden_width), BF16),
            gathered,
        ],
        [VMEM, VMEM] + [ANY] * 5,
        Gather.scratch(micro)
        + PieceReduce.scratch(*shape)
        + [
            pltpu.VMEM((CS, XS, local, model), BF16),
            pltpu.VMEM((SEQ, 3 * wide), BF16),
            pltpu.VMEM((SEQ, model), BF16),
            pltpu.VMEM((SEQ, 3 * wide), BF16),
            DMA((CS + 1, XS)),
            DMA((2,)),
            pltpu.VMEM((2 * ZS, model_rows, hidden_width), BF16),
            pltpu.VMEM((2 * ZS, model_rows, hidden_width), BF16),
            DMA((2 * ZS,)),
            DMA((2 * ZS,)),
            DMA((2 * ZS,)),
            DMA((ZS,)),
            DMA((ZS,)),
            DMA((2 * ZS,)),
            pltpu.VMEM((model, 3 * wide), BF16),
            pltpu.VMEM((wide, model), BF16),
            DMA((2,)),
        ],
        3,
        150e-6,
    )
    rows = seqs * SEQ
    output, gains, query_grad, kv_grad, grad_out, up_grad = connect(
        last_kernel,
        [
            result_two,
            middle,
            gain_first,
            gain_second,
            normed.reshape(rows, model),
            qkv_grad.reshape(rows, 3 * wide),
            attended.reshape(rows, wide),
            result_grad.reshape(rows, model),
            up_grad,
        ],
        [ANY, VMEM, VMEM, VMEM] + [ANY] * 5,
        [
            short,
            jax.ShapeDtypeStruct((8, model), F32),
            jax.ShapeDtypeStruct((model_rows, ZS * wide), BF16),
            jax.ShapeDtypeStruct((kv_rows, 2 * ZS * wide), BF16),
            jax.ShapeDtypeStruct(w_out.shape[1:], F32),
            weight(model_rows, ZS * hidden_width),
        ],
        [VMEM, VMEM, ANY, ANY, VMEM, ANY],
        Reduce.scratch(*shape)
        + [pltpu.VMEM((rows, model), BF16), pltpu.VMEM((rows, 3 * wide), BF16), DMA((4,))]
        + [pltpu.VMEM((ZS, YS, model_rows, wide), BF16), pltpu.VMEM((ZS, model_rows, wide), BF16)]
        + [
            pltpu.VMEM((ZS * YS * XS, CS, kv_rows, 2 * wide), BF16),
            pltpu.VMEM((ZS * YS * XS, kv_rows, 2 * wide), BF16),
            pltpu.VMEM((ZS * YS, kv_rows, 2 * wide), BF16),
            pltpu.VMEM((ZS, kv_rows, 2 * wide), BF16),
        ]
        + [pltpu.VMEM(w_out.shape[1:], kind) for kind in (F32, BF16, BF16)]
        + [DMA((5,)), DMA((5,)), DMA((ZS, 3)), DMA((ZS, 3)), DMA((3,))]
        + [pltpu.VMEM((8, model), F32), pltpu.VMEM((6, 8, model), F32), DMA((6,)), DMA((6,))]
        + [DMA((ZS,)), DMA((ZS,)), DMA],
        4,
        100e-6,
    )
    devices = ZS * YS * XS * CS
    gains = take(gains[:2].reshape(2, devices, model // devices), group * XS * CS + owner, 1)
    grad_gate_up, grad_down, kv_grad, query_grad = widen(
        gate_grad, up_grad, grad_down, down_small, kv_grad, query_grad, y
    )
    return (
        output,
        input_grad,
        gains[0],
        gains[1],
        kv_grad,
        query_grad[None],
        grad_out[None],
        grad_gate_up[None],
        grad_down[None],
    )


def solution(mesh):
    in_specs = (
        P(None, ("group", "expert"), None),
        P(None, ("group", "expert"), None),
        P(),
        P(),
        P(("group", "expert"), None),
        P("expert", "group", None),
        P("expert", "group", None),
        P("expert", "group", None),
        P("expert", "group", None),
        P(None, "group", None),
        P(None, ("group", "expert"), None),
        P(None, "group", None),
        P(None, ("group", "expert"), None),
        P(None, "group", None),
    )
    out_specs = (
        P(None, ("group", "expert"), None),
        P(None, ("group", "expert"), None),
        P(("group", "expert")),
        P(("group", "expert")),
        P(("group", "expert"), None),
        P("expert", "group", None),
        P("expert", "group", None),
        P("expert", "group", None),
        P("expert", "group", None),
    )
    body = fast_device if fits(mesh) else on_device
    return jax.shard_map(
        body, mesh=mesh, in_specs=in_specs, out_specs=out_specs, check_vma=False
    )
```

```python
import functools

import jax
import jax.numpy as jnp
from jax import lax
from jax.experimental import pallas as pl
from jax.experimental.pallas import tpu as pltpu
from jax.sharding import PartitionSpec as P

HEADS = 16
HDIM = 128
CAP = 50


EPS = 1e-06
HIGH = lax.Precision.HIGHEST


def angles(positions):
    half = HDIM // 2
    freq = 10000.0 ** (-jnp.arange(half, dtype=jnp.float32) / half)
    turn = positions.astype(jnp.float32)[:, None] * freq[None, :]
    return (jnp.cos(turn), jnp.sin(turn))


def rotate(values, cosine, sine):
    count = values.shape[0]
    split = values.reshape(count, HEADS, 2, HDIM // 2)
    first = split[:, :, 0]
    second = split[:, :, 1]
    cosine = cosine[:, None, :]
    sine = sine[:, None, :]
    turned = jnp.stack([first * cosine - second * sine, second * cosine + first * sine], axis=2)
    return turned.reshape(count, HEADS * HDIM)


def routing(routes, gates, block_ids, owner, experts):
    local = routes.shape[0] // experts
    per = routes.reshape(experts, local, routes.shape[1])
    flat = per.reshape(experts, -1)
    ids = jnp.arange(experts, dtype=jnp.int32)
    onehot = (flat[:, :, None] == ids[None, None, :]).astype(jnp.int32)
    before = jnp.cumsum(onehot, axis=1) - onehot
    slots = jnp.sum(before * onehot, axis=2).reshape(per.shape)
    places = jnp.arange(CAP, dtype=jnp.int32)
    own_ids = lax.dynamic_index_in_dim(per, owner, 0, keepdims=False)
    own_slots = lax.dynamic_index_in_dim(slots, owner, 0, keepdims=False)
    sent = (
        (own_ids[None, None] == ids[:, None, None, None])
        & (own_slots[None, None] == places[None, :, None, None])
    ).astype(jnp.float32)
    pick = jnp.sum(sent, axis=3)
    weighted = jnp.sum(sent * gates[None, None], axis=3)
    arrived = ((per == owner)[:, None] & (slots[:, None] == places[None, :, None, None])).astype(
        jnp.int32
    )
    length = experts * local
    spots = jnp.arange(length, dtype=jnp.int32).reshape(experts, 1, local, 1)
    marks = block_ids.reshape(experts, 1, local, 1)
    valid = jnp.sum(arrived, axis=(2, 3)).reshape(-1)
    row_pos = jnp.sum(arrived * spots, axis=(2, 3)).reshape(-1)
    row_block = jnp.sum(arrived * marks, axis=(2, 3)).reshape(-1) + (1 - valid) * length
    return (pick, weighted, row_pos, row_block)


def score_block(queries, keys, row_block, key_block):
    count = queries.shape[0]
    raw = jnp.einsum(
        "rhd,khd->hrk",
        queries.reshape(count, HEADS, HDIM),
        keys.reshape(keys.shape[0], HEADS, HDIM),
        preferred_element_type=jnp.float32,
    )
    visible = key_block[None, None, :] <= row_block[None, :, None]
    return jnp.where(visible, raw * HDIM ** (-0.5), -1e30)


def spread(pick, normed):
    return jnp.einsum(
        "ect,td->ecd", pick.astype(jnp.bfloat16), normed, preferred_element_type=jnp.float32
    ).astype(jnp.bfloat16)


def collect(weights, arrived):
    return jnp.einsum("ect,ecd->td", weights, arrived.astype(jnp.float32), precision=HIGH)


def joined_rows(store, chosen, name):
    return jnp.concatenate([store[name][index] for index in chosen], axis=0)


def expert_reduce(store, chosen):
    pairs = (
        ("rows", "query_grad"),
        ("attended", "result_grad"),
        ("rows_two", "both_grad"),
        ("hidden", "down_grad"),
    )
    groups = lax.axis_size("group")
    results = []
    for left_name, right_name in pairs:
        left = joined_rows(store, chosen, left_name)
        right = joined_rows(store, chosen, right_name)

        def term(start, count, left=left, right=right):
            return jnp.einsum("rd,rf->df", left, right, preferred_element_type=jnp.float32)

        shard = lax.psum_scatter(
            term(jnp.int32(0), lax.axis_size("group") * (left.shape[1] // groups)).astype(
                jnp.bfloat16
            ),
            "group",
            scatter_dimension=0,
            tiled=True,
        ).astype(jnp.float32)
        results.append(shard[None])
    return tuple(results)


def reduce_all(store, chosen):
    expert_parts = expert_reduce(store, chosen)
    shared_term = jnp.einsum(
        "td,tf->df",
        joined_rows(store, chosen, "normed"),
        joined_rows(store, chosen, "mixed_grad"),
        preferred_element_type=jnp.float32,
    )
    gain_first = jnp.sum(joined_rows(store, chosen, "gain_first"), axis=0)
    gain_second = jnp.sum(joined_rows(store, chosen, "gain_second"), axis=0)
    shared_parts = (
        lax.psum_scatter(shared_term, ("group", "expert"), scatter_dimension=0, tiled=True),
        lax.psum_scatter(gain_first, ("group", "expert"), scatter_dimension=0, tiled=True),
        lax.psum_scatter(gain_second, ("group", "expert"), scatter_dimension=0, tiled=True),
    )
    return tuple(expert_parts) + tuple(shared_parts)


def on_device(
    tokens,
    cotangent,
    gain_attn,
    gain_mlp,
    w_kv,
    w_query,
    w_out,
    w_gate_up,
    w_down,
    att_routes,
    att_gates,
    mlp_routes,
    mlp_gates,
    blocks,
):
    experts = lax.axis_size("expert")
    owner = lax.axis_index("expert")
    shared_full = lax.all_gather(w_kv, ("group", "expert"), axis=0, tiled=True)
    gathered = (
        lax.all_gather(w_query, "group", axis=1, tiled=True),
        lax.all_gather(w_out, "group", axis=1, tiled=True),
        lax.all_gather(w_gate_up, "group", axis=1, tiled=True),
        lax.all_gather(w_down, "group", axis=1, tiled=True),
    )
    query_full = gathered[0][0]
    output_full = gathered[1][0]
    gate_up_full = gathered[2][0]
    down_full = gathered[3][0]
    micro = tokens.shape[0]
    local = tokens.shape[1]
    model = tokens.shape[2]
    length = local * experts
    width = HEADS * HDIM
    hidden_width = gate_up_full.shape[1] // 2
    own_cos, own_sin = angles(owner * local + jnp.arange(local, dtype=jnp.int32))
    names = (
        "rows",
        "query_grad",
        "attended",
        "result_grad",
        "rows_two",
        "both_grad",
        "hidden",
        "down_grad",
        "normed",
        "mixed_grad",
        "gain_first",
        "gain_second",
    )
    store = {name: [] for name in names}
    outputs = []
    input_grads = []
    for index in range(micro):
        inputs = tokens[index].astype(jnp.float32)
        block_ids = blocks[index, 0]
        att_pick, att_weight, row_pos, row_block = routing(
            att_routes[index], att_gates[index], block_ids, owner, experts
        )
        mlp_pick, mlp_weight, unused_pos, unused_block = routing(
            mlp_routes[index], mlp_gates[index], block_ids, owner, experts
        )
        scale = lax.rsqrt(jnp.mean(inputs * inputs, axis=1, keepdims=True) + EPS)
        normed = (inputs * scale * gain_attn).astype(jnp.bfloat16)
        mixed = jnp.dot(normed, shared_full, preferred_element_type=jnp.float32)
        keys_here = rotate(mixed[:, :width], own_cos, own_sin).astype(jnp.bfloat16)
        local_kv = jnp.concatenate([keys_here, mixed[:, width:].astype(jnp.bfloat16)], axis=1)
        sequence_kv = lax.all_gather(local_kv, "expert", axis=0, tiled=True)
        keys = sequence_kv[:, :width]
        values = sequence_kv[:, width:].reshape(length, HEADS, HDIM)
        rows = lax.all_to_all(
            spread(att_pick, normed), "expert", split_axis=0, concat_axis=0, tiled=True
        ).reshape(-1, model)
        row_cos, row_sin = angles(row_pos)
        queries = rotate(
            jnp.dot(rows, query_full, preferred_element_type=jnp.float32), row_cos, row_sin
        ).astype(jnp.bfloat16)
        scores = score_block(queries, keys, row_block, block_ids)
        top = jnp.max(scores, axis=2, keepdims=True)
        powers = jnp.exp(scores - top)
        total = jnp.sum(powers, axis=2, keepdims=True)
        log_total = top + jnp.log(total)
        probs = (powers / total).astype(jnp.bfloat16)
        attended = jnp.einsum("hrk,khd->rhd", probs, values, preferred_element_type=jnp.float32)
        attended = attended.reshape(-1, width).astype(jnp.bfloat16)
        result = jnp.dot(attended, output_full, preferred_element_type=jnp.float32).astype(
            jnp.bfloat16
        )
        back = lax.all_to_all(
            result.reshape(experts, CAP, model), "expert", split_axis=0, concat_axis=0, tiled=True
        )
        middle = inputs + collect(att_weight, back)
        scale_two = lax.rsqrt(jnp.mean(middle * middle, axis=1, keepdims=True) + EPS)
        normed_two = (middle * scale_two * gain_mlp).astype(jnp.bfloat16)
        rows_two = lax.all_to_all(
            spread(mlp_pick, normed_two), "expert", split_axis=0, concat_axis=0, tiled=True
        ).reshape(-1, model)
        both = jnp.dot(rows_two, gate_up_full, preferred_element_type=jnp.float32)
        gate = both[:, :hidden_width]
        up = both[:, hidden_width:]
        sigma = 1.0 / (1.0 + jnp.exp(-gate))
        hidden = (gate * sigma * up).astype(jnp.bfloat16)
        result_two = jnp.dot(hidden, down_full, preferred_element_type=jnp.float32).astype(
            jnp.bfloat16
        )
        back_two = lax.all_to_all(
            result_two.reshape(experts, CAP, model),
            "expert",
            split_axis=0,
            concat_axis=0,
            tiled=True,
        )
        final = middle + collect(mlp_weight, back_two)
        outputs.append(final.astype(jnp.bfloat16))
        upstream = cotangent[index].astype(jnp.float32)
        outgoing = jnp.einsum("ect,td->ecd", mlp_weight, upstream, precision=HIGH).astype(
            jnp.bfloat16
        )
        down_grad = lax.all_to_all(
            outgoing, "expert", split_axis=0, concat_axis=0, tiled=True
        ).reshape(-1, model)
        hidden_grad = jnp.einsum(
            "rd,fd->rf", down_grad, down_full, preferred_element_type=jnp.float32
        )
        slope = sigma * (1.0 + gate * (1.0 - sigma))
        both_grad = jnp.concatenate(
            [hidden_grad * up * slope, hidden_grad * gate * sigma], axis=1
        ).astype(jnp.bfloat16)
        row_grad_two = jnp.einsum(
            "rf,df->rd", both_grad, gate_up_full, preferred_element_type=jnp.float32
        ).astype(jnp.bfloat16)
        returned_two = lax.all_to_all(
            row_grad_two.reshape(experts, CAP, model),
            "expert",
            split_axis=0,
            concat_axis=0,
            tiled=True,
        )
        normed_two_grad = collect(mlp_pick, returned_two)
        scaled_two = normed_two_grad * gain_mlp
        gain_second = jnp.sum(normed_two_grad * middle * scale_two, axis=0, keepdims=True)
        middle_grad = (
            upstream
            + scale_two * scaled_two
            - middle * scale_two**3 * jnp.mean(scaled_two * middle, axis=1, keepdims=True)
        )
        outgoing_att = jnp.einsum("ect,td->ecd", att_weight, middle_grad, precision=HIGH).astype(
            jnp.bfloat16
        )
        result_grad = lax.all_to_all(
            outgoing_att, "expert", split_axis=0, concat_axis=0, tiled=True
        ).reshape(-1, model)
        attended_grad = jnp.einsum(
            "rd,fd->rf", result_grad, output_full, preferred_element_type=jnp.float32
        ).astype(jnp.bfloat16)
        again = jnp.exp(score_block(queries, keys, row_block, block_ids) - log_total)
        heads_grad = attended_grad.reshape(-1, HEADS, HDIM)
        value_grad = jnp.einsum(
            "hrk,rhd->khd",
            again.astype(jnp.bfloat16),
            heads_grad,
            preferred_element_type=jnp.float32,
        )
        prob_grad = jnp.einsum(
            "rhd,khd->hrk", heads_grad, values, preferred_element_type=jnp.float32
        )
        inner = jnp.sum(again * prob_grad, axis=2, keepdims=True)
        raw_grad = (again * (prob_grad - inner) * HDIM ** (-0.5)).astype(jnp.bfloat16)
        query_grad = jnp.einsum(
            "hrk,khd->rhd",
            raw_grad,
            keys.reshape(length, HEADS, HDIM),
            preferred_element_type=jnp.float32,
        ).reshape(-1, width)
        query_grad = rotate(query_grad, row_cos, -row_sin).astype(jnp.bfloat16)
        key_grad = jnp.einsum(
            "hrk,rhd->khd",
            raw_grad,
            queries.reshape(-1, HEADS, HDIM),
            preferred_element_type=jnp.float32,
        ).reshape(length, width)
        row_grad = jnp.einsum(
            "rf,df->rd", query_grad, query_full, preferred_element_type=jnp.float32
        ).astype(jnp.bfloat16)
        returned = lax.all_to_all(
            row_grad.reshape(experts, CAP, model), "expert", split_axis=0, concat_axis=0, tiled=True
        )
        kv_grad = lax.psum_scatter(
            jnp.concatenate([key_grad, value_grad.reshape(length, width)], axis=1).astype(
                jnp.bfloat16
            ),
            "expert",
            scatter_dimension=0,
            tiled=True,
        ).astype(jnp.float32)
        mixed_grad = jnp.concatenate(
            [rotate(kv_grad[:, :width], own_cos, -own_sin), kv_grad[:, width:]], axis=1
        ).astype(jnp.bfloat16)
        normed_grad = collect(att_pick, returned) + jnp.einsum(
            "tf,df->td", mixed_grad, shared_full, preferred_element_type=jnp.float32
        )
        scaled = normed_grad * gain_attn
        gain_first = jnp.sum(normed_grad * inputs * scale, axis=0, keepdims=True)
        input_grad = (
            middle_grad
            + scale * scaled
            - inputs * scale**3 * jnp.mean(scaled * inputs, axis=1, keepdims=True)
        )
        input_grads.append(input_grad.astype(jnp.bfloat16))
        kept = (
            rows,
            query_grad,
            attended,
            result_grad,
            rows_two,
            both_grad,
            hidden,
            down_grad,
            normed,
            mixed_grad,
            gain_first,
            gain_second,
        )
        for name, value in zip(names, kept):
            store[name].append(value)
    reduced = reduce_all(store, list(range(micro)))
    grad_query, grad_out, grad_gate_up, grad_down, grad_kv, grad_gain_attn, grad_gain_mlp = reduced
    return (
        jnp.stack(outputs, axis=0),
        jnp.stack(input_grads, axis=0),
        grad_gain_attn,
        grad_gain_mlp,
        grad_kv,
        grad_query,
        grad_out,
        grad_gate_up,
        grad_down,
    )


ZS, YS, XS, CS = 4, 2, 2, 2
SEQ = 320
MICRO = 2
KINDS = 9
F32 = jnp.float32
BF16 = jnp.bfloat16


def fits(mesh):
    return mesh.shape["group"] == ZS * YS and mesh.shape["expert"] == XS * CS


def group_move(value, move):
    pairs = []
    for z in range(ZS):
        for y in range(YS):
            to_z, to_y = move(z, y)
            pairs.append((z * YS + y, to_z * YS + to_y))
    return lax.ppermute(value, "group", pairs)


def z_move(value, step):
    return group_move(value, lambda z, y: ((z + step) % ZS, y))


def y_move(value):
    return group_move(value, lambda z, y: (z, 1 - y))


def x_move(value):
    return lax.ppermute(value, "expert", [(x * CS + c, (1 - x) * CS + c) for x in range(XS) for c in range(CS)])


def c_move(value):
    return lax.ppermute(value, "expert", [(x * CS + c, x * CS + 1 - c) for x in range(XS) for c in range(CS)])


def z_exchange(value):
    columns = [[z * YS + y for z in range(ZS)] for y in range(YS)]
    return lax.all_to_all(
        value, "group", split_axis=0, concat_axis=0, tiled=True, axis_index_groups=columns
    )


def gather_tokens(own):
    column = jnp.stack([own] + [z_move(own, -step) for step in range(1, ZS)], axis=0)
    plane = jnp.stack([column, x_move(column)], axis=1)
    plane = plane.reshape((ZS, XS * own.shape[0]) + own.shape[1:])
    return jnp.stack([plane, c_move(plane)], axis=0)


def reduce_tokens(other, mine):
    local = mine.shape[1] // XS
    total = mine.astype(F32) + c_move(other).astype(F32)
    arrived = x_move(total[:, local:].astype(BF16))
    total = total[:, :local] + arrived.astype(F32)
    result = total[0]
    for step in range(1, ZS):
        result = result + z_move(total[step].astype(BF16), step).astype(F32)
    return result


def merge(index, own, other, axis):
    return jnp.where(index == 0, jnp.stack([own, other], axis), jnp.stack([other, own], axis))


def take(value, index, axis):
    return lax.dynamic_index_in_dim(value, index, axis, keepdims=False)


def dot(left, right):
    return jnp.dot(left, right, preferred_element_type=F32)


def dot_t(left, right):
    return lax.dot_general(left, right, (((1,), (1,)), ((), ())), preferred_element_type=F32)


def dot_l(left, right):
    return lax.dot_general(left, right, (((0,), (0,)), ((), ())), preferred_element_type=F32)


def turned(value, cosine, sine):
    return value * cosine + pltpu.roll(value, HDIM // 2, 1) * sine


def masked_probs(query, key, row_block, key_block):
    scores = jnp.where(key_block <= row_block, dot_t(query, key) * HDIM ** (-0.5), -1e30)
    powers = jnp.exp(scores - jnp.max(scores, axis=1, keepdims=True))
    return powers / jnp.sum(powers, axis=1, keepdims=True)


MESH = pl.DeviceIdType.MESH
ORDER = (3, 1, 2, 0)
STEP = 16
DMA = pltpu.SemaphoreType.DMA
ANY = pl.BlockSpec(memory_space=pl.ANY)
VMEM = pl.BlockSpec(memory_space=pltpu.VMEM)


def by_rows(rows, body):
    def step(index, carry):
        body(pl.ds(pl.multiple_of(index * STEP, STEP), STEP))
        return carry

    lax.fori_loop(0, rows // STEP, step, 0)


class Place:
    def __init__(self):
        group, owner = lax.axis_index("group"), lax.axis_index("expert")
        self.z, self.y = lax.div(group, YS), lax.rem(group, YS)
        self.x, self.core = lax.div(owner, CS), lax.rem(owner, CS)
        self.group, self.owner = group, owner

        def device(z, y, x, core):
            return (z * YS + y, x * CS + core)

        self.x_peer = device(self.z, self.y, 1 - self.x, self.core)
        self.y_peer = device(self.z, 1 - self.y, self.x, self.core)
        self.core_peer = device(self.z, self.y, self.x, 1 - self.core)
        self.z_peers = [device(lax.rem(self.z + step, ZS), self.y, self.x, self.core) for step in range(ZS)]

    def enter(self, with_y):
        peers = [self.x_peer, self.core_peer] + self.z_peers[1:] + ([self.y_peer] if with_y else [])
        barrier = pltpu.get_barrier_semaphore()
        for peer in peers:
            pl.semaphore_signal(barrier, inc=1, device_id=peer, device_id_type=MESH)
        pl.semaphore_wait(barrier, len(peers))


def remote(src, dst, send, arrive, peer):
    return pltpu.make_async_remote_copy(
        src_ref=src, dst_ref=dst, send_sem=send, recv_sem=arrive, device_id=peer, device_id_type=MESH
    )


class Reduce:
    @staticmethod
    def scratch(micro, rows, model):
        return [
            pltpu.VMEM((micro, ZS, XS, rows, model), BF16),
            pltpu.VMEM((micro, ZS, XS, rows, model), BF16),
            pltpu.VMEM((micro, ZS, rows, model), BF16),
            pltpu.VMEM((micro, 2, ZS - 1, rows, model), BF16),
            pltpu.VMEM((micro, rows, model), F32),
            DMA((micro, ZS, XS)),
            DMA((micro, ZS, XS)),
            DMA((micro, ZS, XS)),
            DMA((micro, ZS)),
            DMA((micro, ZS)),
            DMA((micro, 2, ZS)),
            DMA((micro, 2, ZS)),
        ]

    def __init__(self, place, part, refs):
        self.place, self.part = place, part
        self.core_in, self.kept, self.x_in, self.z_in, self.total = [refs.pop(0) for _ in range(5)]
        self.sems = [refs.pop(0) for _ in range(7)]
        self.micro, self.rows = part.shape[0], part.shape[4]

    def core_copy(self, m, k, dx):
        send, arrive = self.sems[:2]
        return remote(
            self.part.at[m, k, 1, dx],
            self.core_in.at[m, k, dx],
            send.at[m, k, dx],
            arrive.at[m, k, dx],
            self.place.core_peer,
        )

    def kept_copy(self, m, k, dx):
        return pltpu.make_async_copy(
            self.part.at[m, k, 0, dx], self.kept.at[m, k, dx], self.sems[2].at[m, k, dx]
        )

    def x_copy(self, m, k):
        send, arrive = self.sems[3:5]
        return remote(
            self.core_in.at[m, k, 1], self.x_in.at[m, k], send.at[m, k], arrive.at[m, k], self.place.x_peer
        )

    def z_copy(self, m, down, far):
        send, arrive = self.sems[5:7]
        return remote(
            self.x_in.at[m, ZS - far if down else far],
            self.z_in.at[m, down, far - 1],
            send.at[m, down, far - 1],
            arrive.at[m, down, far - 1],
            self.place.z_peers[ZS - 1 if down else 1],
        )

    def begin(self):
        for m in range(self.micro):
            for dx in (1, 0):
                for k in ORDER:
                    self.core_copy(m, k, dx).start()
                    self.kept_copy(m, k, dx).start()

    def pass_x(self, m):
        for k in ORDER:
            self.core_copy(m, k, 1).wait_recv()
            self.kept_copy(m, k, 1).wait()

            def add(span, k=k):
                value = self.core_in[m, k, 1, span, :].astype(F32) + self.kept[m, k, 1, span, :].astype(F32)
                self.core_in[m, k, 1, span, :] = value.astype(BF16)

            by_rows(self.rows, add)
            self.x_copy(m, k).start()

    def z_unit(self, m, k):
        self.x_copy(m, k).wait_recv()
        self.core_copy(m, k, 0).wait_recv()
        self.kept_copy(m, k, 0).wait()

        def add(span):
            value = (
                self.x_in[m, k, span, :].astype(F32)
                + self.core_in[m, k, 0, span, :].astype(F32)
                + self.kept[m, k, 0, span, :].astype(F32)
            )
            if k:
                self.x_in[m, k, span, :] = value.astype(BF16)
            else:
                self.total[m, span, :] = value

        by_rows(self.rows, add)

    def beyond(self, down, far):
        return self.place.z >= far if down else self.place.z + far < ZS

    def chain(self, m, far):
        for down in (0, 1):

            def send(down=down):
                if far < ZS - 1:
                    pl.when(self.beyond(1 - down, 1))(functools.partial(self.join, m, down, far))
                self.z_copy(m, down, far).start()

            pl.when(self.beyond(down, far))(send)

    def join(self, m, down, far):
        self.z_copy(m, down, far + 1).wait_recv()
        place = ZS - far if down else far

        def add(span):
            value = self.x_in[m, place, span, :].astype(F32) + self.z_in[m, down, far, span, :].astype(F32)
            self.x_in[m, place, span, :] = value.astype(BF16)

        by_rows(self.rows, add)

    def finish(self, m):
        for down in (0, 1):

            def last(down=down):
                self.z_copy(m, down, 1).wait_recv()

                def add(span):
                    self.total[m, span, :] += self.z_in[m, down, 0, span, :].astype(F32)

                by_rows(self.rows, add)

            pl.when(self.beyond(1 - down, 1))(last)

    def sums(self, m):
        for turn, k in enumerate(ORDER):
            self.z_unit(m, k)
            if turn:
                self.chain(m, ZS - turn)

    def run(self):
        self.begin()
        for m in range(self.micro):
            self.pass_x(m)
        for m in range(self.micro):
            self.sums(m)

    def drain(self):
        for m in range(self.micro):
            for k in ORDER:
                for dx in range(XS):
                    self.core_copy(m, k, dx).wait_send()
                self.x_copy(m, k).wait_send()
            for down in (0, 1):
                for far in range(1, ZS):
                    pl.when(self.beyond(down, far))(self.z_copy(m, down, far).wait_send)


class Gather:
    @staticmethod
    def scratch(micro):
        return [
            DMA((micro,)),
            DMA((micro, ZS)),
            DMA((micro, ZS)),
            DMA((micro, ZS)),
            DMA((micro, ZS, XS)),
            DMA((micro, ZS, CS, XS)),
        ]

    def __init__(self, place, own, out, refs):
        self.place, self.own, self.out = place, own, out
        self.sems = [refs.pop(0) for _ in range(6)]
        self.micro = out.shape[0]

    def slot(self, m, k, dc, dx):
        return self.out.at[m, k, dc, dx]

    def local(self, m):
        return pltpu.make_async_copy(self.own.at[m], self.slot(m, 0, 0, 0), self.sems[0].at[m])

    def up(self, m, source, k):
        return remote(
            source, self.slot(m, k, 0, 0), self.sems[1].at[m, k], self.sems[5].at[m, k, 0, 0], self.place.z_peers[1]
        )

    def down(self, m, source, k):
        return remote(
            source,
            self.slot(m, k, 0, 0),
            self.sems[2].at[m, k],
            self.sems[5].at[m, k, 0, 0],
            self.place.z_peers[ZS - 1],
        )

    def over_x(self, m, source, k):
        return remote(
            source, self.slot(m, k, 0, 1), self.sems[3].at[m, k], self.sems[5].at[m, k, 0, 1], self.place.x_peer
        )

    def over_core(self, m, source, k, dx):
        return remote(
            source,
            self.slot(m, k, 1, dx),
            self.sems[4].at[m, k, dx],
            self.sems[5].at[m, k, 1, dx],
            self.place.core_peer,
        )

    def send_own(self, m):
        source, z = self.own.at[m], self.place.z
        pl.when(z < ZS - 1)(lambda: self.up(m, source, ZS - 1).start())
        pl.when(z > 0)(lambda: self.down(m, source, 1).start())
        self.over_x(m, source, 0).start()
        self.over_core(m, source, 0, 0).start()
        self.local(m).start()

    def pass_on(self, m, k):
        self.over_x(m, self.slot(m, k, 0, 0), k).start()
        self.over_core(m, self.slot(m, k, 0, 0), k, 0).start()

    def from_above(self, m, far):
        self.up(m, self.own.at[m], far).wait_recv()
        pl.when(self.place.z > 0)(lambda: self.down(m, self.slot(m, far, 0, 0), far + 1).start())
        self.pass_on(m, far)

    def from_below(self, m, far):
        self.up(m, self.own.at[m], ZS - far).wait_recv()
        source = self.slot(m, ZS - far, 0, 0)
        pl.when(self.place.z < ZS - 1)(lambda: self.up(m, source, ZS - far - 1).start())
        self.pass_on(m, ZS - far)

    def z_arrival(self, m, far):
        pl.when(self.place.z + far < ZS)(lambda: self.from_above(m, far))
        pl.when(self.place.z - far >= 0)(lambda: self.from_below(m, far))

    def x_arrival(self, m, k):
        self.over_x(m, self.own.at[m], k).wait_recv()
        self.over_core(m, self.slot(m, k, 0, 1), k, 1).start()

    def piece_arrival(self, m, k):
        for dx in range(XS):
            self.over_core(m, self.own.at[m], k, dx).wait_recv()

    def arrivals(self, m=0):
        for k in range(ZS):
            self.piece_arrival(m, k)
        self.local(m).wait()

    def z_round(self, far, chosen=None):
        for m in range(self.micro) if chosen is None else [chosen]:
            self.z_arrival(m, far)

    def x_round(self, far, chosen=None):
        for m in range(self.micro) if chosen is None else [chosen]:
            if far == 0:
                self.x_arrival(m, 0)
            else:
                pl.when(self.place.z + far < ZS)(lambda: self.x_arrival(m, far))
                pl.when(self.place.z - far >= 0)(lambda: self.x_arrival(m, ZS - far))

    def run(self):
        self.z_round(1)
        self.x_round(0)
        self.z_round(2)
        self.x_round(1)
        self.z_round(3)
        self.x_round(2)
        self.x_round(3)

    def drain(self, waited=False):
        z = self.place.z
        for m in range(self.micro):
            own = self.own.at[m]
            if not waited:
                self.arrivals(m)
            pl.when(z < ZS - 1)(lambda: self.up(m, own, ZS - 1).wait_send())
            pl.when(z > 0)(lambda: self.down(m, own, 1).wait_send())
            for far in range(1, ZS - 1):
                pl.when((z + far < ZS) & (z > 0))(lambda: self.down(m, own, far + 1).wait_send())
                pl.when((z - far >= 0) & (z < ZS - 1))(lambda: self.up(m, own, ZS - far - 1).wait_send())
            for k in range(ZS):
                self.over_x(m, own, k).wait_send()
                for dx in range(XS):
                    self.over_core(m, own, k, dx).wait_send()


class PieceReduce(Reduce):
    @staticmethod
    def scratch(micro, rows, model):
        return [
            pltpu.VMEM((micro, ZS, CS * XS * rows, model), BF16),
            pltpu.VMEM((micro, ZS, XS, rows, model), BF16),
            pltpu.VMEM((micro, ZS, rows, model), BF16),
            pltpu.VMEM((micro, 2, ZS - 1, rows, model), BF16),
            pltpu.VMEM((micro, rows, model), F32),
            DMA((micro, ZS, XS)),
            DMA((micro, ZS, XS)),
            DMA((micro, ZS)),
            DMA((micro, ZS)),
            DMA((micro, 2, ZS)),
            DMA((micro, 2, ZS)),
        ]

    def __init__(self, place, refs):
        self.place = place
        self.part, self.core_in, self.x_in, self.z_in, self.total = [refs.pop(0) for _ in range(5)]
        core_send, core_recv, x_send, x_recv, z_send, z_recv = [refs.pop(0) for _ in range(6)]
        self.sems = [core_send, core_recv, None, x_send, x_recv, z_send, z_recv]
        self.micro, self.rows = self.total.shape[0], self.total.shape[1]

    def unit(self, m, k, dc, dx):
        return self.part.at[m, k, pl.ds((dc * XS + dx) * self.rows, self.rows)]

    def core_copy(self, m, k, dx):
        send, arrive = self.sems[:2]
        return remote(
            self.unit(m, k, 1, dx),
            self.core_in.at[m, k, dx],
            send.at[m, k, dx],
            arrive.at[m, k, dx],
            self.place.core_peer,
        )

    def begin_piece(self, m, k):
        for dx in (1, 0):
            self.core_copy(m, k, dx).start()

    def x_piece(self, m, k):
        self.core_copy(m, k, 1).wait_recv()
        kept = self.unit(m, k, 0, 1)

        def add(span):
            value = self.core_in[m, k, 1, span, :].astype(F32) + kept[span, :].astype(F32)
            self.core_in[m, k, 1, span, :] = value.astype(BF16)

        by_rows(self.rows, add)
        self.x_copy(m, k).start()

    def z_piece(self, m, k):
        self.x_copy(m, k).wait_recv()
        self.core_copy(m, k, 0).wait_recv()
        kept = self.unit(m, k, 0, 0)

        def sum_of(span):
            return (
                self.x_in[m, k, span, :].astype(F32)
                + self.core_in[m, k, 0, span, :].astype(F32)
                + kept[span, :].astype(F32)
            )

        def away(span):
            self.x_in[m, k, span, :] = sum_of(span).astype(BF16)

        def here(span):
            self.total[m, span, :] = sum_of(span)

        pl.when(k != 0)(lambda: by_rows(self.rows, away))
        pl.when(k == 0)(lambda: by_rows(self.rows, here))

    def drain(self):
        for m in range(self.micro):
            for k in range(ZS):
                for dx in range(XS):
                    self.core_copy(m, k, dx).wait_send()
                self.x_copy(m, k).wait_send()
            for down in (0, 1):
                for far in range(1, ZS):
                    pl.when(self.beyond(down, far))(self.z_copy(m, down, far).wait_send)


def piece_of(place, index, micro):
    turn = lax.rem(index, ZS)
    inner = turn + lax.div(turn, 2) * (5 - 2 * turn)
    last = lax.rem(ZS - turn, ZS)
    z = place.z
    return lax.div(index, ZS), jnp.where(z == 0, turn, jnp.where(z == ZS - 1, last, inner))


def run_pieces(place, reduce, piece, between):
    pieces = reduce.micro * ZS

    def step(index, carry):
        @pl.when(index < pieces)
        def _():
            m, k = piece_of(place, index, reduce.micro)
            piece(index, m, k)
            reduce.begin_piece(m, k)

        between(index)

        @pl.when((index >= 1) & (index < pieces + 1))
        def _():
            reduce.x_piece(*piece_of(place, index - 1, reduce.micro))

        @pl.when((index >= 3) & (index < pieces + 3))
        def _():
            reduce.z_piece(*piece_of(place, index - 3, reduce.micro))

        for m in range(reduce.micro):
            first = (m + 1) * ZS + 2
            for far in range(1, ZS):
                pl.when(index == first + ZS - 1 - far)(functools.partial(reduce.chain, m, far))
        return carry

    lax.fori_loop(0, pieces + 5, step, 0)


def begin_gathers(gathers):
    for m in range(gathers[0].micro):
        for gather in gathers:
            gather.send_own(m)
        if m == 0:
            for gather in gathers:
                gather.z_round(1, 0)
            for gather in gathers:
                gather.x_round(0, 0)


def gather_steps(gathers, index):
    for m in range(gathers[0].micro):
        for far in range(0 if m else 1, ZS):

            @pl.when(index == (max(0, m * (ZS - 2) - 1) + far if m else far - 1))
            def _(m=m, far=far):
                for gather in gathers:
                    if far + 1 < ZS:
                        gather.z_round(far + 1, m)
                for gather in gathers:
                    gather.x_round(far, m)


def wait_local(gather, m):
    gather.local(m).wait()


def by_lanes(count, width, body):
    def step(index, carry):
        body(pl.ds(pl.multiple_of(index * width, width), width))
        return carry

    lax.fori_loop(0, count, step, 0)


class Spread:
    @staticmethod
    def scratch(pieces, depth):
        return [DMA((pieces,)), DMA((ZS, pieces)), DMA((ZS, pieces))] + [
            DMA((ZS << step,)) for step in range(depth) for _ in range(2)
        ]

    def __init__(self, place, sources, targets, view, depth, refs):
        self.place, self.sources, self.targets, self.view, self.depth = place, sources, targets, view, depth
        self.local_sem, self.z_send, self.z_recv = [refs.pop(0) for _ in range(3)]
        self.sems = [(refs.pop(0), refs.pop(0)) for _ in range(depth)]
        self.pieces = self.local_sem.shape[0]

    def z_copy(self, step, piece):
        place = self.place
        mine = self.targets(self.view(place.z, place.y, place.x, place.core))
        return remote(
            self.sources(lax.rem(place.z + step, ZS))[piece],
            mine[piece],
            self.z_send.at[step, piece],
            self.z_recv.at[step, piece],
            place.z_peers[step],
        )

    def local(self, piece):
        place = self.place
        mine = self.targets(self.view(place.z, place.y, place.x, place.core))
        return pltpu.make_async_copy(self.sources(place.z)[piece], mine[piece], self.local_sem.at[piece])

    def hop(self, axis, index):
        place = self.place
        z = lax.rem(place.z - (index >> axis) + ZS, ZS)
        y = place.y if axis < 1 else (place.y + ((index >> (axis - 1)) & 1)) % 2
        x = place.x if axis < 2 else (place.x + (index & 1)) % 2
        block = self.view(z, y, x, place.core)
        peer = (place.y_peer, place.x_peer, place.core_peer)[axis]
        send, arrive = self.sems[axis]
        return remote(block, block, send.at[index], arrive.at[index], peer)

    def begin(self):
        for piece in range(self.pieces):
            self.local(piece).start()
        for step in (1, 3, 2):
            for piece in range(self.pieces):
                self.z_copy(step, piece).start()

    def forward(self, axis, index):
        for later in range(axis, self.depth):
            self.hop(later, index << (later - axis)).start()

    def send(self, step):
        for piece in range(self.pieces):
            (self.z_copy(step, piece) if step else self.local(piece)).start()

    def z_round(self, step):
        for piece in range(self.pieces):
            if step:
                self.z_copy(step, piece).wait_recv()
            else:
                self.local(piece).wait()
        self.forward(0, step)

    def hop_round(self, axis, index):
        self.hop(axis, index).wait_recv()
        self.forward(axis + 1, index * 2 + 1)

    def drain(self):
        for step in range(1, ZS):
            for piece in range(self.pieces):
                self.z_copy(step, piece).wait_send()
        for axis in range(self.depth):
            for index in range(ZS << axis):
                self.hop(axis, index).wait_send()


class Share:
    @staticmethod
    def scratch(pieces):
        return [DMA((pieces,)), DMA((pieces,)), DMA((pieces,))]

    def __init__(self, place, blocks, refs):
        local, send, arrive = [refs.pop(0) for _ in range(3)]
        self.copies = []
        for index, (source, target) in enumerate(blocks):
            self.copies.append(pltpu.make_async_copy(source, target, local.at[index]))
            self.copies.append(remote(source, target, send.at[index], arrive.at[index], place.y_peer))

    def begin(self):
        for copy in self.copies:
            copy.start()

    def drain(self):
        for copy in self.copies:
            copy.wait()


def normed_rows(rows, gain):
    return rows * lax.rsqrt(jnp.mean(rows * rows, axis=1, keepdims=True) + EPS) * gain


def norm_back(grad, rows, upstream, gain):
    scale = lax.rsqrt(jnp.mean(rows * rows, axis=1, keepdims=True) + EPS)
    scaled = grad * gain
    inner = jnp.mean(scaled * rows, axis=1, keepdims=True)
    return upstream + scale * scaled - rows * (scale * scale * scale) * inner, grad * rows * scale


def y_half(place, target, rows):
    return target.at[pl.ds(pl.multiple_of(place.y * rows, rows), rows)]


def by_heads(width, body):
    def step(head, carry):
        body(lambda kind: pl.ds(pl.multiple_of(kind * width + head * HDIM, HDIM), HDIM))
        return carry

    lax.fori_loop(0, width // HDIM, step, 0)


def columns_of(marks, place, m, k):
    local, lanes = marks.shape[3:]
    length = CS * XS * local
    block = marks[k].reshape(length, lanes)
    across = jnp.transpose(block)

    def pick(kind, source, axis):
        value = None
        for index in range(MICRO):
            at = index * KINDS + kind
            part = source[:, at : at + 1] if axis else source[at : at + 1, :]
            value = part if value is None else jnp.where(m == index, part, value)
        return value

    owner = place.owner.astype(F32)
    gates = [jnp.where(pick(kind, block, 1) == owner, pick(kind + 2, block, 1), 0.0) for kind in range(2)]
    return gates[0] + gates[1], pick(KINDS - 1, block, 1), pick(KINDS - 1, across, 0)


def attention_kernel(
    sizes,
    tokens,
    cotangent,
    first_gain,
    second_gain,
    table,
    cosine,
    sine,
    w_kv,
    w_query,
    w_out,
    w_gate_up,
    w_down,
    *refs,
):
    refs = list(refs)
    normed_out, middle_out, everyone, cotangent_out, table_out, turned_out, attended_out = [
        refs.pop(0) for _ in range(7)
    ]
    qkv_weight, out_weight, gate_up_weight, down_weight = [refs.pop(0) for _ in range(4)]
    wide, kv_rows, model_rows, out_rows, down_rows = sizes
    place = Place()
    own = refs.pop(0)
    normed = Gather(place, own, everyone, refs)
    upstream = Gather(place, cotangent, cotangent_out, refs)
    tables = Gather(place, table, table_out, refs)
    reduce = PieceReduce(place, refs)

    def lanes(start, width):
        return pl.ds(pl.multiple_of(start, HDIM), width)

    def kv_view(z, y, x, core):
        row = ((z * YS + y) * (XS * CS) + x * CS + core) * kv_rows
        return qkv_weight.at[pl.ds(pl.multiple_of(row, kv_rows), kv_rows), pl.ds(wide, 2 * wide)]

    def rows_of(z, y):
        return pl.ds(pl.multiple_of((z * YS + y) * model_rows, model_rows), model_rows)

    kv = Spread(
        place,
        lambda z: [w_kv.at[:, lanes((kind * ZS + z) * wide, wide)] for kind in range(2)],
        lambda block: [block.at[:, pl.ds(kind * wide, wide)] for kind in range(2)],
        kv_view,
        3,
        refs,
    )
    query = Spread(
        place,
        lambda z: [w_query.at[0, :, lanes(z * wide, wide)]],
        lambda block: [block],
        lambda z, y, x, core: qkv_weight.at[rows_of(z, y), pl.ds(0, wide)],
        1,
        refs,
    )
    hidden_width = gate_up_weight.shape[2]
    gate_up = Spread(
        place,
        lambda z: [w_gate_up.at[0, :, lanes((kind * ZS + z) * hidden_width, hidden_width)] for kind in range(2)],
        lambda block: [block.at[kind] for kind in range(2)],
        lambda z, y, x, core: gate_up_weight.at[:, rows_of(z, y)],
        1,
        refs,
    )
    shared = Share(place, [(w_out.at[0], y_half(place, out_weight, out_rows))], refs)
    down = Share(place, [(w_down.at[0], y_half(place, down_weight, down_rows))], refs)
    arrived, qkv, attended, marks, weight, out_here, load, store, late_load = [refs.pop(0) for _ in range(9)]
    model = tokens.shape[2]
    tile = model // 2
    late_loads = [
        pltpu.make_async_copy(qkv_weight, weight, late_load.at[0]),
        pltpu.make_async_copy(out_weight, out_here, late_load.at[1]),
        pltpu.make_async_copy(table_out.at[0], marks, late_load.at[2]),
    ]

    def stores(sequence):
        return [
            pltpu.make_async_copy(qkv, turned_out.at[sequence], store.at[0]),
            pltpu.make_async_copy(attended, attended_out.at[sequence], store.at[1]),
        ]

    def piece(index, m, k):
        sequence = m * ZS + k
        normed.piece_arrival(m, k)
        pl.when(k == 0)(functools.partial(wait_local, normed, m))
        loads = [
            pltpu.make_async_copy(everyone.at[m, k, dc, dx], arrived.at[dc, dx], load.at[dc, dx])
            for dc in range(CS)
            for dx in range(XS)
        ]
        for copy in loads:
            copy.start()

        @pl.when(index == 0)
        def _():
            for copy in late_loads:
                copy.wait()

        @pl.when(index > 0)
        def _():
            for copy in stores(0):
                copy.wait()

        row_gate, row_block, key_block = columns_of(marks, place, m, k)
        for copy in loads:
            copy.wait()
        length = qkv.shape[0]
        for kind in range(3):
            value = dot(arrived[...].reshape(length, model), weight[:, kind * wide : (kind + 1) * wide])
            for head in range(wide // HDIM):
                part = value[:, head * HDIM : (head + 1) * HDIM]
                if kind < 2:
                    part = turned(part, cosine[...], sine[...])
                start = kind * wide + head * HDIM
                qkv[:, start : start + HDIM] = part.astype(BF16)

        def head(span_of):
            query, key, value = [qkv[:, span_of(kind)] for kind in range(3)]
            probs = masked_probs(query, key, row_block, key_block).astype(BF16)
            attended[:, span_of(0)] = dot(probs, value).astype(BF16)

        by_heads(wide, head)
        for start in range(0, model, tile):
            value = dot(attended[...], out_here[:, start : start + tile]) * row_gate
            reduce.part[m, k, :, start : start + tile] = value.astype(BF16)
        for copy in stores(sequence):
            copy.start()

    def between(index):
        due = {
            2: [lambda: gate_up.z_round(1)],
            3: [lambda: gate_up.z_round(3)],
            4: [lambda: upstream.send_own(0)],
            5: [lambda: gate_up.z_round(2), lambda: upstream.send_own(1)],
            6: [lambda: upstream.z_round(1)],
            7: [lambda: upstream.x_round(0), lambda: upstream.z_round(2)],
            8: [lambda: upstream.x_round(1), lambda: upstream.z_round(3)],
            9: [lambda: upstream.x_round(2)],
            10: [lambda: upstream.x_round(3)],
        }
        for at, tasks in due.items():

            @pl.when(index == at)
            def _(tasks=tasks):
                for task in tasks:
                    task()

    place.enter(True)
    shared.begin()
    kv.begin()
    tables.send_own(0)
    for m in range(normed.micro):

        def body(span, m=m):
            own[m, span, :] = normed_rows(tokens[m, span, :].astype(F32), first_gain[...]).astype(BF16)

        by_rows(tokens.shape[1], body)
        normed.send_own(m)
    query.begin()
    kv.z_round(0)
    tables.z_round(1)
    kv.z_round(1)
    kv.z_round(3)
    normed.z_round(1)
    kv.z_round(2)
    for index in (0, 1, 3, 2):
        kv.hop_round(0, index)
    normed.x_round(0)
    for step in (0, 1, 3, 2):
        gate_up.send(step)
    gate_up.z_round(0)
    tables.z_round(2)
    normed.z_round(2)
    normed.x_round(1)
    for step in (0, 1, 3, 2):
        query.z_round(step)
    for index in (0, 2, 6, 4, 1, 3, 7, 5):
        kv.hop_round(1, index)
    normed.z_round(3)
    tables.z_round(3)
    for far in range(ZS):
        tables.x_round(far)
    normed.x_round(2)
    normed.x_round(3)
    for index in range(ZS << 2):
        kv.hop_round(2, index)
    for index in range(ZS):
        query.hop_round(0, index)
    shared.drain()
    tables.arrivals()
    for copy in late_loads:
        copy.start()
    down.begin()
    run_pieces(place, reduce, piece, between)
    for m in range(reduce.micro):
        reduce.finish(m)

        def body(span, m=m):
            middle = tokens[m, span, :].astype(F32) + reduce.total[m, span, :]
            middle_out[m, span, :] = middle
            normed_out[m, span, :] = normed_rows(middle, second_gain[...]).astype(BF16)

        by_rows(reduce.rows, body)
    for copy in stores(0):
        copy.wait()
    for index in range(ZS):
        gate_up.hop_round(0, index)
    for gather in (tables, normed):
        gather.drain(True)
    for part in (upstream, kv, query, gate_up, down, reduce):
        part.drain()


def attend_back_kernel(
    rows, weight_in, out_in, marks, cosine, sine, turned_qkv, tokens, middle_grad, gain, gate_grads, up_grads, *refs
):
    refs = list(refs)
    input_out, terms_out, row_grad_out, qkv_grad_out, weight_grad_out, sums_out, everyone = [
        refs.pop(0) for _ in range(7)
    ]
    place = Place()
    gather = Gather(place, rows, everyone, refs)
    reduce = PieceReduce(place, refs)
    arrived, kept, row_grad, qkv_grad, load, store = [refs.pop(0) for _ in range(6)]
    mine, theirs, mine_sem, y_send, y_recv, z_send, z_recv, sum_local = [refs.pop(0) for _ in range(8)]
    weight, out_weight, weight_load = [refs.pop(0) for _ in range(3)]
    weight_loads = [
        pltpu.make_async_copy(weight_in, weight, weight_load.at[0]),
        pltpu.make_async_copy(out_in, out_weight, weight_load.at[1]),
    ]
    wide, model = out_weight.shape
    tile = model // 2
    width = mine.shape[2]

    def stores(sequence):
        return [
            pltpu.make_async_copy(row_grad, row_grad_out.at[sequence], store.at[0]),
            pltpu.make_async_copy(qkv_grad, qkv_grad_out.at[sequence], store.at[1]),
        ]

    def piece(index, m, k):
        sequence = m * ZS + k
        gather.piece_arrival(m, k)
        pl.when(k == 0)(lambda: gather.local(m).wait())
        loads = [
            pltpu.make_async_copy(everyone.at[m, k, dc, dx], arrived.at[dc, dx], load.at[dc, dx])
            for dc in range(CS)
            for dx in range(XS)
        ]
        loads.append(pltpu.make_async_copy(turned_qkv.at[sequence], kept, load.at[CS, 0]))
        for copy in loads:
            copy.start()

        @pl.when(index == 0)
        def _():
            for copy in weight_loads:
                copy.wait()

        @pl.when(index > 0)
        def _():
            for copy in stores(0):
                copy.wait()

        for copy in loads:
            copy.wait()
        length = kept.shape[0]
        row_gate, row_block, key_block = columns_of(marks, place, m, k)
        for start in range(0, model, tile):
            value = arrived[:, :, :, start : start + tile].astype(F32).reshape(length, tile) * row_gate
            row_grad[:, start : start + tile] = value.astype(BF16)
        qkv_grad[:, :wide] = dot_t(row_grad[...], out_weight[...]).astype(BF16)

        def head(span_of):
            query, key, value = [kept[:, span_of(kind)] for kind in range(3)]
            grad = qkv_grad[:, span_of(0)]
            probs = masked_probs(query, key, row_block, key_block)
            prob_grad = dot_t(grad, value)
            inner = jnp.sum(probs * prob_grad, axis=1, keepdims=True)
            raw_grad = (probs * (prob_grad - inner) * HDIM ** (-0.5)).astype(BF16)
            qkv_grad[:, span_of(0)] = turned(dot(raw_grad, key), cosine[...], -sine[...]).astype(BF16)
            qkv_grad[:, span_of(1)] = turned(dot_l(raw_grad, query), cosine[...], -sine[...]).astype(BF16)
            qkv_grad[:, span_of(2)] = dot_l(probs.astype(BF16), grad).astype(BF16)

        by_heads(wide, head)
        for start in range(0, model, tile):
            value = dot_t(qkv_grad[...], weight[start : start + tile, :])
            reduce.part[m, k, :, start : start + tile] = value.astype(BF16)
        for copy in stores(sequence):
            copy.start()

    steps = (1, 3, 2, 0)
    sources = (gate_grads, up_grads)

    def z_of(turn):
        return lax.rem(place.z + steps[turn], ZS)

    def own_copy(part):
        kind, turn = divmod(part, ZS)
        return pltpu.make_async_copy(sources[kind].at[z_of(turn), place.y], mine.at[part], mine_sem.at[part])

    def y_copy(part):
        kind, turn = divmod(part, ZS)
        return remote(
            sources[kind].at[z_of(turn), 1 - place.y],
            theirs.at[part],
            y_send.at[part],
            y_recv.at[part],
            place.y_peer,
        )

    columns = weight_grad_out.at[:, pl.ds(pl.multiple_of(place.z * width, HDIM), width)]

    def sum_copy(part):
        kind, turn = divmod(part, ZS)
        if kind:
            return pltpu.make_async_copy(theirs.at[part], sums_out.at[z_of(turn)], sum_local.at[part])
        if steps[turn] == 0:
            return pltpu.make_async_copy(theirs.at[part], columns, sum_local.at[part])
        return remote(
            theirs.at[part], columns, z_send.at[steps[turn]], z_recv.at[steps[turn]], place.z_peers[steps[turn]]
        )

    def pass_grads(part):
        y_copy(part).wait()
        if part + 2 < 2 * ZS:
            y_copy(part + 2).start()
        own_copy(part).wait()

        def add(span):
            value = mine[part, span, :].astype(F32) + theirs[part, span, :].astype(F32)
            theirs[part, span, :] = value.astype(BF16)

        by_rows(mine.shape[1], add)
        sum_copy(part).start()

    def between(index):
        gather_steps([gather], index)
        for part, at in enumerate((2, 3, 5, 6, 8, 9)):
            pl.when(index == at)(functools.partial(pass_grads, part))

    for copy in weight_loads:
        copy.start()
    for part in range(2 * ZS):
        own_copy(part).start()
    place.enter(True)
    for part in range(2):
        y_copy(part).start()
    begin_gathers([gather])
    run_pieces(place, reduce, piece, between)
    for part in range(6, 2 * ZS):
        pass_grads(part)
    terms_out[...] = jnp.zeros_like(terms_out)
    for m in range(gather.micro):
        reduce.finish(m)

        def body(span, m=m):
            result, found = norm_back(
                reduce.total[m, span, :], tokens[m, span, :].astype(F32), middle_grad[m, span, :], gain[...]
            )
            input_out[m, span, :] = result.astype(BF16)
            terms_out[...] += found

        by_rows(reduce.rows, body)
    for copy in stores(0):
        copy.wait()
    gather.drain(True)
    reduce.drain()
    for part in range(2 * ZS):
        sum_copy(part).wait()


def mlp_kernel(
    normed, gate_up_part, down_part, select, select_back, gates, cotangents, middle, cotangent, gain, *refs
):
    refs = list(refs)
    own_out, grad_out, terms_out, rows_out, up_grad_out, hidden_out, down_grad_out, result_out = [
        refs.pop(0) for _ in range(8)
    ]
    everyone = refs.pop(0)
    place = Place()
    gathers = [Gather(place, normed, everyone, refs)]
    reduce = PieceReduce(place, refs)
    arrived, upstream, rows, down_grad, hidden, both_grad, result = [refs.pop(0) for _ in range(7)]
    gate_weight, up_weight, down, load, store, weight_load = [refs.pop(0) for _ in range(6)]
    width = down.shape[0]
    model = middle.shape[2]
    tile = model // 2
    pieces = reduce.micro * ZS
    weight_loads = [
        pltpu.make_async_copy(source, target, weight_load.at[i])
        for i, (source, target) in enumerate(
            ((gate_up_part.at[0], gate_weight), (gate_up_part.at[1], up_weight), (down_part, down))
        )
    ]

    kept = (
        (rows, rows_out),
        (down_grad, down_grad_out),
        (hidden, hidden_out),
        (both_grad, up_grad_out),
        (result, result_out),
    )

    def store_of(number, sequence):
        here, there = kept[number]
        return pltpu.make_async_copy(here, there.at[sequence], store.at[number])

    def loads_of(number, source, target, m, k):
        return [
            pltpu.make_async_copy(source.at[m, k, dc, dx], target.at[dc, dx], load.at[number, dc, dx])
            for dc in range(CS)
            for dx in range(XS)
        ]

    def piece(index, m, k):
        for gather in gathers:
            gather.piece_arrival(m, k)
            pl.when(k == 0)(functools.partial(wait_local, gather, m))
        sequence = m * ZS + k
        loads = loads_of(0, everyone, arrived, m, k)
        for copy in loads:
            copy.start()

        def stored(*numbers):
            @pl.when(index > 0)
            def _():
                for number in numbers:
                    store_of(number, 0).wait()

        def store_out(*numbers):
            for number in numbers:
                store_of(number, sequence).start()

        @pl.when(index == 0)
        def _():
            for copy in loads_of(1, cotangents, upstream, m, k):
                copy.start()
            for copy in weight_loads:
                copy.wait()

        stored(0, 1)
        for copy in loads + loads_of(1, cotangents, upstream, m, k):
            copy.wait()
        chosen, back, gate_of_row = select[sequence], select_back[sequence], gates[sequence]
        length = select.shape[2]

        def to_rows(span):
            rows[:, span] = dot(chosen, arrived[:, :, :, span].reshape(length, tile)).astype(BF16)
            down_grad[:, span] = (dot(chosen, upstream[:, :, :, span].reshape(length, tile)) * gate_of_row).astype(BF16)

        by_lanes(model // tile, tile, to_rows)
        store_out(0, 1)

        @pl.when(index + 1 < pieces)
        def _():
            for copy in loads_of(1, cotangents, upstream, *piece_of(place, index + 1, reduce.micro)):
                copy.start()

        stored(2, 3)

        half = width // (2 * HDIM) * HDIM
        for start, stop in ((0, half), (half, width)):
            gate = dot(rows[...], gate_weight[:, start:stop])
            up = dot(rows[...], up_weight[:, start:stop])
            hidden_grad = dot_t(down_grad[...], down[start:stop, :])
            sigma = 0.5 * jnp.tanh(0.5 * gate) + 0.5
            silu = gate * sigma
            hidden[:, start:stop] = (silu * up).astype(BF16)
            slope = sigma + silu * (1.0 - sigma)
            both_grad[:, start:stop] = (hidden_grad * up * slope).astype(BF16)
            both_grad[:, width + start : width + stop] = (hidden_grad * silu).astype(BF16)

        store_out(2, 3)
        stored(4)

        def to_tokens(span):
            row_grad = dot_t(both_grad[:, :width], gate_weight[span, :])
            row_grad = (row_grad + dot_t(both_grad[:, width:], up_weight[span, :])).astype(BF16)
            reduce.part[m, k, :, span] = dot(back, row_grad).astype(BF16)
            value = (dot(hidden[...], down[:, span]) * gate_of_row).astype(BF16)
            result[:, span] = dot(back, value).astype(BF16)

        by_lanes(model // tile, tile, to_tokens)
        store_out(4)

    for copy in weight_loads:
        copy.start()
    place.enter(False)
    begin_gathers(gathers)
    run_pieces(place, reduce, piece, functools.partial(gather_steps, gathers))
    terms_out[...] = jnp.zeros_like(terms_out)
    for m in range(reduce.micro):
        reduce.finish(m)

        def body(span, m=m):
            found, terms = norm_back(
                reduce.total[m, span, :], middle[m, span, :], cotangent[m, span, :].astype(F32), gain[...]
            )
            grad_out[m, span, :] = found
            own_out[m, span, :] = found.astype(BF16)
            terms_out[...] += terms

        by_rows(reduce.rows, body)
    for number in range(len(kept)):
        store_of(number, 0).wait()
    for gather in gathers:
        gather.drain(True)
    reduce.drain()


class Halves:
    def __init__(self, own, other, copy):
        self.own, self.other, self.copy = own, other, copy

    def begin(self):
        self.copy.start()

    def add(self):
        self.copy.wait()

        def body(index, carry):
            value = self.own[index].astype(F32) + self.other[index].astype(F32)
            self.other[index] = value.astype(BF16)
            return carry

        lax.fori_loop(0, self.other.shape[0], body, 0)


def last_kernel(part, middle, first_terms, second_terms, rows, grads, attended, row_grads, up_grad, *refs):
    refs = list(refs)
    output, gains_out, query_out, kv_out, out_out, up_out = [refs.pop(0) for _ in range(6)]
    place = Place()
    reduce = Reduce(place, part, refs)
    tall, long, load = [refs.pop(0) for _ in range(3)]
    query_all, query_in, kv_all, core_in, x_in, y_in, out_own, out_send, out_in = [refs.pop(0) for _ in range(9)]
    hop_send, hop_recv, z_send, z_recv, z_local = [refs.pop(0) for _ in range(5)]
    terms, gain_in, gain_send, gain_recv = [refs.pop(0) for _ in range(4)]
    up_send, up_recv, up_local = [refs.pop(0) for _ in range(3)]
    wide, kv_rows = query_out.shape[1] // ZS, kv_out.shape[0]
    model = tall.shape[1]
    tile = model // ZS

    def swap(number, source, target, peer):
        return remote(source, target, hop_send.at[number], hop_recv.at[number], peer)

    query = Halves(
        query_all.at[:, place.y], query_in, swap(0, query_all.at[:, 1 - place.y], query_in, place.y_peer)
    )
    over_core = Halves(
        kv_all.at[:, place.core], core_in, swap(1, kv_all.at[:, 1 - place.core], core_in, place.core_peer)
    )
    by_x = core_in.reshape(ZS * YS, XS, kv_rows, 2 * wide)
    over_x = Halves(by_x.at[:, place.x], x_in, swap(2, by_x.at[:, 1 - place.x], x_in, place.x_peer))
    by_y = x_in.reshape(ZS, YS, kv_rows, 2 * wide)
    over_y = Halves(by_y.at[:, place.y], y_in, swap(3, by_y.at[:, 1 - place.y], y_in, place.y_peer))
    over_out = swap(4, out_send, out_in, place.y_peer)

    def lanes(start):
        return pl.ds(pl.multiple_of(start, HDIM), wide)

    def z_parts(step):
        to = lax.rem(place.z + step, ZS)
        pairs = [(query_in.at[to], query_out.at[:, lanes(place.z * wide)])]
        for kind in range(2):
            pairs.append(
                (y_in.at[to, :, pl.ds(kind * wide, wide)], kv_out.at[:, lanes((kind * ZS + place.z) * wide)])
            )
        return pairs

    def z_copy(step, piece):
        source, target = z_parts(step)[piece]
        if step == 0:
            return pltpu.make_async_copy(source, target, z_local.at[piece])
        return remote(source, target, z_send.at[step, piece], z_recv.at[step, piece], place.z_peers[step])

    hops = [[place.core_peer], [place.x_peer], [place.y_peer], place.z_peers[1:]]

    def gain_copies(hop):
        return [
            remote(terms, gain_in.at[hop + i], gain_send.at[hop + i], gain_recv.at[hop + i], peer)
            for i, peer in enumerate(hops[hop])
        ]

    def send_gains(hop):
        for copy in gain_copies(hop):
            copy.start()

    def add_gains(hop):
        copies = gain_copies(hop)
        for copy in copies:
            copy.wait()
        for i in range(len(copies)):
            terms[...] += gain_in[hop + i]
        if hop + 1 < len(hops):
            send_gains(hop + 1)

    width = up_grad.shape[2]
    columns = up_out.at[:, pl.ds(pl.multiple_of(place.z * width, HDIM), width)]
    up_copies = [pltpu.make_async_copy(up_grad.at[place.z], columns, up_local)]
    for step in (1, 3, 2):
        source = up_grad.at[lax.rem(place.z + step, ZS)]
        up_copies.append(remote(source, columns, up_send.at[step], up_recv.at[step], place.z_peers[step]))
    loads = [pltpu.make_async_copy(rows, tall, load.at[0]), pltpu.make_async_copy(grads, long, load.at[1])]
    later_loads = [
        pltpu.make_async_copy(row_grads, tall, load.at[2]),
        pltpu.make_async_copy(attended, long.at[:, pl.ds(0, wide)], load.at[3]),
    ]

    def small_grads(z):
        span = slice(z * tile, (z + 1) * tile)
        value = dot_l(tall[:, span], long[:, :wide]).astype(BF16)
        query_all[z] = value.reshape(query_all.shape[1:])
        blocks = kv_all.shape[0] // ZS
        for kind in range(2):
            value = dot_l(tall[:, span], long[:, (kind + 1) * wide : (kind + 2) * wide]).astype(BF16)
            kv_all[z * blocks : (z + 1) * blocks, :, :, kind * wide : (kind + 1) * wide] = value.reshape(
                (blocks,) + kv_all.shape[1:3] + (wide,)
            )

    def out_grads():
        out_rows = out_own.shape[0]
        for start in range(0, model, model // 2):
            span = slice(start, start + model // 2)
            value = dot_l(long[:, :wide], tall[:, span])
            first, second = value[:out_rows], value[out_rows:]
            out_own[:, span] = jnp.where(place.y == 0, first, second)
            out_send[:, span] = jnp.where(place.y == 0, second, first).astype(BF16)

    for copy in loads:
        copy.start()
    place.enter(True)
    reduce.begin()
    for copy in up_copies:
        copy.start()
    terms[...] = jnp.zeros_like(terms)
    terms[0:1, :] = jnp.sum(first_terms[...], axis=0, keepdims=True)
    terms[1:2, :] = jnp.sum(second_terms[...], axis=0, keepdims=True)
    send_gains(0)
    for copy in loads:
        copy.wait()
    small_grads(0)
    reduce.pass_x(0)
    for z in range(1, ZS):
        small_grads(z)
    for copy in later_loads:
        copy.start()
    over_core.begin()
    query.begin()
    add_gains(0)
    over_core.add()
    over_x.begin()
    for m in range(1, reduce.micro):
        reduce.pass_x(m)
    add_gains(1)
    for copy in later_loads:
        copy.wait()
    out_grads()
    over_out.start()
    reduce.sums(0)
    over_x.add()
    over_y.begin()
    query.add()
    for step in (1, 3, 2, 0):
        z_copy(step, 0).start()
    add_gains(2)
    for m in range(1, reduce.micro):
        reduce.sums(m)
    over_y.add()
    for step in (1, 3, 2, 0):
        for piece in (1, 2):
            z_copy(step, piece).start()
    add_gains(3)
    gains_out[...] = terms[...]
    for m in range(reduce.micro):
        reduce.finish(m)

        def finish(span, m=m):
            output[m, span, :] = (middle[m, span, :] + reduce.total[m, span, :]).astype(BF16)

        by_rows(reduce.rows, finish)
    over_out.wait()

    def add_out(span):
        out_out[span, :] = out_own[span, :] + out_in[span, :].astype(F32)

    by_rows(out_own.shape[0], add_out)
    reduce.drain()
    for copy in up_copies:
        copy.wait()
    for step in range(ZS):
        for piece in range(3):
            z_copy(step, piece).wait()


def gate_up_grads_kernel(rows, both_grad, gate_out, up_out):
    value = dot_l(rows[...], both_grad[...]).astype(BF16)
    width = both_grad.shape[1] // 2
    gate_out[0] = value[:, :width].reshape(gate_out.shape[1:])
    up_out[0] = value[:, width:].reshape(up_out.shape[1:])


def gate_up_grads(rows, both_grad, model_rows):
    count, model = rows.shape
    width = both_grad.shape[1] // 2
    block = pl.BlockSpec((1, YS, model_rows, width), lambda z: (z, 0, 0, 0))
    return pl.pallas_call(
        gate_up_grads_kernel,
        grid=(ZS,),
        in_specs=[
            pl.BlockSpec((count, model // ZS), lambda z: (0, z)),
            pl.BlockSpec((count, 2 * width), lambda z: (0, 0)),
        ],
        out_specs=[block, block],
        out_shape=[jax.ShapeDtypeStruct((ZS, YS, model_rows, width), BF16)] * 2,
        compiler_params=pltpu.CompilerParams(vmem_limit_bytes=60 << 20),
        cost_estimate=pl.CostEstimate(
            flops=4 * count * model * width, bytes_accessed=12 * model * width, transcendentals=0
        ),
    )(rows, both_grad)


def down_grads_kernel(hidden, down_grad, down_out, small_out):
    value = dot_l(hidden[...], down_grad[...])
    down_out[...] = value
    small_out[...] = value.astype(BF16)


def down_grads(hidden, down_grad):
    count, model = down_grad.shape
    width = hidden.shape[1]
    tile = model // ZS
    return pl.pallas_call(
        down_grads_kernel,
        grid=(ZS,),
        in_specs=[
            pl.BlockSpec((count, width), lambda z: (0, 0)),
            pl.BlockSpec((count, tile), lambda z: (0, z)),
        ],
        out_specs=[pl.BlockSpec((width, tile), lambda z: (0, z))] * 2,
        out_shape=[jax.ShapeDtypeStruct((width, model), F32), jax.ShapeDtypeStruct((width, model), BF16)],
        compiler_params=pltpu.CompilerParams(vmem_limit_bytes=60 << 20),
        cost_estimate=pl.CostEstimate(
            flops=2 * count * model * width, bytes_accessed=10 * model * width, transcendentals=0
        ),
    )(hidden, down_grad)


def widen_kernel(first, second, own, other, kv, query, weight_out, down_out, kv_out, query_out):
    step = pl.program_id(0)
    pl.when(step < ZS)(lambda: weight_out.__setitem__(..., first[...].astype(F32)))
    pl.when(step >= ZS)(lambda: weight_out.__setitem__(..., second[...].astype(F32)))
    down_out[...] = own[0] + other[...].astype(F32)
    kv_out[...] = kv[...].astype(F32)
    query_out[...] = query[...].astype(F32)


def widen(first, second, own, other, kv, query, y):
    steps = 2 * ZS
    rows, width = first.shape[0], first.shape[1] // ZS
    down_rows, model = other.shape
    down_step = down_rows // ZS

    def block(*dims):
        return pl.BlockSpec(dims, lambda i, y: (i // 2,) + (0,) * (len(dims) - 1))

    small = [(value.shape[0] // ZS, value.shape[1]) for value in (kv, query)]
    return pl.pallas_call(
        lambda y, *refs: widen_kernel(*refs),
        grid_spec=pltpu.PrefetchScalarGridSpec(
            num_scalar_prefetch=1,
            grid=(steps,),
            in_specs=[
                pl.BlockSpec((rows, width), lambda i, y: (0, jnp.minimum(i, ZS - 1))),
                pl.BlockSpec((rows, width), lambda i, y: (0, jnp.maximum(i - ZS, 0))),
                pl.BlockSpec((1, down_step, model), lambda i, y: (y[0], i // 2, 0)),
                block(down_step, model),
                block(*small[0]),
                block(*small[1]),
            ],
            out_specs=[
                pl.BlockSpec((rows, width), lambda i, y: (0, i)),
                block(down_step, model),
                block(*small[0]),
                block(*small[1]),
            ],
        ),
        out_shape=[
            jax.ShapeDtypeStruct((rows, steps * width), F32),
            jax.ShapeDtypeStruct(other.shape, F32),
            jax.ShapeDtypeStruct(kv.shape, F32),
            jax.ShapeDtypeStruct(query.shape, F32),
        ],
        compiler_params=pltpu.CompilerParams(vmem_limit_bytes=60 << 20),
        cost_estimate=pl.CostEstimate(flops=0, bytes_accessed=12 * rows * steps * width, transcendentals=0),
    )(jnp.full((1,), y, jnp.int32), first, second, own, other, kv, query)


def connect(kernel, operands, spaces, out_shapes, out_spaces, scratch, number, seconds):
    return pl.pallas_call(
        kernel,
        in_specs=spaces,
        out_specs=out_spaces,
        out_shape=out_shapes,
        scratch_shapes=scratch,
        compiler_params=pltpu.CompilerParams(
            collective_id=number, has_side_effects=True, vmem_limit_bytes=60 << 20
        ),
        cost_estimate=pl.CostEstimate(flops=0, bytes_accessed=int(seconds * 3e12), transcendentals=0),
    )(*operands)


def fast_device(
    tokens,
    cotangent,
    gain_attn,
    gain_mlp,
    w_kv,
    w_query,
    w_out,
    w_gate_up,
    w_down,
    att_routes,
    att_gates,
    mlp_routes,
    mlp_gates,
    blocks,
):
    group, owner = lax.axis_index("group"), lax.axis_index("expert")
    y = group % YS
    x, core = owner // CS, owner % CS
    micro, local, model = tokens.shape
    wide = w_query.shape[2] // ZS
    hidden_width = w_gate_up.shape[2] // (2 * ZS)
    kv_rows = w_kv.shape[0]
    model_rows = w_query.shape[1]

    def own_rows(table):
        return lax.dynamic_slice_in_dim(table, owner * local, local, 0).astype(F32)

    lines = []
    for m in range(micro):
        lines += [own_rows(att_routes[m]), att_gates[m], own_rows(mlp_routes[m]), mlp_gates[m]]
        lines += [own_rows(blocks[m, 0][:, None])]
    table = jnp.concatenate(lines, axis=1)
    table = jnp.pad(table, ((0, 0), (0, -table.shape[1] % HDIM)))[None]

    positions = (
        (x ^ jnp.arange(XS)[None, :, None]) * CS + (core ^ jnp.arange(CS)[:, None, None])
    ) * local + jnp.arange(local)[None, None, :]
    cosine, sine = angles(positions.reshape(-1))
    cosine = jnp.concatenate([cosine, cosine], axis=1)
    sine = jnp.concatenate([-sine, sine], axis=1)

    shape = (micro, local, model)
    everyone = (micro, ZS, CS, XS, local, model)
    seqs = micro * ZS
    first_gain, second_gain = gain_attn[None], gain_mlp[None]
    tall = jax.ShapeDtypeStruct(shape, F32)
    short = jax.ShapeDtypeStruct(shape, BF16)
    gathered = jax.ShapeDtypeStruct(everyone, BF16)
    terms = jax.ShapeDtypeStruct((STEP, model), F32)
    own_buffer = pltpu.VMEM(shape, BF16)

    def kept(width, rows=SEQ):
        return jax.ShapeDtypeStruct((seqs, rows, width), BF16)

    def weight(*dims):
        return jax.ShapeDtypeStruct(dims, BF16)

    marks = (ZS, CS, XS) + table.shape[1:]
    (
        normed_two,
        middle,
        normed,
        cotangents,
        table,
        turned_qkv,
        attended,
        qkv_weight,
        out_weight,
        gate_up_weight,
        down_weight,
    ) = connect(
        functools.partial(attention_kernel, (wide, kv_rows, model_rows, w_out.shape[1], w_down.shape[1])),
        [
            tokens,
            cotangent,
            first_gain,
            second_gain,
            table,
            cosine,
            sine,
            w_kv,
            w_query,
            w_out,
            w_gate_up,
            w_down,
        ],
        [VMEM] * 7 + [ANY] * 5,
        [
            short,
            tall,
            gathered,
            gathered,
            jax.ShapeDtypeStruct((1,) + marks, F32),
            kept(3 * wide),
            kept(wide),
            weight(model, 3 * wide),
            weight(wide, model),
            weight(2, model, hidden_width),
            weight(hidden_width, model),
        ],
        [VMEM, VMEM] + [ANY] * 9,
        [own_buffer]
        + Gather.scratch(micro)
        + Gather.scratch(micro)
        + Gather.scratch(1)
        + PieceReduce.scratch(*shape)
        + Spread.scratch(2, 3)
        + Spread.scratch(1, 1)
        + Spread.scratch(2, 1)
        + Share.scratch(1)
        + Share.scratch(1)
        + [
            pltpu.VMEM((CS, XS, local, model), BF16),
            pltpu.VMEM((SEQ, 3 * wide), BF16),
            pltpu.VMEM((SEQ, wide), BF16),
            pltpu.VMEM(marks, F32),
            pltpu.VMEM((model, 3 * wide), BF16),
            pltpu.VMEM((wide, model), BF16),
            DMA((CS, XS)),
            DMA((2,)),
            DMA((3,)),
        ],
        1,
        250e-6,
    )
    table = table[0]
    part = table[..., : KINDS * micro].reshape(ZS, SEQ, micro, KINDS).transpose(2, 0, 1, 3)
    part = part.reshape(seqs, SEQ, KINDS)
    hit = jnp.any(part[..., 4:6] == owner, axis=-1)
    mlp_weight = jnp.sum(jnp.where(part[..., 4:6] == owner, part[..., 6:8], 0.0), axis=-1)
    before_mask = jnp.arange(SEQ)[:, None] < jnp.arange(SEQ)[None, :]
    before = dot(hit.astype(BF16), before_mask.astype(BF16)).astype(jnp.int32)
    slots = jnp.arange(XS * CS * CAP + -XS * CS * CAP % STEP)
    chosen = hit[:, None, :] & (before[:, None, :] == slots[None, :, None])
    row_gate = jnp.sum(jnp.where(chosen, mlp_weight[:, None, :], 0.0), axis=2)
    select = chosen.astype(BF16)
    slot_count = select.shape[1]
    middle_rows, middle_grad, gain_second, rows_two, both_grad, hidden, down_grad, result_two, *_ = connect(
        mlp_kernel,
        [
            normed_two,
            gate_up_weight,
            down_weight,
            select,
            select.transpose(0, 2, 1),
            row_gate[:, :, None],
            cotangents,
            middle,
            cotangent,
            second_gain,
        ],
        [VMEM] + [ANY] * 2 + [VMEM] * 3 + [ANY] + [VMEM] * 3,
        [
            short,
            tall,
            terms,
            kept(model, slot_count),
            kept(2 * hidden_width, slot_count),
            kept(hidden_width, slot_count),
            kept(model, slot_count),
            kept(model),
            gathered,
        ],
        [VMEM, VMEM, VMEM] + [ANY] * 6,
        Gather.scratch(micro)
        + PieceReduce.scratch(*shape)
        + [
            pltpu.VMEM((CS, XS, local, model), BF16),
            pltpu.VMEM((CS, XS, local, model), BF16),
            pltpu.VMEM((slot_count, model), BF16),
            pltpu.VMEM((slot_count, model), BF16),
            pltpu.VMEM((slot_count, hidden_width), BF16),
            pltpu.VMEM((slot_count, 2 * hidden_width), BF16),
            pltpu.VMEM((SEQ, model), BF16),
            pltpu.VMEM((model, hidden_width), BF16),
            pltpu.VMEM((model, hidden_width), BF16),
            pltpu.VMEM((hidden_width, model), BF16),
            DMA((2, CS, XS)),
            DMA((5,)),
            DMA((3,)),
        ],
        5,
        150e-6,
    )
    rows_two, both_grad, hidden, down_grad = [
        value.reshape(-1, value.shape[2]) for value in (rows_two, both_grad, hidden, down_grad)
    ]
    result_two = result_two.reshape(everyone)

    grad_down, down_small = [value.reshape(YS, -1, model) for value in down_grads(hidden, down_grad)]
    down_small = take(down_small, 1 - y, 0)
    rows_two, down_small = lax.optimization_barrier((rows_two, down_small))
    down_small = y_move(down_small)
    gate_grad, up_grad = gate_up_grads(rows_two, both_grad, model_rows)
    input_grad, gain_first, result_grad, qkv_grad, gate_grad, up_grad, _ = connect(
        attend_back_kernel,
        [
            middle_rows,
            qkv_weight,
            out_weight,
            table,
            cosine,
            sine,
            turned_qkv,
            tokens,
            middle_grad,
            first_gain,
            gate_grad,
            up_grad,
        ],
        [VMEM] + [ANY] * 2 + [VMEM] * 3 + [ANY] + [VMEM] * 3 + [ANY] * 2,
        [
            short,
            terms,
            kept(model),
            kept(3 * wide),
            jax.ShapeDtypeStruct((model_rows, ZS * hidden_width), BF16),
            jax.ShapeDtypeStruct((ZS, model_rows, hidden_width), BF16),
            gathered,
        ],
        [VMEM, VMEM] + [ANY] * 5,
        Gather.scratch(micro)
        + PieceReduce.scratch(*shape)
        + [
            pltpu.VMEM((CS, XS, local, model), BF16),
            pltpu.VMEM((SEQ, 3 * wide), BF16),
            pltpu.VMEM((SEQ, model), BF16),
            pltpu.VMEM((SEQ, 3 * wide), BF16),
            DMA((CS + 1, XS)),
            DMA((2,)),
            pltpu.VMEM((2 * ZS, model_rows, hidden_width), BF16),
            pltpu.VMEM((2 * ZS, model_rows, hidden_width), BF16),
            DMA((2 * ZS,)),
            DMA((2 * ZS,)),
            DMA((2 * ZS,)),
            DMA((ZS,)),
            DMA((ZS,)),
            DMA((2 * ZS,)),
            pltpu.VMEM((model, 3 * wide), BF16),
            pltpu.VMEM((wide, model), BF16),
            DMA((2,)),
        ],
        3,
        150e-6,
    )
    rows = seqs * SEQ
    output, gains, query_grad, kv_grad, grad_out, up_grad = connect(
        last_kernel,
        [
            result_two,
            middle,
            gain_first,
            gain_second,
            normed.reshape(rows, model),
            qkv_grad.reshape(rows, 3 * wide),
            attended.reshape(rows, wide),
            result_grad.reshape(rows, model),
            up_grad,
        ],
        [ANY, VMEM, VMEM, VMEM] + [ANY] * 5,
        [
            short,
            jax.ShapeDtypeStruct((8, model), F32),
            jax.ShapeDtypeStruct((model_rows, ZS * wide), BF16),
            jax.ShapeDtypeStruct((kv_rows, 2 * ZS * wide), BF16),
            jax.ShapeDtypeStruct(w_out.shape[1:], F32),
            weight(model_rows, ZS * hidden_width),
        ],
        [VMEM, VMEM, ANY, ANY, VMEM, ANY],
        Reduce.scratch(*shape)
        + [pltpu.VMEM((rows, model), BF16), pltpu.VMEM((rows, 3 * wide), BF16), DMA((4,))]
        + [pltpu.VMEM((ZS, YS, model_rows, wide), BF16), pltpu.VMEM((ZS, model_rows, wide), BF16)]
        + [
            pltpu.VMEM((ZS * YS * XS, CS, kv_rows, 2 * wide), BF16),
            pltpu.VMEM((ZS * YS * XS, kv_rows, 2 * wide), BF16),
            pltpu.VMEM((ZS * YS, kv_rows, 2 * wide), BF16),
            pltpu.VMEM((ZS, kv_rows, 2 * wide), BF16),
        ]
        + [pltpu.VMEM(w_out.shape[1:], kind) for kind in (F32, BF16, BF16)]
        + [DMA((5,)), DMA((5,)), DMA((ZS, 3)), DMA((ZS, 3)), DMA((3,))]
        + [pltpu.VMEM((8, model), F32), pltpu.VMEM((6, 8, model), F32), DMA((6,)), DMA((6,))]
        + [DMA((ZS,)), DMA((ZS,)), DMA],
        4,
        100e-6,
    )
    devices = ZS * YS * XS * CS
    gains = take(gains[:2].reshape(2, devices, model // devices), group * XS * CS + owner, 1)
    grad_gate_up, grad_down, kv_grad, query_grad = widen(
        gate_grad, up_grad, grad_down, down_small, kv_grad, query_grad, y
    )
    return (
        output,
        input_grad,
        gains[0],
        gains[1],
        kv_grad,
        query_grad[None],
        grad_out[None],
        grad_gate_up[None],
        grad_down[None],
    )


def solution(mesh):
    in_specs = (
        P(None, ("group", "expert"), None),
        P(None, ("group", "expert"), None),
        P(),
        P(),
        P(("group", "expert"), None),
        P("expert", "group", None),
        P("expert", "group", None),
        P("expert", "group", None),
        P("expert", "group", None),
        P(None, "group", None),
        P(None, ("group", "expert"), None),
        P(None, "group", None),
        P(None, ("group", "expert"), None),
        P(None, "group", None),
    )
    out_specs = (
        P(None, ("group", "expert"), None),
        P(None, ("group", "expert"), None),
        P(("group", "expert")),
        P(("group", "expert")),
        P(("group", "expert"), None),
        P("expert", "group", None),
        P("expert", "group", None),
        P("expert", "group", None),
        P("expert", "group", None),
    )
    body = fast_device if fits(mesh) else on_device
    return jax.shard_map(
        body, mesh=mesh, in_specs=in_specs, out_specs=out_specs, check_vma=False
    )
```

```python
import functools

import jax
import jax.numpy as jnp
from jax import lax
from jax.experimental import pallas as pl
from jax.experimental.pallas import tpu as pltpu
from jax.sharding import PartitionSpec as P

HEADS = 16
HDIM = 128
CAP = 50


EPS = 1e-06
HIGH = lax.Precision.HIGHEST


def angles(positions):
    half = HDIM // 2
    freq = 10000.0 ** (-jnp.arange(half, dtype=jnp.float32) / half)
    turn = positions.astype(jnp.float32)[:, None] * freq[None, :]
    return (jnp.cos(turn), jnp.sin(turn))


def rotate(values, cosine, sine):
    count = values.shape[0]
    split = values.reshape(count, HEADS, 2, HDIM // 2)
    first = split[:, :, 0]
    second = split[:, :, 1]
    cosine = cosine[:, None, :]
    sine = sine[:, None, :]
    turned = jnp.stack([first * cosine - second * sine, second * cosine + first * sine], axis=2)
    return turned.reshape(count, HEADS * HDIM)


def routing(routes, gates, block_ids, owner, experts):
    local = routes.shape[0] // experts
    per = routes.reshape(experts, local, routes.shape[1])
    flat = per.reshape(experts, -1)
    ids = jnp.arange(experts, dtype=jnp.int32)
    onehot = (flat[:, :, None] == ids[None, None, :]).astype(jnp.int32)
    before = jnp.cumsum(onehot, axis=1) - onehot
    slots = jnp.sum(before * onehot, axis=2).reshape(per.shape)
    places = jnp.arange(CAP, dtype=jnp.int32)
    own_ids = lax.dynamic_index_in_dim(per, owner, 0, keepdims=False)
    own_slots = lax.dynamic_index_in_dim(slots, owner, 0, keepdims=False)
    sent = (
        (own_ids[None, None] == ids[:, None, None, None])
        & (own_slots[None, None] == places[None, :, None, None])
    ).astype(jnp.float32)
    pick = jnp.sum(sent, axis=3)
    weighted = jnp.sum(sent * gates[None, None], axis=3)
    arrived = ((per == owner)[:, None] & (slots[:, None] == places[None, :, None, None])).astype(
        jnp.int32
    )
    length = experts * local
    spots = jnp.arange(length, dtype=jnp.int32).reshape(experts, 1, local, 1)
    marks = block_ids.reshape(experts, 1, local, 1)
    valid = jnp.sum(arrived, axis=(2, 3)).reshape(-1)
    row_pos = jnp.sum(arrived * spots, axis=(2, 3)).reshape(-1)
    row_block = jnp.sum(arrived * marks, axis=(2, 3)).reshape(-1) + (1 - valid) * length
    return (pick, weighted, row_pos, row_block)


def score_block(queries, keys, row_block, key_block):
    count = queries.shape[0]
    raw = jnp.einsum(
        "rhd,khd->hrk",
        queries.reshape(count, HEADS, HDIM),
        keys.reshape(keys.shape[0], HEADS, HDIM),
        preferred_element_type=jnp.float32,
    )
    visible = key_block[None, None, :] <= row_block[None, :, None]
    return jnp.where(visible, raw * HDIM ** (-0.5), -1e30)


def spread(pick, normed):
    return jnp.einsum(
        "ect,td->ecd", pick.astype(jnp.bfloat16), normed, preferred_element_type=jnp.float32
    ).astype(jnp.bfloat16)


def collect(weights, arrived):
    return jnp.einsum("ect,ecd->td", weights, arrived.astype(jnp.float32), precision=HIGH)


def joined_rows(store, chosen, name):
    return jnp.concatenate([store[name][index] for index in chosen], axis=0)


def expert_reduce(store, chosen):
    pairs = (
        ("rows", "query_grad"),
        ("attended", "result_grad"),
        ("rows_two", "both_grad"),
        ("hidden", "down_grad"),
    )
    groups = lax.axis_size("group")
    results = []
    for left_name, right_name in pairs:
        left = joined_rows(store, chosen, left_name)
        right = joined_rows(store, chosen, right_name)

        def term(start, count, left=left, right=right):
            return jnp.einsum("rd,rf->df", left, right, preferred_element_type=jnp.float32)

        shard = lax.psum_scatter(
            term(jnp.int32(0), lax.axis_size("group") * (left.shape[1] // groups)).astype(
                jnp.bfloat16
            ),
            "group",
            scatter_dimension=0,
            tiled=True,
        ).astype(jnp.float32)
        results.append(shard[None])
    return tuple(results)


def reduce_all(store, chosen):
    expert_parts = expert_reduce(store, chosen)
    shared_term = jnp.einsum(
        "td,tf->df",
        joined_rows(store, chosen, "normed"),
        joined_rows(store, chosen, "mixed_grad"),
        preferred_element_type=jnp.float32,
    )
    gain_first = jnp.sum(joined_rows(store, chosen, "gain_first"), axis=0)
    gain_second = jnp.sum(joined_rows(store, chosen, "gain_second"), axis=0)
    shared_parts = (
        lax.psum_scatter(shared_term, ("group", "expert"), scatter_dimension=0, tiled=True),
        lax.psum_scatter(gain_first, ("group", "expert"), scatter_dimension=0, tiled=True),
        lax.psum_scatter(gain_second, ("group", "expert"), scatter_dimension=0, tiled=True),
    )
    return tuple(expert_parts) + tuple(shared_parts)


def on_device(
    tokens,
    cotangent,
    gain_attn,
    gain_mlp,
    w_kv,
    w_query,
    w_out,
    w_gate_up,
    w_down,
    att_routes,
    att_gates,
    mlp_routes,
    mlp_gates,
    blocks,
):
    experts = lax.axis_size("expert")
    owner = lax.axis_index("expert")
    shared_full = lax.all_gather(w_kv, ("group", "expert"), axis=0, tiled=True)
    gathered = (
        lax.all_gather(w_query, "group", axis=1, tiled=True),
        lax.all_gather(w_out, "group", axis=1, tiled=True),
        lax.all_gather(w_gate_up, "group", axis=1, tiled=True),
        lax.all_gather(w_down, "group", axis=1, tiled=True),
    )
    query_full = gathered[0][0]
    output_full = gathered[1][0]
    gate_up_full = gathered[2][0]
    down_full = gathered[3][0]
    micro = tokens.shape[0]
    local = tokens.shape[1]
    model = tokens.shape[2]
    length = local * experts
    width = HEADS * HDIM
    hidden_width = gate_up_full.shape[1] // 2
    own_cos, own_sin = angles(owner * local + jnp.arange(local, dtype=jnp.int32))
    names = (
        "rows",
        "query_grad",
        "attended",
        "result_grad",
        "rows_two",
        "both_grad",
        "hidden",
        "down_grad",
        "normed",
        "mixed_grad",
        "gain_first",
        "gain_second",
    )
    store = {name: [] for name in names}
    outputs = []
    input_grads = []
    for index in range(micro):
        inputs = tokens[index].astype(jnp.float32)
        block_ids = blocks[index, 0]
        att_pick, att_weight, row_pos, row_block = routing(
            att_routes[index], att_gates[index], block_ids, owner, experts
        )
        mlp_pick, mlp_weight, unused_pos, unused_block = routing(
            mlp_routes[index], mlp_gates[index], block_ids, owner, experts
        )
        scale = lax.rsqrt(jnp.mean(inputs * inputs, axis=1, keepdims=True) + EPS)
        normed = (inputs * scale * gain_attn).astype(jnp.bfloat16)
        mixed = jnp.dot(normed, shared_full, preferred_element_type=jnp.float32)
        keys_here = rotate(mixed[:, :width], own_cos, own_sin).astype(jnp.bfloat16)
        local_kv = jnp.concatenate([keys_here, mixed[:, width:].astype(jnp.bfloat16)], axis=1)
        sequence_kv = lax.all_gather(local_kv, "expert", axis=0, tiled=True)
        keys = sequence_kv[:, :width]
        values = sequence_kv[:, width:].reshape(length, HEADS, HDIM)
        rows = lax.all_to_all(
            spread(att_pick, normed), "expert", split_axis=0, concat_axis=0, tiled=True
        ).reshape(-1, model)
        row_cos, row_sin = angles(row_pos)
        queries = rotate(
            jnp.dot(rows, query_full, preferred_element_type=jnp.float32), row_cos, row_sin
        ).astype(jnp.bfloat16)
        scores = score_block(queries, keys, row_block, block_ids)
        top = jnp.max(scores, axis=2, keepdims=True)
        powers = jnp.exp(scores - top)
        total = jnp.sum(powers, axis=2, keepdims=True)
        log_total = top + jnp.log(total)
        probs = (powers / total).astype(jnp.bfloat16)
        attended = jnp.einsum("hrk,khd->rhd", probs, values, preferred_element_type=jnp.float32)
        attended = attended.reshape(-1, width).astype(jnp.bfloat16)
        result = jnp.dot(attended, output_full, preferred_element_type=jnp.float32).astype(
            jnp.bfloat16
        )
        back = lax.all_to_all(
            result.reshape(experts, CAP, model), "expert", split_axis=0, concat_axis=0, tiled=True
        )
        middle = inputs + collect(att_weight, back)
        scale_two = lax.rsqrt(jnp.mean(middle * middle, axis=1, keepdims=True) + EPS)
        normed_two = (middle * scale_two * gain_mlp).astype(jnp.bfloat16)
        rows_two = lax.all_to_all(
            spread(mlp_pick, normed_two), "expert", split_axis=0, concat_axis=0, tiled=True
        ).reshape(-1, model)
        both = jnp.dot(rows_two, gate_up_full, preferred_element_type=jnp.float32)
        gate = both[:, :hidden_width]
        up = both[:, hidden_width:]
        sigma = 1.0 / (1.0 + jnp.exp(-gate))
        hidden = (gate * sigma * up).astype(jnp.bfloat16)
        result_two = jnp.dot(hidden, down_full, preferred_element_type=jnp.float32).astype(
            jnp.bfloat16
        )
        back_two = lax.all_to_all(
            result_two.reshape(experts, CAP, model),
            "expert",
            split_axis=0,
            concat_axis=0,
            tiled=True,
        )
        final = middle + collect(mlp_weight, back_two)
        outputs.append(final.astype(jnp.bfloat16))
        upstream = cotangent[index].astype(jnp.float32)
        outgoing = jnp.einsum("ect,td->ecd", mlp_weight, upstream, precision=HIGH).astype(
            jnp.bfloat16
        )
        down_grad = lax.all_to_all(
            outgoing, "expert", split_axis=0, concat_axis=0, tiled=True
        ).reshape(-1, model)
        hidden_grad = jnp.einsum(
            "rd,fd->rf", down_grad, down_full, preferred_element_type=jnp.float32
        )
        slope = sigma * (1.0 + gate * (1.0 - sigma))
        both_grad = jnp.concatenate(
            [hidden_grad * up * slope, hidden_grad * gate * sigma], axis=1
        ).astype(jnp.bfloat16)
        row_grad_two = jnp.einsum(
            "rf,df->rd", both_grad, gate_up_full, preferred_element_type=jnp.float32
        ).astype(jnp.bfloat16)
        returned_two = lax.all_to_all(
            row_grad_two.reshape(experts, CAP, model),
            "expert",
            split_axis=0,
            concat_axis=0,
            tiled=True,
        )
        normed_two_grad = collect(mlp_pick, returned_two)
        scaled_two = normed_two_grad * gain_mlp
        gain_second = jnp.sum(normed_two_grad * middle * scale_two, axis=0, keepdims=True)
        middle_grad = (
            upstream
            + scale_two * scaled_two
            - middle * scale_two**3 * jnp.mean(scaled_two * middle, axis=1, keepdims=True)
        )
        outgoing_att = jnp.einsum("ect,td->ecd", att_weight, middle_grad, precision=HIGH).astype(
            jnp.bfloat16
        )
        result_grad = lax.all_to_all(
            outgoing_att, "expert", split_axis=0, concat_axis=0, tiled=True
        ).reshape(-1, model)
        attended_grad = jnp.einsum(
            "rd,fd->rf", result_grad, output_full, preferred_element_type=jnp.float32
        ).astype(jnp.bfloat16)
        again = jnp.exp(score_block(queries, keys, row_block, block_ids) - log_total)
        heads_grad = attended_grad.reshape(-1, HEADS, HDIM)
        value_grad = jnp.einsum(
            "hrk,rhd->khd",
            again.astype(jnp.bfloat16),
            heads_grad,
            preferred_element_type=jnp.float32,
        )
        prob_grad = jnp.einsum(
            "rhd,khd->hrk", heads_grad, values, preferred_element_type=jnp.float32
        )
        inner = jnp.sum(again * prob_grad, axis=2, keepdims=True)
        raw_grad = (again * (prob_grad - inner) * HDIM ** (-0.5)).astype(jnp.bfloat16)
        query_grad = jnp.einsum(
            "hrk,khd->rhd",
            raw_grad,
            keys.reshape(length, HEADS, HDIM),
            preferred_element_type=jnp.float32,
        ).reshape(-1, width)
        query_grad = rotate(query_grad, row_cos, -row_sin).astype(jnp.bfloat16)
        key_grad = jnp.einsum(
            "hrk,rhd->khd",
            raw_grad,
            queries.reshape(-1, HEADS, HDIM),
            preferred_element_type=jnp.float32,
        ).reshape(length, width)
        row_grad = jnp.einsum(
            "rf,df->rd", query_grad, query_full, preferred_element_type=jnp.float32
        ).astype(jnp.bfloat16)
        returned = lax.all_to_all(
            row_grad.reshape(experts, CAP, model), "expert", split_axis=0, concat_axis=0, tiled=True
        )
        kv_grad = lax.psum_scatter(
            jnp.concatenate([key_grad, value_grad.reshape(length, width)], axis=1).astype(
                jnp.bfloat16
            ),
            "expert",
            scatter_dimension=0,
            tiled=True,
        ).astype(jnp.float32)
        mixed_grad = jnp.concatenate(
            [rotate(kv_grad[:, :width], own_cos, -own_sin), kv_grad[:, width:]], axis=1
        ).astype(jnp.bfloat16)
        normed_grad = collect(att_pick, returned) + jnp.einsum(
            "tf,df->td", mixed_grad, shared_full, preferred_element_type=jnp.float32
        )
        scaled = normed_grad * gain_attn
        gain_first = jnp.sum(normed_grad * inputs * scale, axis=0, keepdims=True)
        input_grad = (
            middle_grad
            + scale * scaled
            - inputs * scale**3 * jnp.mean(scaled * inputs, axis=1, keepdims=True)
        )
        input_grads.append(input_grad.astype(jnp.bfloat16))
        kept = (
            rows,
            query_grad,
            attended,
            result_grad,
            rows_two,
            both_grad,
            hidden,
            down_grad,
            normed,
            mixed_grad,
            gain_first,
            gain_second,
        )
        for name, value in zip(names, kept):
            store[name].append(value)
    reduced = reduce_all(store, list(range(micro)))
    grad_query, grad_out, grad_gate_up, grad_down, grad_kv, grad_gain_attn, grad_gain_mlp = reduced
    return (
        jnp.stack(outputs, axis=0),
        jnp.stack(input_grads, axis=0),
        grad_gain_attn,
        grad_gain_mlp,
        grad_kv,
        grad_query,
        grad_out,
        grad_gate_up,
        grad_down,
    )


ZS, YS, XS, CS = 4, 2, 2, 2
SEQ = 320
MICRO = 2
KINDS = 9
F32 = jnp.float32
BF16 = jnp.bfloat16


def fits(mesh):
    return mesh.shape["group"] == ZS * YS and mesh.shape["expert"] == XS * CS


def group_move(value, move):
    pairs = []
    for z in range(ZS):
        for y in range(YS):
            to_z, to_y = move(z, y)
            pairs.append((z * YS + y, to_z * YS + to_y))
    return lax.ppermute(value, "group", pairs)


def z_move(value, step):
    return group_move(value, lambda z, y: ((z + step) % ZS, y))


def y_move(value):
    return group_move(value, lambda z, y: (z, 1 - y))


def x_move(value):
    return lax.ppermute(value, "expert", [(x * CS + c, (1 - x) * CS + c) for x in range(XS) for c in range(CS)])


def c_move(value):
    return lax.ppermute(value, "expert", [(x * CS + c, x * CS + 1 - c) for x in range(XS) for c in range(CS)])


def z_exchange(value):
    columns = [[z * YS + y for z in range(ZS)] for y in range(YS)]
    return lax.all_to_all(
        value, "group", split_axis=0, concat_axis=0, tiled=True, axis_index_groups=columns
    )


def gather_tokens(own):
    column = jnp.stack([own] + [z_move(own, -step) for step in range(1, ZS)], axis=0)
    plane = jnp.stack([column, x_move(column)], axis=1)
    plane = plane.reshape((ZS, XS * own.shape[0]) + own.shape[1:])
    return jnp.stack([plane, c_move(plane)], axis=0)


def reduce_tokens(other, mine):
    local = mine.shape[1] // XS
    total = mine.astype(F32) + c_move(other).astype(F32)
    arrived = x_move(total[:, local:].astype(BF16))
    total = total[:, :local] + arrived.astype(F32)
    result = total[0]
    for step in range(1, ZS):
        result = result + z_move(total[step].astype(BF16), step).astype(F32)
    return result


def merge(index, own, other, axis):
    return jnp.where(index == 0, jnp.stack([own, other], axis), jnp.stack([other, own], axis))


def take(value, index, axis):
    return lax.dynamic_index_in_dim(value, index, axis, keepdims=False)


def dot(left, right):
    return jnp.dot(left, right, preferred_element_type=F32)


def dot_t(left, right):
    return lax.dot_general(left, right, (((1,), (1,)), ((), ())), preferred_element_type=F32)


def dot_l(left, right):
    return lax.dot_general(left, right, (((0,), (0,)), ((), ())), preferred_element_type=F32)


def turned(value, cosine, sine):
    return value * cosine + pltpu.roll(value, HDIM // 2, 1) * sine


def masked_probs(query, key, row_block, key_block):
    scores = jnp.where(key_block <= row_block, dot_t(query, key) * HDIM ** (-0.5), -1e30)
    powers = jnp.exp(scores - jnp.max(scores, axis=1, keepdims=True))
    return powers / jnp.sum(powers, axis=1, keepdims=True)


MESH = pl.DeviceIdType.MESH
ORDER = (3, 1, 2, 0)
STEP = 16
DMA = pltpu.SemaphoreType.DMA
ANY = pl.BlockSpec(memory_space=pl.ANY)
VMEM = pl.BlockSpec(memory_space=pltpu.VMEM)


def by_rows(rows, body):
    def step(index, carry):
        body(pl.ds(pl.multiple_of(index * STEP, STEP), STEP))
        return carry

    lax.fori_loop(0, rows // STEP, step, 0)


class Place:
    def __init__(self):
        group, owner = lax.axis_index("group"), lax.axis_index("expert")
        self.z, self.y = lax.div(group, YS), lax.rem(group, YS)
        self.x, self.core = lax.div(owner, CS), lax.rem(owner, CS)
        self.group, self.owner = group, owner

        def device(z, y, x, core):
            return (z * YS + y, x * CS + core)

        self.x_peer = device(self.z, self.y, 1 - self.x, self.core)
        self.y_peer = device(self.z, 1 - self.y, self.x, self.core)
        self.core_peer = device(self.z, self.y, self.x, 1 - self.core)
        self.z_peers = [device(lax.rem(self.z + step, ZS), self.y, self.x, self.core) for step in range(ZS)]

    def enter(self, with_y):
        peers = [self.x_peer, self.core_peer] + self.z_peers[1:] + ([self.y_peer] if with_y else [])
        barrier = pltpu.get_barrier_semaphore()
        for peer in peers:
            pl.semaphore_signal(barrier, inc=1, device_id=peer, device_id_type=MESH)
        pl.semaphore_wait(barrier, len(peers))


def remote(src, dst, send, arrive, peer):
    return pltpu.make_async_remote_copy(
        src_ref=src, dst_ref=dst, send_sem=send, recv_sem=arrive, device_id=peer, device_id_type=MESH
    )


class Reduce:
    @staticmethod
    def scratch(micro, rows, model):
        return [
            pltpu.VMEM((micro, ZS, XS, rows, model), BF16),
            pltpu.VMEM((micro, ZS, XS, rows, model), BF16),
            pltpu.VMEM((micro, ZS, rows, model), BF16),
            pltpu.VMEM((micro, 2, ZS - 1, rows, model), BF16),
            pltpu.VMEM((micro, rows, model), F32),
            DMA((micro, ZS, XS)),
            DMA((micro, ZS, XS)),
            DMA((micro, ZS, XS)),
            DMA((micro, ZS)),
            DMA((micro, ZS)),
            DMA((micro, 2, ZS)),
            DMA((micro, 2, ZS)),
        ]

    def __init__(self, place, part, refs):
        self.place, self.part = place, part
        self.core_in, self.kept, self.x_in, self.z_in, self.total = [refs.pop(0) for _ in range(5)]
        self.sems = [refs.pop(0) for _ in range(7)]
        self.micro, self.rows = part.shape[0], part.shape[4]

    def core_copy(self, m, k, dx):
        send, arrive = self.sems[:2]
        return remote(
            self.part.at[m, k, 1, dx],
            self.core_in.at[m, k, dx],
            send.at[m, k, dx],
            arrive.at[m, k, dx],
            self.place.core_peer,
        )

    def kept_copy(self, m, k, dx):
        return pltpu.make_async_copy(
            self.part.at[m, k, 0, dx], self.kept.at[m, k, dx], self.sems[2].at[m, k, dx]
        )

    def x_copy(self, m, k):
        send, arrive = self.sems[3:5]
        return remote(
            self.core_in.at[m, k, 1], self.x_in.at[m, k], send.at[m, k], arrive.at[m, k], self.place.x_peer
        )

    def z_copy(self, m, down, far):
        send, arrive = self.sems[5:7]
        return remote(
            self.x_in.at[m, ZS - far if down else far],
            self.z_in.at[m, down, far - 1],
            send.at[m, down, far - 1],
            arrive.at[m, down, far - 1],
            self.place.z_peers[ZS - 1 if down else 1],
        )

    def begin(self):
        for m in range(self.micro):
            for dx in (1, 0):
                for k in ORDER:
                    self.core_copy(m, k, dx).start()
                    self.kept_copy(m, k, dx).start()

    def pass_x(self, m):
        for k in ORDER:
            self.core_copy(m, k, 1).wait_recv()
            self.kept_copy(m, k, 1).wait()

            def add(span, k=k):
                value = self.core_in[m, k, 1, span, :].astype(F32) + self.kept[m, k, 1, span, :].astype(F32)
                self.core_in[m, k, 1, span, :] = value.astype(BF16)

            by_rows(self.rows, add)
            self.x_copy(m, k).start()

    def z_unit(self, m, k):
        self.x_copy(m, k).wait_recv()
        self.core_copy(m, k, 0).wait_recv()
        self.kept_copy(m, k, 0).wait()

        def add(span):
            value = (
                self.x_in[m, k, span, :].astype(F32)
                + self.core_in[m, k, 0, span, :].astype(F32)
                + self.kept[m, k, 0, span, :].astype(F32)
            )
            if k:
                self.x_in[m, k, span, :] = value.astype(BF16)
            else:
                self.total[m, span, :] = value

        by_rows(self.rows, add)

    def beyond(self, down, far):
        return self.place.z >= far if down else self.place.z + far < ZS

    def chain(self, m, far):
        for down in (0, 1):

            def send(down=down):
                if far < ZS - 1:
                    pl.when(self.beyond(1 - down, 1))(functools.partial(self.join, m, down, far))
                self.z_copy(m, down, far).start()

            pl.when(self.beyond(down, far))(send)

    def join(self, m, down, far):
        self.z_copy(m, down, far + 1).wait_recv()
        place = ZS - far if down else far

        def add(span):
            value = self.x_in[m, place, span, :].astype(F32) + self.z_in[m, down, far, span, :].astype(F32)
            self.x_in[m, place, span, :] = value.astype(BF16)

        by_rows(self.rows, add)

    def finish(self, m):
        for down in (0, 1):

            def last(down=down):
                self.z_copy(m, down, 1).wait_recv()

                def add(span):
                    self.total[m, span, :] += self.z_in[m, down, 0, span, :].astype(F32)

                by_rows(self.rows, add)

            pl.when(self.beyond(1 - down, 1))(last)

    def sums(self, m):
        for turn, k in enumerate(ORDER):
            self.z_unit(m, k)
            if turn:
                self.chain(m, ZS - turn)

    def run(self):
        self.begin()
        for m in range(self.micro):
            self.pass_x(m)
        for m in range(self.micro):
            self.sums(m)

    def drain(self):
        for m in range(self.micro):
            for k in ORDER:
                for dx in range(XS):
                    self.core_copy(m, k, dx).wait_send()
                self.x_copy(m, k).wait_send()
            for down in (0, 1):
                for far in range(1, ZS):
                    pl.when(self.beyond(down, far))(self.z_copy(m, down, far).wait_send)


class Gather:
    @staticmethod
    def scratch(micro):
        return [
            DMA((micro,)),
            DMA((micro, ZS)),
            DMA((micro, ZS)),
            DMA((micro, ZS)),
            DMA((micro, ZS, XS)),
            DMA((micro, ZS, CS, XS)),
        ]

    def __init__(self, place, own, out, refs):
        self.place, self.own, self.out = place, own, out
        self.sems = [refs.pop(0) for _ in range(6)]
        self.micro = out.shape[0]

    def slot(self, m, k, dc, dx):
        return self.out.at[m, k, dc, dx]

    def local(self, m):
        return pltpu.make_async_copy(self.own.at[m], self.slot(m, 0, 0, 0), self.sems[0].at[m])

    def up(self, m, source, k):
        return remote(
            source, self.slot(m, k, 0, 0), self.sems[1].at[m, k], self.sems[5].at[m, k, 0, 0], self.place.z_peers[1]
        )

    def down(self, m, source, k):
        return remote(
            source,
            self.slot(m, k, 0, 0),
            self.sems[2].at[m, k],
            self.sems[5].at[m, k, 0, 0],
            self.place.z_peers[ZS - 1],
        )

    def over_x(self, m, source, k):
        return remote(
            source, self.slot(m, k, 0, 1), self.sems[3].at[m, k], self.sems[5].at[m, k, 0, 1], self.place.x_peer
        )

    def over_core(self, m, source, k, dx):
        return remote(
            source,
            self.slot(m, k, 1, dx),
            self.sems[4].at[m, k, dx],
            self.sems[5].at[m, k, 1, dx],
            self.place.core_peer,
        )

    def send_own(self, m):
        source, z = self.own.at[m], self.place.z
        pl.when(z < ZS - 1)(lambda: self.up(m, source, ZS - 1).start())
        pl.when(z > 0)(lambda: self.down(m, source, 1).start())
        self.over_x(m, source, 0).start()
        self.over_core(m, source, 0, 0).start()
        self.local(m).start()

    def pass_on(self, m, k):
        self.over_x(m, self.slot(m, k, 0, 0), k).start()
        self.over_core(m, self.slot(m, k, 0, 0), k, 0).start()

    def from_above(self, m, far):
        self.up(m, self.own.at[m], far).wait_recv()
        pl.when(self.place.z > 0)(lambda: self.down(m, self.slot(m, far, 0, 0), far + 1).start())
        self.pass_on(m, far)

    def from_below(self, m, far):
        self.up(m, self.own.at[m], ZS - far).wait_recv()
        source = self.slot(m, ZS - far, 0, 0)
        pl.when(self.place.z < ZS - 1)(lambda: self.up(m, source, ZS - far - 1).start())
        self.pass_on(m, ZS - far)

    def z_arrival(self, m, far):
        pl.when(self.place.z + far < ZS)(lambda: self.from_above(m, far))
        pl.when(self.place.z - far >= 0)(lambda: self.from_below(m, far))

    def x_arrival(self, m, k):
        self.over_x(m, self.own.at[m], k).wait_recv()
        self.over_core(m, self.slot(m, k, 0, 1), k, 1).start()

    def piece_arrival(self, m, k):
        for dx in range(XS):
            self.over_core(m, self.own.at[m], k, dx).wait_recv()

    def arrivals(self, m=0):
        for k in range(ZS):
            self.piece_arrival(m, k)
        self.local(m).wait()

    def z_round(self, far, chosen=None):
        for m in range(self.micro) if chosen is None else [chosen]:
            self.z_arrival(m, far)

    def x_round(self, far, chosen=None):
        for m in range(self.micro) if chosen is None else [chosen]:
            if far == 0:
                self.x_arrival(m, 0)
            else:
                pl.when(self.place.z + far < ZS)(lambda: self.x_arrival(m, far))
                pl.when(self.place.z - far >= 0)(lambda: self.x_arrival(m, ZS - far))

    def run(self):
        self.z_round(1)
        self.x_round(0)
        self.z_round(2)
        self.x_round(1)
        self.z_round(3)
        self.x_round(2)
        self.x_round(3)

    def drain(self, waited=False):
        z = self.place.z
        for m in range(self.micro):
            own = self.own.at[m]
            if not waited:
                self.arrivals(m)
            pl.when(z < ZS - 1)(lambda: self.up(m, own, ZS - 1).wait_send())
            pl.when(z > 0)(lambda: self.down(m, own, 1).wait_send())
            for far in range(1, ZS - 1):
                pl.when((z + far < ZS) & (z > 0))(lambda: self.down(m, own, far + 1).wait_send())
                pl.when((z - far >= 0) & (z < ZS - 1))(lambda: self.up(m, own, ZS - far - 1).wait_send())
            for k in range(ZS):
                self.over_x(m, own, k).wait_send()
                for dx in range(XS):
                    self.over_core(m, own, k, dx).wait_send()


class PieceReduce(Reduce):
    @staticmethod
    def scratch(micro, rows, model):
        return [
            pltpu.VMEM((micro, ZS, CS * XS * rows, model), BF16),
            pltpu.VMEM((micro, ZS, XS, rows, model), BF16),
            pltpu.VMEM((micro, ZS, rows, model), BF16),
            pltpu.VMEM((micro, 2, ZS - 1, rows, model), BF16),
            pltpu.VMEM((micro, rows, model), F32),
            DMA((micro, ZS, XS)),
            DMA((micro, ZS, XS)),
            DMA((micro, ZS)),
            DMA((micro, ZS)),
            DMA((micro, 2, ZS)),
            DMA((micro, 2, ZS)),
        ]

    def __init__(self, place, refs):
        self.place = place
        self.part, self.core_in, self.x_in, self.z_in, self.total = [refs.pop(0) for _ in range(5)]
        core_send, core_recv, x_send, x_recv, z_send, z_recv = [refs.pop(0) for _ in range(6)]
        self.sems = [core_send, core_recv, None, x_send, x_recv, z_send, z_recv]
        self.micro, self.rows = self.total.shape[0], self.total.shape[1]

    def unit(self, m, k, dc, dx):
        return self.part.at[m, k, pl.ds((dc * XS + dx) * self.rows, self.rows)]

    def core_copy(self, m, k, dx):
        send, arrive = self.sems[:2]
        return remote(
            self.unit(m, k, 1, dx),
            self.core_in.at[m, k, dx],
            send.at[m, k, dx],
            arrive.at[m, k, dx],
            self.place.core_peer,
        )

    def begin_piece(self, m, k):
        for dx in (1, 0):
            self.core_copy(m, k, dx).start()

    def x_piece(self, m, k):
        self.core_copy(m, k, 1).wait_recv()
        kept = self.unit(m, k, 0, 1)

        def add(span):
            value = self.core_in[m, k, 1, span, :].astype(F32) + kept[span, :].astype(F32)
            self.core_in[m, k, 1, span, :] = value.astype(BF16)

        by_rows(self.rows, add)
        self.x_copy(m, k).start()

    def z_piece(self, m, k):
        self.x_copy(m, k).wait_recv()
        self.core_copy(m, k, 0).wait_recv()
        kept = self.unit(m, k, 0, 0)

        def sum_of(span):
            return (
                self.x_in[m, k, span, :].astype(F32)
                + self.core_in[m, k, 0, span, :].astype(F32)
                + kept[span, :].astype(F32)
            )

        def away(span):
            self.x_in[m, k, span, :] = sum_of(span).astype(BF16)

        def here(span):
            self.total[m, span, :] = sum_of(span)

        pl.when(k != 0)(lambda: by_rows(self.rows, away))
        pl.when(k == 0)(lambda: by_rows(self.rows, here))

    def drain(self):
        for m in range(self.micro):
            for k in range(ZS):
                for dx in range(XS):
                    self.core_copy(m, k, dx).wait_send()
                self.x_copy(m, k).wait_send()
            for down in (0, 1):
                for far in range(1, ZS):
                    pl.when(self.beyond(down, far))(self.z_copy(m, down, far).wait_send)


def piece_of(place, index, outward=False):
    turn = lax.rem(index, ZS)
    if outward:
        turn = ZS - 1 - turn
    inner = turn + lax.div(turn, 2) * (5 - 2 * turn)
    last = lax.rem(ZS - turn, ZS)
    z = place.z
    return lax.div(index, ZS), jnp.where(z == 0, turn, jnp.where(z == ZS - 1, last, inner))


def run_pieces(place, reduce, piece, between, outward=False):
    pieces = reduce.micro * ZS

    def step(index, carry):
        @pl.when(index < pieces)
        def _():
            m, k = piece_of(place, index, outward)
            piece(index, m, k)
            reduce.begin_piece(m, k)

        between(index)

        @pl.when((index >= 1) & (index < pieces + 1))
        def _():
            reduce.x_piece(*piece_of(place, index - 1, outward))

        @pl.when((index >= 3) & (index < pieces + 3))
        def _():
            reduce.z_piece(*piece_of(place, index - 3, outward))

        for m in range(reduce.micro):
            first = m * ZS + 3 if outward else (m + 1) * ZS + 2
            for far in range(1, ZS):
                pl.when(index == first + ZS - 1 - far)(functools.partial(reduce.chain, m, far))
        return carry

    lax.fori_loop(0, pieces + 5, step, 0)


def begin_gathers(gathers):
    for m in range(gathers[0].micro):
        for gather in gathers:
            gather.send_own(m)
        if m == 0:
            for gather in gathers:
                gather.z_round(1, 0)
            for gather in gathers:
                gather.x_round(0, 0)


def gather_steps(gathers, index):
    for m in range(gathers[0].micro):
        for far in range(0 if m else 1, ZS):

            @pl.when(index == (max(0, m * (ZS - 2) - 1) + far if m else far - 1))
            def _(m=m, far=far):
                for gather in gathers:
                    if far + 1 < ZS:
                        gather.z_round(far + 1, m)
                for gather in gathers:
                    gather.x_round(far, m)


def wait_local(gather, m):
    gather.local(m).wait()


def by_lanes(count, width, body):
    def step(index, carry):
        body(pl.ds(pl.multiple_of(index * width, width), width))
        return carry

    lax.fori_loop(0, count, step, 0)


class Spread:
    @staticmethod
    def scratch(pieces, depth):
        return [DMA((pieces,)), DMA((ZS, pieces)), DMA((ZS, pieces))] + [
            DMA((ZS << step,)) for step in range(depth) for _ in range(2)
        ]

    def __init__(self, place, sources, targets, view, depth, refs):
        self.place, self.sources, self.targets, self.view, self.depth = place, sources, targets, view, depth
        self.local_sem, self.z_send, self.z_recv = [refs.pop(0) for _ in range(3)]
        self.sems = [(refs.pop(0), refs.pop(0)) for _ in range(depth)]
        self.pieces = self.local_sem.shape[0]

    def z_copy(self, step, piece):
        place = self.place
        mine = self.targets(self.view(place.z, place.y, place.x, place.core))
        return remote(
            self.sources(lax.rem(place.z + step, ZS))[piece],
            mine[piece],
            self.z_send.at[step, piece],
            self.z_recv.at[step, piece],
            place.z_peers[step],
        )

    def local(self, piece):
        place = self.place
        mine = self.targets(self.view(place.z, place.y, place.x, place.core))
        return pltpu.make_async_copy(self.sources(place.z)[piece], mine[piece], self.local_sem.at[piece])

    def hop(self, axis, index):
        place = self.place
        z = lax.rem(place.z - (index >> axis) + ZS, ZS)
        y = place.y if axis < 1 else (place.y + ((index >> (axis - 1)) & 1)) % 2
        x = place.x if axis < 2 else (place.x + (index & 1)) % 2
        block = self.view(z, y, x, place.core)
        peer = (place.y_peer, place.x_peer, place.core_peer)[axis]
        send, arrive = self.sems[axis]
        return remote(block, block, send.at[index], arrive.at[index], peer)

    def begin(self):
        for piece in range(self.pieces):
            self.local(piece).start()
        for step in (1, 3, 2):
            for piece in range(self.pieces):
                self.z_copy(step, piece).start()

    def forward(self, axis, index):
        for later in range(axis, self.depth):
            self.hop(later, index << (later - axis)).start()

    def send(self, step):
        for piece in range(self.pieces):
            (self.z_copy(step, piece) if step else self.local(piece)).start()

    def z_round(self, step):
        for piece in range(self.pieces):
            if step:
                self.z_copy(step, piece).wait_recv()
            else:
                self.local(piece).wait()
        self.forward(0, step)

    def hop_round(self, axis, index):
        self.hop(axis, index).wait_recv()
        self.forward(axis + 1, index * 2 + 1)

    def drain(self):
        for step in range(1, ZS):
            for piece in range(self.pieces):
                self.z_copy(step, piece).wait_send()
        for axis in range(self.depth):
            for index in range(ZS << axis):
                self.hop(axis, index).wait_send()


class Share:
    @staticmethod
    def scratch(pieces):
        return [DMA((pieces,)), DMA((pieces,)), DMA((pieces,))]

    def __init__(self, place, blocks, refs):
        local, send, arrive = [refs.pop(0) for _ in range(3)]
        self.copies = []
        for index, (source, target) in enumerate(blocks):
            self.copies.append(pltpu.make_async_copy(source, target, local.at[index]))
            self.copies.append(remote(source, target, send.at[index], arrive.at[index], place.y_peer))

    def begin(self):
        for copy in self.copies:
            copy.start()

    def drain(self):
        for copy in self.copies:
            copy.wait()


def normed_rows(rows, gain):
    return rows * lax.rsqrt(jnp.mean(rows * rows, axis=1, keepdims=True) + EPS) * gain


def norm_back(grad, rows, upstream, gain):
    scale = lax.rsqrt(jnp.mean(rows * rows, axis=1, keepdims=True) + EPS)
    scaled = grad * gain
    inner = jnp.mean(scaled * rows, axis=1, keepdims=True)
    return upstream + scale * scaled - rows * (scale * scale * scale) * inner, grad * rows * scale


def y_half(place, target, rows):
    return target.at[pl.ds(pl.multiple_of(place.y * rows, rows), rows)]


def by_heads(width, body):
    def step(head, carry):
        body(lambda kind: pl.ds(pl.multiple_of(kind * width + head * HDIM, HDIM), HDIM))
        return carry

    lax.fori_loop(0, width // HDIM, step, 0)


def columns_of(marks, place, m, k):
    local, lanes = marks.shape[3:]
    length = CS * XS * local
    block = marks[k].reshape(length, lanes)
    across = jnp.transpose(block)

    def pick(kind, source, axis):
        value = None
        for index in range(MICRO):
            at = index * KINDS + kind
            part = source[:, at : at + 1] if axis else source[at : at + 1, :]
            value = part if value is None else jnp.where(m == index, part, value)
        return value

    owner = place.owner.astype(F32)
    gates = [jnp.where(pick(kind, block, 1) == owner, pick(kind + 2, block, 1), 0.0) for kind in range(2)]
    return gates[0] + gates[1], pick(KINDS - 1, block, 1), pick(KINDS - 1, across, 0)


def attention_kernel(
    sizes,
    tokens,
    cotangent,
    first_gain,
    second_gain,
    table,
    cosine,
    sine,
    w_kv,
    w_query,
    w_out,
    w_gate_up,
    w_down,
    *refs,
):
    refs = list(refs)
    normed_out, middle_out, everyone, cotangent_out, table_out, turned_out, attended_out = [
        refs.pop(0) for _ in range(7)
    ]
    qkv_weight, out_weight, gate_up_weight, down_weight = [refs.pop(0) for _ in range(4)]
    wide, kv_rows, model_rows, out_rows, down_rows = sizes
    place = Place()
    own = refs.pop(0)
    normed = Gather(place, own, everyone, refs)
    upstream = Gather(place, cotangent, cotangent_out, refs)
    tables = Gather(place, table, table_out, refs)
    reduce = PieceReduce(place, refs)

    def lanes(start, width):
        return pl.ds(pl.multiple_of(start, HDIM), width)

    def kv_view(z, y, x, core):
        row = ((z * YS + y) * (XS * CS) + x * CS + core) * kv_rows
        return qkv_weight.at[pl.ds(pl.multiple_of(row, kv_rows), kv_rows), pl.ds(wide, 2 * wide)]

    def rows_of(z, y):
        return pl.ds(pl.multiple_of((z * YS + y) * model_rows, model_rows), model_rows)

    kv = Spread(
        place,
        lambda z: [w_kv.at[:, lanes((kind * ZS + z) * wide, wide)] for kind in range(2)],
        lambda block: [block.at[:, pl.ds(kind * wide, wide)] for kind in range(2)],
        kv_view,
        3,
        refs,
    )
    query = Spread(
        place,
        lambda z: [w_query.at[0, :, lanes(z * wide, wide)]],
        lambda block: [block],
        lambda z, y, x, core: qkv_weight.at[rows_of(z, y), pl.ds(0, wide)],
        1,
        refs,
    )
    hidden_width = gate_up_weight.shape[2]
    gate_up = Spread(
        place,
        lambda z: [w_gate_up.at[0, :, lanes((kind * ZS + z) * hidden_width, hidden_width)] for kind in range(2)],
        lambda block: [block.at[kind] for kind in range(2)],
        lambda z, y, x, core: gate_up_weight.at[:, rows_of(z, y)],
        1,
        refs,
    )
    shared = Share(place, [(w_out.at[0], y_half(place, out_weight, out_rows))], refs)
    down = Share(place, [(w_down.at[0], y_half(place, down_weight, down_rows))], refs)
    arrived, qkv, attended, marks, weight, out_here, load, store, late_load = [refs.pop(0) for _ in range(9)]
    model = tokens.shape[2]
    tile = model // 2
    late_loads = [
        pltpu.make_async_copy(qkv_weight, weight, late_load.at[0]),
        pltpu.make_async_copy(out_weight, out_here, late_load.at[1]),
        pltpu.make_async_copy(table_out.at[0], marks, late_load.at[2]),
    ]

    def stores(sequence):
        return [
            pltpu.make_async_copy(qkv, turned_out.at[sequence], store.at[0]),
            pltpu.make_async_copy(attended, attended_out.at[sequence], store.at[1]),
        ]

    def piece(index, m, k):
        sequence = m * ZS + k
        normed.piece_arrival(m, k)
        pl.when(k == 0)(functools.partial(wait_local, normed, m))
        loads = [
            pltpu.make_async_copy(everyone.at[m, k, dc, dx], arrived.at[dc, dx], load.at[dc, dx])
            for dc in range(CS)
            for dx in range(XS)
        ]
        for copy in loads:
            copy.start()

        @pl.when(index == 0)
        def _():
            for copy in late_loads:
                copy.wait()

        @pl.when(index > 0)
        def _():
            for copy in stores(0):
                copy.wait()

        row_gate, row_block, key_block = columns_of(marks, place, m, k)
        for copy in loads:
            copy.wait()
        length = qkv.shape[0]
        for kind in range(3):
            value = dot(arrived[...].reshape(length, model), weight[:, kind * wide : (kind + 1) * wide])
            for head in range(wide // HDIM):
                part = value[:, head * HDIM : (head + 1) * HDIM]
                if kind < 2:
                    part = turned(part, cosine[...], sine[...])
                start = kind * wide + head * HDIM
                qkv[:, start : start + HDIM] = part.astype(BF16)

        def head(span_of):
            query, key, value = [qkv[:, span_of(kind)] for kind in range(3)]
            probs = masked_probs(query, key, row_block, key_block).astype(BF16)
            attended[:, span_of(0)] = dot(probs, value).astype(BF16)

        by_heads(wide, head)
        for start in range(0, model, tile):
            value = dot(attended[...], out_here[:, start : start + tile]) * row_gate
            reduce.part[m, k, :, start : start + tile] = value.astype(BF16)
        for copy in stores(sequence):
            copy.start()

    def between(index):
        due = {
            2: [lambda: gate_up.z_round(1)],
            3: [lambda: gate_up.z_round(3)],
            4: [lambda: upstream.send_own(0)],
            5: [lambda: gate_up.z_round(2), lambda: upstream.send_own(1)],
            6: [lambda: upstream.z_round(1)],
            7: [lambda: upstream.x_round(0), lambda: upstream.z_round(2)],
            8: [lambda: upstream.x_round(1), lambda: upstream.z_round(3)],
            9: [lambda: upstream.x_round(2)],
            10: [lambda: upstream.x_round(3)],
        }
        for at, tasks in due.items():

            @pl.when(index == at)
            def _(tasks=tasks):
                for task in tasks:
                    task()

    place.enter(True)
    shared.begin()
    kv.begin()
    tables.send_own(0)
    for m in range(normed.micro):

        def body(span, m=m):
            own[m, span, :] = normed_rows(tokens[m, span, :].astype(F32), first_gain[...]).astype(BF16)

        by_rows(tokens.shape[1], body)
        normed.send_own(m)
    query.begin()
    kv.z_round(0)
    tables.z_round(1)
    kv.z_round(1)
    kv.z_round(3)
    normed.z_round(1)
    kv.z_round(2)
    for index in (0, 1, 3, 2):
        kv.hop_round(0, index)
    normed.x_round(0)
    for step in (0, 1, 3):
        gate_up.send(step)
    gate_up.z_round(0)
    tables.z_round(2)
    normed.z_round(2)
    normed.x_round(1)
    for step in (0, 1, 3, 2):
        query.z_round(step)
    for index in (0, 2, 6, 4, 1, 3, 7, 5):
        kv.hop_round(1, index)
    normed.z_round(3)
    tables.z_round(3)
    for far in range(ZS):
        tables.x_round(far)
    normed.x_round(2)
    normed.x_round(3)
    for index in range(ZS << 2):
        kv.hop_round(2, index)
    for index in range(ZS):
        query.hop_round(0, index)
    shared.drain()
    tables.arrivals()
    for copy in late_loads:
        copy.start()
    gate_up.send(2)
    down.begin()
    run_pieces(place, reduce, piece, between, True)
    for m in range(reduce.micro):
        reduce.finish(m)

        def body(span, m=m):
            middle = tokens[m, span, :].astype(F32) + reduce.total[m, span, :]
            middle_out[m, span, :] = middle
            normed_out[m, span, :] = normed_rows(middle, second_gain[...]).astype(BF16)

        by_rows(reduce.rows, body)
    for copy in stores(0):
        copy.wait()
    for index in range(ZS):
        gate_up.hop_round(0, index)
    for gather in (tables, normed):
        gather.drain(True)
    for part in (upstream, kv, query, gate_up, down, reduce):
        part.drain()


def attend_back_kernel(
    rows, weight_in, out_in, marks, cosine, sine, turned_qkv, tokens, middle_grad, gain, gate_grads, up_grads, *refs
):
    refs = list(refs)
    input_out, terms_out, row_grad_out, qkv_grad_out, weight_grad_out, sums_out, everyone = [
        refs.pop(0) for _ in range(7)
    ]
    place = Place()
    gather = Gather(place, rows, everyone, refs)
    reduce = PieceReduce(place, refs)
    arrived, kept, row_grad, qkv_grad, load, store = [refs.pop(0) for _ in range(6)]
    mine, theirs, mine_sem, y_send, y_recv, z_send, z_recv, sum_local = [refs.pop(0) for _ in range(8)]
    weight, out_weight, weight_load = [refs.pop(0) for _ in range(3)]
    weight_loads = [
        pltpu.make_async_copy(weight_in, weight, weight_load.at[0]),
        pltpu.make_async_copy(out_in, out_weight, weight_load.at[1]),
    ]
    wide, model = out_weight.shape
    tile = model // 2
    width = mine.shape[2]

    def stores(sequence):
        return [
            pltpu.make_async_copy(row_grad, row_grad_out.at[sequence], store.at[0]),
            pltpu.make_async_copy(qkv_grad, qkv_grad_out.at[sequence], store.at[1]),
        ]

    def piece(index, m, k):
        sequence = m * ZS + k
        gather.piece_arrival(m, k)
        pl.when(k == 0)(lambda: gather.local(m).wait())
        loads = [
            pltpu.make_async_copy(everyone.at[m, k, dc, dx], arrived.at[dc, dx], load.at[dc, dx])
            for dc in range(CS)
            for dx in range(XS)
        ]
        loads.append(pltpu.make_async_copy(turned_qkv.at[sequence], kept, load.at[CS, 0]))
        for copy in loads:
            copy.start()

        @pl.when(index == 0)
        def _():
            for copy in weight_loads:
                copy.wait()

        @pl.when(index > 0)
        def _():
            for copy in stores(0):
                copy.wait()

        for copy in loads:
            copy.wait()
        length = kept.shape[0]
        row_gate, row_block, key_block = columns_of(marks, place, m, k)
        for start in range(0, model, tile):
            value = arrived[:, :, :, start : start + tile].astype(F32).reshape(length, tile) * row_gate
            row_grad[:, start : start + tile] = value.astype(BF16)
        qkv_grad[:, :wide] = dot_t(row_grad[...], out_weight[...]).astype(BF16)

        def head(span_of):
            query, key, value = [kept[:, span_of(kind)] for kind in range(3)]
            grad = qkv_grad[:, span_of(0)]
            probs = masked_probs(query, key, row_block, key_block)
            prob_grad = dot_t(grad, value)
            inner = jnp.sum(probs * prob_grad, axis=1, keepdims=True)
            raw_grad = (probs * (prob_grad - inner) * HDIM ** (-0.5)).astype(BF16)
            qkv_grad[:, span_of(0)] = turned(dot(raw_grad, key), cosine[...], -sine[...]).astype(BF16)
            qkv_grad[:, span_of(1)] = turned(dot_l(raw_grad, query), cosine[...], -sine[...]).astype(BF16)
            qkv_grad[:, span_of(2)] = dot_l(probs.astype(BF16), grad).astype(BF16)

        by_heads(wide, head)
        for start in range(0, model, tile):
            value = dot_t(qkv_grad[...], weight[start : start + tile, :])
            reduce.part[m, k, :, start : start + tile] = value.astype(BF16)
        for copy in stores(sequence):
            copy.start()

    steps = (1, 3, 2, 0)
    sources = (gate_grads, up_grads)

    def z_of(turn):
        return lax.rem(place.z + steps[turn], ZS)

    def own_copy(part):
        kind, turn = divmod(part, ZS)
        return pltpu.make_async_copy(sources[kind].at[z_of(turn), place.y], mine.at[part], mine_sem.at[part])

    def y_copy(part):
        kind, turn = divmod(part, ZS)
        return remote(
            sources[kind].at[z_of(turn), 1 - place.y],
            theirs.at[part],
            y_send.at[part],
            y_recv.at[part],
            place.y_peer,
        )

    columns = weight_grad_out.at[:, pl.ds(pl.multiple_of(place.z * width, HDIM), width)]

    def sum_copy(part):
        kind, turn = divmod(part, ZS)
        if kind:
            return pltpu.make_async_copy(theirs.at[part], sums_out.at[z_of(turn)], sum_local.at[part])
        if steps[turn] == 0:
            return pltpu.make_async_copy(theirs.at[part], columns, sum_local.at[part])
        return remote(
            theirs.at[part], columns, z_send.at[steps[turn]], z_recv.at[steps[turn]], place.z_peers[steps[turn]]
        )

    def pass_grads(part):
        y_copy(part).wait()
        if part + 2 < 2 * ZS:
            y_copy(part + 2).start()
        own_copy(part).wait()

        def add(span):
            value = mine[part, span, :].astype(F32) + theirs[part, span, :].astype(F32)
            theirs[part, span, :] = value.astype(BF16)

        by_rows(mine.shape[1], add)
        sum_copy(part).start()

    def between(index):
        gather_steps([gather], index)
        for part, at in enumerate((2, 3, 5, 6, 8, 9)):
            pl.when(index == at)(functools.partial(pass_grads, part))

    for copy in weight_loads:
        copy.start()
    for part in range(2 * ZS):
        own_copy(part).start()
    place.enter(True)
    for part in range(2):
        y_copy(part).start()
    begin_gathers([gather])
    run_pieces(place, reduce, piece, between)
    for part in range(6, 2 * ZS):
        pass_grads(part)
    terms_out[...] = jnp.zeros_like(terms_out)
    for m in range(gather.micro):
        reduce.finish(m)

        def body(span, m=m):
            result, found = norm_back(
                reduce.total[m, span, :], tokens[m, span, :].astype(F32), middle_grad[m, span, :], gain[...]
            )
            input_out[m, span, :] = result.astype(BF16)
            terms_out[...] += found

        by_rows(reduce.rows, body)
    for copy in stores(0):
        copy.wait()
    gather.drain(True)
    reduce.drain()
    for part in range(2 * ZS):
        sum_copy(part).wait()


def mlp_kernel(
    normed, gate_up_part, down_part, select, select_back, gates, cotangents, middle, cotangent, gain, *refs
):
    refs = list(refs)
    own_out, grad_out, terms_out, rows_out, up_grad_out, hidden_out, down_grad_out, result_out = [
        refs.pop(0) for _ in range(8)
    ]
    everyone = refs.pop(0)
    place = Place()
    gathers = [Gather(place, normed, everyone, refs)]
    reduce = PieceReduce(place, refs)
    arrived, upstream, rows, down_grad, hidden, both_grad, result = [refs.pop(0) for _ in range(7)]
    gate_weight, up_weight, down, load, store, weight_load = [refs.pop(0) for _ in range(6)]
    width = down.shape[0]
    model = middle.shape[2]
    tile = model // 2
    pieces = reduce.micro * ZS
    weight_loads = [
        pltpu.make_async_copy(source, target, weight_load.at[i])
        for i, (source, target) in enumerate(
            ((gate_up_part.at[0], gate_weight), (gate_up_part.at[1], up_weight), (down_part, down))
        )
    ]

    kept = (
        (rows, rows_out),
        (down_grad, down_grad_out),
        (hidden, hidden_out),
        (both_grad, up_grad_out),
        (result, result_out),
    )

    def store_of(number, sequence):
        here, there = kept[number]
        return pltpu.make_async_copy(here, there.at[sequence], store.at[number])

    def loads_of(number, source, target, m, k):
        return [
            pltpu.make_async_copy(source.at[m, k, dc, dx], target.at[dc, dx], load.at[number, dc, dx])
            for dc in range(CS)
            for dx in range(XS)
        ]

    def piece(index, m, k):
        for gather in gathers:
            gather.piece_arrival(m, k)
            pl.when(k == 0)(functools.partial(wait_local, gather, m))
        sequence = m * ZS + k
        loads = loads_of(0, everyone, arrived, m, k)
        for copy in loads:
            copy.start()

        def stored(*numbers):
            @pl.when(index > 0)
            def _():
                for number in numbers:
                    store_of(number, 0).wait()

        def store_out(*numbers):
            for number in numbers:
                store_of(number, sequence).start()

        @pl.when(index == 0)
        def _():
            for copy in loads_of(1, cotangents, upstream, m, k):
                copy.start()
            for copy in weight_loads:
                copy.wait()

        stored(0, 1)
        for copy in loads + loads_of(1, cotangents, upstream, m, k):
            copy.wait()
        chosen, back, gate_of_row = select[sequence], select_back[sequence], gates[sequence]
        length = select.shape[2]

        def to_rows(span):
            rows[:, span] = dot(chosen, arrived[:, :, :, span].reshape(length, tile)).astype(BF16)
            down_grad[:, span] = (dot(chosen, upstream[:, :, :, span].reshape(length, tile)) * gate_of_row).astype(BF16)

        by_lanes(model // tile, tile, to_rows)
        store_out(0, 1)

        @pl.when(index + 1 < pieces)
        def _():
            for copy in loads_of(1, cotangents, upstream, *piece_of(place, index + 1)):
                copy.start()

        stored(2, 3)

        half = width // (2 * HDIM) * HDIM
        for start, stop in ((0, half), (half, width)):
            gate = dot(rows[...], gate_weight[:, start:stop])
            up = dot(rows[...], up_weight[:, start:stop])
            hidden_grad = dot_t(down_grad[...], down[start:stop, :])
            sigma = 0.5 * jnp.tanh(0.5 * gate) + 0.5
            silu = gate * sigma
            hidden[:, start:stop] = (silu * up).astype(BF16)
            slope = sigma + silu * (1.0 - sigma)
            both_grad[:, start:stop] = (hidden_grad * up * slope).astype(BF16)
            both_grad[:, width + start : width + stop] = (hidden_grad * silu).astype(BF16)

        store_out(2, 3)
        stored(4)

        def to_tokens(span):
            row_grad = dot_t(both_grad[:, :width], gate_weight[span, :])
            row_grad = (row_grad + dot_t(both_grad[:, width:], up_weight[span, :])).astype(BF16)
            reduce.part[m, k, :, span] = dot(back, row_grad).astype(BF16)
            value = (dot(hidden[...], down[:, span]) * gate_of_row).astype(BF16)
            result[:, span] = dot(back, value).astype(BF16)

        by_lanes(model // tile, tile, to_tokens)
        store_out(4)

    for copy in weight_loads:
        copy.start()
    place.enter(False)
    begin_gathers(gathers)
    run_pieces(place, reduce, piece, functools.partial(gather_steps, gathers))
    terms_out[...] = jnp.zeros_like(terms_out)
    for m in range(reduce.micro):
        reduce.finish(m)

        def body(span, m=m):
            found, terms = norm_back(
                reduce.total[m, span, :], middle[m, span, :], cotangent[m, span, :].astype(F32), gain[...]
            )
            grad_out[m, span, :] = found
            own_out[m, span, :] = found.astype(BF16)
            terms_out[...] += terms

        by_rows(reduce.rows, body)
    for number in range(len(kept)):
        store_of(number, 0).wait()
    for gather in gathers:
        gather.drain(True)
    reduce.drain()


class Halves:
    def __init__(self, own, other, copy):
        self.own, self.other, self.copy = own, other, copy

    def begin(self):
        self.copy.start()

    def add(self):
        self.copy.wait()

        def body(index, carry):
            value = self.own[index].astype(F32) + self.other[index].astype(F32)
            self.other[index] = value.astype(BF16)
            return carry

        lax.fori_loop(0, self.other.shape[0], body, 0)


def last_kernel(part, middle, first_terms, second_terms, rows, grads, attended, row_grads, up_grad, *refs):
    refs = list(refs)
    output, gains_out, query_out, kv_out, out_out, up_out = [refs.pop(0) for _ in range(6)]
    place = Place()
    reduce = Reduce(place, part, refs)
    tall, long, load = [refs.pop(0) for _ in range(3)]
    query_all, query_in, kv_all, core_in, x_in, y_in, out_own, out_send, out_in = [refs.pop(0) for _ in range(9)]
    hop_send, hop_recv, z_send, z_recv, z_local = [refs.pop(0) for _ in range(5)]
    terms, gain_in, gain_send, gain_recv = [refs.pop(0) for _ in range(4)]
    up_send, up_recv, up_local = [refs.pop(0) for _ in range(3)]
    wide, kv_rows = query_out.shape[1] // ZS, kv_out.shape[0]
    model = tall.shape[1]
    tile = model // ZS

    def swap(number, source, target, peer):
        return remote(source, target, hop_send.at[number], hop_recv.at[number], peer)

    query = Halves(
        query_all.at[:, place.y], query_in, swap(0, query_all.at[:, 1 - place.y], query_in, place.y_peer)
    )
    over_core = Halves(
        kv_all.at[:, place.core], core_in, swap(1, kv_all.at[:, 1 - place.core], core_in, place.core_peer)
    )
    by_x = core_in.reshape(ZS * YS, XS, kv_rows, 2 * wide)
    over_x = Halves(by_x.at[:, place.x], x_in, swap(2, by_x.at[:, 1 - place.x], x_in, place.x_peer))
    by_y = x_in.reshape(ZS, YS, kv_rows, 2 * wide)
    over_y = Halves(by_y.at[:, place.y], y_in, swap(3, by_y.at[:, 1 - place.y], y_in, place.y_peer))
    over_out = swap(4, out_send, out_in, place.y_peer)

    def lanes(start):
        return pl.ds(pl.multiple_of(start, HDIM), wide)

    def z_parts(step):
        to = lax.rem(place.z + step, ZS)
        pairs = [(query_in.at[to], query_out.at[:, lanes(place.z * wide)])]
        for kind in range(2):
            pairs.append(
                (y_in.at[to, :, pl.ds(kind * wide, wide)], kv_out.at[:, lanes((kind * ZS + place.z) * wide)])
            )
        return pairs

    def z_copy(step, piece):
        source, target = z_parts(step)[piece]
        if step == 0:
            return pltpu.make_async_copy(source, target, z_local.at[piece])
        return remote(source, target, z_send.at[step, piece], z_recv.at[step, piece], place.z_peers[step])

    hops = [[place.core_peer], [place.x_peer], [place.y_peer], place.z_peers[1:]]

    def gain_copies(hop):
        return [
            remote(terms, gain_in.at[hop + i], gain_send.at[hop + i], gain_recv.at[hop + i], peer)
            for i, peer in enumerate(hops[hop])
        ]

    def send_gains(hop):
        for copy in gain_copies(hop):
            copy.start()

    def add_gains(hop):
        copies = gain_copies(hop)
        for copy in copies:
            copy.wait()
        for i in range(len(copies)):
            terms[...] += gain_in[hop + i]
        if hop + 1 < len(hops):
            send_gains(hop + 1)

    width = up_grad.shape[2]
    columns = up_out.at[:, pl.ds(pl.multiple_of(place.z * width, HDIM), width)]
    up_copies = [pltpu.make_async_copy(up_grad.at[place.z], columns, up_local)]
    for step in (1, 3, 2):
        source = up_grad.at[lax.rem(place.z + step, ZS)]
        up_copies.append(remote(source, columns, up_send.at[step], up_recv.at[step], place.z_peers[step]))
    loads = [pltpu.make_async_copy(rows, tall, load.at[0]), pltpu.make_async_copy(grads, long, load.at[1])]
    later_loads = [
        pltpu.make_async_copy(row_grads, tall, load.at[2]),
        pltpu.make_async_copy(attended, long.at[:, pl.ds(0, wide)], load.at[3]),
    ]

    def small_grads(z):
        span = slice(z * tile, (z + 1) * tile)
        value = dot_l(tall[:, span], long[:, :wide]).astype(BF16)
        query_all[z] = value.reshape(query_all.shape[1:])
        blocks = kv_all.shape[0] // ZS
        for kind in range(2):
            value = dot_l(tall[:, span], long[:, (kind + 1) * wide : (kind + 2) * wide]).astype(BF16)
            kv_all[z * blocks : (z + 1) * blocks, :, :, kind * wide : (kind + 1) * wide] = value.reshape(
                (blocks,) + kv_all.shape[1:3] + (wide,)
            )

    def out_grads():
        out_rows = out_own.shape[0]
        for start in range(0, model, model // 2):
            span = slice(start, start + model // 2)
            value = dot_l(long[:, :wide], tall[:, span])
            first, second = value[:out_rows], value[out_rows:]
            out_own[:, span] = jnp.where(place.y == 0, first, second)
            out_send[:, span] = jnp.where(place.y == 0, second, first).astype(BF16)

    for copy in loads:
        copy.start()
    place.enter(True)
    reduce.begin()
    for copy in up_copies:
        copy.start()
    terms[...] = jnp.zeros_like(terms)
    terms[0:1, :] = jnp.sum(first_terms[...], axis=0, keepdims=True)
    terms[1:2, :] = jnp.sum(second_terms[...], axis=0, keepdims=True)
    send_gains(0)
    for copy in loads:
        copy.wait()
    small_grads(0)
    reduce.pass_x(0)
    for z in range(1, ZS):
        small_grads(z)
    for copy in later_loads:
        copy.start()
    over_core.begin()
    query.begin()
    add_gains(0)
    over_core.add()
    over_x.begin()
    for m in range(1, reduce.micro):
        reduce.pass_x(m)
    add_gains(1)
    for copy in later_loads:
        copy.wait()
    out_grads()
    over_out.start()
    reduce.sums(0)
    over_x.add()
    over_y.begin()
    query.add()
    for step in (1, 3, 2, 0):
        z_copy(step, 0).start()
    add_gains(2)
    for m in range(1, reduce.micro):
        reduce.sums(m)
    over_y.add()
    for step in (1, 3, 2, 0):
        for piece in (1, 2):
            z_copy(step, piece).start()
    add_gains(3)
    gains_out[...] = terms[...]
    for m in range(reduce.micro):
        reduce.finish(m)

        def finish(span, m=m):
            output[m, span, :] = (middle[m, span, :] + reduce.total[m, span, :]).astype(BF16)

        by_rows(reduce.rows, finish)
    over_out.wait()

    def add_out(span):
        out_out[span, :] = out_own[span, :] + out_in[span, :].astype(F32)

    by_rows(out_own.shape[0], add_out)
    reduce.drain()
    for copy in up_copies:
        copy.wait()
    for step in range(ZS):
        for piece in range(3):
            z_copy(step, piece).wait()


def gate_up_grads_kernel(rows, both_grad, gate_out, up_out):
    value = dot_l(rows[...], both_grad[...]).astype(BF16)
    width = both_grad.shape[1] // 2
    gate_out[0] = value[:, :width].reshape(gate_out.shape[1:])
    up_out[0] = value[:, width:].reshape(up_out.shape[1:])


def gate_up_grads(rows, both_grad, model_rows):
    count, model = rows.shape
    width = both_grad.shape[1] // 2
    block = pl.BlockSpec((1, YS, model_rows, width), lambda z: (z, 0, 0, 0))
    return pl.pallas_call(
        gate_up_grads_kernel,
        grid=(ZS,),
        in_specs=[
            pl.BlockSpec((count, model // ZS), lambda z: (0, z)),
            pl.BlockSpec((count, 2 * width), lambda z: (0, 0)),
        ],
        out_specs=[block, block],
        out_shape=[jax.ShapeDtypeStruct((ZS, YS, model_rows, width), BF16)] * 2,
        compiler_params=pltpu.CompilerParams(vmem_limit_bytes=60 << 20),
        cost_estimate=pl.CostEstimate(
            flops=4 * count * model * width, bytes_accessed=12 * model * width, transcendentals=0
        ),
    )(rows, both_grad)


def down_grads_kernel(hidden, down_grad, down_out, small_out):
    value = dot_l(hidden[...], down_grad[...])
    down_out[...] = value
    small_out[...] = value.astype(BF16)


def down_grads(hidden, down_grad):
    count, model = down_grad.shape
    width = hidden.shape[1]
    tile = model // ZS
    return pl.pallas_call(
        down_grads_kernel,
        grid=(ZS,),
        in_specs=[
            pl.BlockSpec((count, width), lambda z: (0, 0)),
            pl.BlockSpec((count, tile), lambda z: (0, z)),
        ],
        out_specs=[pl.BlockSpec((width, tile), lambda z: (0, z))] * 2,
        out_shape=[jax.ShapeDtypeStruct((width, model), F32), jax.ShapeDtypeStruct((width, model), BF16)],
        compiler_params=pltpu.CompilerParams(vmem_limit_bytes=60 << 20),
        cost_estimate=pl.CostEstimate(
            flops=2 * count * model * width, bytes_accessed=10 * model * width, transcendentals=0
        ),
    )(hidden, down_grad)


def widen_kernel(first, second, own, other_first, other_last, kv, query, weight_out, down_out, kv_out, query_out):
    step = pl.program_id(0)
    pl.when(step < ZS)(lambda: weight_out.__setitem__(..., first[...].astype(F32)))
    pl.when(step >= ZS)(lambda: weight_out.__setitem__(..., second[...].astype(F32)))
    pl.when(step < ZS)(lambda: down_out.__setitem__(..., own[0] + other_first[...].astype(F32)))
    pl.when(step >= ZS)(lambda: down_out.__setitem__(..., own[0] + other_last[...].astype(F32)))
    kv_out[...] = kv[...].astype(F32)
    query_out[...] = query[...].astype(F32)


def widen(first, second, own, other_first, other_last, kv, query, y):
    steps = 2 * ZS
    rows, width = first.shape[0], first.shape[1] // ZS
    _, down_rows, model = own.shape
    down_step = down_rows // ZS

    def block(*dims):
        return pl.BlockSpec(dims, lambda i, y: (i // 2,) + (0,) * (len(dims) - 1))

    small = [(value.shape[0] // ZS, value.shape[1]) for value in (kv, query)]
    return pl.pallas_call(
        lambda y, *refs: widen_kernel(*refs),
        grid_spec=pltpu.PrefetchScalarGridSpec(
            num_scalar_prefetch=1,
            grid=(steps,),
            in_specs=[
                pl.BlockSpec((rows, width), lambda i, y: (0, jnp.minimum(i, ZS - 1))),
                pl.BlockSpec((rows, width), lambda i, y: (0, jnp.maximum(i - ZS, 0))),
                pl.BlockSpec((1, down_step, model), lambda i, y: (y[0], i // 2, 0)),
                pl.BlockSpec((down_step, model), lambda i, y: (jnp.minimum(i // 2, ZS // 2 - 1), 0)),
                pl.BlockSpec((down_step, model), lambda i, y: (jnp.maximum(i // 2 - ZS // 2, 0), 0)),
                block(*small[0]),
                block(*small[1]),
            ],
            out_specs=[
                pl.BlockSpec((rows, width), lambda i, y: (0, i)),
                block(down_step, model),
                block(*small[0]),
                block(*small[1]),
            ],
        ),
        out_shape=[
            jax.ShapeDtypeStruct((rows, steps * width), F32),
            jax.ShapeDtypeStruct((down_rows, model), F32),
            jax.ShapeDtypeStruct(kv.shape, F32),
            jax.ShapeDtypeStruct(query.shape, F32),
        ],
        compiler_params=pltpu.CompilerParams(vmem_limit_bytes=60 << 20),
        cost_estimate=pl.CostEstimate(flops=0, bytes_accessed=12 * rows * steps * width, transcendentals=0),
    )(jnp.full((1,), y, jnp.int32), first, second, own, other_first, other_last, kv, query)


def connect(kernel, operands, spaces, out_shapes, out_spaces, scratch, number, seconds):
    return pl.pallas_call(
        kernel,
        in_specs=spaces,
        out_specs=out_spaces,
        out_shape=out_shapes,
        scratch_shapes=scratch,
        compiler_params=pltpu.CompilerParams(
            collective_id=number, has_side_effects=True, vmem_limit_bytes=60 << 20
        ),
        cost_estimate=pl.CostEstimate(flops=0, bytes_accessed=int(seconds * 3e12), transcendentals=0),
    )(*operands)


def fast_device(
    tokens,
    cotangent,
    gain_attn,
    gain_mlp,
    w_kv,
    w_query,
    w_out,
    w_gate_up,
    w_down,
    att_routes,
    att_gates,
    mlp_routes,
    mlp_gates,
    blocks,
):
    group, owner = lax.axis_index("group"), lax.axis_index("expert")
    y = group % YS
    x, core = owner // CS, owner % CS
    micro, local, model = tokens.shape
    wide = w_query.shape[2] // ZS
    hidden_width = w_gate_up.shape[2] // (2 * ZS)
    kv_rows = w_kv.shape[0]
    model_rows = w_query.shape[1]

    def own_rows(table):
        return lax.dynamic_slice_in_dim(table, owner * local, local, 0).astype(F32)

    lines = []
    for m in range(micro):
        lines += [own_rows(att_routes[m]), att_gates[m], own_rows(mlp_routes[m]), mlp_gates[m]]
        lines += [own_rows(blocks[m, 0][:, None])]
    table = jnp.concatenate(lines, axis=1)
    table = jnp.pad(table, ((0, 0), (0, -table.shape[1] % HDIM)))[None]

    positions = (
        (x ^ jnp.arange(XS)[None, :, None]) * CS + (core ^ jnp.arange(CS)[:, None, None])
    ) * local + jnp.arange(local)[None, None, :]
    cosine, sine = angles(positions.reshape(-1))
    cosine = jnp.concatenate([cosine, cosine], axis=1)
    sine = jnp.concatenate([-sine, sine], axis=1)

    shape = (micro, local, model)
    everyone = (micro, ZS, CS, XS, local, model)
    seqs = micro * ZS
    first_gain, second_gain = gain_attn[None], gain_mlp[None]
    tall = jax.ShapeDtypeStruct(shape, F32)
    short = jax.ShapeDtypeStruct(shape, BF16)
    gathered = jax.ShapeDtypeStruct(everyone, BF16)
    terms = jax.ShapeDtypeStruct((STEP, model), F32)
    own_buffer = pltpu.VMEM(shape, BF16)

    def kept(width, rows=SEQ):
        return jax.ShapeDtypeStruct((seqs, rows, width), BF16)

    def weight(*dims):
        return jax.ShapeDtypeStruct(dims, BF16)

    marks = (ZS, CS, XS) + table.shape[1:]
    (
        normed_two,
        middle,
        normed,
        cotangents,
        table,
        turned_qkv,
        attended,
        qkv_weight,
        out_weight,
        gate_up_weight,
        down_weight,
    ) = connect(
        functools.partial(attention_kernel, (wide, kv_rows, model_rows, w_out.shape[1], w_down.shape[1])),
        [
            tokens,
            cotangent,
            first_gain,
            second_gain,
            table,
            cosine,
            sine,
            w_kv,
            w_query,
            w_out,
            w_gate_up,
            w_down,
        ],
        [VMEM] * 7 + [ANY] * 5,
        [
            short,
            tall,
            gathered,
            gathered,
            jax.ShapeDtypeStruct((1,) + marks, F32),
            kept(3 * wide),
            kept(wide),
            weight(model, 3 * wide),
            weight(wide, model),
            weight(2, model, hidden_width),
            weight(hidden_width, model),
        ],
        [VMEM, VMEM] + [ANY] * 9,
        [own_buffer]
        + Gather.scratch(micro)
        + Gather.scratch(micro)
        + Gather.scratch(1)
        + PieceReduce.scratch(*shape)
        + Spread.scratch(2, 3)
        + Spread.scratch(1, 1)
        + Spread.scratch(2, 1)
        + Share.scratch(1)
        + Share.scratch(1)
        + [
            pltpu.VMEM((CS, XS, local, model), BF16),
            pltpu.VMEM((SEQ, 3 * wide), BF16),
            pltpu.VMEM((SEQ, wide), BF16),
            pltpu.VMEM(marks, F32),
            pltpu.VMEM((model, 3 * wide), BF16),
            pltpu.VMEM((wide, model), BF16),
            DMA((CS, XS)),
            DMA((2,)),
            DMA((3,)),
        ],
        1,
        250e-6,
    )
    table = table[0]
    part = table[..., : KINDS * micro].reshape(ZS, SEQ, micro, KINDS).transpose(2, 0, 1, 3)
    part = part.reshape(seqs, SEQ, KINDS)
    hit = jnp.any(part[..., 4:6] == owner, axis=-1)
    mlp_weight = jnp.sum(jnp.where(part[..., 4:6] == owner, part[..., 6:8], 0.0), axis=-1)
    before_mask = jnp.arange(SEQ)[:, None] < jnp.arange(SEQ)[None, :]
    before = dot(hit.astype(BF16), before_mask.astype(BF16)).astype(jnp.int32)
    slots = jnp.arange(XS * CS * CAP + -XS * CS * CAP % STEP)
    chosen = hit[:, None, :] & (before[:, None, :] == slots[None, :, None])
    row_gate = jnp.sum(jnp.where(chosen, mlp_weight[:, None, :], 0.0), axis=2)
    select = chosen.astype(BF16)
    slot_count = select.shape[1]
    middle_rows, middle_grad, gain_second, rows_two, both_grad, hidden, down_grad, result_two, *_ = connect(
        mlp_kernel,
        [
            normed_two,
            gate_up_weight,
            down_weight,
            select,
            select.transpose(0, 2, 1),
            row_gate[:, :, None],
            cotangents,
            middle,
            cotangent,
            second_gain,
        ],
        [VMEM] + [ANY] * 2 + [VMEM] * 3 + [ANY] + [VMEM] * 3,
        [
            short,
            tall,
            terms,
            kept(model, slot_count),
            kept(2 * hidden_width, slot_count),
            kept(hidden_width, slot_count),
            kept(model, slot_count),
            kept(model),
            gathered,
        ],
        [VMEM, VMEM, VMEM] + [ANY] * 6,
        Gather.scratch(micro)
        + PieceReduce.scratch(*shape)
        + [
            pltpu.VMEM((CS, XS, local, model), BF16),
            pltpu.VMEM((CS, XS, local, model), BF16),
            pltpu.VMEM((slot_count, model), BF16),
            pltpu.VMEM((slot_count, model), BF16),
            pltpu.VMEM((slot_count, hidden_width), BF16),
            pltpu.VMEM((slot_count, 2 * hidden_width), BF16),
            pltpu.VMEM((SEQ, model), BF16),
            pltpu.VMEM((model, hidden_width), BF16),
            pltpu.VMEM((model, hidden_width), BF16),
            pltpu.VMEM((hidden_width, model), BF16),
            DMA((2, CS, XS)),
            DMA((5,)),
            DMA((3,)),
        ],
        5,
        150e-6,
    )
    rows_two, both_grad, hidden, down_grad = [
        value.reshape(-1, value.shape[2]) for value in (rows_two, both_grad, hidden, down_grad)
    ]
    result_two = result_two.reshape(everyone)

    grad_down, down_small = [value.reshape(YS, -1, model) for value in down_grads(hidden, down_grad)]
    down_small = take(down_small, 1 - y, 0)
    half = down_small.shape[0] // 2
    down_first, down_last = down_small[:half], down_small[half:]
    rows_two, down_first, down_last = lax.optimization_barrier((rows_two, down_first, down_last))
    down_first = y_move(down_first)
    gate_grad, up_grad = gate_up_grads(rows_two, both_grad, model_rows)
    input_grad, gain_first, result_grad, qkv_grad, gate_grad, up_grad, _ = connect(
        attend_back_kernel,
        [
            middle_rows,
            qkv_weight,
            out_weight,
            table,
            cosine,
            sine,
            turned_qkv,
            tokens,
            middle_grad,
            first_gain,
            gate_grad,
            up_grad,
        ],
        [VMEM] + [ANY] * 2 + [VMEM] * 3 + [ANY] + [VMEM] * 3 + [ANY] * 2,
        [
            short,
            terms,
            kept(model),
            kept(3 * wide),
            jax.ShapeDtypeStruct((model_rows, ZS * hidden_width), BF16),
            jax.ShapeDtypeStruct((ZS, model_rows, hidden_width), BF16),
            gathered,
        ],
        [VMEM, VMEM] + [ANY] * 5,
        Gather.scratch(micro)
        + PieceReduce.scratch(*shape)
        + [
            pltpu.VMEM((CS, XS, local, model), BF16),
            pltpu.VMEM((SEQ, 3 * wide), BF16),
            pltpu.VMEM((SEQ, model), BF16),
            pltpu.VMEM((SEQ, 3 * wide), BF16),
            DMA((CS + 1, XS)),
            DMA((2,)),
            pltpu.VMEM((2 * ZS, model_rows, hidden_width), BF16),
            pltpu.VMEM((2 * ZS, model_rows, hidden_width), BF16),
            DMA((2 * ZS,)),
            DMA((2 * ZS,)),
            DMA((2 * ZS,)),
            DMA((ZS,)),
            DMA((ZS,)),
            DMA((2 * ZS,)),
            pltpu.VMEM((model, 3 * wide), BF16),
            pltpu.VMEM((wide, model), BF16),
            DMA((2,)),
        ],
        3,
        150e-6,
    )
    down_last, input_grad = lax.optimization_barrier((down_last, input_grad))
    down_last = y_move(down_last)
    rows = seqs * SEQ
    output, gains, query_grad, kv_grad, grad_out, up_grad = connect(
        last_kernel,
        [
            result_two,
            middle,
            gain_first,
            gain_second,
            normed.reshape(rows, model),
            qkv_grad.reshape(rows, 3 * wide),
            attended.reshape(rows, wide),
            result_grad.reshape(rows, model),
            up_grad,
        ],
        [ANY, VMEM, VMEM, VMEM] + [ANY] * 5,
        [
            short,
            jax.ShapeDtypeStruct((8, model), F32),
            jax.ShapeDtypeStruct((model_rows, ZS * wide), BF16),
            jax.ShapeDtypeStruct((kv_rows, 2 * ZS * wide), BF16),
            jax.ShapeDtypeStruct(w_out.shape[1:], F32),
            weight(model_rows, ZS * hidden_width),
        ],
        [VMEM, VMEM, ANY, ANY, VMEM, ANY],
        Reduce.scratch(*shape)
        + [pltpu.VMEM((rows, model), BF16), pltpu.VMEM((rows, 3 * wide), BF16), DMA((4,))]
        + [pltpu.VMEM((ZS, YS, model_rows, wide), BF16), pltpu.VMEM((ZS, model_rows, wide), BF16)]
        + [
            pltpu.VMEM((ZS * YS * XS, CS, kv_rows, 2 * wide), BF16),
            pltpu.VMEM((ZS * YS * XS, kv_rows, 2 * wide), BF16),
            pltpu.VMEM((ZS * YS, kv_rows, 2 * wide), BF16),
            pltpu.VMEM((ZS, kv_rows, 2 * wide), BF16),
        ]
        + [pltpu.VMEM(w_out.shape[1:], kind) for kind in (F32, BF16, BF16)]
        + [DMA((5,)), DMA((5,)), DMA((ZS, 3)), DMA((ZS, 3)), DMA((3,))]
        + [pltpu.VMEM((8, model), F32), pltpu.VMEM((6, 8, model), F32), DMA((6,)), DMA((6,))]
        + [DMA((ZS,)), DMA((ZS,)), DMA],
        4,
        100e-6,
    )
    devices = ZS * YS * XS * CS
    gains = take(gains[:2].reshape(2, devices, model // devices), group * XS * CS + owner, 1)
    grad_gate_up, grad_down, kv_grad, query_grad = widen(
        gate_grad, up_grad, grad_down, down_first, down_last, kv_grad, query_grad, y
    )
    return (
        output,
        input_grad,
        gains[0],
        gains[1],
        kv_grad,
        query_grad[None],
        grad_out[None],
        grad_gate_up[None],
        grad_down[None],
    )


def solution(mesh):
    in_specs = (
        P(None, ("group", "expert"), None),
        P(None, ("group", "expert"), None),
        P(),
        P(),
        P(("group", "expert"), None),
        P("expert", "group", None),
        P("expert", "group", None),
        P("expert", "group", None),
        P("expert", "group", None),
        P(None, "group", None),
        P(None, ("group", "expert"), None),
        P(None, "group", None),
        P(None, ("group", "expert"), None),
        P(None, "group", None),
    )
    out_specs = (
        P(None, ("group", "expert"), None),
        P(None, ("group", "expert"), None),
        P(("group", "expert")),
        P(("group", "expert")),
        P(("group", "expert"), None),
        P("expert", "group", None),
        P("expert", "group", None),
        P("expert", "group", None),
        P("expert", "group", None),
    )
    body = fast_device if fits(mesh) else on_device
    return jax.shard_map(
        body, mesh=mesh, in_specs=in_specs, out_specs=out_specs, check_vma=False
    )
```

```python
import functools

import jax
import jax.numpy as jnp
from jax import lax
from jax.experimental import pallas as pl
from jax.experimental.pallas import tpu as pltpu
from jax.sharding import PartitionSpec as P

HEADS = 16
HDIM = 128
CAP = 50


EPS = 1e-06
HIGH = lax.Precision.HIGHEST


def angles(positions):
    half = HDIM // 2
    freq = 10000.0 ** (-jnp.arange(half, dtype=jnp.float32) / half)
    turn = positions.astype(jnp.float32)[:, None] * freq[None, :]
    return (jnp.cos(turn), jnp.sin(turn))


def rotate(values, cosine, sine):
    count = values.shape[0]
    split = values.reshape(count, HEADS, 2, HDIM // 2)
    first = split[:, :, 0]
    second = split[:, :, 1]
    cosine = cosine[:, None, :]
    sine = sine[:, None, :]
    turned = jnp.stack([first * cosine - second * sine, second * cosine + first * sine], axis=2)
    return turned.reshape(count, HEADS * HDIM)


def routing(routes, gates, block_ids, owner, experts):
    local = routes.shape[0] // experts
    per = routes.reshape(experts, local, routes.shape[1])
    flat = per.reshape(experts, -1)
    ids = jnp.arange(experts, dtype=jnp.int32)
    onehot = (flat[:, :, None] == ids[None, None, :]).astype(jnp.int32)
    before = jnp.cumsum(onehot, axis=1) - onehot
    slots = jnp.sum(before * onehot, axis=2).reshape(per.shape)
    places = jnp.arange(CAP, dtype=jnp.int32)
    own_ids = lax.dynamic_index_in_dim(per, owner, 0, keepdims=False)
    own_slots = lax.dynamic_index_in_dim(slots, owner, 0, keepdims=False)
    sent = (
        (own_ids[None, None] == ids[:, None, None, None])
        & (own_slots[None, None] == places[None, :, None, None])
    ).astype(jnp.float32)
    pick = jnp.sum(sent, axis=3)
    weighted = jnp.sum(sent * gates[None, None], axis=3)
    arrived = ((per == owner)[:, None] & (slots[:, None] == places[None, :, None, None])).astype(
        jnp.int32
    )
    length = experts * local
    spots = jnp.arange(length, dtype=jnp.int32).reshape(experts, 1, local, 1)
    marks = block_ids.reshape(experts, 1, local, 1)
    valid = jnp.sum(arrived, axis=(2, 3)).reshape(-1)
    row_pos = jnp.sum(arrived * spots, axis=(2, 3)).reshape(-1)
    row_block = jnp.sum(arrived * marks, axis=(2, 3)).reshape(-1) + (1 - valid) * length
    return (pick, weighted, row_pos, row_block)


def score_block(queries, keys, row_block, key_block):
    count = queries.shape[0]
    raw = jnp.einsum(
        "rhd,khd->hrk",
        queries.reshape(count, HEADS, HDIM),
        keys.reshape(keys.shape[0], HEADS, HDIM),
        preferred_element_type=jnp.float32,
    )
    visible = key_block[None, None, :] <= row_block[None, :, None]
    return jnp.where(visible, raw * HDIM ** (-0.5), -1e30)


def spread(pick, normed):
    return jnp.einsum(
        "ect,td->ecd", pick.astype(jnp.bfloat16), normed, preferred_element_type=jnp.float32
    ).astype(jnp.bfloat16)


def collect(weights, arrived):
    return jnp.einsum("ect,ecd->td", weights, arrived.astype(jnp.float32), precision=HIGH)


def joined_rows(store, chosen, name):
    return jnp.concatenate([store[name][index] for index in chosen], axis=0)


def expert_reduce(store, chosen):
    pairs = (
        ("rows", "query_grad"),
        ("attended", "result_grad"),
        ("rows_two", "both_grad"),
        ("hidden", "down_grad"),
    )
    groups = lax.axis_size("group")
    results = []
    for left_name, right_name in pairs:
        left = joined_rows(store, chosen, left_name)
        right = joined_rows(store, chosen, right_name)

        def term(start, count, left=left, right=right):
            return jnp.einsum("rd,rf->df", left, right, preferred_element_type=jnp.float32)

        shard = lax.psum_scatter(
            term(jnp.int32(0), lax.axis_size("group") * (left.shape[1] // groups)).astype(
                jnp.bfloat16
            ),
            "group",
            scatter_dimension=0,
            tiled=True,
        ).astype(jnp.float32)
        results.append(shard[None])
    return tuple(results)


def reduce_all(store, chosen):
    expert_parts = expert_reduce(store, chosen)
    shared_term = jnp.einsum(
        "td,tf->df",
        joined_rows(store, chosen, "normed"),
        joined_rows(store, chosen, "mixed_grad"),
        preferred_element_type=jnp.float32,
    )
    gain_first = jnp.sum(joined_rows(store, chosen, "gain_first"), axis=0)
    gain_second = jnp.sum(joined_rows(store, chosen, "gain_second"), axis=0)
    shared_parts = (
        lax.psum_scatter(shared_term, ("group", "expert"), scatter_dimension=0, tiled=True),
        lax.psum_scatter(gain_first, ("group", "expert"), scatter_dimension=0, tiled=True),
        lax.psum_scatter(gain_second, ("group", "expert"), scatter_dimension=0, tiled=True),
    )
    return tuple(expert_parts) + tuple(shared_parts)


def on_device(
    tokens,
    cotangent,
    gain_attn,
    gain_mlp,
    w_kv,
    w_query,
    w_out,
    w_gate_up,
    w_down,
    att_routes,
    att_gates,
    mlp_routes,
    mlp_gates,
    blocks,
):
    experts = lax.axis_size("expert")
    owner = lax.axis_index("expert")
    shared_full = lax.all_gather(w_kv, ("group", "expert"), axis=0, tiled=True)
    gathered = (
        lax.all_gather(w_query, "group", axis=1, tiled=True),
        lax.all_gather(w_out, "group", axis=1, tiled=True),
        lax.all_gather(w_gate_up, "group", axis=1, tiled=True),
        lax.all_gather(w_down, "group", axis=1, tiled=True),
    )
    query_full = gathered[0][0]
    output_full = gathered[1][0]
    gate_up_full = gathered[2][0]
    down_full = gathered[3][0]
    micro = tokens.shape[0]
    local = tokens.shape[1]
    model = tokens.shape[2]
    length = local * experts
    width = HEADS * HDIM
    hidden_width = gate_up_full.shape[1] // 2
    own_cos, own_sin = angles(owner * local + jnp.arange(local, dtype=jnp.int32))
    names = (
        "rows",
        "query_grad",
        "attended",
        "result_grad",
        "rows_two",
        "both_grad",
        "hidden",
        "down_grad",
        "normed",
        "mixed_grad",
        "gain_first",
        "gain_second",
    )
    store = {name: [] for name in names}
    outputs = []
    input_grads = []
    for index in range(micro):
        inputs = tokens[index].astype(jnp.float32)
        block_ids = blocks[index, 0]
        att_pick, att_weight, row_pos, row_block = routing(
            att_routes[index], att_gates[index], block_ids, owner, experts
        )
        mlp_pick, mlp_weight, unused_pos, unused_block = routing(
            mlp_routes[index], mlp_gates[index], block_ids, owner, experts
        )
        scale = lax.rsqrt(jnp.mean(inputs * inputs, axis=1, keepdims=True) + EPS)
        normed = (inputs * scale * gain_attn).astype(jnp.bfloat16)
        mixed = jnp.dot(normed, shared_full, preferred_element_type=jnp.float32)
        keys_here = rotate(mixed[:, :width], own_cos, own_sin).astype(jnp.bfloat16)
        local_kv = jnp.concatenate([keys_here, mixed[:, width:].astype(jnp.bfloat16)], axis=1)
        sequence_kv = lax.all_gather(local_kv, "expert", axis=0, tiled=True)
        keys = sequence_kv[:, :width]
        values = sequence_kv[:, width:].reshape(length, HEADS, HDIM)
        rows = lax.all_to_all(
            spread(att_pick, normed), "expert", split_axis=0, concat_axis=0, tiled=True
        ).reshape(-1, model)
        row_cos, row_sin = angles(row_pos)
        queries = rotate(
            jnp.dot(rows, query_full, preferred_element_type=jnp.float32), row_cos, row_sin
        ).astype(jnp.bfloat16)
        scores = score_block(queries, keys, row_block, block_ids)
        top = jnp.max(scores, axis=2, keepdims=True)
        powers = jnp.exp(scores - top)
        total = jnp.sum(powers, axis=2, keepdims=True)
        log_total = top + jnp.log(total)
        probs = (powers / total).astype(jnp.bfloat16)
        attended = jnp.einsum("hrk,khd->rhd", probs, values, preferred_element_type=jnp.float32)
        attended = attended.reshape(-1, width).astype(jnp.bfloat16)
        result = jnp.dot(attended, output_full, preferred_element_type=jnp.float32).astype(
            jnp.bfloat16
        )
        back = lax.all_to_all(
            result.reshape(experts, CAP, model), "expert", split_axis=0, concat_axis=0, tiled=True
        )
        middle = inputs + collect(att_weight, back)
        scale_two = lax.rsqrt(jnp.mean(middle * middle, axis=1, keepdims=True) + EPS)
        normed_two = (middle * scale_two * gain_mlp).astype(jnp.bfloat16)
        rows_two = lax.all_to_all(
            spread(mlp_pick, normed_two), "expert", split_axis=0, concat_axis=0, tiled=True
        ).reshape(-1, model)
        both = jnp.dot(rows_two, gate_up_full, preferred_element_type=jnp.float32)
        gate = both[:, :hidden_width]
        up = both[:, hidden_width:]
        sigma = 1.0 / (1.0 + jnp.exp(-gate))
        hidden = (gate * sigma * up).astype(jnp.bfloat16)
        result_two = jnp.dot(hidden, down_full, preferred_element_type=jnp.float32).astype(
            jnp.bfloat16
        )
        back_two = lax.all_to_all(
            result_two.reshape(experts, CAP, model),
            "expert",
            split_axis=0,
            concat_axis=0,
            tiled=True,
        )
        final = middle + collect(mlp_weight, back_two)
        outputs.append(final.astype(jnp.bfloat16))
        upstream = cotangent[index].astype(jnp.float32)
        outgoing = jnp.einsum("ect,td->ecd", mlp_weight, upstream, precision=HIGH).astype(
            jnp.bfloat16
        )
        down_grad = lax.all_to_all(
            outgoing, "expert", split_axis=0, concat_axis=0, tiled=True
        ).reshape(-1, model)
        hidden_grad = jnp.einsum(
            "rd,fd->rf", down_grad, down_full, preferred_element_type=jnp.float32
        )
        slope = sigma * (1.0 + gate * (1.0 - sigma))
        both_grad = jnp.concatenate(
            [hidden_grad * up * slope, hidden_grad * gate * sigma], axis=1
        ).astype(jnp.bfloat16)
        row_grad_two = jnp.einsum(
            "rf,df->rd", both_grad, gate_up_full, preferred_element_type=jnp.float32
        ).astype(jnp.bfloat16)
        returned_two = lax.all_to_all(
            row_grad_two.reshape(experts, CAP, model),
            "expert",
            split_axis=0,
            concat_axis=0,
            tiled=True,
        )
        normed_two_grad = collect(mlp_pick, returned_two)
        scaled_two = normed_two_grad * gain_mlp
        gain_second = jnp.sum(normed_two_grad * middle * scale_two, axis=0, keepdims=True)
        middle_grad = (
            upstream
            + scale_two * scaled_two
            - middle * scale_two**3 * jnp.mean(scaled_two * middle, axis=1, keepdims=True)
        )
        outgoing_att = jnp.einsum("ect,td->ecd", att_weight, middle_grad, precision=HIGH).astype(
            jnp.bfloat16
        )
        result_grad = lax.all_to_all(
            outgoing_att, "expert", split_axis=0, concat_axis=0, tiled=True
        ).reshape(-1, model)
        attended_grad = jnp.einsum(
            "rd,fd->rf", result_grad, output_full, preferred_element_type=jnp.float32
        ).astype(jnp.bfloat16)
        again = jnp.exp(score_block(queries, keys, row_block, block_ids) - log_total)
        heads_grad = attended_grad.reshape(-1, HEADS, HDIM)
        value_grad = jnp.einsum(
            "hrk,rhd->khd",
            again.astype(jnp.bfloat16),
            heads_grad,
            preferred_element_type=jnp.float32,
        )
        prob_grad = jnp.einsum(
            "rhd,khd->hrk", heads_grad, values, preferred_element_type=jnp.float32
        )
        inner = jnp.sum(again * prob_grad, axis=2, keepdims=True)
        raw_grad = (again * (prob_grad - inner) * HDIM ** (-0.5)).astype(jnp.bfloat16)
        query_grad = jnp.einsum(
            "hrk,khd->rhd",
            raw_grad,
            keys.reshape(length, HEADS, HDIM),
            preferred_element_type=jnp.float32,
        ).reshape(-1, width)
        query_grad = rotate(query_grad, row_cos, -row_sin).astype(jnp.bfloat16)
        key_grad = jnp.einsum(
            "hrk,rhd->khd",
            raw_grad,
            queries.reshape(-1, HEADS, HDIM),
            preferred_element_type=jnp.float32,
        ).reshape(length, width)
        row_grad = jnp.einsum(
            "rf,df->rd", query_grad, query_full, preferred_element_type=jnp.float32
        ).astype(jnp.bfloat16)
        returned = lax.all_to_all(
            row_grad.reshape(experts, CAP, model), "expert", split_axis=0, concat_axis=0, tiled=True
        )
        kv_grad = lax.psum_scatter(
            jnp.concatenate([key_grad, value_grad.reshape(length, width)], axis=1).astype(
                jnp.bfloat16
            ),
            "expert",
            scatter_dimension=0,
            tiled=True,
        ).astype(jnp.float32)
        mixed_grad = jnp.concatenate(
            [rotate(kv_grad[:, :width], own_cos, -own_sin), kv_grad[:, width:]], axis=1
        ).astype(jnp.bfloat16)
        normed_grad = collect(att_pick, returned) + jnp.einsum(
            "tf,df->td", mixed_grad, shared_full, preferred_element_type=jnp.float32
        )
        scaled = normed_grad * gain_attn
        gain_first = jnp.sum(normed_grad * inputs * scale, axis=0, keepdims=True)
        input_grad = (
            middle_grad
            + scale * scaled
            - inputs * scale**3 * jnp.mean(scaled * inputs, axis=1, keepdims=True)
        )
        input_grads.append(input_grad.astype(jnp.bfloat16))
        kept = (
            rows,
            query_grad,
            attended,
            result_grad,
            rows_two,
            both_grad,
            hidden,
            down_grad,
            normed,
            mixed_grad,
            gain_first,
            gain_second,
        )
        for name, value in zip(names, kept):
            store[name].append(value)
    reduced = reduce_all(store, list(range(micro)))
    grad_query, grad_out, grad_gate_up, grad_down, grad_kv, grad_gain_attn, grad_gain_mlp = reduced
    return (
        jnp.stack(outputs, axis=0),
        jnp.stack(input_grads, axis=0),
        grad_gain_attn,
        grad_gain_mlp,
        grad_kv,
        grad_query,
        grad_out,
        grad_gate_up,
        grad_down,
    )


ZS, YS, XS, CS = 4, 2, 2, 2
SEQ = 320
MICRO = 2
KINDS = 9
F32 = jnp.float32
BF16 = jnp.bfloat16


def fits(mesh):
    return mesh.shape["group"] == ZS * YS and mesh.shape["expert"] == XS * CS


def group_move(value, move):
    pairs = []
    for z in range(ZS):
        for y in range(YS):
            to_z, to_y = move(z, y)
            pairs.append((z * YS + y, to_z * YS + to_y))
    return lax.ppermute(value, "group", pairs)


def z_move(value, step):
    return group_move(value, lambda z, y: ((z + step) % ZS, y))


def y_move(value):
    return group_move(value, lambda z, y: (z, 1 - y))


def x_move(value):
    return lax.ppermute(value, "expert", [(x * CS + c, (1 - x) * CS + c) for x in range(XS) for c in range(CS)])


def c_move(value):
    return lax.ppermute(value, "expert", [(x * CS + c, x * CS + 1 - c) for x in range(XS) for c in range(CS)])


def z_exchange(value):
    columns = [[z * YS + y for z in range(ZS)] for y in range(YS)]
    return lax.all_to_all(
        value, "group", split_axis=0, concat_axis=0, tiled=True, axis_index_groups=columns
    )


def gather_tokens(own):
    column = jnp.stack([own] + [z_move(own, -step) for step in range(1, ZS)], axis=0)
    plane = jnp.stack([column, x_move(column)], axis=1)
    plane = plane.reshape((ZS, XS * own.shape[0]) + own.shape[1:])
    return jnp.stack([plane, c_move(plane)], axis=0)


def reduce_tokens(other, mine):
    local = mine.shape[1] // XS
    total = mine.astype(F32) + c_move(other).astype(F32)
    arrived = x_move(total[:, local:].astype(BF16))
    total = total[:, :local] + arrived.astype(F32)
    result = total[0]
    for step in range(1, ZS):
        result = result + z_move(total[step].astype(BF16), step).astype(F32)
    return result


def merge(index, own, other, axis):
    return jnp.where(index == 0, jnp.stack([own, other], axis), jnp.stack([other, own], axis))


def take(value, index, axis):
    return lax.dynamic_index_in_dim(value, index, axis, keepdims=False)


def dot(left, right):
    return jnp.dot(left, right, preferred_element_type=F32)


def dot_t(left, right):
    return lax.dot_general(left, right, (((1,), (1,)), ((), ())), preferred_element_type=F32)


def dot_l(left, right):
    return lax.dot_general(left, right, (((0,), (0,)), ((), ())), preferred_element_type=F32)


def turned(value, cosine, sine):
    return value * cosine + pltpu.roll(value, HDIM // 2, 1) * sine


def masked_probs(query, key, row_block, key_block):
    scores = jnp.where(key_block <= row_block, dot_t(query, key) * HDIM ** (-0.5), -1e30)
    powers = jnp.exp(scores - jnp.max(scores, axis=1, keepdims=True))
    return powers / jnp.sum(powers, axis=1, keepdims=True)


MESH = pl.DeviceIdType.MESH
ORDER = (3, 1, 2, 0)
STEP = 16
DMA = pltpu.SemaphoreType.DMA
ANY = pl.BlockSpec(memory_space=pl.ANY)
VMEM = pl.BlockSpec(memory_space=pltpu.VMEM)


def by_rows(rows, body):
    def step(index, carry):
        body(pl.ds(pl.multiple_of(index * STEP, STEP), STEP))
        return carry

    lax.fori_loop(0, rows // STEP, step, 0)


class Place:
    def __init__(self):
        group, owner = lax.axis_index("group"), lax.axis_index("expert")
        self.z, self.y = lax.div(group, YS), lax.rem(group, YS)
        self.x, self.core = lax.div(owner, CS), lax.rem(owner, CS)
        self.group, self.owner = group, owner

        def device(z, y, x, core):
            return (z * YS + y, x * CS + core)

        self.x_peer = device(self.z, self.y, 1 - self.x, self.core)
        self.y_peer = device(self.z, 1 - self.y, self.x, self.core)
        self.core_peer = device(self.z, self.y, self.x, 1 - self.core)
        self.z_peers = [device(lax.rem(self.z + step, ZS), self.y, self.x, self.core) for step in range(ZS)]

    def enter(self, with_y):
        peers = [self.x_peer, self.core_peer] + self.z_peers[1:] + ([self.y_peer] if with_y else [])
        barrier = pltpu.get_barrier_semaphore()
        for peer in peers:
            pl.semaphore_signal(barrier, inc=1, device_id=peer, device_id_type=MESH)
        pl.semaphore_wait(barrier, len(peers))


def remote(src, dst, send, arrive, peer):
    return pltpu.make_async_remote_copy(
        src_ref=src, dst_ref=dst, send_sem=send, recv_sem=arrive, device_id=peer, device_id_type=MESH
    )


class Reduce:
    @staticmethod
    def scratch(micro, rows, model):
        return [
            pltpu.VMEM((micro, ZS, XS, rows, model), BF16),
            pltpu.VMEM((micro, ZS, XS, rows, model), BF16),
            pltpu.VMEM((micro, ZS, rows, model), BF16),
            pltpu.VMEM((micro, 2, ZS - 1, rows, model), BF16),
            pltpu.VMEM((micro, rows, model), F32),
            DMA((micro, ZS, XS)),
            DMA((micro, ZS, XS)),
            DMA((micro, ZS, XS)),
            DMA((micro, ZS)),
            DMA((micro, ZS)),
            DMA((micro, 2, ZS)),
            DMA((micro, 2, ZS)),
        ]

    def __init__(self, place, part, refs):
        self.place, self.part = place, part
        self.core_in, self.kept, self.x_in, self.z_in, self.total = [refs.pop(0) for _ in range(5)]
        self.sems = [refs.pop(0) for _ in range(7)]
        self.micro, self.rows = part.shape[0], part.shape[4]

    def core_copy(self, m, k, dx):
        send, arrive = self.sems[:2]
        return remote(
            self.part.at[m, k, 1, dx],
            self.core_in.at[m, k, dx],
            send.at[m, k, dx],
            arrive.at[m, k, dx],
            self.place.core_peer,
        )

    def kept_copy(self, m, k, dx):
        return pltpu.make_async_copy(
            self.part.at[m, k, 0, dx], self.kept.at[m, k, dx], self.sems[2].at[m, k, dx]
        )

    def x_copy(self, m, k):
        send, arrive = self.sems[3:5]
        return remote(
            self.core_in.at[m, k, 1], self.x_in.at[m, k], send.at[m, k], arrive.at[m, k], self.place.x_peer
        )

    def z_copy(self, m, down, far):
        send, arrive = self.sems[5:7]
        return remote(
            self.x_in.at[m, ZS - far if down else far],
            self.z_in.at[m, down, far - 1],
            send.at[m, down, far - 1],
            arrive.at[m, down, far - 1],
            self.place.z_peers[ZS - 1 if down else 1],
        )

    def begin(self):
        for m in range(self.micro):
            for dx in (1, 0):
                for k in ORDER:
                    self.core_copy(m, k, dx).start()
                    self.kept_copy(m, k, dx).start()

    def pass_x(self, m):
        for k in ORDER:
            self.core_copy(m, k, 1).wait_recv()
            self.kept_copy(m, k, 1).wait()

            def add(span, k=k):
                value = self.core_in[m, k, 1, span, :].astype(F32) + self.kept[m, k, 1, span, :].astype(F32)
                self.core_in[m, k, 1, span, :] = value.astype(BF16)

            by_rows(self.rows, add)
            self.x_copy(m, k).start()

    def z_unit(self, m, k):
        self.x_copy(m, k).wait_recv()
        self.core_copy(m, k, 0).wait_recv()
        self.kept_copy(m, k, 0).wait()

        def add(span):
            value = (
                self.x_in[m, k, span, :].astype(F32)
                + self.core_in[m, k, 0, span, :].astype(F32)
                + self.kept[m, k, 0, span, :].astype(F32)
            )
            if k:
                self.x_in[m, k, span, :] = value.astype(BF16)
            else:
                self.total[m, span, :] = value

        by_rows(self.rows, add)

    def beyond(self, down, far):
        return self.place.z >= far if down else self.place.z + far < ZS

    def chain(self, m, far):
        for down in (0, 1):

            def send(down=down):
                if far < ZS - 1:
                    pl.when(self.beyond(1 - down, 1))(functools.partial(self.join, m, down, far))
                self.z_copy(m, down, far).start()

            pl.when(self.beyond(down, far))(send)

    def join(self, m, down, far):
        self.z_copy(m, down, far + 1).wait_recv()
        place = ZS - far if down else far

        def add(span):
            value = self.x_in[m, place, span, :].astype(F32) + self.z_in[m, down, far, span, :].astype(F32)
            self.x_in[m, place, span, :] = value.astype(BF16)

        by_rows(self.rows, add)

    def finish(self, m):
        for down in (0, 1):

            def last(down=down):
                self.z_copy(m, down, 1).wait_recv()

                def add(span):
                    self.total[m, span, :] += self.z_in[m, down, 0, span, :].astype(F32)

                by_rows(self.rows, add)

            pl.when(self.beyond(1 - down, 1))(last)

    def sums(self, m):
        for turn, k in enumerate(ORDER):
            self.z_unit(m, k)
            if turn:
                self.chain(m, ZS - turn)

    def run(self):
        self.begin()
        for m in range(self.micro):
            self.pass_x(m)
        for m in range(self.micro):
            self.sums(m)

    def drain(self):
        for m in range(self.micro):
            for k in ORDER:
                for dx in range(XS):
                    self.core_copy(m, k, dx).wait_send()
                self.x_copy(m, k).wait_send()
            for down in (0, 1):
                for far in range(1, ZS):
                    pl.when(self.beyond(down, far))(self.z_copy(m, down, far).wait_send)


class Gather:
    @staticmethod
    def scratch(micro):
        return [
            DMA((micro,)),
            DMA((micro, ZS)),
            DMA((micro, ZS)),
            DMA((micro, ZS)),
            DMA((micro, ZS, XS)),
            DMA((micro, ZS, CS, XS)),
        ]

    def __init__(self, place, own, out, refs):
        self.place, self.own, self.out = place, own, out
        self.sems = [refs.pop(0) for _ in range(6)]
        self.micro = out.shape[0]

    def slot(self, m, k, dc, dx):
        return self.out.at[m, k, dc, dx]

    def local(self, m):
        return pltpu.make_async_copy(self.own.at[m], self.slot(m, 0, 0, 0), self.sems[0].at[m])

    def up(self, m, source, k):
        return remote(
            source, self.slot(m, k, 0, 0), self.sems[1].at[m, k], self.sems[5].at[m, k, 0, 0], self.place.z_peers[1]
        )

    def down(self, m, source, k):
        return remote(
            source,
            self.slot(m, k, 0, 0),
            self.sems[2].at[m, k],
            self.sems[5].at[m, k, 0, 0],
            self.place.z_peers[ZS - 1],
        )

    def over_x(self, m, source, k):
        return remote(
            source, self.slot(m, k, 0, 1), self.sems[3].at[m, k], self.sems[5].at[m, k, 0, 1], self.place.x_peer
        )

    def over_core(self, m, source, k, dx):
        return remote(
            source,
            self.slot(m, k, 1, dx),
            self.sems[4].at[m, k, dx],
            self.sems[5].at[m, k, 1, dx],
            self.place.core_peer,
        )

    def send_own(self, m):
        source, z = self.own.at[m], self.place.z
        pl.when(z < ZS - 1)(lambda: self.up(m, source, ZS - 1).start())
        pl.when(z > 0)(lambda: self.down(m, source, 1).start())
        self.over_x(m, source, 0).start()
        self.over_core(m, source, 0, 0).start()
        self.local(m).start()

    def pass_on(self, m, k):
        self.over_x(m, self.slot(m, k, 0, 0), k).start()
        self.over_core(m, self.slot(m, k, 0, 0), k, 0).start()

    def from_above(self, m, far):
        self.up(m, self.own.at[m], far).wait_recv()
        pl.when(self.place.z > 0)(lambda: self.down(m, self.slot(m, far, 0, 0), far + 1).start())
        self.pass_on(m, far)

    def from_below(self, m, far):
        self.up(m, self.own.at[m], ZS - far).wait_recv()
        source = self.slot(m, ZS - far, 0, 0)
        pl.when(self.place.z < ZS - 1)(lambda: self.up(m, source, ZS - far - 1).start())
        self.pass_on(m, ZS - far)

    def z_arrival(self, m, far):
        pl.when(self.place.z + far < ZS)(lambda: self.from_above(m, far))
        pl.when(self.place.z - far >= 0)(lambda: self.from_below(m, far))

    def x_arrival(self, m, k):
        self.over_x(m, self.own.at[m], k).wait_recv()
        self.over_core(m, self.slot(m, k, 0, 1), k, 1).start()

    def piece_arrival(self, m, k):
        for dx in range(XS):
            self.over_core(m, self.own.at[m], k, dx).wait_recv()

    def arrivals(self, m=0):
        for k in range(ZS):
            self.piece_arrival(m, k)
        self.local(m).wait()

    def z_round(self, far, chosen=None):
        for m in range(self.micro) if chosen is None else [chosen]:
            self.z_arrival(m, far)

    def x_round(self, far, chosen=None):
        for m in range(self.micro) if chosen is None else [chosen]:
            if far == 0:
                self.x_arrival(m, 0)
            else:
                pl.when(self.place.z + far < ZS)(lambda: self.x_arrival(m, far))
                pl.when(self.place.z - far >= 0)(lambda: self.x_arrival(m, ZS - far))

    def run(self):
        self.z_round(1)
        self.x_round(0)
        self.z_round(2)
        self.x_round(1)
        self.z_round(3)
        self.x_round(2)
        self.x_round(3)

    def drain(self, waited=False):
        z = self.place.z
        for m in range(self.micro):
            own = self.own.at[m]
            if not waited:
                self.arrivals(m)
            pl.when(z < ZS - 1)(lambda: self.up(m, own, ZS - 1).wait_send())
            pl.when(z > 0)(lambda: self.down(m, own, 1).wait_send())
            for far in range(1, ZS - 1):
                pl.when((z + far < ZS) & (z > 0))(lambda: self.down(m, own, far + 1).wait_send())
                pl.when((z - far >= 0) & (z < ZS - 1))(lambda: self.up(m, own, ZS - far - 1).wait_send())
            for k in range(ZS):
                self.over_x(m, own, k).wait_send()
                for dx in range(XS):
                    self.over_core(m, own, k, dx).wait_send()


class PieceReduce(Reduce):
    @staticmethod
    def scratch(micro, rows, model):
        return [
            pltpu.VMEM((micro, ZS, CS * XS * rows, model), BF16),
            pltpu.VMEM((micro, ZS, XS, rows, model), BF16),
            pltpu.VMEM((micro, ZS, rows, model), BF16),
            pltpu.VMEM((micro, 2, ZS - 1, rows, model), BF16),
            pltpu.VMEM((micro, rows, model), F32),
            DMA((micro, ZS, XS)),
            DMA((micro, ZS, XS)),
            DMA((micro, ZS)),
            DMA((micro, ZS)),
            DMA((micro, 2, ZS)),
            DMA((micro, 2, ZS)),
        ]

    def __init__(self, place, refs):
        self.place = place
        self.part, self.core_in, self.x_in, self.z_in, self.total = [refs.pop(0) for _ in range(5)]
        core_send, core_recv, x_send, x_recv, z_send, z_recv = [refs.pop(0) for _ in range(6)]
        self.sems = [core_send, core_recv, None, x_send, x_recv, z_send, z_recv]
        self.micro, self.rows = self.total.shape[0], self.total.shape[1]

    def unit(self, m, k, dc, dx):
        return self.part.at[m, k, pl.ds((dc * XS + dx) * self.rows, self.rows)]

    def core_copy(self, m, k, dx):
        send, arrive = self.sems[:2]
        return remote(
            self.unit(m, k, 1, dx),
            self.core_in.at[m, k, dx],
            send.at[m, k, dx],
            arrive.at[m, k, dx],
            self.place.core_peer,
        )

    def begin_piece(self, m, k):
        for dx in (1, 0):
            self.core_copy(m, k, dx).start()

    def x_piece(self, m, k):
        self.core_copy(m, k, 1).wait_recv()
        kept = self.unit(m, k, 0, 1)

        def add(span):
            value = self.core_in[m, k, 1, span, :].astype(F32) + kept[span, :].astype(F32)
            self.core_in[m, k, 1, span, :] = value.astype(BF16)

        by_rows(self.rows, add)
        self.x_copy(m, k).start()

    def z_piece(self, m, k):
        self.x_copy(m, k).wait_recv()
        self.core_copy(m, k, 0).wait_recv()
        kept = self.unit(m, k, 0, 0)

        def sum_of(span):
            return (
                self.x_in[m, k, span, :].astype(F32)
                + self.core_in[m, k, 0, span, :].astype(F32)
                + kept[span, :].astype(F32)
            )

        def away(span):
            self.x_in[m, k, span, :] = sum_of(span).astype(BF16)

        def here(span):
            self.total[m, span, :] = sum_of(span)

        pl.when(k != 0)(lambda: by_rows(self.rows, away))
        pl.when(k == 0)(lambda: by_rows(self.rows, here))

    def drain(self):
        for m in range(self.micro):
            for k in range(ZS):
                for dx in range(XS):
                    self.core_copy(m, k, dx).wait_send()
                self.x_copy(m, k).wait_send()
            for down in (0, 1):
                for far in range(1, ZS):
                    pl.when(self.beyond(down, far))(self.z_copy(m, down, far).wait_send)


def piece_of(place, index, outward=False):
    turn = lax.rem(index, ZS)
    if outward:
        turn = ZS - 1 - turn
    inner = turn + lax.div(turn, 2) * (5 - 2 * turn)
    last = lax.rem(ZS - turn, ZS)
    z = place.z
    return lax.div(index, ZS), jnp.where(z == 0, turn, jnp.where(z == ZS - 1, last, inner))


def run_pieces(place, reduce, piece, between, outward=False):
    pieces = reduce.micro * ZS

    def step(index, carry):
        @pl.when(index < pieces)
        def _():
            m, k = piece_of(place, index, outward)
            piece(index, m, k)
            reduce.begin_piece(m, k)

        between(index)

        @pl.when((index >= 1) & (index < pieces + 1))
        def _():
            reduce.x_piece(*piece_of(place, index - 1, outward))

        @pl.when((index >= 3) & (index < pieces + 3))
        def _():
            reduce.z_piece(*piece_of(place, index - 3, outward))

        for m in range(reduce.micro):
            first = m * ZS + 3 if outward else (m + 1) * ZS + 2
            for far in range(1, ZS):
                pl.when(index == first + ZS - 1 - far)(functools.partial(reduce.chain, m, far))
        return carry

    lax.fori_loop(0, pieces + 5, step, 0)


def begin_gathers(gathers):
    for m in range(gathers[0].micro):
        for gather in gathers:
            gather.send_own(m)
        if m == 0:
            for gather in gathers:
                gather.z_round(1, 0)
            for gather in gathers:
                gather.x_round(0, 0)


def gather_steps(gathers, index):
    for m in range(gathers[0].micro):
        for far in range(0 if m else 1, ZS):

            @pl.when(index == (max(0, m * (ZS - 2) - 1) + far if m else far - 1))
            def _(m=m, far=far):
                for gather in gathers:
                    if far + 1 < ZS:
                        gather.z_round(far + 1, m)
                for gather in gathers:
                    gather.x_round(far, m)


def wait_local(gather, m):
    gather.local(m).wait()


def by_lanes(count, width, body):
    def step(index, carry):
        body(pl.ds(pl.multiple_of(index * width, width), width))
        return carry

    lax.fori_loop(0, count, step, 0)


class Spread:
    @staticmethod
    def scratch(pieces, depth):
        return [DMA((pieces,)), DMA((ZS, pieces)), DMA((ZS, pieces))] + [
            DMA((ZS << step,)) for step in range(depth) for _ in range(2)
        ]

    def __init__(self, place, sources, targets, view, depth, refs):
        self.place, self.sources, self.targets, self.view, self.depth = place, sources, targets, view, depth
        self.local_sem, self.z_send, self.z_recv = [refs.pop(0) for _ in range(3)]
        self.sems = [(refs.pop(0), refs.pop(0)) for _ in range(depth)]
        self.pieces = self.local_sem.shape[0]

    def z_copy(self, step, piece):
        place = self.place
        mine = self.targets(self.view(place.z, place.y, place.x, place.core))
        return remote(
            self.sources(lax.rem(place.z + step, ZS))[piece],
            mine[piece],
            self.z_send.at[step, piece],
            self.z_recv.at[step, piece],
            place.z_peers[step],
        )

    def local(self, piece):
        place = self.place
        mine = self.targets(self.view(place.z, place.y, place.x, place.core))
        return pltpu.make_async_copy(self.sources(place.z)[piece], mine[piece], self.local_sem.at[piece])

    def hop(self, axis, index):
        place = self.place
        z = lax.rem(place.z - (index >> axis) + ZS, ZS)
        y = place.y if axis < 1 else (place.y + ((index >> (axis - 1)) & 1)) % 2
        x = place.x if axis < 2 else (place.x + (index & 1)) % 2
        block = self.view(z, y, x, place.core)
        peer = (place.y_peer, place.x_peer, place.core_peer)[axis]
        send, arrive = self.sems[axis]
        return remote(block, block, send.at[index], arrive.at[index], peer)

    def begin(self):
        for piece in range(self.pieces):
            self.local(piece).start()
        for step in (1, 3, 2):
            for piece in range(self.pieces):
                self.z_copy(step, piece).start()

    def forward(self, axis, index):
        for later in range(axis, self.depth):
            self.hop(later, index << (later - axis)).start()

    def send(self, step):
        for piece in range(self.pieces):
            (self.z_copy(step, piece) if step else self.local(piece)).start()

    def z_round(self, step):
        for piece in range(self.pieces):
            if step:
                self.z_copy(step, piece).wait_recv()
            else:
                self.local(piece).wait()
        self.forward(0, step)

    def hop_round(self, axis, index):
        self.hop(axis, index).wait_recv()
        self.forward(axis + 1, index * 2 + 1)

    def drain(self):
        for step in range(1, ZS):
            for piece in range(self.pieces):
                self.z_copy(step, piece).wait_send()
        for axis in range(self.depth):
            for index in range(ZS << axis):
                self.hop(axis, index).wait_send()


class Share:
    @staticmethod
    def scratch(pieces):
        return [DMA((pieces,)), DMA((pieces,)), DMA((pieces,))]

    def __init__(self, place, blocks, refs):
        local, send, arrive = [refs.pop(0) for _ in range(3)]
        self.copies = []
        for index, (source, target) in enumerate(blocks):
            self.copies.append(pltpu.make_async_copy(source, target, local.at[index]))
            self.copies.append(remote(source, target, send.at[index], arrive.at[index], place.y_peer))

    def begin(self):
        for copy in self.copies:
            copy.start()

    def drain(self):
        for copy in self.copies:
            copy.wait()


def normed_rows(rows, gain):
    return rows * lax.rsqrt(jnp.mean(rows * rows, axis=1, keepdims=True) + EPS) * gain


def norm_back(grad, rows, upstream, gain):
    scale = lax.rsqrt(jnp.mean(rows * rows, axis=1, keepdims=True) + EPS)
    scaled = grad * gain
    inner = jnp.mean(scaled * rows, axis=1, keepdims=True)
    return upstream + scale * scaled - rows * (scale * scale * scale) * inner, grad * rows * scale


def y_half(place, target, rows):
    return target.at[pl.ds(pl.multiple_of(place.y * rows, rows), rows)]


def by_heads(width, body):
    def step(head, carry):
        body(lambda kind: pl.ds(pl.multiple_of(kind * width + head * HDIM, HDIM), HDIM))
        return carry

    lax.fori_loop(0, width // HDIM, step, 0)


def columns_of(marks, place, m, k):
    local, lanes = marks.shape[3:]
    length = CS * XS * local
    block = marks[k].reshape(length, lanes)
    across = jnp.transpose(block)

    def pick(kind, source, axis):
        value = None
        for index in range(MICRO):
            at = index * KINDS + kind
            part = source[:, at : at + 1] if axis else source[at : at + 1, :]
            value = part if value is None else jnp.where(m == index, part, value)
        return value

    owner = place.owner.astype(F32)
    gates = [jnp.where(pick(kind, block, 1) == owner, pick(kind + 2, block, 1), 0.0) for kind in range(2)]
    return gates[0] + gates[1], pick(KINDS - 1, block, 1), pick(KINDS - 1, across, 0)


def attention_kernel(
    sizes,
    tokens,
    cotangent,
    first_gain,
    second_gain,
    table,
    cosine,
    sine,
    w_kv,
    w_query,
    w_out,
    w_gate_up,
    w_down,
    *refs,
):
    refs = list(refs)
    normed_out, middle_out, everyone, cotangent_out, table_out, turned_out, attended_out = [
        refs.pop(0) for _ in range(7)
    ]
    qkv_weight, out_weight, gate_up_weight, down_weight = [refs.pop(0) for _ in range(4)]
    wide, kv_rows, model_rows, out_rows, down_rows = sizes
    place = Place()
    own = refs.pop(0)
    normed = Gather(place, own, everyone, refs)
    upstream = Gather(place, cotangent, cotangent_out, refs)
    tables = Gather(place, table, table_out, refs)
    reduce = PieceReduce(place, refs)

    def lanes(start, width):
        return pl.ds(pl.multiple_of(start, HDIM), width)

    def kv_view(z, y, x, core):
        row = ((z * YS + y) * (XS * CS) + x * CS + core) * kv_rows
        return qkv_weight.at[pl.ds(pl.multiple_of(row, kv_rows), kv_rows), pl.ds(wide, 2 * wide)]

    def rows_of(z, y):
        return pl.ds(pl.multiple_of((z * YS + y) * model_rows, model_rows), model_rows)

    kv = Spread(
        place,
        lambda z: [w_kv.at[:, lanes((kind * ZS + z) * wide, wide)] for kind in range(2)],
        lambda block: [block.at[:, pl.ds(kind * wide, wide)] for kind in range(2)],
        kv_view,
        3,
        refs,
    )
    query = Spread(
        place,
        lambda z: [w_query.at[0, :, lanes(z * wide, wide)]],
        lambda block: [block],
        lambda z, y, x, core: qkv_weight.at[rows_of(z, y), pl.ds(0, wide)],
        1,
        refs,
    )
    hidden_width = gate_up_weight.shape[2]
    gate_up = Spread(
        place,
        lambda z: [w_gate_up.at[0, :, lanes((kind * ZS + z) * hidden_width, hidden_width)] for kind in range(2)],
        lambda block: [block.at[kind] for kind in range(2)],
        lambda z, y, x, core: gate_up_weight.at[:, rows_of(z, y)],
        1,
        refs,
    )
    shared = Share(place, [(w_out.at[0], y_half(place, out_weight, out_rows))], refs)
    down = Share(place, [(w_down.at[0], y_half(place, down_weight, down_rows))], refs)
    arrived, qkv, attended, marks, weight, out_here, load, store, late_load = [refs.pop(0) for _ in range(9)]
    model = tokens.shape[2]
    tile = model // 2
    late_loads = [
        pltpu.make_async_copy(qkv_weight, weight, late_load.at[0]),
        pltpu.make_async_copy(out_weight, out_here, late_load.at[1]),
        pltpu.make_async_copy(table_out.at[0], marks, late_load.at[2]),
    ]

    def stores(sequence):
        return [
            pltpu.make_async_copy(qkv, turned_out.at[sequence], store.at[0]),
            pltpu.make_async_copy(attended, attended_out.at[sequence], store.at[1]),
        ]

    def piece(index, m, k):
        sequence = m * ZS + k
        normed.piece_arrival(m, k)
        pl.when(k == 0)(functools.partial(wait_local, normed, m))
        loads = [
            pltpu.make_async_copy(everyone.at[m, k, dc, dx], arrived.at[dc, dx], load.at[dc, dx])
            for dc in range(CS)
            for dx in range(XS)
        ]
        for copy in loads:
            copy.start()

        @pl.when(index == 0)
        def _():
            for copy in late_loads:
                copy.wait()

        @pl.when(index > 0)
        def _():
            for copy in stores(0):
                copy.wait()

        row_gate, row_block, key_block = columns_of(marks, place, m, k)
        for copy in loads:
            copy.wait()
        length = qkv.shape[0]
        for kind in range(3):
            value = dot(arrived[...].reshape(length, model), weight[:, kind * wide : (kind + 1) * wide])
            for head in range(wide // HDIM):
                part = value[:, head * HDIM : (head + 1) * HDIM]
                if kind < 2:
                    part = turned(part, cosine[...], sine[...])
                start = kind * wide + head * HDIM
                qkv[:, start : start + HDIM] = part.astype(BF16)

        def head(span_of):
            query, key, value = [qkv[:, span_of(kind)] for kind in range(3)]
            probs = masked_probs(query, key, row_block, key_block).astype(BF16)
            attended[:, span_of(0)] = dot(probs, value).astype(BF16)

        by_heads(wide, head)
        for start in range(0, model, tile):
            value = dot(attended[...], out_here[:, start : start + tile]) * row_gate
            reduce.part[m, k, :, start : start + tile] = value.astype(BF16)
        for copy in stores(sequence):
            copy.start()

    def between(index):
        due = {
            2: [lambda: gate_up.z_round(1)],
            3: [lambda: gate_up.z_round(3)],
            4: [lambda: upstream.send_own(0)],
            5: [lambda: gate_up.z_round(2), lambda: upstream.send_own(1)],
            6: [lambda: upstream.z_round(1)],
            7: [lambda: upstream.x_round(0), lambda: upstream.z_round(2)],
            8: [lambda: upstream.x_round(1), lambda: upstream.z_round(3)],
            9: [lambda: upstream.x_round(2)],
            10: [lambda: upstream.x_round(3)],
        }
        for at, tasks in due.items():

            @pl.when(index == at)
            def _(tasks=tasks):
                for task in tasks:
                    task()

    place.enter(True)
    shared.begin()
    kv.begin()
    tables.send_own(0)
    for m in range(normed.micro):

        def body(span, m=m):
            own[m, span, :] = normed_rows(tokens[m, span, :].astype(F32), first_gain[...]).astype(BF16)

        by_rows(tokens.shape[1], body)
        normed.send_own(m)
    query.begin()
    kv.z_round(0)
    tables.z_round(1)
    kv.z_round(1)
    kv.z_round(3)
    normed.z_round(1)
    kv.z_round(2)
    for index in (0, 1, 3, 2):
        kv.hop_round(0, index)
    normed.x_round(0)
    for step in (0, 1, 3):
        gate_up.send(step)
    gate_up.z_round(0)
    tables.z_round(2)
    normed.z_round(2)
    normed.x_round(1)
    for step in (0, 1, 3, 2):
        query.z_round(step)
    for index in (0, 2, 6, 4, 1, 3, 7, 5):
        kv.hop_round(1, index)
    normed.z_round(3)
    tables.z_round(3)
    for far in range(ZS):
        tables.x_round(far)
    normed.x_round(2)
    normed.x_round(3)
    for index in range(ZS << 2):
        kv.hop_round(2, index)
    for index in range(ZS):
        query.hop_round(0, index)
    shared.drain()
    tables.arrivals()
    for copy in late_loads:
        copy.start()
    gate_up.send(2)
    down.begin()
    run_pieces(place, reduce, piece, between, True)
    for m in range(reduce.micro):
        reduce.finish(m)

        def body(span, m=m):
            middle = tokens[m, span, :].astype(F32) + reduce.total[m, span, :]
            middle_out[m, span, :] = middle
            normed_out[m, span, :] = normed_rows(middle, second_gain[...]).astype(BF16)

        by_rows(reduce.rows, body)
    for copy in stores(0):
        copy.wait()
    for index in range(ZS):
        gate_up.hop_round(0, index)
    for gather in (tables, normed):
        gather.drain(True)
    for part in (upstream, kv, query, gate_up, down, reduce):
        part.drain()


def attend_back_kernel(
    rows, weight_in, out_in, marks, cosine, sine, turned_qkv, tokens, middle_grad, gain, gate_grads, up_grads, *refs
):
    refs = list(refs)
    input_out, terms_out, row_grad_out, qkv_grad_out, weight_grad_out, sums_out, everyone = [
        refs.pop(0) for _ in range(7)
    ]
    place = Place()
    gather = Gather(place, rows, everyone, refs)
    reduce = PieceReduce(place, refs)
    arrived, kept, row_grad, qkv_grad, load, store = [refs.pop(0) for _ in range(6)]
    mine, theirs, mine_sem, y_send, y_recv, z_send, z_recv, sum_local = [refs.pop(0) for _ in range(8)]
    weight, out_weight, weight_load = [refs.pop(0) for _ in range(3)]
    weight_loads = [
        pltpu.make_async_copy(weight_in, weight, weight_load.at[0]),
        pltpu.make_async_copy(out_in, out_weight, weight_load.at[1]),
    ]
    wide, model = out_weight.shape
    tile = model // 2
    width = mine.shape[2]

    def stores(sequence):
        return [
            pltpu.make_async_copy(row_grad, row_grad_out.at[sequence], store.at[0]),
            pltpu.make_async_copy(qkv_grad, qkv_grad_out.at[sequence], store.at[1]),
        ]

    def piece(index, m, k):
        sequence = m * ZS + k
        gather.piece_arrival(m, k)
        pl.when(k == 0)(lambda: gather.local(m).wait())
        loads = [
            pltpu.make_async_copy(everyone.at[m, k, dc, dx], arrived.at[dc, dx], load.at[dc, dx])
            for dc in range(CS)
            for dx in range(XS)
        ]
        loads.append(pltpu.make_async_copy(turned_qkv.at[sequence], kept, load.at[CS, 0]))
        for copy in loads:
            copy.start()

        @pl.when(index == 0)
        def _():
            for copy in weight_loads:
                copy.wait()

        @pl.when(index > 0)
        def _():
            for copy in stores(0):
                copy.wait()

        for copy in loads:
            copy.wait()
        length = kept.shape[0]
        row_gate, row_block, key_block = columns_of(marks, place, m, k)
        for start in range(0, model, tile):
            value = arrived[:, :, :, start : start + tile].astype(F32).reshape(length, tile) * row_gate
            row_grad[:, start : start + tile] = value.astype(BF16)
        qkv_grad[:, :wide] = dot_t(row_grad[...], out_weight[...]).astype(BF16)

        def head(span_of):
            query, key, value = [kept[:, span_of(kind)] for kind in range(3)]
            grad = qkv_grad[:, span_of(0)]
            probs = masked_probs(query, key, row_block, key_block)
            prob_grad = dot_t(grad, value)
            inner = jnp.sum(probs * prob_grad, axis=1, keepdims=True)
            raw_grad = (probs * (prob_grad - inner) * HDIM ** (-0.5)).astype(BF16)
            qkv_grad[:, span_of(0)] = turned(dot(raw_grad, key), cosine[...], -sine[...]).astype(BF16)
            qkv_grad[:, span_of(1)] = turned(dot_l(raw_grad, query), cosine[...], -sine[...]).astype(BF16)
            qkv_grad[:, span_of(2)] = dot_l(probs.astype(BF16), grad).astype(BF16)

        by_heads(wide, head)
        for start in range(0, model, tile):
            value = dot_t(qkv_grad[...], weight[start : start + tile, :])
            reduce.part[m, k, :, start : start + tile] = value.astype(BF16)
        for copy in stores(sequence):
            copy.start()

    steps = (1, 3, 2, 0)
    sources = (gate_grads, up_grads)

    def z_of(turn):
        return lax.rem(place.z + steps[turn], ZS)

    def own_copy(part):
        kind, turn = divmod(part, ZS)
        return pltpu.make_async_copy(sources[kind].at[z_of(turn), place.y], mine.at[part], mine_sem.at[part])

    def y_copy(part):
        kind, turn = divmod(part, ZS)
        return remote(
            sources[kind].at[z_of(turn), 1 - place.y],
            theirs.at[part],
            y_send.at[part],
            y_recv.at[part],
            place.y_peer,
        )

    columns = weight_grad_out.at[:, pl.ds(pl.multiple_of(place.z * width, HDIM), width)]

    def sum_copy(part):
        kind, turn = divmod(part, ZS)
        if kind:
            return pltpu.make_async_copy(theirs.at[part], sums_out.at[z_of(turn)], sum_local.at[part])
        if steps[turn] == 0:
            return pltpu.make_async_copy(theirs.at[part], columns, sum_local.at[part])
        return remote(
            theirs.at[part], columns, z_send.at[steps[turn]], z_recv.at[steps[turn]], place.z_peers[steps[turn]]
        )

    def pass_grads(part):
        y_copy(part).wait()
        if part + 4 < 2 * ZS:
            y_copy(part + 4).start()
        own_copy(part).wait()

        def add(span):
            value = mine[part, span, :].astype(F32) + theirs[part, span, :].astype(F32)
            theirs[part, span, :] = value.astype(BF16)

        by_rows(mine.shape[1], add)
        sum_copy(part).start()

    def between(index):
        gather_steps([gather], index)
        for part, at in enumerate((2, 3, 5, 6, 8, 9)):
            pl.when(index == at)(functools.partial(pass_grads, part))

    for copy in weight_loads:
        copy.start()
    for part in range(2 * ZS):
        own_copy(part).start()
    place.enter(True)
    for part in range(4):
        y_copy(part).start()
    begin_gathers([gather])
    run_pieces(place, reduce, piece, between)
    for part in range(6, 2 * ZS):
        pass_grads(part)
    terms_out[...] = jnp.zeros_like(terms_out)
    for m in range(gather.micro):
        reduce.finish(m)

        def body(span, m=m):
            result, found = norm_back(
                reduce.total[m, span, :], tokens[m, span, :].astype(F32), middle_grad[m, span, :], gain[...]
            )
            input_out[m, span, :] = result.astype(BF16)
            terms_out[...] += found

        by_rows(reduce.rows, body)
    for copy in stores(0):
        copy.wait()
    gather.drain(True)
    reduce.drain()
    for part in range(2 * ZS):
        sum_copy(part).wait()


def mlp_kernel(
    normed, gate_up_part, down_part, select, select_back, gates, cotangents, middle, cotangent, gain, *refs
):
    refs = list(refs)
    own_out, grad_out, terms_out, rows_out, up_grad_out, hidden_out, down_grad_out, result_out = [
        refs.pop(0) for _ in range(8)
    ]
    everyone = refs.pop(0)
    place = Place()
    gathers = [Gather(place, normed, everyone, refs)]
    reduce = PieceReduce(place, refs)
    arrived, upstream, rows, down_grad, hidden, both_grad, result = [refs.pop(0) for _ in range(7)]
    gate_weight, up_weight, down, load, store, weight_load = [refs.pop(0) for _ in range(6)]
    width = down.shape[0]
    model = middle.shape[2]
    tile = model // 2
    pieces = reduce.micro * ZS
    weight_loads = [
        pltpu.make_async_copy(source, target, weight_load.at[i])
        for i, (source, target) in enumerate(
            ((gate_up_part.at[0], gate_weight), (gate_up_part.at[1], up_weight), (down_part, down))
        )
    ]

    kept = (
        (rows, rows_out),
        (down_grad, down_grad_out),
        (hidden, hidden_out),
        (both_grad, up_grad_out),
        (result, result_out),
    )

    def store_of(number, sequence):
        here, there = kept[number]
        return pltpu.make_async_copy(here, there.at[sequence], store.at[number])

    def loads_of(number, source, target, m, k):
        return [
            pltpu.make_async_copy(source.at[m, k, dc, dx], target.at[dc, dx], load.at[number, dc, dx])
            for dc in range(CS)
            for dx in range(XS)
        ]

    def piece(index, m, k):
        for gather in gathers:
            gather.piece_arrival(m, k)
            pl.when(k == 0)(functools.partial(wait_local, gather, m))
        sequence = m * ZS + k
        loads = loads_of(0, everyone, arrived, m, k)
        for copy in loads:
            copy.start()

        def stored(*numbers):
            @pl.when(index > 0)
            def _():
                for number in numbers:
                    store_of(number, 0).wait()

        def store_out(*numbers):
            for number in numbers:
                store_of(number, sequence).start()

        @pl.when(index == 0)
        def _():
            for copy in loads_of(1, cotangents, upstream, m, k):
                copy.start()
            for copy in weight_loads:
                copy.wait()

        stored(0, 1)
        for copy in loads + loads_of(1, cotangents, upstream, m, k):
            copy.wait()
        chosen, back, gate_of_row = select[sequence], select_back[sequence], gates[sequence]
        length = select.shape[2]

        def to_rows(span):
            rows[:, span] = dot(chosen, arrived[:, :, :, span].reshape(length, tile)).astype(BF16)
            down_grad[:, span] = (dot(chosen, upstream[:, :, :, span].reshape(length, tile)) * gate_of_row).astype(BF16)

        by_lanes(model // tile, tile, to_rows)
        store_out(0, 1)

        @pl.when(index + 1 < pieces)
        def _():
            for copy in loads_of(1, cotangents, upstream, *piece_of(place, index + 1)):
                copy.start()

        stored(2, 3)

        half = width // (2 * HDIM) * HDIM
        for start, stop in ((0, half), (half, width)):
            gate = dot(rows[...], gate_weight[:, start:stop])
            up = dot(rows[...], up_weight[:, start:stop])
            hidden_grad = dot_t(down_grad[...], down[start:stop, :])
            sigma = 0.5 * jnp.tanh(0.5 * gate) + 0.5
            silu = gate * sigma
            hidden[:, start:stop] = (silu * up).astype(BF16)
            slope = sigma + silu * (1.0 - sigma)
            both_grad[:, start:stop] = (hidden_grad * up * slope).astype(BF16)
            both_grad[:, width + start : width + stop] = (hidden_grad * silu).astype(BF16)

        store_out(2, 3)
        stored(4)

        def to_tokens(span):
            row_grad = dot_t(both_grad[:, :width], gate_weight[span, :])
            row_grad = (row_grad + dot_t(both_grad[:, width:], up_weight[span, :])).astype(BF16)
            reduce.part[m, k, :, span] = dot(back, row_grad).astype(BF16)
            value = (dot(hidden[...], down[:, span]) * gate_of_row).astype(BF16)
            result[:, span] = dot(back, value).astype(BF16)

        by_lanes(model // tile, tile, to_tokens)
        store_out(4)

    for copy in weight_loads:
        copy.start()
    place.enter(False)
    begin_gathers(gathers)
    run_pieces(place, reduce, piece, functools.partial(gather_steps, gathers))
    terms_out[...] = jnp.zeros_like(terms_out)
    for m in range(reduce.micro):
        reduce.finish(m)

        def body(span, m=m):
            found, terms = norm_back(
                reduce.total[m, span, :], middle[m, span, :], cotangent[m, span, :].astype(F32), gain[...]
            )
            grad_out[m, span, :] = found
            own_out[m, span, :] = found.astype(BF16)
            terms_out[...] += terms

        by_rows(reduce.rows, body)
    for number in range(len(kept)):
        store_of(number, 0).wait()
    for gather in gathers:
        gather.drain(True)
    reduce.drain()


class Halves:
    def __init__(self, own, other, copy):
        self.own, self.other, self.copy = own, other, copy

    def begin(self):
        self.copy.start()

    def add(self):
        self.copy.wait()

        def body(index, carry):
            value = self.own[index].astype(F32) + self.other[index].astype(F32)
            self.other[index] = value.astype(BF16)
            return carry

        lax.fori_loop(0, self.other.shape[0], body, 0)


def last_kernel(part, middle, first_terms, second_terms, rows, grads, attended, row_grads, up_grad, *refs):
    refs = list(refs)
    output, gains_out, query_out, kv_out, out_out, up_out = [refs.pop(0) for _ in range(6)]
    place = Place()
    reduce = Reduce(place, part, refs)
    tall, long, load = [refs.pop(0) for _ in range(3)]
    query_all, query_in, kv_all, core_in, x_in, y_in, out_own, out_send, out_in = [refs.pop(0) for _ in range(9)]
    hop_send, hop_recv, z_send, z_recv, z_local = [refs.pop(0) for _ in range(5)]
    terms, gain_in, gain_send, gain_recv = [refs.pop(0) for _ in range(4)]
    up_send, up_recv, up_local = [refs.pop(0) for _ in range(3)]
    wide, kv_rows = query_out.shape[1] // ZS, kv_out.shape[0]
    model = tall.shape[1]
    tile = model // ZS

    def swap(number, source, target, peer):
        return remote(source, target, hop_send.at[number], hop_recv.at[number], peer)

    query = Halves(
        query_all.at[:, place.y], query_in, swap(0, query_all.at[:, 1 - place.y], query_in, place.y_peer)
    )
    over_core = Halves(
        kv_all.at[:, place.core], core_in, swap(1, kv_all.at[:, 1 - place.core], core_in, place.core_peer)
    )
    by_x = core_in.reshape(ZS * YS, XS, kv_rows, 2 * wide)
    over_x = Halves(by_x.at[:, place.x], x_in, swap(2, by_x.at[:, 1 - place.x], x_in, place.x_peer))
    by_y = x_in.reshape(ZS, YS, kv_rows, 2 * wide)
    over_y = Halves(by_y.at[:, place.y], y_in, swap(3, by_y.at[:, 1 - place.y], y_in, place.y_peer))
    over_out = swap(4, out_send, out_in, place.y_peer)

    def lanes(start):
        return pl.ds(pl.multiple_of(start, HDIM), wide)

    def z_parts(step):
        to = lax.rem(place.z + step, ZS)
        pairs = [(query_in.at[to], query_out.at[:, lanes(place.z * wide)])]
        for kind in range(2):
            pairs.append(
                (y_in.at[to, :, pl.ds(kind * wide, wide)], kv_out.at[:, lanes((kind * ZS + place.z) * wide)])
            )
        return pairs

    def z_copy(step, piece):
        source, target = z_parts(step)[piece]
        if step == 0:
            return pltpu.make_async_copy(source, target, z_local.at[piece])
        return remote(source, target, z_send.at[step, piece], z_recv.at[step, piece], place.z_peers[step])

    hops = [[place.core_peer], [place.x_peer], [place.y_peer], place.z_peers[1:]]

    def gain_copies(hop):
        return [
            remote(terms, gain_in.at[hop + i], gain_send.at[hop + i], gain_recv.at[hop + i], peer)
            for i, peer in enumerate(hops[hop])
        ]

    def send_gains(hop):
        for copy in gain_copies(hop):
            copy.start()

    def add_gains(hop):
        copies = gain_copies(hop)
        for copy in copies:
            copy.wait()
        for i in range(len(copies)):
            terms[...] += gain_in[hop + i]
        if hop + 1 < len(hops):
            send_gains(hop + 1)

    width = up_grad.shape[2]
    columns = up_out.at[:, pl.ds(pl.multiple_of(place.z * width, HDIM), width)]
    up_copies = [pltpu.make_async_copy(up_grad.at[place.z], columns, up_local)]
    for step in (1, 3, 2):
        source = up_grad.at[lax.rem(place.z + step, ZS)]
        up_copies.append(remote(source, columns, up_send.at[step], up_recv.at[step], place.z_peers[step]))
    loads = [pltpu.make_async_copy(rows, tall, load.at[0]), pltpu.make_async_copy(grads, long, load.at[1])]
    later_loads = [
        pltpu.make_async_copy(row_grads, tall, load.at[2]),
        pltpu.make_async_copy(attended, long.at[:, pl.ds(0, wide)], load.at[3]),
    ]

    def small_grads(z):
        span = slice(z * tile, (z + 1) * tile)
        value = dot_l(tall[:, span], long[:, :wide]).astype(BF16)
        query_all[z] = value.reshape(query_all.shape[1:])
        blocks = kv_all.shape[0] // ZS
        for kind in range(2):
            value = dot_l(tall[:, span], long[:, (kind + 1) * wide : (kind + 2) * wide]).astype(BF16)
            kv_all[z * blocks : (z + 1) * blocks, :, :, kind * wide : (kind + 1) * wide] = value.reshape(
                (blocks,) + kv_all.shape[1:3] + (wide,)
            )

    def out_grads():
        out_rows = out_own.shape[0]
        for start in range(0, model, model // 2):
            span = slice(start, start + model // 2)
            value = dot_l(long[:, :wide], tall[:, span])
            first, second = value[:out_rows], value[out_rows:]
            out_own[:, span] = jnp.where(place.y == 0, first, second)
            out_send[:, span] = jnp.where(place.y == 0, second, first).astype(BF16)

    for copy in loads:
        copy.start()
    place.enter(True)
    reduce.begin()
    for copy in up_copies:
        copy.start()
    terms[...] = jnp.zeros_like(terms)
    terms[0:1, :] = jnp.sum(first_terms[...], axis=0, keepdims=True)
    terms[1:2, :] = jnp.sum(second_terms[...], axis=0, keepdims=True)
    send_gains(0)
    for copy in loads:
        copy.wait()
    small_grads(0)
    reduce.pass_x(0)
    for z in range(1, ZS):
        small_grads(z)
    for copy in later_loads:
        copy.start()
    over_core.begin()
    query.begin()
    add_gains(0)
    over_core.add()
    over_x.begin()
    for m in range(1, reduce.micro):
        reduce.pass_x(m)
    add_gains(1)
    for copy in later_loads:
        copy.wait()
    out_grads()
    over_out.start()
    reduce.sums(0)
    over_x.add()
    over_y.begin()
    query.add()
    for step in (1, 3, 2, 0):
        z_copy(step, 0).start()
    add_gains(2)
    for m in range(1, reduce.micro):
        reduce.sums(m)
    over_y.add()
    for step in (1, 3, 2, 0):
        for piece in (1, 2):
            z_copy(step, piece).start()
    add_gains(3)
    gains_out[...] = terms[...]
    for m in range(reduce.micro):
        reduce.finish(m)

        def finish(span, m=m):
            output[m, span, :] = (middle[m, span, :] + reduce.total[m, span, :]).astype(BF16)

        by_rows(reduce.rows, finish)
    over_out.wait()

    def add_out(span):
        out_out[span, :] = out_own[span, :] + out_in[span, :].astype(F32)

    by_rows(out_own.shape[0], add_out)
    reduce.drain()
    for copy in up_copies:
        copy.wait()
    for step in range(ZS):
        for piece in range(3):
            z_copy(step, piece).wait()


def gate_up_grads_kernel(rows, both_grad, gate_out, up_out):
    value = dot_l(rows[...], both_grad[...]).astype(BF16)
    width = both_grad.shape[1] // 2
    gate_out[0] = value[:, :width].reshape(gate_out.shape[1:])
    up_out[0] = value[:, width:].reshape(up_out.shape[1:])


def gate_up_grads(rows, both_grad, model_rows):
    count, model = rows.shape
    width = both_grad.shape[1] // 2
    block = pl.BlockSpec((1, YS, model_rows, width), lambda z: (z, 0, 0, 0))
    return pl.pallas_call(
        gate_up_grads_kernel,
        grid=(ZS,),
        in_specs=[
            pl.BlockSpec((count, model // ZS), lambda z: (0, z)),
            pl.BlockSpec((count, 2 * width), lambda z: (0, 0)),
        ],
        out_specs=[block, block],
        out_shape=[jax.ShapeDtypeStruct((ZS, YS, model_rows, width), BF16)] * 2,
        compiler_params=pltpu.CompilerParams(vmem_limit_bytes=60 << 20),
        cost_estimate=pl.CostEstimate(
            flops=4 * count * model * width, bytes_accessed=12 * model * width, transcendentals=0
        ),
    )(rows, both_grad)


def down_grads_kernel(hidden, down_grad, down_out, small_out):
    value = dot_l(hidden[...], down_grad[...])
    down_out[...] = value
    small_out[...] = value.astype(BF16)


def down_grads(hidden, down_grad):
    count, model = down_grad.shape
    width = hidden.shape[1]
    tile = model // ZS
    return pl.pallas_call(
        down_grads_kernel,
        grid=(ZS,),
        in_specs=[
            pl.BlockSpec((count, width), lambda z: (0, 0)),
            pl.BlockSpec((count, tile), lambda z: (0, z)),
        ],
        out_specs=[pl.BlockSpec((width, tile), lambda z: (0, z))] * 2,
        out_shape=[jax.ShapeDtypeStruct((width, model), F32), jax.ShapeDtypeStruct((width, model), BF16)],
        compiler_params=pltpu.CompilerParams(vmem_limit_bytes=60 << 20),
        cost_estimate=pl.CostEstimate(
            flops=2 * count * model * width, bytes_accessed=10 * model * width, transcendentals=0
        ),
    )(hidden, down_grad)


def widen_kernel(first, second, own, other_first, other_last, kv, query, weight_out, down_out, kv_out, query_out):
    step = pl.program_id(0)
    pl.when(step < ZS)(lambda: weight_out.__setitem__(..., first[...].astype(F32)))
    pl.when(step >= ZS)(lambda: weight_out.__setitem__(..., second[...].astype(F32)))
    pl.when(step < ZS)(lambda: down_out.__setitem__(..., own[0] + other_first[...].astype(F32)))
    pl.when(step >= ZS)(lambda: down_out.__setitem__(..., own[0] + other_last[...].astype(F32)))
    kv_out[...] = kv[...].astype(F32)
    query_out[...] = query[...].astype(F32)


def widen(first, second, own, other_first, other_last, kv, query, y):
    steps = 2 * ZS
    rows, width = first.shape[0], first.shape[1] // ZS
    _, down_rows, model = own.shape
    down_step = down_rows // ZS

    def block(*dims):
        return pl.BlockSpec(dims, lambda i, y: (i // 2,) + (0,) * (len(dims) - 1))

    small = [(value.shape[0] // ZS, value.shape[1]) for value in (kv, query)]
    return pl.pallas_call(
        lambda y, *refs: widen_kernel(*refs),
        grid_spec=pltpu.PrefetchScalarGridSpec(
            num_scalar_prefetch=1,
            grid=(steps,),
            in_specs=[
                pl.BlockSpec((rows, width), lambda i, y: (0, jnp.minimum(i, ZS - 1))),
                pl.BlockSpec((rows, width), lambda i, y: (0, jnp.maximum(i - ZS, 0))),
                pl.BlockSpec((1, down_step, model), lambda i, y: (y[0], i // 2, 0)),
                pl.BlockSpec((down_step, model), lambda i, y: (jnp.minimum(i // 2, ZS // 2 - 1), 0)),
                pl.BlockSpec((down_step, model), lambda i, y: (jnp.maximum(i // 2 - ZS // 2, 0), 0)),
                block(*small[0]),
                block(*small[1]),
            ],
            out_specs=[
                pl.BlockSpec((rows, width), lambda i, y: (0, i)),
                block(down_step, model),
                block(*small[0]),
                block(*small[1]),
            ],
        ),
        out_shape=[
            jax.ShapeDtypeStruct((rows, steps * width), F32),
            jax.ShapeDtypeStruct((down_rows, model), F32),
            jax.ShapeDtypeStruct(kv.shape, F32),
            jax.ShapeDtypeStruct(query.shape, F32),
        ],
        compiler_params=pltpu.CompilerParams(vmem_limit_bytes=60 << 20),
        cost_estimate=pl.CostEstimate(flops=0, bytes_accessed=12 * rows * steps * width, transcendentals=0),
    )(jnp.full((1,), y, jnp.int32), first, second, own, other_first, other_last, kv, query)


def connect(kernel, operands, spaces, out_shapes, out_spaces, scratch, number, seconds):
    return pl.pallas_call(
        kernel,
        in_specs=spaces,
        out_specs=out_spaces,
        out_shape=out_shapes,
        scratch_shapes=scratch,
        compiler_params=pltpu.CompilerParams(
            collective_id=number, has_side_effects=True, vmem_limit_bytes=60 << 20
        ),
        cost_estimate=pl.CostEstimate(flops=0, bytes_accessed=int(seconds * 3e12), transcendentals=0),
    )(*operands)


def fast_device(
    tokens,
    cotangent,
    gain_attn,
    gain_mlp,
    w_kv,
    w_query,
    w_out,
    w_gate_up,
    w_down,
    att_routes,
    att_gates,
    mlp_routes,
    mlp_gates,
    blocks,
):
    group, owner = lax.axis_index("group"), lax.axis_index("expert")
    y = group % YS
    x, core = owner // CS, owner % CS
    micro, local, model = tokens.shape
    wide = w_query.shape[2] // ZS
    hidden_width = w_gate_up.shape[2] // (2 * ZS)
    kv_rows = w_kv.shape[0]
    model_rows = w_query.shape[1]

    def own_rows(table):
        return lax.dynamic_slice_in_dim(table, owner * local, local, 0).astype(F32)

    lines = []
    for m in range(micro):
        lines += [own_rows(att_routes[m]), att_gates[m], own_rows(mlp_routes[m]), mlp_gates[m]]
        lines += [own_rows(blocks[m, 0][:, None])]
    table = jnp.concatenate(lines, axis=1)
    table = jnp.pad(table, ((0, 0), (0, -table.shape[1] % HDIM)))[None]

    positions = (
        (x ^ jnp.arange(XS)[None, :, None]) * CS + (core ^ jnp.arange(CS)[:, None, None])
    ) * local + jnp.arange(local)[None, None, :]
    cosine, sine = angles(positions.reshape(-1))
    cosine = jnp.concatenate([cosine, cosine], axis=1)
    sine = jnp.concatenate([-sine, sine], axis=1)

    shape = (micro, local, model)
    everyone = (micro, ZS, CS, XS, local, model)
    seqs = micro * ZS
    first_gain, second_gain = gain_attn[None], gain_mlp[None]
    tall = jax.ShapeDtypeStruct(shape, F32)
    short = jax.ShapeDtypeStruct(shape, BF16)
    gathered = jax.ShapeDtypeStruct(everyone, BF16)
    terms = jax.ShapeDtypeStruct((STEP, model), F32)
    own_buffer = pltpu.VMEM(shape, BF16)

    def kept(width, rows=SEQ):
        return jax.ShapeDtypeStruct((seqs, rows, width), BF16)

    def weight(*dims):
        return jax.ShapeDtypeStruct(dims, BF16)

    marks = (ZS, CS, XS) + table.shape[1:]
    (
        normed_two,
        middle,
        normed,
        cotangents,
        table,
        turned_qkv,
        attended,
        qkv_weight,
        out_weight,
        gate_up_weight,
        down_weight,
    ) = connect(
        functools.partial(attention_kernel, (wide, kv_rows, model_rows, w_out.shape[1], w_down.shape[1])),
        [
            tokens,
            cotangent,
            first_gain,
            second_gain,
            table,
            cosine,
            sine,
            w_kv,
            w_query,
            w_out,
            w_gate_up,
            w_down,
        ],
        [VMEM] * 7 + [ANY] * 5,
        [
            short,
            tall,
            gathered,
            gathered,
            jax.ShapeDtypeStruct((1,) + marks, F32),
            kept(3 * wide),
            kept(wide),
            weight(model, 3 * wide),
            weight(wide, model),
            weight(2, model, hidden_width),
            weight(hidden_width, model),
        ],
        [VMEM, VMEM] + [ANY] * 9,
        [own_buffer]
        + Gather.scratch(micro)
        + Gather.scratch(micro)
        + Gather.scratch(1)
        + PieceReduce.scratch(*shape)
        + Spread.scratch(2, 3)
        + Spread.scratch(1, 1)
        + Spread.scratch(2, 1)
        + Share.scratch(1)
        + Share.scratch(1)
        + [
            pltpu.VMEM((CS, XS, local, model), BF16),
            pltpu.VMEM((SEQ, 3 * wide), BF16),
            pltpu.VMEM((SEQ, wide), BF16),
            pltpu.VMEM(marks, F32),
            pltpu.VMEM((model, 3 * wide), BF16),
            pltpu.VMEM((wide, model), BF16),
            DMA((CS, XS)),
            DMA((2,)),
            DMA((3,)),
        ],
        1,
        250e-6,
    )
    table = table[0]
    part = table[..., : KINDS * micro].reshape(ZS, SEQ, micro, KINDS).transpose(2, 0, 1, 3)
    part = part.reshape(seqs, SEQ, KINDS)
    hit = jnp.any(part[..., 4:6] == owner, axis=-1)
    mlp_weight = jnp.sum(jnp.where(part[..., 4:6] == owner, part[..., 6:8], 0.0), axis=-1)
    before_mask = jnp.arange(SEQ)[:, None] < jnp.arange(SEQ)[None, :]
    before = dot(hit.astype(BF16), before_mask.astype(BF16)).astype(jnp.int32)
    slots = jnp.arange(XS * CS * CAP + -XS * CS * CAP % STEP)
    chosen = hit[:, None, :] & (before[:, None, :] == slots[None, :, None])
    row_gate = jnp.sum(jnp.where(chosen, mlp_weight[:, None, :], 0.0), axis=2)
    select = chosen.astype(BF16)
    slot_count = select.shape[1]
    middle_rows, middle_grad, gain_second, rows_two, both_grad, hidden, down_grad, result_two, *_ = connect(
        mlp_kernel,
        [
            normed_two,
            gate_up_weight,
            down_weight,
            select,
            select.transpose(0, 2, 1),
            row_gate[:, :, None],
            cotangents,
            middle,
            cotangent,
            second_gain,
        ],
        [VMEM] + [ANY] * 2 + [VMEM] * 3 + [ANY] + [VMEM] * 3,
        [
            short,
            tall,
            terms,
            kept(model, slot_count),
            kept(2 * hidden_width, slot_count),
            kept(hidden_width, slot_count),
            kept(model, slot_count),
            kept(model),
            gathered,
        ],
        [VMEM, VMEM, VMEM] + [ANY] * 6,
        Gather.scratch(micro)
        + PieceReduce.scratch(*shape)
        + [
            pltpu.VMEM((CS, XS, local, model), BF16),
            pltpu.VMEM((CS, XS, local, model), BF16),
            pltpu.VMEM((slot_count, model), BF16),
            pltpu.VMEM((slot_count, model), BF16),
            pltpu.VMEM((slot_count, hidden_width), BF16),
            pltpu.VMEM((slot_count, 2 * hidden_width), BF16),
            pltpu.VMEM((SEQ, model), BF16),
            pltpu.VMEM((model, hidden_width), BF16),
            pltpu.VMEM((model, hidden_width), BF16),
            pltpu.VMEM((hidden_width, model), BF16),
            DMA((2, CS, XS)),
            DMA((5,)),
            DMA((3,)),
        ],
        5,
        150e-6,
    )
    rows_two, both_grad, hidden, down_grad = [
        value.reshape(-1, value.shape[2]) for value in (rows_two, both_grad, hidden, down_grad)
    ]
    result_two = result_two.reshape(everyone)

    grad_down, down_small = [value.reshape(YS, -1, model) for value in down_grads(hidden, down_grad)]
    down_small = take(down_small, 1 - y, 0)
    half = down_small.shape[0] // 2
    down_first, down_last = down_small[:half], down_small[half:]
    rows_two, down_first, down_last = lax.optimization_barrier((rows_two, down_first, down_last))
    down_first = y_move(down_first)
    gate_grad, up_grad = gate_up_grads(rows_two, both_grad, model_rows)
    input_grad, gain_first, result_grad, qkv_grad, gate_grad, up_grad, _ = connect(
        attend_back_kernel,
        [
            middle_rows,
            qkv_weight,
            out_weight,
            table,
            cosine,
            sine,
            turned_qkv,
            tokens,
            middle_grad,
            first_gain,
            gate_grad,
            up_grad,
        ],
        [VMEM] + [ANY] * 2 + [VMEM] * 3 + [ANY] + [VMEM] * 3 + [ANY] * 2,
        [
            short,
            terms,
            kept(model),
            kept(3 * wide),
            jax.ShapeDtypeStruct((model_rows, ZS * hidden_width), BF16),
            jax.ShapeDtypeStruct((ZS, model_rows, hidden_width), BF16),
            gathered,
        ],
        [VMEM, VMEM] + [ANY] * 5,
        Gather.scratch(micro)
        + PieceReduce.scratch(*shape)
        + [
            pltpu.VMEM((CS, XS, local, model), BF16),
            pltpu.VMEM((SEQ, 3 * wide), BF16),
            pltpu.VMEM((SEQ, model), BF16),
            pltpu.VMEM((SEQ, 3 * wide), BF16),
            DMA((CS + 1, XS)),
            DMA((2,)),
            pltpu.VMEM((2 * ZS, model_rows, hidden_width), BF16),
            pltpu.VMEM((2 * ZS, model_rows, hidden_width), BF16),
            DMA((2 * ZS,)),
            DMA((2 * ZS,)),
            DMA((2 * ZS,)),
            DMA((ZS,)),
            DMA((ZS,)),
            DMA((2 * ZS,)),
            pltpu.VMEM((model, 3 * wide), BF16),
            pltpu.VMEM((wide, model), BF16),
            DMA((2,)),
        ],
        3,
        150e-6,
    )
    down_last, input_grad = lax.optimization_barrier((down_last, input_grad))
    down_last = y_move(down_last)
    rows = seqs * SEQ
    output, gains, query_grad, kv_grad, grad_out, up_grad = connect(
        last_kernel,
        [
            result_two,
            middle,
            gain_first,
            gain_second,
            normed.reshape(rows, model),
            qkv_grad.reshape(rows, 3 * wide),
            attended.reshape(rows, wide),
            result_grad.reshape(rows, model),
            up_grad,
        ],
        [ANY, VMEM, VMEM, VMEM] + [ANY] * 5,
        [
            short,
            jax.ShapeDtypeStruct((8, model), F32),
            jax.ShapeDtypeStruct((model_rows, ZS * wide), BF16),
            jax.ShapeDtypeStruct((kv_rows, 2 * ZS * wide), BF16),
            jax.ShapeDtypeStruct(w_out.shape[1:], F32),
            weight(model_rows, ZS * hidden_width),
        ],
        [VMEM, VMEM, ANY, ANY, VMEM, ANY],
        Reduce.scratch(*shape)
        + [pltpu.VMEM((rows, model), BF16), pltpu.VMEM((rows, 3 * wide), BF16), DMA((4,))]
        + [pltpu.VMEM((ZS, YS, model_rows, wide), BF16), pltpu.VMEM((ZS, model_rows, wide), BF16)]
        + [
            pltpu.VMEM((ZS * YS * XS, CS, kv_rows, 2 * wide), BF16),
            pltpu.VMEM((ZS * YS * XS, kv_rows, 2 * wide), BF16),
            pltpu.VMEM((ZS * YS, kv_rows, 2 * wide), BF16),
            pltpu.VMEM((ZS, kv_rows, 2 * wide), BF16),
        ]
        + [pltpu.VMEM(w_out.shape[1:], kind) for kind in (F32, BF16, BF16)]
        + [DMA((5,)), DMA((5,)), DMA((ZS, 3)), DMA((ZS, 3)), DMA((3,))]
        + [pltpu.VMEM((8, model), F32), pltpu.VMEM((6, 8, model), F32), DMA((6,)), DMA((6,))]
        + [DMA((ZS,)), DMA((ZS,)), DMA],
        4,
        100e-6,
    )
    devices = ZS * YS * XS * CS
    gains = take(gains[:2].reshape(2, devices, model // devices), group * XS * CS + owner, 1)
    grad_gate_up, grad_down, kv_grad, query_grad = widen(
        gate_grad, up_grad, grad_down, down_first, down_last, kv_grad, query_grad, y
    )
    return (
        output,
        input_grad,
        gains[0],
        gains[1],
        kv_grad,
        query_grad[None],
        grad_out[None],
        grad_gate_up[None],
        grad_down[None],
    )


def solution(mesh):
    in_specs = (
        P(None, ("group", "expert"), None),
        P(None, ("group", "expert"), None),
        P(),
        P(),
        P(("group", "expert"), None),
        P("expert", "group", None),
        P("expert", "group", None),
        P("expert", "group", None),
        P("expert", "group", None),
        P(None, "group", None),
        P(None, ("group", "expert"), None),
        P(None, "group", None),
        P(None, ("group", "expert"), None),
        P(None, "group", None),
    )
    out_specs = (
        P(None, ("group", "expert"), None),
        P(None, ("group", "expert"), None),
        P(("group", "expert")),
        P(("group", "expert")),
        P(("group", "expert"), None),
        P("expert", "group", None),
        P("expert", "group", None),
        P("expert", "group", None),
        P("expert", "group", None),
    )
    body = fast_device if fits(mesh) else on_device
    return jax.shard_map(
        body, mesh=mesh, in_specs=in_specs, out_specs=out_specs, check_vma=False
    )
```
